32 devices in a mesh: dp: 4 (over z), ctx: 2 (over x), fsdp: 4 (over y, core).
Axes of the slice: x: 2, y: 2, z: 4, core: 2. Of those that a mesh axis runs over, the one named last changes fastest.
Arguments:
- hidden_in: bfloat16 [4, 1024, 2304], P('dp', ('ctx', 'fsdp')), may hold values from -6 to 6
- positions: int32 [4, 1024], P('dp', ('ctx', 'fsdp')), may hold values from 0 to 5118, as said below
- cotangent: bfloat16 [4, 1024, 2304], P('dp', ('ctx', 'fsdp')), may hold values from -6 to 6
- w_qkv: bfloat16 [2304, 4096], P(('dp', 'ctx', 'fsdp')), may hold values from -0.1875 to 0.1875
- w_out: bfloat16 [2048, 2304], P(('dp', 'ctx', 'fsdp')), may hold values from -0.125 to 0.125
- w_gate_up: bfloat16 [2304, 18432], P(('dp', 'ctx', 'fsdp')), may hold values from -0.125 to 0.125
- w_down: bfloat16 [9216, 2304], P(('dp', 'ctx', 'fsdp')), may hold values from -0.0625 to 0.0625
- gains: bfloat16 [4, 2304], P(None, ('dp', 'ctx', 'fsdp')), may hold values from -0.5 to 0.5
- m_qkv: float32 [2304, 4096], P(('dp', 'ctx', 'fsdp')), may hold values from -64.128 to 64.128
- v_qkv: float32 [2304, 4096], P(('dp', 'ctx', 'fsdp')), may hold values from 241.664 to 3878.912
- m_out: float32 [2048, 2304], P(('dp', 'ctx', 'fsdp')), may hold values from -64.128 to 64.128
- v_out: float32 [2048, 2304], P(('dp', 'ctx', 'fsdp')), may hold values from 241.664 to 3878.912
- m_gate_up: float32 [2304, 18432], P(('dp', 'ctx', 'fsdp')), may hold values from -21.312 to 21.312
- v_gate_up: float32 [2304, 18432], P(('dp', 'ctx', 'fsdp')), may hold values from 26.9312 to 431.104
- m_down: float32 [9216, 2304], P(('dp', 'ctx', 'fsdp')), may hold values from -42.624 to 42.624
- v_down: float32 [9216, 2304], P(('dp', 'ctx', 'fsdp')), may hold values from 107.7248 to 1724.416
- m_gains: float32 [4, 2304], P(None, ('dp', 'ctx', 'fsdp')), may hold values from -64.128 to 64.128
- v_gains: float32 [4, 2304], P(None, ('dp', 'ctx', 'fsdp')), may hold values from 241.664 to 3878.912
Outputs:
- block_out: bfloat16 [4, 1024, 2304], P('dp', ('ctx', 'fsdp'))
- input_grad: float32 [4, 1024, 2304], P('dp', ('ctx', 'fsdp'))
- new_qkv: float32 [2304, 4096], P(('dp', 'ctx', 'fsdp'))
- new_m_qkv: float32 [2304, 4096], P(('dp', 'ctx', 'fsdp'))
- new_v_qkv: float32 [2304, 4096], P(('dp', 'ctx', 'fsdp'))
- new_out: float32 [2048, 2304], P(('dp', 'ctx', 'fsdp'))
- new_m_out: float32 [2048, 2304], P(('dp', 'ctx', 'fsdp'))
- new_v_out: float32 [2048, 2304], P(('dp', 'ctx', 'fsdp'))
- new_gate_up: float32 [2304, 18432], P(('dp', 'ctx', 'fsdp'))
- new_m_gate_up: float32 [2304, 18432], P(('dp', 'ctx', 'fsdp'))
- new_v_gate_up: float32 [2304, 18432], P(('dp', 'ctx', 'fsdp'))
- new_down: float32 [9216, 2304], P(('dp', 'ctx', 'fsdp'))
- new_m_down: float32 [9216, 2304], P(('dp', 'ctx', 'fsdp'))
- new_v_down: float32 [9216, 2304], P(('dp', 'ctx', 'fsdp'))
- new_gains: float32 [4, 2304], P(None, ('dp', 'ctx', 'fsdp'))
- new_m_gains: float32 [4, 2304], P(None, ('dp', 'ctx', 'fsdp'))
- new_v_gains: float32 [4, 2304], P(None, ('dp', 'ctx', 'fsdp'))
The draws below stay inside these ranges and needn't reach their ends.
Inputs may be any that keep to these rules, and one draw needn't show every extreme that they name: In each sequence the stored tokens fall into 4 aligned blocks of 256 slots holding rising consecutive positions; the blocks start at p0, p0 + 256, ..., p0 + 768 for one p0 of 0 to 4095 per sequence, one sequence having p0 = 0 and another p0 = 4095; the two blocks stored at slots 2c and 2c + 1 are the blocks numbered b and 3 - b in either order.
All inputs are finite; a program needn't handle non-finite values.
Results may differ from the reference program's by a relative error of at most 0.018.
Values may be sent and summed in bfloat16 or wider, within the bound.
No kernel may reach another device: no remote copies, remote signals or barrier semaphores. Data moves between devices by JAX's collectives and lax.ppermute only.
A program may use at most 960 MiB of HBM per device.

```python
import math
import jax
import jax.numpy as jnp
from jax import lax

D = 2304
FF = 9216
HEADS = 8
KV_HEADS = 4
HEAD_DIM = 256
BLK = 256
STEP = 10
LEN = 1024
TOKENS = 4096
N_DP = 4
N_CTX = 2


def base_values(key, shape):
    return jnp.clip(jax.random.normal(key, shape, jnp.float32), -6.0, 6.0)


def draw_hidden_in(key, part):
    key = jax.random.fold_in(key, 11)
    return base_values(key, (N_DP, LEN, D)).astype(jnp.bfloat16)


def draw_w_qkv(key, part):
    key = jax.random.fold_in(key, 12)
    columns = (HEADS + 2 * KV_HEADS) * HEAD_DIM
    random_part = base_values(key, (D, columns))
    col_index = jnp.arange(columns, dtype=jnp.int32)
    rotated = col_index < (HEADS + KV_HEADS) * HEAD_DIM
    col_scale = jnp.where(rotated, 1.5, 1.0)
    return (random_part * col_scale[None, :] / D ** 0.5).astype(jnp.bfloat16)


def draw_w_gate_up(key, part):
    key = jax.random.fold_in(key, 13)
    return (base_values(key, (D, 2 * FF)) / D ** 0.5).astype(jnp.bfloat16)


def draw_positions(key, part):
    key = jax.random.fold_in(key, 7)
    key_start, key_order, key_flip, key_pick = jax.random.split(key, 4)
    starts = jax.random.randint(key_start, (N_DP,), 0, 4096).astype(jnp.int32)
    picked = jax.random.permutation(key_pick, N_DP).astype(jnp.int32)
    seq_index = jnp.arange(N_DP, dtype=jnp.int32)
    starts = jnp.where(seq_index == picked[0], 0, starts)
    starts = jnp.where(seq_index == picked[1], 4095, starts)
    starts = starts[:, None, None]
    order_keys = jax.random.split(key_order, N_DP)
    fronts = jax.vmap(lambda single: jax.random.permutation(single, N_CTX))(order_keys).astype(jnp.int32)
    backs = 2 * N_CTX - 1 - fronts
    flips = jax.random.randint(key_flip, (N_DP, N_CTX), 0, 2)
    first_block = jnp.where(flips == 1, backs, fronts)
    second_block = jnp.where(flips == 1, fronts, backs)
    blocks = jnp.stack([first_block, second_block], axis=2).reshape(N_DP, 2 * N_CTX)
    offsets = jnp.arange(BLK, dtype=jnp.int32)
    places = starts + blocks[:, :, None] * BLK + offsets[None, None, :]
    return places.reshape(N_DP, LEN).astype(jnp.int32)


def steps_of(rng, dims, cuts, smallest, high):
    def one(position, shards_of):
        heights = jax.random.uniform(jax.random.fold_in(jax.random.fold_in(rng, 6), position), (shards_of,), jnp.float32, smallest / len(cuts), high / len(cuts))
        return jnp.repeat(jnp.exp(heights), dims[position] // shards_of).reshape((-1,) + (1,) * (len(dims) - position - 1))

    factor_of = one(*cuts[0])
    for cut in cuts[1:]:
        factor_of = factor_of * one(*cut)
    return factor_of


def centred(own_key, shape, spread, bound, cuts=(), held_as=jnp.bfloat16):
    result = jax.random.normal(own_key, shape, jnp.float32) * spread
    if len(cuts) > 0:
        result = steps_of(own_key, shape, cuts, -0.22, 0.18) * result
    return jnp.clip(result, min=-bound, max=bound).astype(held_as)


def setup_inputs(seed: int = 0) -> dict:
    arg_keys = jax.random.split(jax.random.key(seed), 19)
    return {
        "hidden_in": draw_hidden_in(jax.random.fold_in(arg_keys[18], 71), 0),
        "positions": draw_positions(jax.random.fold_in(arg_keys[18], 71), 0),
        "cotangent": centred(arg_keys[2], (N_DP, LEN, D), 1.0, 6.0, ((0, 4), (1, 8))),
        "w_qkv": draw_w_qkv(jax.random.fold_in(arg_keys[18], 71), 0),
        "w_out": centred(arg_keys[4], (HEADS * HEAD_DIM, D), (HEADS * HEAD_DIM) ** -0.5, 0.125, ((0, 32),)),
        "w_gate_up": draw_w_gate_up(jax.random.fold_in(arg_keys[18], 71), 0),
        "w_down": centred(arg_keys[6], (FF, D), FF ** -0.5, 0.0625, ((0, 32),)),
        "gains": jnp.clip(jax.random.uniform(arg_keys[7], (4, D), jnp.float32, -0.5, 0.5) * steps_of(arg_keys[7], (4, D), ((1, 32),), -0.4, 0.0), -0.5, 0.5).astype(jnp.bfloat16),
        "m_qkv": centred(arg_keys[8], (D, (HEADS + 2 * KV_HEADS) * HEAD_DIM), (0.167 * TOKENS ** 0.5), 64.128, ((0, 32),), jnp.float32),
        "v_qkv": jnp.clip(jnp.exp(math.log(3878.912) - 2.7757617 * jax.random.uniform(arg_keys[9], (D, (HEADS + 2 * KV_HEADS) * HEAD_DIM), jnp.float32) ** steps_of(arg_keys[9], (D, (HEADS + 2 * KV_HEADS) * HEAD_DIM), ((0, 32),), -0.2, 0.2)), 241.664, 3878.912),
        "m_out": centred(arg_keys[10], (HEADS * HEAD_DIM, D), (0.167 * TOKENS ** 0.5), 64.128, ((0, 32),), jnp.float32),
        "v_out": jnp.clip(jnp.exp(math.log(3878.912) - 2.7757617 * jax.random.uniform(arg_keys[11], (HEADS * HEAD_DIM, D), jnp.float32) ** steps_of(arg_keys[11], (HEADS * HEAD_DIM, D), ((0, 32),), -0.2, 0.2)), 241.664, 3878.912),
        "m_gate_up": centred(arg_keys[12], (D, 2 * FF), (0.111 * (TOKENS * D / FF) ** 0.5), 21.312, ((0, 32),), jnp.float32),
        "v_gate_up": jnp.clip(jnp.exp(math.log(431.104) - 2.773064 * jax.random.uniform(arg_keys[13], (D, 2 * FF), jnp.float32) ** steps_of(arg_keys[13], (D, 2 * FF), ((0, 32),), -0.2, 0.2)), 26.9312, 431.104),
        "m_down": centred(arg_keys[14], (FF, D), (0.111 * TOKENS ** 0.5), 42.624, ((0, 32),), jnp.float32),
        "v_down": jnp.clip(jnp.exp(math.log(1724.416) - 2.773064 * jax.random.uniform(arg_keys[15], (FF, D), jnp.float32) ** steps_of(arg_keys[15], (FF, D), ((0, 32),), -0.2, 0.2)), 107.7248, 1724.416),
        "m_gains": centred(arg_keys[16], (4, D), (0.167 * TOKENS ** 0.5), 64.128, ((1, 32),), jnp.float32),
        "v_gains": jnp.clip(jnp.exp(math.log(3878.912) - 2.7757617 * jax.random.uniform(arg_keys[17], (4, D), jnp.float32) ** steps_of(arg_keys[17], (4, D), ((1, 32),), -0.2, 0.2)), 241.664, 3878.912),
    }


@jax.custom_vjp
def low(v):
    return lax.optimization_barrier(v.astype(jnp.bfloat16)).astype(jnp.float32)

@jax.custom_vjp
def low_back(v):
    return v

def low_keep(v):
    return (low(v), None)

def low_pass(kept, grad):
    return (grad,)

def back_keep(v):
    return (v, None)

def back_low(kept, grad):
    return (low(grad),)
low.defvjp(low_keep, low_pass)
low_back.defvjp(back_keep, back_low)
NORM_EPS = 1e-06
SOFT_CAP = 50.0
THETA = 10000.0
BETA_ONE = 0.9
BETA_TWO = 0.95
ADAM_EPS = 1e-08
MATRIX_RATE = 0.03
GAIN_RATE = 0.2
WEIGHT_DECAY = 0.1

def product(left, right):
    return jnp.dot(left, right, precision=lax.Precision.HIGHEST, preferred_element_type=jnp.float32)

def rms_scale(values, gain):
    inverse = lax.rsqrt(lax.optimization_barrier(jnp.mean(values * values, axis=-1, keepdims=True)) + NORM_EPS)
    return values * inverse * (1.0 + gain)

def rotary(values, places):
    half = HEAD_DIM // 2
    freqs = THETA ** (-(jnp.arange(half, dtype=jnp.float32) * 2.0 / HEAD_DIM))
    angles = places.astype(jnp.float32)[:, None] * freqs[None, :]
    cosine = jnp.cos(angles)[:, None, :]
    sine = jnp.sin(angles)[:, None, :]
    first = values[..., :half]
    second = values[..., half:]
    return jnp.concatenate([first * cosine - second * sine, second * cosine + first * sine], axis=-1)

def sequence_forward(inputs, places, w_qkv, w_out, w_gate_up, w_down, gains):
    q_width = HEADS * HEAD_DIM
    k_width = KV_HEADS * HEAD_DIM
    groups = HEADS // KV_HEADS
    normed = low(rms_scale(inputs, gains[0]))
    qkv = product(normed, w_qkv)
    query = low_back(qkv[:, :q_width]).reshape(LEN, HEADS, HEAD_DIM)
    key = low_back(qkv[:, q_width:q_width + k_width]).reshape(LEN, KV_HEADS, HEAD_DIM)
    value = low(low_back(qkv[:, q_width + k_width:])).reshape(LEN, KV_HEADS, HEAD_DIM)
    query = low(rotary(query, places) * HEAD_DIM ** (-0.5)).reshape(LEN, KV_HEADS, groups, HEAD_DIM)
    key = low(rotary(key, places))

    def attend_block(pair):
        q_block, p_block = pair
        scores = low_back(jnp.einsum('tgjd,sgd->gjts', q_block, key, precision=lax.Precision.HIGHEST))
        capped = SOFT_CAP * jnp.tanh(scores / SOFT_CAP)
        allowed = p_block[:, None] >= places[None, :]
        weights = jnp.where(allowed, jnp.exp(capped), 0.0)
        total = lax.optimization_barrier(jnp.sum(weights, axis=-1))
        summed = low_back(jnp.einsum('gjts,sgd->gjtd', low(weights), value, precision=lax.Precision.HIGHEST))
        return summed / total[..., None]
    blocks = LEN // BLK
    q_blocks = query.reshape(blocks, BLK, KV_HEADS, groups, HEAD_DIM)
    p_blocks = places.reshape(blocks, BLK)
    attended = lax.map(jax.checkpoint(attend_block), (q_blocks, p_blocks))
    attended = jnp.transpose(attended, (0, 3, 1, 2, 4)).reshape(LEN, q_width)
    mixed = low_back(product(low(attended), w_out))
    resid = inputs + rms_scale(mixed, gains[1])
    normed_two = low(rms_scale(resid, gains[2]))
    gate_up = product(normed_two, w_gate_up)
    gate = low_back(gate_up[:, :FF])
    up_part = low_back(gate_up[:, FF:])
    inner = low(jax.nn.gelu(gate, approximate=True) * up_part)
    down = low_back(product(inner, w_down))
    return resid + rms_scale(down, gains[3])

def adam_step(weight, grad, first, second, rate, decay):
    first_new = BETA_ONE * first + (1.0 - BETA_ONE) * grad
    second_new = BETA_TWO * second + (1.0 - BETA_TWO) * grad * grad
    ratio = first_new / (1.0 - BETA_ONE ** STEP) / (jnp.sqrt(second_new / (1.0 - BETA_TWO ** STEP)) + ADAM_EPS)
    return (weight - rate * (ratio + decay * weight), first_new, second_new)

def reference(hidden_in, positions, cotangent, w_qkv, w_out, w_gate_up, w_down, gains, m_qkv, v_qkv, m_out, v_out, m_gate_up, v_gate_up, m_down, v_down, m_gains, v_gains):
    params = tuple((w.astype(jnp.float32) for w in (w_qkv, w_out, w_gate_up, w_down, gains)))
    inputs = hidden_in.astype(jnp.float32)

    def forward(inputs, p_qkv, p_out, p_gate_up, p_down, p_gains):

        def one_sequence(pair):
            return sequence_forward(pair[0], pair[1], p_qkv, p_out, p_gate_up, p_down, p_gains)
        return lax.map(jax.checkpoint(one_sequence), (inputs, positions))
    outputs, pullback = jax.vjp(forward, inputs, *params)
    grads = pullback(cotangent.astype(jnp.float32))
    input_grad = grads[0]
    new_qkv, new_m_qkv, new_v_qkv = adam_step(params[0], grads[1], m_qkv, v_qkv, MATRIX_RATE, WEIGHT_DECAY)
    new_out, new_m_out, new_v_out = adam_step(params[1], grads[2], m_out, v_out, MATRIX_RATE, WEIGHT_DECAY)
    new_gate_up, new_m_gate_up, new_v_gate_up = adam_step(params[2], grads[3], m_gate_up, v_gate_up, MATRIX_RATE, WEIGHT_DECAY)
    new_down, new_m_down, new_v_down = adam_step(params[3], grads[4], m_down, v_down, MATRIX_RATE, WEIGHT_DECAY)
    new_gains, new_m_gains, new_v_gains = adam_step(params[4], grads[5], m_gains, v_gains, GAIN_RATE, 0.0)
    return (outputs.astype(jnp.bfloat16), input_grad, new_qkv, new_m_qkv, new_v_qkv, new_out, new_m_out, new_v_out, new_gate_up, new_m_gate_up, new_v_gate_up, new_down, new_m_down, new_v_down, new_gains, new_m_gains, new_v_gains)
```

```python
import jax
import jax.numpy as jnp
from jax import lax
from jax.sharding import Mesh, PartitionSpec as P

HEADS = 8
KV_HEADS = 4
HEAD_DIM = 256
STEP = 10

NORM_EPS = 1e-06
SOFT_CAP = 50.0
THETA = 10000.0
BETA_ONE = 0.9
BETA_TWO = 0.95
ADAM_EPS = 1e-08
MATRIX_RATE = 0.03
GAIN_RATE = 0.2
WEIGHT_DECAY = 0.1

DP = ("dh", "dl")
PLANE = ("ctx", "fy", "core")
ALL = DP + PLANE
GROUP = PLANE
ACROSS = DP


def f32(v):
    return v.astype(jnp.float32)


def bf(v):
    return v.astype(jnp.bfloat16)


def dot(left, right, dims):
    return lax.dot_general(left, right, (dims, ((), ())), preferred_element_type=jnp.float32)


def mm(left, right):
    return dot(left, right, ((1,), (0,)))


def mm_nt(left, right):
    return dot(left, right, ((1,), (1,)))


def mm_tn(left, right):
    return dot(left, right, ((0,), (0,)))


def rms_scale(values, gain):
    inverse = lax.rsqrt(jnp.mean(values * values, axis=-1, keepdims=True) + NORM_EPS)
    return values * inverse * (1.0 + gain)


def rotary_tables(places):
    half = HEAD_DIM // 2
    freqs = THETA ** (-(jnp.arange(half, dtype=jnp.float32) * 2.0 / HEAD_DIM))
    angles = f32(places)[:, None] * freqs[None, :]
    return (jnp.cos(angles), jnp.sin(angles))


def rotary(values, cosine, sine):
    half = HEAD_DIM // 2
    first = values[..., :half]
    second = values[..., half:]
    return jnp.concatenate(
        [first * cosine - second * sine, second * cosine + first * sine], axis=-1
    )


def unrotary(values, cosine, sine):
    return rotary(values, cosine, -sine)


def adam_step(weight, grad, first, second, rate, decay):
    first_new = BETA_ONE * first + (1.0 - BETA_ONE) * grad
    second_new = BETA_TWO * second + (1.0 - BETA_TWO) * grad * grad
    ratio = (
        first_new
        / (1.0 - BETA_ONE**STEP)
        / (jnp.sqrt(second_new / (1.0 - BETA_TWO**STEP)) + ADAM_EPS)
    )
    return (weight - rate * (ratio + decay * weight), first_new, second_new)


def gather(v, axes, axis=0):
    return lax.all_gather(v, axes, axis=axis, tiled=True)


def scatter_sum(v, axes):
    return lax.psum_scatter(v, axes, scatter_dimension=0, tiled=True)


def swap(v, axes):
    return lax.all_to_all(v, axes, split_axis=0, concat_axis=0, tiled=True)


def exchange(v, axes):
    count = lax.axis_size(axes)
    me = lax.axis_index(axes)
    got = [lax.dynamic_index_in_dim(v, me, 0, keepdims=False)]
    for step in range(1, count):
        pairs = [(i, i ^ step) for i in range(count)]
        piece = lax.dynamic_index_in_dim(v, me ^ step, 0, keepdims=False)
        got.append(lax.ppermute(piece, axes, pairs))
    return jnp.take(jnp.stack(got), jnp.arange(count) ^ me, axis=0)


def score_parts(query, key, pos_q, pos_k):
    scores = mm_nt(query, key)
    capped = SOFT_CAP * jnp.tanh(scores / SOFT_CAP)
    weights = jnp.where(pos_q[:, None] >= pos_k[None, :], jnp.exp(capped), 0.0)
    return capped, weights


def head_attention(x_own, pos_own, w_qkv, w_out, gains):
    rows = w_qkv.shape[0]
    tok = x_own.shape[0]
    width = x_own.shape[1]
    planes = lax.axis_size(DP)
    q_width = HEADS * HEAD_DIM
    core = lax.axis_index("core")
    x_all = gather(x_own, PLANE)
    pos_all = gather(pos_own, PLANE)
    q_cols = w_qkv[:, :q_width].reshape(rows, HEADS, HEAD_DIM)
    kv_cols = w_qkv[:, q_width:].reshape(rows, 2, KV_HEADS, HEAD_DIM)
    kv_cols = jnp.swapaxes(kv_cols, 1, 2).reshape(rows, HEADS, HEAD_DIM)
    pieces = jnp.swapaxes(jnp.concatenate([q_cols, kv_cols], axis=2), 0, 1)
    own_gains = gains.reshape(1, 1, 4 * rows)
    own_gains = jnp.pad(own_gains, ((0, 0), (0, 7), (0, 2 * HEAD_DIM - 4 * rows)))
    pieces = jnp.concatenate(
        [pieces, jnp.broadcast_to(own_gains, (HEADS,) + own_gains.shape[1:])], axis=1
    )
    got = gather(swap(pieces, PLANE), DP)
    w_own = got[:, :rows].reshape(width, 2 * HEAD_DIM)
    gain_vals = got[:, rows, : 4 * rows].reshape(planes * HEADS, 4, rows)
    gain_vals = f32(jnp.swapaxes(gain_vals, 0, 1).reshape(4, width))
    out_full = gather(w_out, ALL)

    normed_all = bf(rms_scale(f32(x_all), gain_vals[0]))
    qkv = mm(normed_all, w_own)
    cosine, sine = rotary_tables(pos_all)
    query = bf(rotary(qkv[:, :HEAD_DIM], cosine, sine) * HEAD_DIM ** (-0.5))
    half = qkv[:, HEAD_DIM:]
    mine = jnp.where(core == 0, bf(rotary(half, cosine, sine)), bf(half))
    flip = [(0, 1), (1, 0)]
    other = lax.ppermute(mine, "core", flip)
    key = jnp.where(core == 0, mine, other)
    value = jnp.where(core == 0, other, mine)
    capped, weights = score_parts(query, key, pos_all, pos_all)
    weights_b = bf(weights)
    total = jnp.sum(weights, axis=-1, keepdims=True)
    attn = mm(weights_b, value) / total
    attn_own = exchange(bf(attn).reshape(HEADS, tok, HEAD_DIM), PLANE)
    attn_own = jnp.swapaxes(attn_own, 0, 1).reshape(tok, q_width)
    mixed = mm(attn_own, out_full)

    def backward(grad_mixed_b):
        grad_attn = bf(mm_nt(grad_mixed_b, out_full)).reshape(tok, HEADS, HEAD_DIM)
        grad_head = exchange(jnp.swapaxes(grad_attn, 0, 1), PLANE).reshape(HEADS * tok, HEAD_DIM)
        grad_head = f32(grad_head)
        rho = bf(grad_head / total)
        delta = jnp.sum(grad_head * attn, axis=-1, keepdims=True) / total
        pulled = mm_nt(rho, value)
        grad_scores = bf((pulled - delta) * weights * (1.0 - (capped / SOFT_CAP) ** 2))
        grad_query = mm(grad_scores, key) * HEAD_DIM ** (-0.5)
        grad_key = mm_tn(grad_scores, query)
        grad_value = mm_tn(weights_b, rho)
        sent = lax.ppermute(jnp.where(core == 0, grad_value, grad_key), "core", flip)
        grad_half = jnp.where(core == 0, grad_key, grad_value) + sent
        grad_half = jnp.where(core == 0, unrotary(grad_half, cosine, sine), grad_half)
        grad_qkv = bf(jnp.concatenate([unrotary(grad_query, cosine, sine), grad_half], axis=1))
        grad_normed = f32(scatter_sum(bf(mm_nt(grad_qkv, w_own)), PLANE))
        grad_out_w = f32(scatter_sum(bf(mm_tn(attn_own, grad_mixed_b)), ALL))
        grad_w = swap(scatter_sum(bf(mm_tn(normed_all, grad_qkv)), DP), PLANE)
        grad_w = f32(jnp.swapaxes(grad_w.reshape(HEADS, rows, 2 * HEAD_DIM), 0, 1))
        grad_q_w = grad_w[:, :, :HEAD_DIM].reshape(rows, q_width)
        grad_kv_w = grad_w[:, :, HEAD_DIM:].reshape(rows, KV_HEADS, 2, HEAD_DIM)
        grad_kv_w = jnp.swapaxes(grad_kv_w, 1, 2).reshape(rows, q_width)
        return grad_normed, jnp.concatenate([grad_q_w, grad_kv_w], axis=1), grad_out_w

    return mixed, gain_vals, backward


def token_attention(x_own, pos_own, w_qkv, w_out, gains):
    tok = x_own.shape[0]
    q_width = HEADS * HEAD_DIM
    k_width = KV_HEADS * HEAD_DIM
    groups = HEADS // KV_HEADS
    qkv_full = gather(w_qkv, ALL)
    out_full = gather(w_out, ALL)
    gain_vals = f32(gather(gains, ALL, 1))
    normed = bf(rms_scale(f32(x_own), gain_vals[0]))
    qkv = mm(normed, qkv_full)
    cosine, sine = rotary_tables(pos_own)
    cosine, sine = (cosine[:, None, :], sine[:, None, :])
    query = rotary(qkv[:, :q_width].reshape(tok, HEADS, HEAD_DIM), cosine, sine)
    query = bf(query * HEAD_DIM ** (-0.5)).reshape(tok, KV_HEADS, groups, HEAD_DIM)
    key_own = qkv[:, q_width : q_width + k_width].reshape(tok, KV_HEADS, HEAD_DIM)
    key = gather(bf(rotary(key_own, cosine, sine)), PLANE)
    value = gather(bf(qkv[:, q_width + k_width :]).reshape(tok, KV_HEADS, HEAD_DIM), PLANE)
    pos_all = gather(pos_own, PLANE)
    count = pos_all.shape[0]
    scores = jnp.einsum("tgjd,sgd->gjts", query, key, preferred_element_type=jnp.float32)
    capped = SOFT_CAP * jnp.tanh(scores / SOFT_CAP)
    weights = jnp.where(pos_own[:, None] >= pos_all[None, :], jnp.exp(capped), 0.0)
    weights_b = bf(weights)
    total = jnp.sum(weights, axis=-1)
    attn = jnp.einsum("gjts,sgd->gjtd", weights_b, value, preferred_element_type=jnp.float32)
    attn = attn / total[..., None]
    attn_b = bf(jnp.transpose(attn, (2, 0, 1, 3)).reshape(tok, q_width))
    mixed = mm(attn_b, out_full)

    def backward(grad_mixed_b):
        grad_attn = mm_nt(grad_mixed_b, out_full).reshape(tok, KV_HEADS, groups, HEAD_DIM)
        grad_heads = jnp.transpose(grad_attn, (1, 2, 0, 3))
        rho = bf(grad_heads / total[..., None])
        delta = jnp.sum(grad_heads * attn, axis=-1) / total
        pulled = jnp.einsum("gjtd,sgd->gjts", rho, value, preferred_element_type=jnp.float32)
        grad_scores = bf(
            (pulled - delta[..., None]) * weights * (1.0 - (capped / SOFT_CAP) ** 2)
        )
        grad_query = jnp.einsum(
            "gjts,sgd->tgjd", grad_scores, key, preferred_element_type=jnp.float32
        ).reshape(tok, HEADS, HEAD_DIM)
        grad_key = jnp.einsum(
            "gjts,tgjd->sgd", grad_scores, query, preferred_element_type=jnp.float32
        ).reshape(count, k_width)
        grad_value = jnp.einsum(
            "gjts,gjtd->sgd", weights_b, rho, preferred_element_type=jnp.float32
        ).reshape(count, k_width)
        grad_kv = scatter_sum(jnp.concatenate([grad_key, grad_value], axis=1), PLANE)
        grad_query = unrotary(grad_query * HEAD_DIM ** (-0.5), cosine, sine)
        grad_key = unrotary(grad_kv[:, :k_width].reshape(tok, KV_HEADS, HEAD_DIM), cosine, sine)
        grad_qkv = bf(
            jnp.concatenate(
                [
                    grad_query.reshape(tok, q_width),
                    grad_key.reshape(tok, k_width),
                    grad_kv[:, k_width:],
                ],
                axis=1,
            )
        )
        grad_normed = mm_nt(grad_qkv, qkv_full)
        grad_qkv_w = f32(scatter_sum(bf(mm_tn(normed, grad_qkv)), ALL))
        grad_out_w = f32(scatter_sum(bf(mm_tn(attn_b, grad_mixed_b)), ALL))
        return grad_normed, grad_qkv_w, grad_out_w

    return mixed, gain_vals, backward


def shards(
    hidden_in,
    positions,
    cotangent,
    w_qkv,
    w_out,
    w_gate_up,
    w_down,
    gains,
    m_qkv,
    v_qkv,
    m_out,
    v_out,
    m_gate_up,
    v_gate_up,
    m_down,
    v_down,
    m_gains,
    v_gains,
):
    x_own = hidden_in[0]
    rows, width = (w_qkv.shape[0], x_own.shape[1])
    group, across = (lax.axis_size(GROUP), lax.axis_size(ACROSS))
    ff_piece = w_down.shape[0]
    ff_own = across * ff_piece
    gu_pieces = w_gate_up.reshape(rows, 2, across, group, ff_piece)
    gu_pieces = jnp.transpose(gu_pieces, (3, 0, 1, 2, 4)).reshape(group * rows, 2 * ff_own)

    attention = head_attention if lax.axis_size(PLANE) == HEADS else token_attention
    mixed, gain_vals, attention_back = attention(x_own, positions[0], w_qkv, w_out, gains)
    gu_own = gather(swap(gu_pieces, GROUP), ACROSS)
    down_own = gather(w_down, ACROSS)

    x_rows = f32(x_own)
    branch_one, pull_one = jax.vjp(rms_scale, mixed, gain_vals[1])
    resid = x_rows + branch_one
    normed_two, pull_two = jax.vjp(rms_scale, resid, gain_vals[2])
    tokens_b = gather(bf(normed_two), GROUP)
    gate_up = mm(tokens_b, gu_own)
    inner, pull_gelu = jax.vjp(
        lambda gate, up_part: jax.nn.gelu(gate, approximate=True) * up_part,
        gate_up[:, :ff_own],
        gate_up[:, ff_own:],
    )
    inner_b = bf(inner)
    down = f32(scatter_sum(bf(mm(inner_b, down_own)), GROUP))
    branch_two, pull_three = jax.vjp(rms_scale, down, gain_vals[3])
    block_out = bf(resid + branch_two)[None]
    grad_top = f32(cotangent[0])
    grad_down_in, gain_grad_three = pull_three(grad_top)
    grad_down_b = gather(bf(grad_down_in), GROUP)
    grad_gate, grad_up = pull_gelu(mm_nt(grad_down_b, down_own))
    grad_gu_b = bf(jnp.concatenate([grad_gate, grad_up], axis=1))
    grad_normed_two = f32(scatter_sum(bf(mm_nt(grad_gu_b, gu_own)), GROUP))
    grad_gate_up_w = scatter_sum(bf(mm_tn(tokens_b, grad_gu_b)), ACROSS)
    grad_down_w = f32(scatter_sum(bf(mm_tn(inner_b, grad_down_b)), ACROSS))

    grad_resid_two, gain_grad_two = pull_two(grad_normed_two)
    grad_resid = grad_top + grad_resid_two
    grad_mixed, gain_grad_one = pull_one(grad_resid)
    grad_normed, grad_qkv_w, grad_out_w = attention_back(bf(grad_mixed))
    _, pull_zero = jax.vjp(rms_scale, x_rows, gain_vals[0])
    grad_x_zero, gain_grad_zero = pull_zero(grad_normed)
    input_grad = (grad_resid + grad_x_zero)[None]

    grad_gate_up_w = swap(grad_gate_up_w, GROUP).reshape(group, rows, 2, across, ff_piece)
    grad_gate_up_w = f32(jnp.transpose(grad_gate_up_w, (1, 2, 3, 0, 4)).reshape(rows, -1))
    gain_term = jnp.stack([gain_grad_zero, gain_grad_one, gain_grad_two, gain_grad_three], axis=0)
    grad_gains = lax.psum_scatter(gain_term, ALL, scatter_dimension=1, tiled=True)

    return (
        (block_out, input_grad)
        + adam_step(f32(w_qkv), grad_qkv_w, m_qkv, v_qkv, MATRIX_RATE, WEIGHT_DECAY)
        + adam_step(f32(w_out), grad_out_w, m_out, v_out, MATRIX_RATE, WEIGHT_DECAY)
        + adam_step(f32(w_gate_up), grad_gate_up_w, m_gate_up, v_gate_up, MATRIX_RATE, WEIGHT_DECAY)
        + adam_step(f32(w_down), grad_down_w, m_down, v_down, MATRIX_RATE, WEIGHT_DECAY)
        + adam_step(f32(gains), grad_gains, m_gains, v_gains, GAIN_RATE, 0.0)
    )


def solution(mesh):
    sizes = dict(mesh.shape)
    fine = Mesh(
        mesh.devices.reshape(sizes["dp"] // 2, 2, sizes["ctx"], sizes["fsdp"] // 2, 2),
        ("dh", "dl", "ctx", "fy", "core"),
    )
    acts = P(DP, PLANE, None)
    mats = P(ALL, None)
    vecs = P(None, ALL)
    return jax.shard_map(
        shards,
        mesh=fine,
        in_specs=(acts, P(DP, PLANE), acts) + (mats,) * 4 + (vecs,) + (mats,) * 8 + (vecs,) * 2,
        out_specs=(acts, acts) + (mats,) * 12 + (vecs,) * 3,
        check_vma=False,
    )
```

```python
import jax
import jax.numpy as jnp
from jax import lax
from jax.sharding import Mesh, PartitionSpec as P

HEADS = 8
KV_HEADS = 4
HEAD_DIM = 256
STEP = 10

NORM_EPS = 1e-06
SOFT_CAP = 50.0
THETA = 10000.0
BETA_ONE = 0.9
BETA_TWO = 0.95
ADAM_EPS = 1e-08
MATRIX_RATE = 0.03
GAIN_RATE = 0.2
WEIGHT_DECAY = 0.1

DP = ("dh", "dl")
PLANE = ("ctx", "fy", "core")
ALL = DP + PLANE
LADDER = DP + ("ctx",)
GROUP = PLANE
ACROSS = DP
ORDER = (0, 2, 4, 6, 1, 3, 5, 7)


def f32(v):
    return v.astype(jnp.float32)


def bf(v):
    return v.astype(jnp.bfloat16)


def dot(left, right, dims):
    return lax.dot_general(left, right, (dims, ((), ())), preferred_element_type=jnp.float32)


def mm(left, right):
    return dot(left, right, ((1,), (0,)))


def mm_nt(left, right):
    return dot(left, right, ((1,), (1,)))


def mm_tn(left, right):
    return dot(left, right, ((0,), (0,)))


def rms_scale(values, gain):
    inverse = lax.rsqrt(jnp.mean(values * values, axis=-1, keepdims=True) + NORM_EPS)
    return values * inverse * (1.0 + gain)


def rotary_tables(places):
    half = HEAD_DIM // 2
    freqs = THETA ** (-(jnp.arange(half, dtype=jnp.float32) * 2.0 / HEAD_DIM))
    angles = f32(places)[:, None] * freqs[None, :]
    return (jnp.cos(angles), jnp.sin(angles))


def rotary(values, cosine, sine):
    half = HEAD_DIM // 2
    first = values[..., :half]
    second = values[..., half:]
    return jnp.concatenate(
        [first * cosine - second * sine, second * cosine + first * sine], axis=-1
    )


def unrotary(values, cosine, sine):
    return rotary(values, cosine, -sine)


def adam_step(weight, grad, first, second, rate, decay):
    first_new = BETA_ONE * first + (1.0 - BETA_ONE) * grad
    second_new = BETA_TWO * second + (1.0 - BETA_TWO) * grad * grad
    ratio = (
        first_new
        / (1.0 - BETA_ONE**STEP)
        / (jnp.sqrt(second_new / (1.0 - BETA_TWO**STEP)) + ADAM_EPS)
    )
    return (weight - rate * (ratio + decay * weight), first_new, second_new)


def gather(v, axes, axis=0):
    return lax.all_gather(v, axes, axis=axis, tiled=True)


def scatter_sum(v, axes):
    return lax.psum_scatter(v, axes, scatter_dimension=0, tiled=True)


def swap(v, axes):
    return lax.all_to_all(v, axes, split_axis=0, concat_axis=0, tiled=True)


def hold(v):
    return lax.optimization_barrier(v)


def flip(v, axis):
    return lax.ppermute(v, axis, [(0, 1), (1, 0)])


def differ(v, axes, bits):
    count = lax.axis_size(axes)
    return lax.ppermute(v, axes, [(i, i ^ bits) for i in range(count)])


def exchange(v, axes):
    count = lax.axis_size(axes)
    me = lax.axis_index(axes)
    sent = jnp.take(v, jnp.arange(count) ^ me, axis=0)
    got = [sent[0]] + [differ(sent[bits], axes, bits) for bits in range(1, count)]
    return jnp.take(jnp.stack(got), jnp.arange(count) ^ me, axis=0)


def plane_gather(own):
    half = own.shape[0] // 2
    over_x = flip(own, "ctx")
    over_y = flip(own, "fy")
    corner = [flip(over_y[:half], "ctx"), flip(over_x[half:], "fy")]
    mine = [own, over_y, over_x] + corner
    return jnp.concatenate(mine + [flip(v, "core") for v in mine], axis=0)


def plane_scatter(parts):
    size = parts.shape[0] // 8
    half = size // 2
    got = flip(parts[4 * size :], "core")
    both = bf(f32(parts[: 4 * size]) + f32(got))
    own, over_y, over_x, corner = (both[i * size : (i + 1) * size] for i in range(4))
    got_y = flip(corner[:half], "ctx")
    got_x = flip(corner[half:], "fy")
    over_y = jnp.concatenate([bf(f32(over_y[:half]) + f32(got_y)), over_y[half:]], axis=0)
    over_x = jnp.concatenate([over_x[:half], bf(f32(over_x[half:]) + f32(got_x))], axis=0)
    return f32(own) + f32(flip(over_x, "ctx")) + f32(flip(over_y, "fy"))


def line_gather(own):
    count = lax.axis_size(DP)
    ups, downs = ([], [])
    up, down = (own, own)
    for step in range(1, count):
        up = lax.ppermute(up, DP, [(i, i + 1) for i in range(step - 1, count - 1)])
        down = lax.ppermute(down, DP, [(i + 1, i) for i in range(count - step)])
        ups.append(up)
        downs.append(down)
    row = jnp.stack(ups[::-1] + [own] + downs)
    return lax.dynamic_slice_in_dim(row, count - 1 - lax.axis_index(DP), count, axis=0)


def line_scatter(parts):
    count = lax.axis_size(DP)
    me = lax.axis_index(DP)
    total = f32(lax.dynamic_index_in_dim(parts, me, 0, keepdims=False))
    for step in range(1, count):
        piece = lax.dynamic_index_in_dim(parts, (me + step) % count, 0, keepdims=False)
        total = total + f32(lax.ppermute(piece, DP, [(i, (i + step) % count) for i in range(count)]))
    return total


def ring_pairs():
    count = lax.axis_size(DP)
    ring = [2 * z for z in range(count)] + [2 * z + 1 for z in reversed(range(count))]
    onward = [(ring[i], ring[(i + 1) % len(ring)]) for i in range(len(ring))]
    return onward, [(b, a) for a, b in onward]


def ring_gather(own):
    onward, back = ring_pairs()
    half = own.shape[0] // 2
    pieces = [own]
    behind, ahead = (own, own)
    for _ in range(len(onward) // 2 - 1):
        behind = lax.ppermute(behind, LADDER, onward)
        ahead = lax.ppermute(ahead, LADDER, back)
        pieces.append(jnp.concatenate([behind, ahead], axis=0))
    last = [
        lax.ppermute(behind[:half], LADDER, onward),
        lax.ppermute(ahead[half:], LADDER, back),
    ]
    return pieces + [jnp.concatenate(last, axis=0)]


def ring_scatter(pieces):
    onward, back = ring_pairs()
    size = pieces[0].shape[0]
    half = size // 2
    ahead = lax.ppermute(pieces[-1][:half], LADDER, onward)
    behind = lax.ppermute(pieces[-1][half:], LADDER, back)
    for step in range(len(pieces) - 2, 0, -1):
        to_behind, to_ahead = (pieces[step][:size], pieces[step][size:])
        if step == len(pieces) - 2:
            to_ahead = jnp.concatenate(
                [bf(f32(to_ahead[:half]) + f32(ahead)), to_ahead[half:]], axis=0
            )
            to_behind = jnp.concatenate(
                [to_behind[:half], bf(f32(to_behind[half:]) + f32(behind))], axis=0
            )
        else:
            to_ahead = bf(f32(to_ahead) + f32(ahead))
            to_behind = bf(f32(to_behind) + f32(behind))
        ahead = lax.ppermute(to_ahead, LADDER, onward)
        behind = lax.ppermute(to_behind, LADDER, back)
    return f32(pieces[0]) + f32(ahead) + f32(behind)


def quad_gather(own):
    over_y = flip(own, "fy")
    blocks = [own, flip(own, "core"), over_y, flip(over_y, "core")]
    me = lax.axis_index(("fy", "core"))
    whole = jnp.zeros(own.shape[:1] + (4,) + own.shape[1:], own.dtype)
    for bits, block in enumerate(blocks):
        whole = lax.dynamic_update_index_in_dim(whole, block, me ^ bits, 1)
    return whole


def quad_scatter(parts):
    core, row = (lax.axis_index("core"), lax.axis_index("fy"))
    parts = parts.reshape(parts.shape[:1] + (2, 2) + parts.shape[2:])
    sent = lax.dynamic_index_in_dim(parts, 1 - core, 2, keepdims=False)
    kept = lax.dynamic_index_in_dim(parts, core, 2, keepdims=False)
    both = bf(f32(kept) + f32(flip(sent, "core")))
    sent = lax.dynamic_index_in_dim(both, 1 - row, 1, keepdims=False)
    kept = lax.dynamic_index_in_dim(both, row, 1, keepdims=False)
    return bf(f32(kept) + f32(flip(sent, "fy")))


def ladder_shards(
    hidden_in,
    positions,
    cotangent,
    w_qkv,
    w_out,
    w_gate_up,
    w_down,
    gains,
    m_qkv,
    v_qkv,
    m_out,
    v_out,
    m_gate_up,
    v_gate_up,
    m_down,
    v_down,
    m_gains,
    v_gains,
):
    x_own = hidden_in[0]
    tok, width = x_own.shape
    rows = w_qkv.shape[0]
    planes = lax.axis_size(DP)
    group = lax.axis_size(LADDER)
    q_width = HEADS * HEAD_DIM
    core = lax.axis_index("core")
    spot = lax.axis_index(PLANE)

    q_cols = w_qkv[:, :q_width].reshape(rows, HEADS, HEAD_DIM)
    kv_cols = w_qkv[:, q_width:].reshape(rows, 2, KV_HEADS, HEAD_DIM)
    kv_cols = jnp.swapaxes(kv_cols, 1, 2).reshape(rows, HEADS, HEAD_DIM)
    pieces = jnp.swapaxes(jnp.concatenate([q_cols, kv_cols], axis=2), 0, 1)
    own_gains = gains.reshape(1, 1, 4 * rows)
    own_gains = jnp.pad(own_gains, ((0, 0), (0, 7), (0, 2 * HEAD_DIM - 4 * rows)))
    pieces = jnp.concatenate(
        [pieces, jnp.broadcast_to(own_gains, (HEADS,) + own_gains.shape[1:])], axis=1
    )
    got = line_gather(exchange(pieces, PLANE))
    w_own = got[:, :, :rows].reshape(width, 2 * HEAD_DIM)
    gain_vals = got[:, :, rows, : 4 * rows].reshape(planes * HEADS, 4, rows)
    gain_vals = f32(jnp.swapaxes(gain_vals, 0, 1).reshape(4, width))
    out_full = gather(w_out, ALL)

    x_all = plane_gather(x_own)
    pos_all = positions
    for axis in ("fy", "ctx", "core"):
        pos_all = jnp.concatenate([pos_all, flip(pos_all, axis)], axis=0)
    pos_all = pos_all.reshape(-1)
    cosine, sine = rotary_tables(pos_all)

    ff_own = w_down.shape[0] * 4
    halves = []
    for part in range(2):
        cols = w_gate_up[:, part * group * ff_own : (part + 1) * group * ff_own]
        cols = jnp.swapaxes(cols.reshape(rows, group, ff_own), 0, 1)
        halves.append(exchange(cols, LADDER))
    down_own = quad_gather(w_down[None]).reshape(ff_own, width)
    gate_up_own = quad_gather(jnp.concatenate(halves, axis=2)).reshape(width, 2 * ff_own)

    normed_all = bf(rms_scale(f32(x_all), gain_vals[0]))
    qkv = mm(normed_all, w_own)
    query = bf(rotary(qkv[:, :HEAD_DIM], cosine, sine) * HEAD_DIM ** (-0.5))
    half = qkv[:, HEAD_DIM:]
    mine = jnp.where(core == 0, bf(rotary(half, cosine, sine)), bf(half))
    mid = mine.shape[0] // 2
    other = flip(jnp.concatenate([mine[mid:], mine[:mid]], axis=0), "core")
    key = jnp.where(core == 0, mine, other)
    value = jnp.where(core == 0, other, mine)
    scores = mm_nt(query, key)
    capped = SOFT_CAP * jnp.tanh(scores / SOFT_CAP)
    weights = jnp.where(pos_all[:, None] >= pos_all[None, :], jnp.exp(capped), 0.0)
    weights_b = bf(weights)
    total = jnp.sum(weights, axis=-1, keepdims=True)
    attn = mm(weights_b, value) / total
    attn_b = bf(attn)
    got = [None] * HEADS
    for place, bits in enumerate(ORDER):
        block = attn_b[place * tok : (place + 1) * tok]
        got[bits] = differ(block, PLANE, bits) if bits else block
    attn_own = jnp.take(jnp.stack(got), jnp.arange(HEADS) ^ spot, axis=0)
    attn_own = jnp.swapaxes(attn_own, 0, 1).reshape(tok, q_width)
    mixed = mm(attn_own, out_full)

    x_rows = f32(x_own)
    branch_one, pull_one = jax.vjp(rms_scale, mixed, gain_vals[1])
    resid = x_rows + branch_one
    normed_two, pull_two = jax.vjp(rms_scale, resid, gain_vals[2])

    tokens = ring_gather(bf(normed_two))
    inners, pulls, downs = ([], [], [])
    for piece in tokens:
        gate_up = mm(piece, gate_up_own)
        inner, pull = jax.vjp(
            lambda gate, up_part: jax.nn.gelu(gate, approximate=True) * up_part,
            gate_up[:, :ff_own],
            gate_up[:, ff_own:],
        )
        inners.append(bf(inner))
        pulls.append(pull)
        downs.append(hold(bf(mm(inners[-1], down_own))))
    down = ring_scatter(downs)
    branch_two, pull_three = jax.vjp(rms_scale, down, gain_vals[3])
    block_out = bf(resid + branch_two)[None]
    grad_top = f32(cotangent[0])
    grad_down_in, gain_grad_three = pull_three(grad_top)
    grad_downs = ring_gather(bf(grad_down_in))
    grad_gus, parts = ([], [])
    for piece, pull in zip(grad_downs, pulls):
        grad_gus.append(bf(jnp.concatenate(pull(mm_nt(piece, down_own)), axis=1)))
        parts.append(hold(bf(mm_nt(grad_gus[-1], gate_up_own))))
    grad_normed_two = ring_scatter(parts)
    grad_resid_two, _ = pull_two(grad_normed_two)
    grad_resid = grad_top + grad_resid_two
    grad_mixed, gain_grad_one = pull_one(grad_resid)
    grad_mixed_b = bf(grad_mixed)

    grad_attn = bf(mm_nt(grad_mixed_b, out_full)).reshape(tok, HEADS, HEAD_DIM)
    grad_attn = jnp.take(jnp.swapaxes(grad_attn, 0, 1), jnp.arange(HEADS) ^ spot, axis=0)
    grad_head = jnp.concatenate(
        [differ(grad_attn[bits], PLANE, bits) if bits else grad_attn[0] for bits in ORDER], axis=0
    )
    grad_head = f32(grad_head)
    rho = bf(grad_head / total)
    delta = jnp.sum(grad_head * attn, axis=-1, keepdims=True) / total
    pulled = mm_nt(rho, value)
    grad_scores = bf((pulled - delta) * weights * (1.0 - (capped / SOFT_CAP) ** 2))
    grad_query = mm(grad_scores, key) * HEAD_DIM ** (-0.5)
    grad_key = mm_tn(grad_scores, query)
    grad_value = mm_tn(weights_b, rho)
    sent = jnp.where(core == 0, grad_value, grad_key)
    sent = flip(jnp.concatenate([sent[mid:], sent[:mid]], axis=0), "core")
    grad_half = jnp.where(core == 0, grad_key, grad_value) + sent
    grad_half = jnp.where(core == 0, unrotary(grad_half, cosine, sine), grad_half)
    grad_qkv = bf(jnp.concatenate([unrotary(grad_query, cosine, sine), grad_half], axis=1))
    grad_normed = plane_scatter(bf(mm_nt(grad_qkv, w_own)))
    _, pull_zero = jax.vjp(rms_scale, x_rows, gain_vals[0])
    grad_x_zero, _ = pull_zero(grad_normed)
    input_grad = (grad_resid + grad_x_zero)[None]

    tokens_b = jnp.concatenate(tokens, axis=0)
    inner_b = jnp.concatenate(inners, axis=0)
    grad_down_b = jnp.concatenate(grad_downs, axis=0)
    grad_gu_b = jnp.concatenate(grad_gus, axis=0)
    grad_halves = []
    for part in range(2):
        part_w = mm_tn(tokens_b, grad_gu_b[:, part * ff_own : (part + 1) * ff_own])
        part_w = quad_scatter(bf(part_w).reshape(group, 4, rows, ff_own))
        part_w = jnp.swapaxes(exchange(part_w, LADDER), 0, 1)
        grad_halves.append(part_w.reshape(rows, group * ff_own))
    grad_gate_up_w = f32(jnp.concatenate(grad_halves, axis=1))
    grad_down_w = bf(mm_tn(inner_b, grad_down_b)).reshape(1, 4, ff_own // 4, width)
    grad_down_w = f32(quad_scatter(grad_down_w)[0])
    grad_out_w = f32(scatter_sum(bf(mm_tn(attn_own, grad_mixed_b)), ALL))
    grad_w = bf(mm_tn(normed_all, grad_qkv)).reshape(planes, HEADS * rows, 2 * HEAD_DIM)
    grad_w = bf(line_scatter(grad_w)).reshape(HEADS, rows, 2 * HEAD_DIM)
    grad_w = f32(jnp.swapaxes(exchange(grad_w, PLANE), 0, 1))
    grad_q_w = grad_w[:, :, :HEAD_DIM].reshape(rows, q_width)
    grad_kv_w = grad_w[:, :, HEAD_DIM:].reshape(rows, KV_HEADS, 2, HEAD_DIM)
    grad_kv_w = jnp.swapaxes(grad_kv_w, 1, 2).reshape(rows, q_width)
    grad_qkv_w = jnp.concatenate([grad_q_w, grad_kv_w], axis=1)

    gain_zero = jnp.sum(f32(w_qkv) * grad_qkv_w, axis=1) / (1.0 + f32(gains[0]))
    gain_two = jnp.sum(f32(w_gate_up) * grad_gate_up_w, axis=1) / (1.0 + f32(gains[2]))
    others = jnp.stack([gain_grad_one, gain_grad_three], axis=0)
    for axis in ("core", "fy", "ctx", "dl", "dh"):
        others = others + flip(others, axis)
    others = others.reshape(2, planes * HEADS, rows)
    others = lax.dynamic_index_in_dim(others, lax.axis_index(ALL), 1, keepdims=False)
    grad_gains = jnp.stack([gain_zero, others[0], gain_two, others[1]], axis=0)

    return (
        (block_out, input_grad)
        + adam_step(f32(w_qkv), grad_qkv_w, m_qkv, v_qkv, MATRIX_RATE, WEIGHT_DECAY)
        + adam_step(f32(w_out), grad_out_w, m_out, v_out, MATRIX_RATE, WEIGHT_DECAY)
        + adam_step(f32(w_gate_up), grad_gate_up_w, m_gate_up, v_gate_up, MATRIX_RATE, WEIGHT_DECAY)
        + adam_step(f32(w_down), grad_down_w, m_down, v_down, MATRIX_RATE, WEIGHT_DECAY)
        + adam_step(f32(gains), grad_gains, m_gains, v_gains, GAIN_RATE, 0.0)
    )


def token_attention(x_own, pos_own, w_qkv, w_out, gains):
    tok = x_own.shape[0]
    q_width = HEADS * HEAD_DIM
    k_width = KV_HEADS * HEAD_DIM
    groups = HEADS // KV_HEADS
    qkv_full = gather(w_qkv, ALL)
    out_full = gather(w_out, ALL)
    gain_vals = f32(gather(gains, ALL, 1))
    normed = bf(rms_scale(f32(x_own), gain_vals[0]))
    qkv = mm(normed, qkv_full)
    cosine, sine = rotary_tables(pos_own)
    cosine, sine = (cosine[:, None, :], sine[:, None, :])
    query = rotary(qkv[:, :q_width].reshape(tok, HEADS, HEAD_DIM), cosine, sine)
    query = bf(query * HEAD_DIM ** (-0.5)).reshape(tok, KV_HEADS, groups, HEAD_DIM)
    key_own = qkv[:, q_width : q_width + k_width].reshape(tok, KV_HEADS, HEAD_DIM)
    key = gather(bf(rotary(key_own, cosine, sine)), PLANE)
    value = gather(bf(qkv[:, q_width + k_width :]).reshape(tok, KV_HEADS, HEAD_DIM), PLANE)
    pos_all = gather(pos_own, PLANE)
    count = pos_all.shape[0]
    scores = jnp.einsum("tgjd,sgd->gjts", query, key, preferred_element_type=jnp.float32)
    capped = SOFT_CAP * jnp.tanh(scores / SOFT_CAP)
    weights = jnp.where(pos_own[:, None] >= pos_all[None, :], jnp.exp(capped), 0.0)
    weights_b = bf(weights)
    total = jnp.sum(weights, axis=-1)
    attn = jnp.einsum("gjts,sgd->gjtd", weights_b, value, preferred_element_type=jnp.float32)
    attn = attn / total[..., None]
    attn_b = bf(jnp.transpose(attn, (2, 0, 1, 3)).reshape(tok, q_width))
    mixed = mm(attn_b, out_full)

    def backward(grad_mixed_b):
        grad_attn = mm_nt(grad_mixed_b, out_full).reshape(tok, KV_HEADS, groups, HEAD_DIM)
        grad_heads = jnp.transpose(grad_attn, (1, 2, 0, 3))
        rho = bf(grad_heads / total[..., None])
        delta = jnp.sum(grad_heads * attn, axis=-1) / total
        pulled = jnp.einsum("gjtd,sgd->gjts", rho, value, preferred_element_type=jnp.float32)
        grad_scores = bf(
            (pulled - delta[..., None]) * weights * (1.0 - (capped / SOFT_CAP) ** 2)
        )
        grad_query = jnp.einsum(
            "gjts,sgd->tgjd", grad_scores, key, preferred_element_type=jnp.float32
        ).reshape(tok, HEADS, HEAD_DIM)
        grad_key = jnp.einsum(
            "gjts,tgjd->sgd", grad_scores, query, preferred_element_type=jnp.float32
        ).reshape(count, k_width)
        grad_value = jnp.einsum(
            "gjts,gjtd->sgd", weights_b, rho, preferred_element_type=jnp.float32
        ).reshape(count, k_width)
        grad_kv = scatter_sum(jnp.concatenate([grad_key, grad_value], axis=1), PLANE)
        grad_query = unrotary(grad_query * HEAD_DIM ** (-0.5), cosine, sine)
        grad_key = unrotary(grad_kv[:, :k_width].reshape(tok, KV_HEADS, HEAD_DIM), cosine, sine)
        grad_qkv = bf(
            jnp.concatenate(
                [
                    grad_query.reshape(tok, q_width),
                    grad_key.reshape(tok, k_width),
                    grad_kv[:, k_width:],
                ],
                axis=1,
            )
        )
        grad_normed = mm_nt(grad_qkv, qkv_full)
        grad_qkv_w = f32(scatter_sum(bf(mm_tn(normed, grad_qkv)), ALL))
        grad_out_w = f32(scatter_sum(bf(mm_tn(attn_b, grad_mixed_b)), ALL))
        return grad_normed, grad_qkv_w, grad_out_w

    return mixed, gain_vals, backward


def wide_shards(
    hidden_in,
    positions,
    cotangent,
    w_qkv,
    w_out,
    w_gate_up,
    w_down,
    gains,
    m_qkv,
    v_qkv,
    m_out,
    v_out,
    m_gate_up,
    v_gate_up,
    m_down,
    v_down,
    m_gains,
    v_gains,
):
    x_own = hidden_in[0]
    rows, width = (w_qkv.shape[0], x_own.shape[1])
    group, across = (lax.axis_size(GROUP), lax.axis_size(ACROSS))
    ff_piece = w_down.shape[0]
    ff_own = across * ff_piece
    gu_pieces = w_gate_up.reshape(rows, 2, across, group, ff_piece)
    gu_pieces = jnp.transpose(gu_pieces, (3, 0, 1, 2, 4)).reshape(group * rows, 2 * ff_own)

    mixed, gain_vals, attention_back = token_attention(x_own, positions[0], w_qkv, w_out, gains)
    gu_own = gather(swap(gu_pieces, GROUP), ACROSS)
    down_own = gather(w_down, ACROSS)

    x_rows = f32(x_own)
    branch_one, pull_one = jax.vjp(rms_scale, mixed, gain_vals[1])
    resid = x_rows + branch_one
    normed_two, pull_two = jax.vjp(rms_scale, resid, gain_vals[2])
    tokens_b = gather(bf(normed_two), GROUP)
    gate_up = mm(tokens_b, gu_own)
    inner, pull_gelu = jax.vjp(
        lambda gate, up_part: jax.nn.gelu(gate, approximate=True) * up_part,
        gate_up[:, :ff_own],
        gate_up[:, ff_own:],
    )
    inner_b = bf(inner)
    down = f32(scatter_sum(bf(mm(inner_b, down_own)), GROUP))
    branch_two, pull_three = jax.vjp(rms_scale, down, gain_vals[3])
    block_out = bf(resid + branch_two)[None]
    grad_top = f32(cotangent[0])
    grad_down_in, gain_grad_three = pull_three(grad_top)
    grad_down_b = gather(bf(grad_down_in), GROUP)
    grad_gate, grad_up = pull_gelu(mm_nt(grad_down_b, down_own))
    grad_gu_b = bf(jnp.concatenate([grad_gate, grad_up], axis=1))
    grad_normed_two = f32(scatter_sum(bf(mm_nt(grad_gu_b, gu_own)), GROUP))
    grad_gate_up_w = scatter_sum(bf(mm_tn(tokens_b, grad_gu_b)), ACROSS)
    grad_down_w = f32(scatter_sum(bf(mm_tn(inner_b, grad_down_b)), ACROSS))

    grad_resid_two, gain_grad_two = pull_two(grad_normed_two)
    grad_resid = grad_top + grad_resid_two
    grad_mixed, gain_grad_one = pull_one(grad_resid)
    grad_normed, grad_qkv_w, grad_out_w = attention_back(bf(grad_mixed))
    _, pull_zero = jax.vjp(rms_scale, x_rows, gain_vals[0])
    grad_x_zero, gain_grad_zero = pull_zero(grad_normed)
    input_grad = (grad_resid + grad_x_zero)[None]

    grad_gate_up_w = swap(grad_gate_up_w, GROUP).reshape(group, rows, 2, across, ff_piece)
    grad_gate_up_w = f32(jnp.transpose(grad_gate_up_w, (1, 2, 3, 0, 4)).reshape(rows, -1))
    gain_term = jnp.stack([gain_grad_zero, gain_grad_one, gain_grad_two, gain_grad_three], axis=0)
    grad_gains = lax.psum_scatter(gain_term, ALL, scatter_dimension=1, tiled=True)

    return (
        (block_out, input_grad)
        + adam_step(f32(w_qkv), grad_qkv_w, m_qkv, v_qkv, MATRIX_RATE, WEIGHT_DECAY)
        + adam_step(f32(w_out), grad_out_w, m_out, v_out, MATRIX_RATE, WEIGHT_DECAY)
        + adam_step(f32(w_gate_up), grad_gate_up_w, m_gate_up, v_gate_up, MATRIX_RATE, WEIGHT_DECAY)
        + adam_step(f32(w_down), grad_down_w, m_down, v_down, MATRIX_RATE, WEIGHT_DECAY)
        + adam_step(f32(gains), grad_gains, m_gains, v_gains, GAIN_RATE, 0.0)
    )


def solution(mesh):
    sizes = dict(mesh.shape)
    fine = Mesh(
        mesh.devices.reshape(sizes["dp"] // 2, 2, sizes["ctx"], sizes["fsdp"] // 2, 2),
        ("dh", "dl", "ctx", "fy", "core"),
    )
    acts = P(DP, PLANE, None)
    mats = P(ALL, None)
    vecs = P(None, ALL)
    ladder = sizes["dp"] == 4 and sizes["ctx"] == 2 and sizes["fsdp"] == 4
    return jax.shard_map(
        ladder_shards if ladder else wide_shards,
        mesh=fine,
        in_specs=(acts, P(DP, PLANE), acts) + (mats,) * 4 + (vecs,) + (mats,) * 8 + (vecs,) * 2,
        out_specs=(acts, acts) + (mats,) * 12 + (vecs,) * 3,
        check_vma=False,
    )
```

```python
import jax
import jax.numpy as jnp
from jax import lax
from jax.sharding import Mesh, PartitionSpec as P

HEADS = 8
KV_HEADS = 4
HEAD_DIM = 256
STEP = 10

NORM_EPS = 1e-06
SOFT_CAP = 50.0
THETA = 10000.0
BETA_ONE = 0.9
BETA_TWO = 0.95
ADAM_EPS = 1e-08
MATRIX_RATE = 0.03
GAIN_RATE = 0.2
WEIGHT_DECAY = 0.1

DP = ("dh", "dl")
PLANE = ("ctx", "fy", "core")
ALL = DP + PLANE
LADDER = DP + ("ctx",)
GROUP = PLANE
ACROSS = DP


def f32(v):
    return v.astype(jnp.float32)


def bf(v):
    return v.astype(jnp.bfloat16)


def dot(left, right, dims):
    return lax.dot_general(left, right, (dims, ((), ())), preferred_element_type=jnp.float32)


def mm(left, right):
    return dot(left, right, ((1,), (0,)))


def mm_nt(left, right):
    return dot(left, right, ((1,), (1,)))


def mm_tn(left, right):
    return dot(left, right, ((0,), (0,)))


def rms_scale(values, gain):
    inverse = lax.rsqrt(jnp.mean(values * values, axis=-1, keepdims=True) + NORM_EPS)
    return values * inverse * (1.0 + gain)


def rotary_tables(places):
    half = HEAD_DIM // 2
    freqs = THETA ** (-(jnp.arange(half, dtype=jnp.float32) * 2.0 / HEAD_DIM))
    angles = f32(places)[:, None] * freqs[None, :]
    return (jnp.cos(angles), jnp.sin(angles))


def rotary(values, cosine, sine):
    half = HEAD_DIM // 2
    first = values[..., :half]
    second = values[..., half:]
    return jnp.concatenate(
        [first * cosine - second * sine, second * cosine + first * sine], axis=-1
    )


def unrotary(values, cosine, sine):
    return rotary(values, cosine, -sine)


def adam_step(weight, grad, first, second, rate, decay):
    first_new = BETA_ONE * first + (1.0 - BETA_ONE) * grad
    second_new = BETA_TWO * second + (1.0 - BETA_TWO) * grad * grad
    ratio = (
        first_new
        / (1.0 - BETA_ONE**STEP)
        / (jnp.sqrt(second_new / (1.0 - BETA_TWO**STEP)) + ADAM_EPS)
    )
    return (weight - rate * (ratio + decay * weight), first_new, second_new)


def gather(v, axes, axis=0):
    return lax.all_gather(v, axes, axis=axis, tiled=True)


def scatter_sum(v, axes):
    return lax.psum_scatter(v, axes, scatter_dimension=0, tiled=True)


def swap(v, axes):
    return lax.all_to_all(v, axes, split_axis=0, concat_axis=0, tiled=True)


def hold(v):
    return lax.optimization_barrier(v)


def flip(v, axis):
    return lax.ppermute(v, axis, [(0, 1), (1, 0)])


def plane_scatter(parts):
    size = parts.shape[0] // 8
    half = size // 2
    col, row, core = (lax.axis_index(axis) for axis in PLANE)
    parts = parts.reshape((4, 2, size) + parts.shape[1:])
    sent = lax.dynamic_index_in_dim(parts, 1 - core, 1, keepdims=False)
    kept = lax.dynamic_index_in_dim(parts, core, 1, keepdims=False)
    both = bf(f32(kept) + f32(flip(sent, "core")))
    own, over_y, over_x, corner = (
        lax.dynamic_index_in_dim(both, (2 * col + row) ^ bits, 0, keepdims=False) for bits in range(4)
    )
    got_y = flip(corner[:half], "ctx")
    got_x = flip(corner[half:], "fy")
    over_y = jnp.concatenate([bf(f32(over_y[:half]) + f32(got_y)), over_y[half:]], axis=0)
    over_x = jnp.concatenate([over_x[:half], bf(f32(over_x[half:]) + f32(got_x))], axis=0)
    return f32(own) + f32(flip(over_x, "ctx")) + f32(flip(over_y, "fy"))


def line_gather(own):
    count = lax.axis_size(DP)
    ups, downs = ([], [])
    up, down = (own, own)
    for step in range(1, count):
        up = lax.ppermute(up, DP, [(i, i + 1) for i in range(step - 1, count - 1)])
        down = lax.ppermute(down, DP, [(i + 1, i) for i in range(count - step)])
        ups.append(up)
        downs.append(down)
    row = jnp.stack(ups[::-1] + [own] + downs)
    return lax.dynamic_slice_in_dim(row, count - 1 - lax.axis_index(DP), count, axis=0)


def line_scatter(parts):
    count = lax.axis_size(DP)
    me = lax.axis_index(DP)
    total = f32(lax.dynamic_index_in_dim(parts, me, 0, keepdims=False))
    for step in range(1, count):
        piece = lax.dynamic_index_in_dim(parts, (me + step) % count, 0, keepdims=False)
        total = total + f32(lax.ppermute(piece, DP, [(i, (i + step) % count) for i in range(count)]))
    return total


def ring_pairs():
    count = lax.axis_size(DP)
    ring = [2 * z for z in range(count)] + [2 * z + 1 for z in reversed(range(count))]
    onward = [(ring[i], ring[(i + 1) % len(ring)]) for i in range(len(ring))]
    return onward, [(b, a) for a, b in onward]


def ring_gather(own):
    onward, back = ring_pairs()
    half = own.shape[0] // 2
    pieces = [own]
    behind, ahead = (own, own)
    for _ in range(len(onward) // 2 - 1):
        behind = lax.ppermute(behind, LADDER, onward)
        ahead = lax.ppermute(ahead, LADDER, back)
        pieces.append(jnp.concatenate([behind, ahead], axis=0))
    last = [
        lax.ppermute(behind[:half], LADDER, onward),
        lax.ppermute(ahead[half:], LADDER, back),
    ]
    return pieces + [jnp.concatenate(last, axis=0)]


def ring_scatter(pieces):
    onward, back = ring_pairs()
    size = pieces[0].shape[0]
    half = size // 2
    ahead = lax.ppermute(pieces[-1][:half], LADDER, onward)
    behind = lax.ppermute(pieces[-1][half:], LADDER, back)
    for step in range(len(pieces) - 2, 0, -1):
        to_behind, to_ahead = (pieces[step][:size], pieces[step][size:])
        if step == len(pieces) - 2:
            to_ahead = jnp.concatenate(
                [bf(f32(to_ahead[:half]) + f32(ahead)), to_ahead[half:]], axis=0
            )
            to_behind = jnp.concatenate(
                [to_behind[:half], bf(f32(to_behind[half:]) + f32(behind))], axis=0
            )
        else:
            to_ahead = bf(f32(to_ahead) + f32(ahead))
            to_behind = bf(f32(to_behind) + f32(behind))
        ahead = lax.ppermute(to_ahead, LADDER, onward)
        behind = lax.ppermute(to_behind, LADDER, back)
    return f32(pieces[0]) + f32(ahead) + f32(behind)


def quad_gather(own):
    over_y = flip(own, "fy")
    blocks = [own, flip(own, "core"), over_y, flip(over_y, "core")]
    me = lax.axis_index(("fy", "core"))
    whole = jnp.zeros(own.shape[:1] + (4,) + own.shape[1:], own.dtype)
    for bits, block in enumerate(blocks):
        whole = lax.dynamic_update_index_in_dim(whole, block, me ^ bits, 1)
    return whole


def quad_scatter(parts):
    core, row = (lax.axis_index("core"), lax.axis_index("fy"))
    parts = parts.reshape(parts.shape[:1] + (2, 2) + parts.shape[2:])
    sent = lax.dynamic_index_in_dim(parts, 1 - core, 2, keepdims=False)
    kept = lax.dynamic_index_in_dim(parts, core, 2, keepdims=False)
    both = bf(f32(kept) + f32(flip(sent, "core")))
    sent = lax.dynamic_index_in_dim(both, 1 - row, 1, keepdims=False)
    kept = lax.dynamic_index_in_dim(both, row, 1, keepdims=False)
    return bf(f32(kept) + f32(flip(sent, "fy")))


def ladder_shards(
    hidden_in,
    positions,
    cotangent,
    w_qkv,
    w_out,
    w_gate_up,
    w_down,
    gains,
    m_qkv,
    v_qkv,
    m_out,
    v_out,
    m_gate_up,
    v_gate_up,
    m_down,
    v_down,
    m_gains,
    v_gains,
):
    x_own = hidden_in[0]
    tok, width = x_own.shape
    rows = w_qkv.shape[0]
    planes = lax.axis_size(DP)
    group = lax.axis_size(LADDER)
    q_width = HEADS * HEAD_DIM
    core = lax.axis_index("core")

    q_cols = w_qkv[:, :q_width].reshape(rows, HEADS, HEAD_DIM)
    kv_cols = w_qkv[:, q_width:].reshape(rows, 2, KV_HEADS, HEAD_DIM)
    kv_cols = jnp.swapaxes(kv_cols, 1, 2).reshape(rows, HEADS, HEAD_DIM)
    pieces = jnp.swapaxes(jnp.concatenate([q_cols, kv_cols], axis=2), 0, 1)
    first = jnp.stack([positions[0, 0] // 128, positions[0, 0] % 128])
    own_gains = jnp.concatenate([gains.reshape(4 * rows), bf(first)])[None, None]
    own_gains = jnp.pad(own_gains, ((0, 0), (0, 7), (0, 2 * HEAD_DIM - 4 * rows - 2)))
    pieces = jnp.concatenate(
        [pieces, jnp.broadcast_to(own_gains, (HEADS,) + own_gains.shape[1:])], axis=1
    )
    got = swap(pieces, PLANE)
    first = got[:, rows, 4 * rows : 4 * rows + 2].astype(jnp.int32)
    pos_all = first[:, :1] * 128 + first[:, 1:] + jnp.arange(tok, dtype=jnp.int32)[None]
    pos_all = pos_all.reshape(-1)
    cosine, sine = rotary_tables(pos_all)
    got = line_gather(got)
    w_own = got[:, :, :rows].reshape(width, 2 * HEAD_DIM)
    gain_vals = got[:, :, rows, : 4 * rows].reshape(planes * HEADS, 4, rows)
    gain_vals = f32(jnp.swapaxes(gain_vals, 0, 1).reshape(4, width))
    out_full = gather(w_out, ALL)

    x_all = gather(x_own, PLANE)

    ff_own = w_down.shape[0] * 4
    halves = []
    for part in range(2):
        cols = w_gate_up[:, part * group * ff_own : (part + 1) * group * ff_own]
        cols = jnp.swapaxes(cols.reshape(rows, group, ff_own), 0, 1)
        halves.append(cols)
    down_own = quad_gather(w_down[None]).reshape(ff_own, width)
    gate_up_own = quad_gather(swap(jnp.concatenate(halves, axis=2), LADDER)).reshape(width, 2 * ff_own)

    normed_all = bf(rms_scale(f32(x_all), gain_vals[0]))
    qkv = mm(normed_all, w_own)
    query = bf(rotary(qkv[:, :HEAD_DIM], cosine, sine) * HEAD_DIM ** (-0.5))
    half = qkv[:, HEAD_DIM:]
    mine = jnp.where(core == 0, bf(rotary(half, cosine, sine)), bf(half))
    other = flip(mine, "core")
    key = jnp.where(core == 0, mine, other)
    value = jnp.where(core == 0, other, mine)
    scores = mm_nt(query, key)
    capped = SOFT_CAP * jnp.tanh(scores / SOFT_CAP)
    weights = jnp.where(pos_all[:, None] >= pos_all[None, :], jnp.exp(capped), 0.0)
    weights_b = bf(weights)
    total = jnp.sum(weights, axis=-1, keepdims=True)
    attn = mm(weights_b, value) / total
    attn_own = swap(bf(attn).reshape(HEADS, tok, HEAD_DIM), PLANE)
    attn_own = jnp.swapaxes(attn_own, 0, 1).reshape(tok, q_width)
    mixed = mm(attn_own, out_full)

    x_rows = f32(x_own)
    branch_one, pull_one = jax.vjp(rms_scale, mixed, gain_vals[1])
    resid = x_rows + branch_one
    normed_two, pull_two = jax.vjp(rms_scale, resid, gain_vals[2])

    tokens = ring_gather(bf(normed_two))
    inners, pulls, downs = ([], [], [])
    for piece in tokens:
        gate_up = mm(piece, gate_up_own)
        inner, pull = jax.vjp(
            lambda gate, up_part: jax.nn.gelu(gate, approximate=True) * up_part,
            gate_up[:, :ff_own],
            gate_up[:, ff_own:],
        )
        inners.append(bf(inner))
        pulls.append(pull)
        downs.append(hold(bf(mm(inners[-1], down_own))))
    down = ring_scatter(downs)
    branch_two, pull_three = jax.vjp(rms_scale, down, gain_vals[3])
    block_out = bf(resid + branch_two)[None]
    grad_top = f32(cotangent[0])
    grad_down_in, gain_grad_three = pull_three(grad_top)
    grad_downs = ring_gather(bf(grad_down_in))
    grad_gus, parts = ([], [])
    for piece, pull in zip(grad_downs, pulls):
        grad_gus.append(bf(jnp.concatenate(pull(mm_nt(piece, down_own)), axis=1)))
        parts.append(hold(bf(mm_nt(grad_gus[-1], gate_up_own))))
    grad_normed_two = ring_scatter(parts)
    grad_resid_two, _ = pull_two(grad_normed_two)
    grad_resid = grad_top + grad_resid_two
    grad_mixed, gain_grad_one = pull_one(grad_resid)
    grad_mixed_b = bf(grad_mixed)

    grad_attn = bf(mm_nt(grad_mixed_b, out_full)).reshape(tok, HEADS, HEAD_DIM)
    grad_head = swap(jnp.swapaxes(grad_attn, 0, 1), PLANE).reshape(HEADS * tok, HEAD_DIM)
    grad_head = f32(grad_head)
    rho = bf(grad_head / total)
    delta = jnp.sum(grad_head * attn, axis=-1, keepdims=True) / total
    pulled = mm_nt(rho, value)
    grad_scores = bf((pulled - delta) * weights * (1.0 - (capped / SOFT_CAP) ** 2))
    grad_query = mm(grad_scores, key) * HEAD_DIM ** (-0.5)
    grad_key = mm_tn(grad_scores, query)
    grad_value = mm_tn(weights_b, rho)
    sent = jnp.where(core == 0, grad_value, grad_key)
    grad_half = jnp.where(core == 0, grad_key, grad_value) + flip(sent, "core")
    grad_half = jnp.where(core == 0, unrotary(grad_half, cosine, sine), grad_half)
    grad_qkv = bf(jnp.concatenate([unrotary(grad_query, cosine, sine), grad_half], axis=1))
    grad_normed = plane_scatter(bf(mm_nt(grad_qkv, w_own)))
    _, pull_zero = jax.vjp(rms_scale, x_rows, gain_vals[0])
    grad_x_zero, _ = pull_zero(grad_normed)
    input_grad = (grad_resid + grad_x_zero)[None]

    tokens_b = jnp.concatenate(tokens, axis=0)
    inner_b = jnp.concatenate(inners, axis=0)
    grad_down_b = jnp.concatenate(grad_downs, axis=0)
    grad_gu_b = jnp.concatenate(grad_gus, axis=0)
    grad_halves = []
    for part in range(2):
        part_w = mm_tn(tokens_b, grad_gu_b[:, part * ff_own : (part + 1) * ff_own])
        part_w = quad_scatter(bf(part_w).reshape(group, 4, rows, ff_own))
        part_w = jnp.swapaxes(swap(part_w, LADDER), 0, 1)
        grad_halves.append(part_w.reshape(rows, group * ff_own))
    grad_gate_up_w = f32(jnp.concatenate(grad_halves, axis=1))
    grad_down_w = bf(mm_tn(inner_b, grad_down_b)).reshape(1, 4, ff_own // 4, width)
    grad_down_w = f32(quad_scatter(grad_down_w)[0])
    grad_out_w = f32(scatter_sum(bf(mm_tn(attn_own, grad_mixed_b)), ALL))
    grad_w = bf(mm_tn(normed_all, grad_qkv)).reshape(planes, HEADS * rows, 2 * HEAD_DIM)
    grad_w = bf(line_scatter(grad_w)).reshape(HEADS, rows, 2 * HEAD_DIM)
    grad_w = f32(jnp.swapaxes(swap(grad_w, PLANE), 0, 1))
    grad_q_w = grad_w[:, :, :HEAD_DIM].reshape(rows, q_width)
    grad_kv_w = grad_w[:, :, HEAD_DIM:].reshape(rows, KV_HEADS, 2, HEAD_DIM)
    grad_kv_w = jnp.swapaxes(grad_kv_w, 1, 2).reshape(rows, q_width)
    grad_qkv_w = jnp.concatenate([grad_q_w, grad_kv_w], axis=1)

    gain_zero = jnp.sum(f32(w_qkv) * grad_qkv_w, axis=1) / (1.0 + f32(gains[0]))
    gain_two = jnp.sum(f32(w_gate_up) * grad_gate_up_w, axis=1) / (1.0 + f32(gains[2]))
    others = jnp.stack([gain_grad_one, gain_grad_three], axis=0)
    for axis in ("core", "fy", "ctx", "dl", "dh"):
        others = others + flip(others, axis)
    others = others.reshape(2, planes * HEADS, rows)
    others = lax.dynamic_index_in_dim(others, lax.axis_index(ALL), 1, keepdims=False)
    grad_gains = jnp.stack([gain_zero, others[0], gain_two, others[1]], axis=0)

    return (
        (block_out, input_grad)
        + adam_step(f32(w_qkv), grad_qkv_w, m_qkv, v_qkv, MATRIX_RATE, WEIGHT_DECAY)
        + adam_step(f32(w_out), grad_out_w, m_out, v_out, MATRIX_RATE, WEIGHT_DECAY)
        + adam_step(f32(w_gate_up), grad_gate_up_w, m_gate_up, v_gate_up, MATRIX_RATE, WEIGHT_DECAY)
        + adam_step(f32(w_down), grad_down_w, m_down, v_down, MATRIX_RATE, WEIGHT_DECAY)
        + adam_step(f32(gains), grad_gains, m_gains, v_gains, GAIN_RATE, 0.0)
    )


def token_attention(x_own, pos_own, w_qkv, w_out, gains):
    tok = x_own.shape[0]
    q_width = HEADS * HEAD_DIM
    k_width = KV_HEADS * HEAD_DIM
    groups = HEADS // KV_HEADS
    qkv_full = gather(w_qkv, ALL)
    out_full = gather(w_out, ALL)
    gain_vals = f32(gather(gains, ALL, 1))
    normed = bf(rms_scale(f32(x_own), gain_vals[0]))
    qkv = mm(normed, qkv_full)
    cosine, sine = rotary_tables(pos_own)
    cosine, sine = (cosine[:, None, :], sine[:, None, :])
    query = rotary(qkv[:, :q_width].reshape(tok, HEADS, HEAD_DIM), cosine, sine)
    query = bf(query * HEAD_DIM ** (-0.5)).reshape(tok, KV_HEADS, groups, HEAD_DIM)
    key_own = qkv[:, q_width : q_width + k_width].reshape(tok, KV_HEADS, HEAD_DIM)
    key = gather(bf(rotary(key_own, cosine, sine)), PLANE)
    value = gather(bf(qkv[:, q_width + k_width :]).reshape(tok, KV_HEADS, HEAD_DIM), PLANE)
    pos_all = gather(pos_own, PLANE)
    count = pos_all.shape[0]
    scores = jnp.einsum("tgjd,sgd->gjts", query, key, preferred_element_type=jnp.float32)
    capped = SOFT_CAP * jnp.tanh(scores / SOFT_CAP)
    weights = jnp.where(pos_own[:, None] >= pos_all[None, :], jnp.exp(capped), 0.0)
    weights_b = bf(weights)
    total = jnp.sum(weights, axis=-1)
    attn = jnp.einsum("gjts,sgd->gjtd", weights_b, value, preferred_element_type=jnp.float32)
    attn = attn / total[..., None]
    attn_b = bf(jnp.transpose(attn, (2, 0, 1, 3)).reshape(tok, q_width))
    mixed = mm(attn_b, out_full)

    def backward(grad_mixed_b):
        grad_attn = mm_nt(grad_mixed_b, out_full).reshape(tok, KV_HEADS, groups, HEAD_DIM)
        grad_heads = jnp.transpose(grad_attn, (1, 2, 0, 3))
        rho = bf(grad_heads / total[..., None])
        delta = jnp.sum(grad_heads * attn, axis=-1) / total
        pulled = jnp.einsum("gjtd,sgd->gjts", rho, value, preferred_element_type=jnp.float32)
        grad_scores = bf(
            (pulled - delta[..., None]) * weights * (1.0 - (capped / SOFT_CAP) ** 2)
        )
        grad_query = jnp.einsum(
            "gjts,sgd->tgjd", grad_scores, key, preferred_element_type=jnp.float32
        ).reshape(tok, HEADS, HEAD_DIM)
        grad_key = jnp.einsum(
            "gjts,tgjd->sgd", grad_scores, query, preferred_element_type=jnp.float32
        ).reshape(count, k_width)
        grad_value = jnp.einsum(
            "gjts,gjtd->sgd", weights_b, rho, preferred_element_type=jnp.float32
        ).reshape(count, k_width)
        grad_kv = scatter_sum(jnp.concatenate([grad_key, grad_value], axis=1), PLANE)
        grad_query = unrotary(grad_query * HEAD_DIM ** (-0.5), cosine, sine)
        grad_key = unrotary(grad_kv[:, :k_width].reshape(tok, KV_HEADS, HEAD_DIM), cosine, sine)
        grad_qkv = bf(
            jnp.concatenate(
                [
                    grad_query.reshape(tok, q_width),
                    grad_key.reshape(tok, k_width),
                    grad_kv[:, k_width:],
                ],
                axis=1,
            )
        )
        grad_normed = mm_nt(grad_qkv, qkv_full)
        grad_qkv_w = f32(scatter_sum(bf(mm_tn(normed, grad_qkv)), ALL))
        grad_out_w = f32(scatter_sum(bf(mm_tn(attn_b, grad_mixed_b)), ALL))
        return grad_normed, grad_qkv_w, grad_out_w

    return mixed, gain_vals, backward


def wide_shards(
    hidden_in,
    positions,
    cotangent,
    w_qkv,
    w_out,
    w_gate_up,
    w_down,
    gains,
    m_qkv,
    v_qkv,
    m_out,
    v_out,
    m_gate_up,
    v_gate_up,
    m_down,
    v_down,
    m_gains,
    v_gains,
):
    x_own = hidden_in[0]
    rows, width = (w_qkv.shape[0], x_own.shape[1])
    group, across = (lax.axis_size(GROUP), lax.axis_size(ACROSS))
    ff_piece = w_down.shape[0]
    ff_own = across * ff_piece
    gu_pieces = w_gate_up.reshape(rows, 2, across, group, ff_piece)
    gu_pieces = jnp.transpose(gu_pieces, (3, 0, 1, 2, 4)).reshape(group * rows, 2 * ff_own)

    mixed, gain_vals, attention_back = token_attention(x_own, positions[0], w_qkv, w_out, gains)
    gu_own = gather(swap(gu_pieces, GROUP), ACROSS)
    down_own = gather(w_down, ACROSS)

    x_rows = f32(x_own)
    branch_one, pull_one = jax.vjp(rms_scale, mixed, gain_vals[1])
    resid = x_rows + branch_one
    normed_two, pull_two = jax.vjp(rms_scale, resid, gain_vals[2])
    tokens_b = gather(bf(normed_two), GROUP)
    gate_up = mm(tokens_b, gu_own)
    inner, pull_gelu = jax.vjp(
        lambda gate, up_part: jax.nn.gelu(gate, approximate=True) * up_part,
        gate_up[:, :ff_own],
        gate_up[:, ff_own:],
    )
    inner_b = bf(inner)
    down = f32(scatter_sum(bf(mm(inner_b, down_own)), GROUP))
    branch_two, pull_three = jax.vjp(rms_scale, down, gain_vals[3])
    block_out = bf(resid + branch_two)[None]
    grad_top = f32(cotangent[0])
    grad_down_in, gain_grad_three = pull_three(grad_top)
    grad_down_b = gather(bf(grad_down_in), GROUP)
    grad_gate, grad_up = pull_gelu(mm_nt(grad_down_b, down_own))
    grad_gu_b = bf(jnp.concatenate([grad_gate, grad_up], axis=1))
    grad_normed_two = f32(scatter_sum(bf(mm_nt(grad_gu_b, gu_own)), GROUP))
    grad_gate_up_w = scatter_sum(bf(mm_tn(tokens_b, grad_gu_b)), ACROSS)
    grad_down_w = f32(scatter_sum(bf(mm_tn(inner_b, grad_down_b)), ACROSS))

    grad_resid_two, gain_grad_two = pull_two(grad_normed_two)
    grad_resid = grad_top + grad_resid_two
    grad_mixed, gain_grad_one = pull_one(grad_resid)
    grad_normed, grad_qkv_w, grad_out_w = attention_back(bf(grad_mixed))
    _, pull_zero = jax.vjp(rms_scale, x_rows, gain_vals[0])
    grad_x_zero, gain_grad_zero = pull_zero(grad_normed)
    input_grad = (grad_resid + grad_x_zero)[None]

    grad_gate_up_w = swap(grad_gate_up_w, GROUP).reshape(group, rows, 2, across, ff_piece)
    grad_gate_up_w = f32(jnp.transpose(grad_gate_up_w, (1, 2, 3, 0, 4)).reshape(rows, -1))
    gain_term = jnp.stack([gain_grad_zero, gain_grad_one, gain_grad_two, gain_grad_three], axis=0)
    grad_gains = lax.psum_scatter(gain_term, ALL, scatter_dimension=1, tiled=True)

    return (
        (block_out, input_grad)
        + adam_step(f32(w_qkv), grad_qkv_w, m_qkv, v_qkv, MATRIX_RATE, WEIGHT_DECAY)
        + adam_step(f32(w_out), grad_out_w, m_out, v_out, MATRIX_RATE, WEIGHT_DECAY)
        + adam_step(f32(w_gate_up), grad_gate_up_w, m_gate_up, v_gate_up, MATRIX_RATE, WEIGHT_DECAY)
        + adam_step(f32(w_down), grad_down_w, m_down, v_down, MATRIX_RATE, WEIGHT_DECAY)
        + adam_step(f32(gains), grad_gains, m_gains, v_gains, GAIN_RATE, 0.0)
    )


def solution(mesh):
    sizes = dict(mesh.shape)
    fine = Mesh(
        mesh.devices.reshape(sizes["dp"] // 2, 2, sizes["ctx"], sizes["fsdp"] // 2, 2),
        ("dh", "dl", "ctx", "fy", "core"),
    )
    acts = P(DP, PLANE, None)
    mats = P(ALL, None)
    vecs = P(None, ALL)
    ladder = sizes["dp"] == 4 and sizes["ctx"] == 2 and sizes["fsdp"] == 4
    return jax.shard_map(
        ladder_shards if ladder else wide_shards,
        mesh=fine,
        in_specs=(acts, P(DP, PLANE), acts) + (mats,) * 4 + (vecs,) + (mats,) * 8 + (vecs,) * 2,
        out_specs=(acts, acts) + (mats,) * 12 + (vecs,) * 3,
        check_vma=False,
    )
```

```python
import jax
import jax.numpy as jnp
from jax import lax
from jax.sharding import Mesh, PartitionSpec as P

HEADS = 8
KV_HEADS = 4
HEAD_DIM = 256
STEP = 10

NORM_EPS = 1e-06
SOFT_CAP = 50.0
THETA = 10000.0
BETA_ONE = 0.9
BETA_TWO = 0.95
ADAM_EPS = 1e-08
MATRIX_RATE = 0.03
GAIN_RATE = 0.2
WEIGHT_DECAY = 0.1

DP = ("dh", "dl")
PLANE = ("ctx", "fy", "core")
ALL = DP + PLANE
LADDER = DP + ("ctx",)
GROUP = PLANE
ACROSS = DP


def f32(v):
    return v.astype(jnp.float32)


def bf(v):
    return v.astype(jnp.bfloat16)


def dot(left, right, dims):
    return lax.dot_general(left, right, (dims, ((), ())), preferred_element_type=jnp.float32)


def mm(left, right):
    return dot(left, right, ((1,), (0,)))


def mm_nt(left, right):
    return dot(left, right, ((1,), (1,)))


def mm_tn(left, right):
    return dot(left, right, ((0,), (0,)))


def rms_scale(values, gain):
    inverse = lax.rsqrt(jnp.mean(values * values, axis=-1, keepdims=True) + NORM_EPS)
    return values * inverse * (1.0 + gain)


def rotary_tables(places):
    half = HEAD_DIM // 2
    freqs = THETA ** (-(jnp.arange(half, dtype=jnp.float32) * 2.0 / HEAD_DIM))
    angles = f32(places)[:, None] * freqs[None, :]
    return (jnp.cos(angles), jnp.sin(angles))


def rotary(values, cosine, sine):
    half = HEAD_DIM // 2
    first = values[..., :half]
    second = values[..., half:]
    return jnp.concatenate(
        [first * cosine - second * sine, second * cosine + first * sine], axis=-1
    )


def unrotary(values, cosine, sine):
    return rotary(values, cosine, -sine)


def adam_step(weight, grad, first, second, rate, decay):
    first_new = BETA_ONE * first + (1.0 - BETA_ONE) * grad
    second_new = BETA_TWO * second + (1.0 - BETA_TWO) * grad * grad
    ratio = (
        first_new
        / (1.0 - BETA_ONE**STEP)
        / (jnp.sqrt(second_new / (1.0 - BETA_TWO**STEP)) + ADAM_EPS)
    )
    return (weight - rate * (ratio + decay * weight), first_new, second_new)


def gather(v, axes, axis=0):
    return lax.all_gather(v, axes, axis=axis, tiled=True)


def scatter_sum(v, axes):
    return lax.psum_scatter(v, axes, scatter_dimension=0, tiled=True)


def swap(v, axes):
    return lax.all_to_all(v, axes, split_axis=0, concat_axis=0, tiled=True)


def hold(v):
    return lax.optimization_barrier(v)


def flip(v, axis):
    return lax.ppermute(v, axis, [(0, 1), (1, 0)])


def plane_scatter(parts):
    size = parts.shape[0] // 8
    half = size // 2
    col, row, core = (lax.axis_index(axis) for axis in PLANE)
    parts = parts.reshape((4, 2, size) + parts.shape[1:])
    sent = lax.dynamic_index_in_dim(parts, 1 - core, 1, keepdims=False)
    kept = lax.dynamic_index_in_dim(parts, core, 1, keepdims=False)
    both = bf(f32(kept) + f32(flip(sent, "core")))
    own, over_y, over_x, corner = (
        lax.dynamic_index_in_dim(both, (2 * col + row) ^ bits, 0, keepdims=False) for bits in range(4)
    )
    got_y = flip(corner[:half], "ctx")
    got_x = flip(corner[half:], "fy")
    over_y = jnp.concatenate([bf(f32(over_y[:half]) + f32(got_y)), over_y[half:]], axis=0)
    over_x = jnp.concatenate([over_x[:half], bf(f32(over_x[half:]) + f32(got_x))], axis=0)
    return f32(own) + f32(flip(over_x, "ctx")) + f32(flip(over_y, "fy"))


def line_gather(own):
    count = lax.axis_size(DP)
    ups, downs = ([], [])
    up, down = (own, own)
    for step in range(1, count):
        up = lax.ppermute(up, DP, [(i, i + 1) for i in range(step - 1, count - 1)])
        down = lax.ppermute(down, DP, [(i + 1, i) for i in range(count - step)])
        ups.append(up)
        downs.append(down)
    row = jnp.stack(ups[::-1] + [own] + downs)
    return lax.dynamic_slice_in_dim(row, count - 1 - lax.axis_index(DP), count, axis=0)


def ring_pairs():
    count = lax.axis_size(DP)
    ring = [2 * z for z in range(count)] + [2 * z + 1 for z in reversed(range(count))]
    onward = [(ring[i], ring[(i + 1) % len(ring)]) for i in range(len(ring))]
    return onward, [(b, a) for a, b in onward]


def ring_gather(own):
    onward, back = ring_pairs()
    half = own.shape[0] // 2
    steps = [[own]]
    behind, ahead = (own, own)
    for _ in range(len(onward) // 2 - 1):
        behind = lax.ppermute(behind, LADDER, onward)
        ahead = lax.ppermute(ahead, LADDER, back)
        steps.append([behind, ahead])
    steps.append(
        [
            lax.ppermute(behind[:half], LADDER, onward),
            lax.ppermute(ahead[half:], LADDER, back),
        ]
    )
    return steps


def two_parts(steps):
    return [
        jnp.concatenate(sum(steps[:3], []), axis=0),
        jnp.concatenate(sum(steps[3:], []), axis=0),
    ]


def steps_of(parts, size):
    early, late = parts
    steps = [early[:size], early[size : 3 * size], early[3 * size :]]
    return steps + [late[: 2 * size], late[2 * size :]]


def ring_scatter(pieces):
    onward, back = ring_pairs()
    size = pieces[0].shape[0]
    half = size // 2
    ahead = lax.ppermute(pieces[-1][:half], LADDER, onward)
    behind = lax.ppermute(pieces[-1][half:], LADDER, back)
    for step in range(len(pieces) - 2, 0, -1):
        to_behind, to_ahead = (pieces[step][:size], pieces[step][size:])
        if step == len(pieces) - 2:
            to_ahead = jnp.concatenate(
                [bf(f32(to_ahead[:half]) + f32(ahead)), to_ahead[half:]], axis=0
            )
            to_behind = jnp.concatenate(
                [to_behind[:half], bf(f32(to_behind[half:]) + f32(behind))], axis=0
            )
        else:
            to_ahead = bf(f32(to_ahead) + f32(ahead))
            to_behind = bf(f32(to_behind) + f32(behind))
        ahead = lax.ppermute(to_ahead, LADDER, onward)
        behind = lax.ppermute(to_behind, LADDER, back)
    return f32(pieces[0]) + f32(ahead) + f32(behind)


def quad_blocks(own):
    over_y = flip(own, "fy")
    return [own, flip(own, "core"), over_y, flip(over_y, "core")]


def quad_place(blocks, parts):
    me = lax.axis_index(("fy", "core"))
    count, rows, cols = blocks[0][0].shape
    whole = jnp.zeros((count, 4, rows, parts * cols), blocks[0][0].dtype)
    for part in range(parts):
        for bits, block in enumerate(blocks[part]):
            whole = lax.dynamic_update_slice(
                whole, block[:, None], (0, me ^ bits, 0, part * cols)
            )
    return whole


def quad_scatter(parts):
    core, row = (lax.axis_index("core"), lax.axis_index("fy"))
    parts = parts.reshape(parts.shape[:1] + (2, 2) + parts.shape[2:])
    sent = lax.dynamic_index_in_dim(parts, 1 - core, 2, keepdims=False)
    kept = lax.dynamic_index_in_dim(parts, core, 2, keepdims=False)
    both = bf(f32(kept) + f32(flip(sent, "core")))
    sent = lax.dynamic_index_in_dim(both, 1 - row, 1, keepdims=False)
    kept = lax.dynamic_index_in_dim(both, row, 1, keepdims=False)
    return bf(f32(kept) + f32(flip(sent, "fy")))


def ladder_shards(
    hidden_in,
    positions,
    cotangent,
    w_qkv,
    w_out,
    w_gate_up,
    w_down,
    gains,
    m_qkv,
    v_qkv,
    m_out,
    v_out,
    m_gate_up,
    v_gate_up,
    m_down,
    v_down,
    m_gains,
    v_gains,
):
    x_own = hidden_in[0]
    tok, width = x_own.shape
    rows = w_qkv.shape[0]
    planes = lax.axis_size(DP)
    group = lax.axis_size(LADDER)
    q_width = HEADS * HEAD_DIM
    core = lax.axis_index("core")

    q_cols = w_qkv[:, :q_width].reshape(rows, HEADS, HEAD_DIM)
    kv_cols = w_qkv[:, q_width:].reshape(rows, 2, KV_HEADS, HEAD_DIM)
    kv_cols = jnp.swapaxes(kv_cols, 1, 2).reshape(rows, HEADS, HEAD_DIM)
    pieces = jnp.swapaxes(jnp.concatenate([q_cols, kv_cols], axis=2), 0, 1)
    first = jnp.stack([positions[0, 0] // 128, positions[0, 0] % 128])
    own_gains = jnp.concatenate([gains.reshape(4 * rows), bf(first)])[None, None]
    own_gains = jnp.pad(own_gains, ((0, 0), (0, 7), (0, 2 * HEAD_DIM - 4 * rows - 2)))
    pieces = jnp.concatenate(
        [pieces, jnp.broadcast_to(own_gains, (HEADS,) + own_gains.shape[1:])], axis=1
    )
    got = swap(pieces, PLANE)
    first = got[:, rows, 4 * rows : 4 * rows + 2].astype(jnp.int32)
    pos_all = first[:, :1] * 128 + first[:, 1:] + jnp.arange(tok, dtype=jnp.int32)[None]
    pos_all = pos_all.reshape(-1)
    cosine, sine = rotary_tables(pos_all)
    got = line_gather(got)
    ff_own = w_down.shape[0] * 4
    cols = []
    for part in range(2):
        piece = w_gate_up[:, part * group * ff_own : (part + 1) * group * ff_own]
        cols.append(jnp.swapaxes(piece.reshape(rows, group, ff_own), 0, 1))
    got, cols[0], w_down_late = hold((got, cols[0], w_down))
    w_own = got[:, :, :rows].reshape(width, 2 * HEAD_DIM)
    gain_vals = got[:, :, rows, : 4 * rows].reshape(planes * HEADS, 4, rows)
    gain_vals = f32(jnp.swapaxes(gain_vals, 0, 1).reshape(4, width))
    out_full = lax.all_gather(gather(w_out[None], DP), PLANE, axis=1, tiled=False)
    out_full = out_full.reshape(q_width, width)

    x_all = gather(x_own, PLANE)

    cols[0] = swap(cols[0], LADDER)
    cols[0], cols[1] = hold((cols[0], cols[1]))
    cols[1] = swap(cols[1], LADDER)
    down_own = quad_place([quad_blocks(w_down_late[None])], 1).reshape(ff_own, width)
    gate_up_own = quad_place([quad_blocks(v) for v in cols], 2).reshape(width, 2 * ff_own)

    normed_all = bf(rms_scale(f32(x_all), gain_vals[0]))
    qkv = mm(normed_all, w_own)
    query = bf(rotary(qkv[:, :HEAD_DIM], cosine, sine) * HEAD_DIM ** (-0.5))
    half = qkv[:, HEAD_DIM:]
    mine = jnp.where(core == 0, bf(rotary(half, cosine, sine)), bf(half))
    other = flip(mine, "core")
    key = jnp.where(core == 0, mine, other)
    value = jnp.where(core == 0, other, mine)
    scores = mm_nt(query, key)
    capped = SOFT_CAP * jnp.tanh(scores / SOFT_CAP)
    weights = jnp.where(pos_all[:, None] >= pos_all[None, :], jnp.exp(capped), 0.0)
    weights_b = bf(weights)
    total = jnp.sum(weights, axis=-1, keepdims=True)
    attn = mm(weights_b, value) / total
    attn_own = swap(bf(attn).reshape(HEADS, tok, HEAD_DIM), PLANE)
    attn_own = jnp.swapaxes(attn_own, 0, 1).reshape(tok, q_width)
    mixed = mm(attn_own, out_full)

    x_rows = f32(x_own)
    branch_one, pull_one = jax.vjp(rms_scale, mixed, gain_vals[1])
    resid = x_rows + branch_one
    normed_two, pull_two = jax.vjp(rms_scale, resid, gain_vals[2])

    tokens = two_parts(ring_gather(bf(normed_two)))
    inners, pulls, downs = ([], [], [])
    for piece in tokens:
        gate_up = mm(piece, gate_up_own)
        inner, pull = jax.vjp(
            lambda gate, up_part: jax.nn.gelu(gate, approximate=True) * up_part,
            gate_up[:, :ff_own],
            gate_up[:, ff_own:],
        )
        inners.append(bf(inner))
        pulls.append(pull)
        downs.append(bf(mm(inners[-1], down_own)))
    down = ring_scatter(steps_of(hold(downs), tok))
    branch_two, pull_three = jax.vjp(rms_scale, down, gain_vals[3])
    block_out = bf(resid + branch_two)[None]
    grad_top = f32(cotangent[0])
    grad_down_in, gain_grad_three = pull_three(grad_top)
    grad_downs = two_parts(ring_gather(bf(grad_down_in)))
    grad_gus, parts = ([], [])
    for piece, pull in zip(grad_downs, pulls):
        grad_gus.append(bf(jnp.concatenate(pull(mm_nt(piece, down_own)), axis=1)))
        parts.append(bf(mm_nt(grad_gus[-1], gate_up_own)))
    tokens, inners, grad_downs, grad_gus, parts = hold(
        (tokens, inners, grad_downs, grad_gus, parts)
    )
    grad_normed_two = ring_scatter(steps_of(parts, tok))
    tokens_b = jnp.concatenate(tokens, axis=0)
    grad_gu_b = jnp.concatenate(grad_gus, axis=0)
    grad_halves = [bf(mm_tn(tokens_b, grad_gu_b[:, :ff_own])), bf(mm_tn(tokens_b, grad_gu_b[:, ff_own:]))]
    grad_down_w = bf(mm_tn(jnp.concatenate(inners, axis=0), jnp.concatenate(grad_downs, axis=0)))
    grad_normed_two, grad_halves, grad_down_w = hold((grad_normed_two, grad_halves, grad_down_w))
    grad_resid_two, _ = pull_two(grad_normed_two)
    grad_resid = grad_top + grad_resid_two
    grad_mixed, gain_grad_one = pull_one(grad_resid)
    grad_mixed_b = bf(grad_mixed)

    grad_attn = bf(mm_nt(grad_mixed_b, out_full)).reshape(tok, HEADS, HEAD_DIM)
    grad_head = swap(jnp.swapaxes(grad_attn, 0, 1), PLANE).reshape(HEADS * tok, HEAD_DIM)
    grad_head = f32(grad_head)
    rho = bf(grad_head / total)
    delta = jnp.sum(grad_head * attn, axis=-1, keepdims=True) / total
    pulled = mm_nt(rho, value)
    grad_scores = bf((pulled - delta) * weights * (1.0 - (capped / SOFT_CAP) ** 2))
    grad_query = mm(grad_scores, key) * HEAD_DIM ** (-0.5)
    grad_key = mm_tn(grad_scores, query)
    grad_value = mm_tn(weights_b, rho)
    sent = jnp.where(core == 0, grad_value, grad_key)
    grad_half = jnp.where(core == 0, grad_key, grad_value) + flip(sent, "core")
    grad_half = jnp.where(core == 0, unrotary(grad_half, cosine, sine), grad_half)
    grad_qkv = bf(jnp.concatenate([unrotary(grad_query, cosine, sine), grad_half], axis=1))
    attn_cols = attn_own.reshape(tok, planes, HEADS, w_out.shape[0])
    attn_cols = jnp.transpose(attn_cols, (2, 0, 1, 3)).reshape(HEADS, tok, HEAD_DIM)
    attn_cols = swap(attn_cols, PLANE).reshape(HEADS * tok, HEAD_DIM)
    grad_qkv, attn_cols, grad_mixed_all = hold(
        (grad_qkv, attn_cols, gather(grad_mixed_b, PLANE))
    )
    grad_normed = plane_scatter(bf(mm_nt(grad_qkv, w_own)))
    _, pull_zero = jax.vjp(rms_scale, x_rows, gain_vals[0])
    grad_x_zero, _ = pull_zero(grad_normed)
    input_grad = (grad_resid + grad_x_zero)[None]

    grad_w = bf(mm_tn(normed_all, grad_qkv))
    grad_halves = [quad_scatter(v.reshape(group, 4, rows, ff_own)) for v in grad_halves]
    grad_w, grad_halves = hold((grad_w, grad_halves))
    grad_w = scatter_sum(grad_w, DP).reshape(HEADS, rows, 2 * HEAD_DIM)
    for part in range(2):
        part_w = jnp.swapaxes(swap(grad_halves[part], LADDER), 0, 1)
        grad_halves[part] = part_w.reshape(rows, group * ff_own)
    grad_gate_up_w = f32(jnp.concatenate(grad_halves, axis=1))
    grad_down_w = f32(quad_scatter(grad_down_w.reshape(1, 4, ff_own // 4, width))[0])
    grad_out_w = f32(scatter_sum(bf(mm_tn(attn_cols, grad_mixed_all)), DP))
    grad_w = f32(jnp.swapaxes(swap(grad_w, PLANE), 0, 1))
    grad_q_w = grad_w[:, :, :HEAD_DIM].reshape(rows, q_width)
    grad_kv_w = grad_w[:, :, HEAD_DIM:].reshape(rows, KV_HEADS, 2, HEAD_DIM)
    grad_kv_w = jnp.swapaxes(grad_kv_w, 1, 2).reshape(rows, q_width)
    grad_qkv_w = jnp.concatenate([grad_q_w, grad_kv_w], axis=1)

    gain_zero = jnp.sum(f32(w_qkv) * grad_qkv_w, axis=1) / (1.0 + f32(gains[0]))
    gain_two = jnp.sum(f32(w_gate_up) * grad_gate_up_w, axis=1) / (1.0 + f32(gains[2]))
    others = jnp.stack([gain_grad_one, gain_grad_three]).reshape(2, planes * HEADS, rows)
    others = jnp.sum(swap(jnp.swapaxes(others, 0, 1), ALL), axis=0)
    grad_gains = jnp.stack([gain_zero, others[0], gain_two, others[1]], axis=0)

    return (
        (block_out, input_grad)
        + adam_step(f32(w_qkv), grad_qkv_w, m_qkv, v_qkv, MATRIX_RATE, WEIGHT_DECAY)
        + adam_step(f32(w_out), grad_out_w, m_out, v_out, MATRIX_RATE, WEIGHT_DECAY)
        + adam_step(f32(w_gate_up), grad_gate_up_w, m_gate_up, v_gate_up, MATRIX_RATE, WEIGHT_DECAY)
        + adam_step(f32(w_down), grad_down_w, m_down, v_down, MATRIX_RATE, WEIGHT_DECAY)
        + adam_step(f32(gains), grad_gains, m_gains, v_gains, GAIN_RATE, 0.0)
    )


def token_attention(x_own, pos_own, w_qkv, w_out, gains):
    tok = x_own.shape[0]
    q_width = HEADS * HEAD_DIM
    k_width = KV_HEADS * HEAD_DIM
    groups = HEADS // KV_HEADS
    qkv_full = gather(w_qkv, ALL)
    out_full = gather(w_out, ALL)
    gain_vals = f32(gather(gains, ALL, 1))
    normed = bf(rms_scale(f32(x_own), gain_vals[0]))
    qkv = mm(normed, qkv_full)
    cosine, sine = rotary_tables(pos_own)
    cosine, sine = (cosine[:, None, :], sine[:, None, :])
    query = rotary(qkv[:, :q_width].reshape(tok, HEADS, HEAD_DIM), cosine, sine)
    query = bf(query * HEAD_DIM ** (-0.5)).reshape(tok, KV_HEADS, groups, HEAD_DIM)
    key_own = qkv[:, q_width : q_width + k_width].reshape(tok, KV_HEADS, HEAD_DIM)
    key = gather(bf(rotary(key_own, cosine, sine)), PLANE)
    value = gather(bf(qkv[:, q_width + k_width :]).reshape(tok, KV_HEADS, HEAD_DIM), PLANE)
    pos_all = gather(pos_own, PLANE)
    count = pos_all.shape[0]
    scores = jnp.einsum("tgjd,sgd->gjts", query, key, preferred_element_type=jnp.float32)
    capped = SOFT_CAP * jnp.tanh(scores / SOFT_CAP)
    weights = jnp.where(pos_own[:, None] >= pos_all[None, :], jnp.exp(capped), 0.0)
    weights_b = bf(weights)
    total = jnp.sum(weights, axis=-1)
    attn = jnp.einsum("gjts,sgd->gjtd", weights_b, value, preferred_element_type=jnp.float32)
    attn = attn / total[..., None]
    attn_b = bf(jnp.transpose(attn, (2, 0, 1, 3)).reshape(tok, q_width))
    mixed = mm(attn_b, out_full)

    def backward(grad_mixed_b):
        grad_attn = mm_nt(grad_mixed_b, out_full).reshape(tok, KV_HEADS, groups, HEAD_DIM)
        grad_heads = jnp.transpose(grad_attn, (1, 2, 0, 3))
        rho = bf(grad_heads / total[..., None])
        delta = jnp.sum(grad_heads * attn, axis=-1) / total
        pulled = jnp.einsum("gjtd,sgd->gjts", rho, value, preferred_element_type=jnp.float32)
        grad_scores = bf(
            (pulled - delta[..., None]) * weights * (1.0 - (capped / SOFT_CAP) ** 2)
        )
        grad_query = jnp.einsum(
            "gjts,sgd->tgjd", grad_scores, key, preferred_element_type=jnp.float32
        ).reshape(tok, HEADS, HEAD_DIM)
        grad_key = jnp.einsum(
            "gjts,tgjd->sgd", grad_scores, query, preferred_element_type=jnp.float32
        ).reshape(count, k_width)
        grad_value = jnp.einsum(
            "gjts,gjtd->sgd", weights_b, rho, preferred_element_type=jnp.float32
        ).reshape(count, k_width)
        grad_kv = scatter_sum(jnp.concatenate([grad_key, grad_value], axis=1), PLANE)
        grad_query = unrotary(grad_query * HEAD_DIM ** (-0.5), cosine, sine)
        grad_key = unrotary(grad_kv[:, :k_width].reshape(tok, KV_HEADS, HEAD_DIM), cosine, sine)
        grad_qkv = bf(
            jnp.concatenate(
                [
                    grad_query.reshape(tok, q_width),
                    grad_key.reshape(tok, k_width),
                    grad_kv[:, k_width:],
                ],
                axis=1,
            )
        )
        grad_normed = mm_nt(grad_qkv, qkv_full)
        grad_qkv_w = f32(scatter_sum(bf(mm_tn(normed, grad_qkv)), ALL))
        grad_out_w = f32(scatter_sum(bf(mm_tn(attn_b, grad_mixed_b)), ALL))
        return grad_normed, grad_qkv_w, grad_out_w

    return mixed, gain_vals, backward


def wide_shards(
    hidden_in,
    positions,
    cotangent,
    w_qkv,
    w_out,
    w_gate_up,
    w_down,
    gains,
    m_qkv,
    v_qkv,
    m_out,
    v_out,
    m_gate_up,
    v_gate_up,
    m_down,
    v_down,
    m_gains,
    v_gains,
):
    x_own = hidden_in[0]
    rows, width = (w_qkv.shape[0], x_own.shape[1])
    group, across = (lax.axis_size(GROUP), lax.axis_size(ACROSS))
    ff_piece = w_down.shape[0]
    ff_own = across * ff_piece
    gu_pieces = w_gate_up.reshape(rows, 2, across, group, ff_piece)
    gu_pieces = jnp.transpose(gu_pieces, (3, 0, 1, 2, 4)).reshape(group * rows, 2 * ff_own)

    mixed, gain_vals, attention_back = token_attention(x_own, positions[0], w_qkv, w_out, gains)
    gu_own = gather(swap(gu_pieces, GROUP), ACROSS)
    down_own = gather(w_down, ACROSS)

    x_rows = f32(x_own)
    branch_one, pull_one = jax.vjp(rms_scale, mixed, gain_vals[1])
    resid = x_rows + branch_one
    normed_two, pull_two = jax.vjp(rms_scale, resid, gain_vals[2])
    tokens_b = gather(bf(normed_two), GROUP)
    gate_up = mm(tokens_b, gu_own)
    inner, pull_gelu = jax.vjp(
        lambda gate, up_part: jax.nn.gelu(gate, approximate=True) * up_part,
        gate_up[:, :ff_own],
        gate_up[:, ff_own:],
    )
    inner_b = bf(inner)
    down = f32(scatter_sum(bf(mm(inner_b, down_own)), GROUP))
    branch_two, pull_three = jax.vjp(rms_scale, down, gain_vals[3])
    block_out = bf(resid + branch_two)[None]
    grad_top = f32(cotangent[0])
    grad_down_in, gain_grad_three = pull_three(grad_top)
    grad_down_b = gather(bf(grad_down_in), GROUP)
    grad_gate, grad_up = pull_gelu(mm_nt(grad_down_b, down_own))
    grad_gu_b = bf(jnp.concatenate([grad_gate, grad_up], axis=1))
    grad_normed_two = f32(scatter_sum(bf(mm_nt(grad_gu_b, gu_own)), GROUP))
    grad_gate_up_w = scatter_sum(bf(mm_tn(tokens_b, grad_gu_b)), ACROSS)
    grad_down_w = f32(scatter_sum(bf(mm_tn(inner_b, grad_down_b)), ACROSS))

    grad_resid_two, gain_grad_two = pull_two(grad_normed_two)
    grad_resid = grad_top + grad_resid_two
    grad_mixed, gain_grad_one = pull_one(grad_resid)
    grad_normed, grad_qkv_w, grad_out_w = attention_back(bf(grad_mixed))
    _, pull_zero = jax.vjp(rms_scale, x_rows, gain_vals[0])
    grad_x_zero, gain_grad_zero = pull_zero(grad_normed)
    input_grad = (grad_resid + grad_x_zero)[None]

    grad_gate_up_w = swap(grad_gate_up_w, GROUP).reshape(group, rows, 2, across, ff_piece)
    grad_gate_up_w = f32(jnp.transpose(grad_gate_up_w, (1, 2, 3, 0, 4)).reshape(rows, -1))
    gain_term = jnp.stack([gain_grad_zero, gain_grad_one, gain_grad_two, gain_grad_three], axis=0)
    grad_gains = lax.psum_scatter(gain_term, ALL, scatter_dimension=1, tiled=True)

    return (
        (block_out, input_grad)
        + adam_step(f32(w_qkv), grad_qkv_w, m_qkv, v_qkv, MATRIX_RATE, WEIGHT_DECAY)
        + adam_step(f32(w_out), grad_out_w, m_out, v_out, MATRIX_RATE, WEIGHT_DECAY)
        + adam_step(f32(w_gate_up), grad_gate_up_w, m_gate_up, v_gate_up, MATRIX_RATE, WEIGHT_DECAY)
        + adam_step(f32(w_down), grad_down_w, m_down, v_down, MATRIX_RATE, WEIGHT_DECAY)
        + adam_step(f32(gains), grad_gains, m_gains, v_gains, GAIN_RATE, 0.0)
    )


def solution(mesh):
    sizes = dict(mesh.shape)
    fine = Mesh(
        mesh.devices.reshape(sizes["dp"] // 2, 2, sizes["ctx"], sizes["fsdp"] // 2, 2),
        ("dh", "dl", "ctx", "fy", "core"),
    )
    acts = P(DP, PLANE, None)
    mats = P(ALL, None)
    vecs = P(None, ALL)
    ladder = sizes["dp"] == 4 and sizes["ctx"] == 2 and sizes["fsdp"] == 4
    return jax.shard_map(
        ladder_shards if ladder else wide_shards,
        mesh=fine,
        in_specs=(acts, P(DP, PLANE), acts) + (mats,) * 4 + (vecs,) + (mats,) * 8 + (vecs,) * 2,
        out_specs=(acts, acts) + (mats,) * 12 + (vecs,) * 3,
        check_vma=False,
    )
```

```python
import jax
import jax.numpy as jnp
from jax import lax
from jax.sharding import Mesh, PartitionSpec as P

HEADS = 8
KV_HEADS = 4
HEAD_DIM = 256
STEP = 10

NORM_EPS = 1e-06
SOFT_CAP = 50.0
THETA = 10000.0
BETA_ONE = 0.9
BETA_TWO = 0.95
ADAM_EPS = 1e-08
MATRIX_RATE = 0.03
GAIN_RATE = 0.2
WEIGHT_DECAY = 0.1

DP = ("dh", "dl")
PLANE = ("ctx", "fy", "core")
ALL = DP + PLANE
LADDER = DP + ("ctx",)
GROUP = PLANE
ACROSS = DP


def f32(v):
    return v.astype(jnp.float32)


def bf(v):
    return v.astype(jnp.bfloat16)


def dot(left, right, dims):
    return lax.dot_general(left, right, (dims, ((), ())), preferred_element_type=jnp.float32)


def mm(left, right):
    return dot(left, right, ((1,), (0,)))


def mm_nt(left, right):
    return dot(left, right, ((1,), (1,)))


def mm_tn(left, right):
    return dot(left, right, ((0,), (0,)))


def rms_scale(values, gain):
    inverse = lax.rsqrt(jnp.mean(values * values, axis=-1, keepdims=True) + NORM_EPS)
    return values * inverse * (1.0 + gain)


def rotary_tables(places):
    half = HEAD_DIM // 2
    freqs = THETA ** (-(jnp.arange(half, dtype=jnp.float32) * 2.0 / HEAD_DIM))
    angles = f32(places)[:, None] * freqs[None, :]
    return (jnp.cos(angles), jnp.sin(angles))


def rotary(values, cosine, sine):
    half = HEAD_DIM // 2
    first = values[..., :half]
    second = values[..., half:]
    return jnp.concatenate(
        [first * cosine - second * sine, second * cosine + first * sine], axis=-1
    )


def unrotary(values, cosine, sine):
    return rotary(values, cosine, -sine)


def adam_step(weight, grad, first, second, rate, decay):
    first_new = BETA_ONE * first + (1.0 - BETA_ONE) * grad
    second_new = BETA_TWO * second + (1.0 - BETA_TWO) * grad * grad
    ratio = (
        first_new
        / (1.0 - BETA_ONE**STEP)
        / (jnp.sqrt(second_new / (1.0 - BETA_TWO**STEP)) + ADAM_EPS)
    )
    return (weight - rate * (ratio + decay * weight), first_new, second_new)


def gather(v, axes, axis=0):
    return lax.all_gather(v, axes, axis=axis, tiled=True)


def scatter_sum(v, axes):
    return lax.psum_scatter(v, axes, scatter_dimension=0, tiled=True)


def swap(v, axes):
    return lax.all_to_all(v, axes, split_axis=0, concat_axis=0, tiled=True)


def hold(v):
    return lax.optimization_barrier(v)


def flip(v, axis):
    return lax.ppermute(v, axis, [(0, 1), (1, 0)])


def plane_scatter(parts):
    size = parts.shape[0] // 8
    half = size // 2
    col, row, core = (lax.axis_index(axis) for axis in PLANE)
    parts = parts.reshape((4, 2, size) + parts.shape[1:])
    sent = lax.dynamic_index_in_dim(parts, 1 - core, 1, keepdims=False)
    kept = lax.dynamic_index_in_dim(parts, core, 1, keepdims=False)
    both = bf(f32(kept) + f32(flip(sent, "core")))
    own, over_y, over_x, corner = (
        lax.dynamic_index_in_dim(both, (2 * col + row) ^ bits, 0, keepdims=False) for bits in range(4)
    )
    got_y = flip(corner[:half], "ctx")
    got_x = flip(corner[half:], "fy")
    over_y = jnp.concatenate([bf(f32(over_y[:half]) + f32(got_y)), over_y[half:]], axis=0)
    over_x = jnp.concatenate([over_x[:half], bf(f32(over_x[half:]) + f32(got_x))], axis=0)
    return f32(own) + f32(flip(over_x, "ctx")) + f32(flip(over_y, "fy"))


def line_gather(own):
    count = lax.axis_size(DP)
    ups, downs = ([], [])
    up, down = (own, own)
    for step in range(1, count):
        up = lax.ppermute(up, DP, [(i, i + 1) for i in range(step - 1, count - 1)])
        down = lax.ppermute(down, DP, [(i + 1, i) for i in range(count - step)])
        ups.append(up)
        downs.append(down)
    row = jnp.stack(ups[::-1] + [own] + downs)
    return lax.dynamic_slice_in_dim(row, count - 1 - lax.axis_index(DP), count, axis=0)


def ring_pairs():
    count = lax.axis_size(DP)
    ring = [2 * z for z in range(count)] + [2 * z + 1 for z in reversed(range(count))]
    onward = [(ring[i], ring[(i + 1) % len(ring)]) for i in range(len(ring))]
    return onward, [(b, a) for a, b in onward]


def ring_gather(own):
    onward, back = ring_pairs()
    half = own.shape[0] // 2
    steps = [[own]]
    behind, ahead = (own, own)
    for _ in range(len(onward) // 2 - 1):
        behind = lax.ppermute(behind, LADDER, onward)
        ahead = lax.ppermute(ahead, LADDER, back)
        steps.append([behind, ahead])
    steps.append(
        [
            lax.ppermute(behind[:half], LADDER, onward),
            lax.ppermute(ahead[half:], LADDER, back),
        ]
    )
    return steps


def two_parts(steps):
    return [
        jnp.concatenate(sum(steps[:3], []), axis=0),
        jnp.concatenate(sum(steps[3:], []), axis=0),
    ]


def steps_of(parts, size):
    early, late = parts
    steps = [early[:size], early[size : 3 * size], early[3 * size :]]
    return steps + [late[: 2 * size], late[2 * size :]]


def ring_scatter(pieces):
    onward, back = ring_pairs()
    size = pieces[0].shape[0]
    half = size // 2
    ahead = lax.ppermute(pieces[-1][:half], LADDER, onward)
    behind = lax.ppermute(pieces[-1][half:], LADDER, back)
    for step in range(len(pieces) - 2, 0, -1):
        to_behind, to_ahead = (pieces[step][:size], pieces[step][size:])
        if step == len(pieces) - 2:
            to_ahead = jnp.concatenate(
                [bf(f32(to_ahead[:half]) + f32(ahead)), to_ahead[half:]], axis=0
            )
            to_behind = jnp.concatenate(
                [to_behind[:half], bf(f32(to_behind[half:]) + f32(behind))], axis=0
            )
        else:
            to_ahead = bf(f32(to_ahead) + f32(ahead))
            to_behind = bf(f32(to_behind) + f32(behind))
        to_ahead, to_behind = hold((to_ahead, to_behind))
        ahead = lax.ppermute(to_ahead, LADDER, onward)
        behind = lax.ppermute(to_behind, LADDER, back)
    return f32(pieces[0]) + f32(ahead) + f32(behind)


def quad_blocks(own, late=None):
    over_y = flip(own, "fy")
    if late is not None:
        over_y, _ = hold((over_y, late))
    return [own, flip(own, "core"), over_y, flip(over_y, "core")]


def quad_place(blocks, parts):
    me = lax.axis_index(("fy", "core"))
    count, rows, cols = blocks[0][0].shape
    whole = jnp.zeros((count, 4, rows, parts * cols), blocks[0][0].dtype)
    for part in range(parts):
        for bits, block in enumerate(blocks[part]):
            whole = lax.dynamic_update_slice(
                whole, block[:, None], (0, me ^ bits, 0, part * cols)
            )
    return whole


def quad_scatter(parts):
    core, row = (lax.axis_index("core"), lax.axis_index("fy"))
    parts = parts.reshape(parts.shape[:1] + (2, 2) + parts.shape[2:])
    sent = lax.dynamic_index_in_dim(parts, 1 - core, 2, keepdims=False)
    kept = lax.dynamic_index_in_dim(parts, core, 2, keepdims=False)
    both = bf(f32(kept) + f32(flip(sent, "core")))
    sent = lax.dynamic_index_in_dim(both, 1 - row, 1, keepdims=False)
    kept = lax.dynamic_index_in_dim(both, row, 1, keepdims=False)
    return bf(f32(kept) + f32(flip(sent, "fy")))


def ladder_shards(
    hidden_in,
    positions,
    cotangent,
    w_qkv,
    w_out,
    w_gate_up,
    w_down,
    gains,
    m_qkv,
    v_qkv,
    m_out,
    v_out,
    m_gate_up,
    v_gate_up,
    m_down,
    v_down,
    m_gains,
    v_gains,
):
    x_own = hidden_in[0]
    tok, width = x_own.shape
    rows = w_qkv.shape[0]
    planes = lax.axis_size(DP)
    group = lax.axis_size(LADDER)
    q_width = HEADS * HEAD_DIM
    core = lax.axis_index("core")

    q_cols = w_qkv[:, :q_width].reshape(rows, HEADS, HEAD_DIM)
    kv_cols = w_qkv[:, q_width:].reshape(rows, 2, KV_HEADS, HEAD_DIM)
    kv_cols = jnp.swapaxes(kv_cols, 1, 2).reshape(rows, HEADS, HEAD_DIM)
    pieces = jnp.swapaxes(jnp.concatenate([q_cols, kv_cols], axis=2), 0, 1)
    first = jnp.stack([positions[0, 0] // 128, positions[0, 0] % 128])
    own_gains = jnp.concatenate([gains.reshape(4 * rows), bf(first)])[None, None]
    own_gains = jnp.pad(own_gains, ((0, 0), (0, 7), (0, 2 * HEAD_DIM - 4 * rows - 2)))
    pieces = jnp.concatenate(
        [pieces, jnp.broadcast_to(own_gains, (HEADS,) + own_gains.shape[1:])], axis=1
    )
    x_all = gather(x_own, PLANE)
    out_line = line_gather(w_out)
    got = swap(pieces, PLANE)
    first = got[:, rows, 4 * rows : 4 * rows + 2].astype(jnp.int32)
    pos_all = first[:, :1] * 128 + first[:, 1:] + jnp.arange(tok, dtype=jnp.int32)[None]
    pos_all = pos_all.reshape(-1)
    cosine, sine = rotary_tables(pos_all)
    got = line_gather(got)
    ff_own = w_down.shape[0] * 4
    cols = []
    for part in range(2):
        piece = w_gate_up[:, part * group * ff_own : (part + 1) * group * ff_own]
        cols.append(jnp.swapaxes(piece.reshape(rows, group, ff_own), 0, 1))
    got, cols[0], w_down_late = hold((got, cols[0], w_down))
    w_own = got[:, :, :rows].reshape(width, 2 * HEAD_DIM)
    gain_vals = got[:, :, rows, : 4 * rows].reshape(planes * HEADS, 4, rows)
    gain_vals = f32(jnp.swapaxes(gain_vals, 0, 1).reshape(4, width))
    out_full = lax.all_gather(out_line, PLANE, axis=1, tiled=False).reshape(q_width, width)
    cols[0] = swap(cols[0], LADDER)

    normed_all = bf(rms_scale(f32(x_all), gain_vals[0]))
    qkv = mm(normed_all, w_own)
    query = bf(rotary(qkv[:, :HEAD_DIM], cosine, sine) * HEAD_DIM ** (-0.5))
    half = qkv[:, HEAD_DIM:]
    mine = jnp.where(core == 0, bf(rotary(half, cosine, sine)), bf(half))
    other = flip(mine, "core")
    key = jnp.where(core == 0, mine, other)
    value = jnp.where(core == 0, other, mine)
    scores = mm_nt(query, key)
    capped = SOFT_CAP * jnp.tanh(scores / SOFT_CAP)
    weights = jnp.where(pos_all[:, None] >= pos_all[None, :], jnp.exp(capped), 0.0)
    weights_b = bf(weights)
    total = jnp.sum(weights, axis=-1, keepdims=True)
    attn = mm(weights_b, value) / total
    cols[0], cols[1], _ = hold((cols[0], cols[1], attn))
    attn_own = swap(bf(attn).reshape(HEADS, tok, HEAD_DIM), PLANE)
    cols[1], _ = hold((swap(cols[1], LADDER), attn_own))
    down_own = quad_place([quad_blocks(w_down_late[None], attn)], 1).reshape(ff_own, width)
    gate_up_own = quad_place([quad_blocks(v) for v in cols], 2).reshape(width, 2 * ff_own)
    attn_own = jnp.swapaxes(attn_own, 0, 1).reshape(tok, q_width)
    mixed = mm(attn_own, out_full)

    x_rows = f32(x_own)
    branch_one, pull_one = jax.vjp(rms_scale, mixed, gain_vals[1])
    resid = x_rows + branch_one
    normed_two, pull_two = jax.vjp(rms_scale, resid, gain_vals[2])

    steps = ring_gather(bf(normed_two))
    tokens = two_parts(steps)
    inners, pulls, downs = ([], [], [])
    for piece in tokens:
        gate_up, _ = hold((mm(piece, gate_up_own), steps[3][0]))
        inner, pull = jax.vjp(
            lambda gate, up_part: jax.nn.gelu(gate, approximate=True) * up_part,
            gate_up[:, :ff_own],
            gate_up[:, ff_own:],
        )
        inners.append(bf(inner))
        pulls.append(pull)
        downs.append(bf(mm(inners[-1], down_own)))
    down = ring_scatter(steps_of(hold(downs), tok))
    branch_two, pull_three = jax.vjp(rms_scale, down, gain_vals[3])
    block_out = bf(resid + branch_two)[None]
    grad_top = f32(cotangent[0])
    grad_down_in, gain_grad_three = pull_three(grad_top)
    steps = ring_gather(bf(grad_down_in))
    grad_downs = two_parts(steps)
    grad_gus, parts = ([], [])
    for piece, pull in zip(grad_downs, pulls):
        grad_gus.append(bf(jnp.concatenate(pull(mm_nt(piece, down_own)), axis=1)))
        late, _ = hold((grad_gus[-1], steps[3][0]))
        parts.append(bf(mm_nt(late, gate_up_own)))
    tokens, inners, grad_downs, grad_gus, parts = hold(
        (tokens, inners, grad_downs, grad_gus, parts)
    )
    grad_normed_two = ring_scatter(steps_of(parts, tok))
    tokens_b = jnp.concatenate(tokens, axis=0)
    grad_gu_b = jnp.concatenate(grad_gus, axis=0)
    grad_halves = [bf(mm_tn(tokens_b, grad_gu_b[:, :ff_own])), bf(mm_tn(tokens_b, grad_gu_b[:, ff_own:]))]
    grad_down_w = bf(mm_tn(jnp.concatenate(inners, axis=0), jnp.concatenate(grad_downs, axis=0)))
    grad_normed_two, _, _ = hold((grad_normed_two, grad_halves, grad_down_w))
    grad_resid_two, _ = pull_two(grad_normed_two)
    grad_resid = grad_top + grad_resid_two
    grad_mixed, gain_grad_one = pull_one(grad_resid)
    grad_mixed_b = bf(grad_mixed)

    grad_attn = bf(mm_nt(grad_mixed_b, out_full)).reshape(tok, HEADS, HEAD_DIM)
    grad_head = swap(jnp.swapaxes(grad_attn, 0, 1), PLANE).reshape(HEADS * tok, HEAD_DIM)
    grad_head = f32(grad_head)
    rho = bf(grad_head / total)
    delta = jnp.sum(grad_head * attn, axis=-1, keepdims=True) / total
    pulled = mm_nt(rho, value)
    grad_scores = bf((pulled - delta) * weights * (1.0 - (capped / SOFT_CAP) ** 2))
    grad_query = mm(grad_scores, key) * HEAD_DIM ** (-0.5)
    grad_key = mm_tn(grad_scores, query)
    grad_value = mm_tn(weights_b, rho)
    sent = jnp.where(core == 0, grad_value, grad_key)
    grad_half = jnp.where(core == 0, grad_key, grad_value) + flip(sent, "core")
    grad_half = jnp.where(core == 0, unrotary(grad_half, cosine, sine), grad_half)
    grad_qkv = bf(jnp.concatenate([unrotary(grad_query, cosine, sine), grad_half], axis=1))
    attn_cols = attn_own.reshape(tok, planes, HEADS, w_out.shape[0])
    attn_cols = jnp.transpose(attn_cols, (2, 0, 1, 3)).reshape(HEADS, tok, HEAD_DIM)
    attn_cols = swap(attn_cols, PLANE).reshape(HEADS * tok, HEAD_DIM)
    grad_qkv, attn_cols, grad_mixed_all = hold(
        (grad_qkv, attn_cols, gather(grad_mixed_b, PLANE))
    )
    grad_normed = plane_scatter(bf(mm_nt(grad_qkv, w_own)))
    _, pull_zero = jax.vjp(rms_scale, x_rows, gain_vals[0])
    grad_x_zero, _ = pull_zero(grad_normed)
    input_grad = (grad_resid + grad_x_zero)[None]

    grad_w = bf(mm_tn(normed_all, grad_qkv))
    grad_halves = [quad_scatter(v.reshape(group, 4, rows, ff_own)) for v in grad_halves]
    grad_halves, _ = hold((grad_halves, grad_w))
    grad_w = scatter_sum(grad_w, DP).reshape(HEADS, rows, 2 * HEAD_DIM)
    for part in range(2):
        part_w = jnp.swapaxes(swap(grad_halves[part], LADDER), 0, 1)
        grad_halves[part] = part_w.reshape(rows, group * ff_own)
    grad_gate_up_w = f32(jnp.concatenate(grad_halves, axis=1))
    grad_down_w = f32(quad_scatter(grad_down_w.reshape(1, 4, ff_own // 4, width))[0])
    grad_out_w = f32(scatter_sum(bf(mm_tn(attn_cols, grad_mixed_all)), DP))
    grad_w = f32(jnp.swapaxes(swap(grad_w, PLANE), 0, 1))
    grad_q_w = grad_w[:, :, :HEAD_DIM].reshape(rows, q_width)
    grad_kv_w = grad_w[:, :, HEAD_DIM:].reshape(rows, KV_HEADS, 2, HEAD_DIM)
    grad_kv_w = jnp.swapaxes(grad_kv_w, 1, 2).reshape(rows, q_width)
    grad_qkv_w = jnp.concatenate([grad_q_w, grad_kv_w], axis=1)

    gain_zero = jnp.sum(f32(w_qkv) * grad_qkv_w, axis=1) / (1.0 + f32(gains[0]))
    gain_two = jnp.sum(f32(w_gate_up) * grad_gate_up_w, axis=1) / (1.0 + f32(gains[2]))
    others = jnp.stack([gain_grad_one, gain_grad_three]).reshape(2, planes * HEADS, rows)
    others = jnp.sum(swap(jnp.swapaxes(others, 0, 1), ALL), axis=0)
    grad_gains = jnp.stack([gain_zero, others[0], gain_two, others[1]], axis=0)

    return (
        (block_out, input_grad)
        + adam_step(f32(w_qkv), grad_qkv_w, m_qkv, v_qkv, MATRIX_RATE, WEIGHT_DECAY)
        + adam_step(f32(w_out), grad_out_w, m_out, v_out, MATRIX_RATE, WEIGHT_DECAY)
        + adam_step(f32(w_gate_up), grad_gate_up_w, m_gate_up, v_gate_up, MATRIX_RATE, WEIGHT_DECAY)
        + adam_step(f32(w_down), grad_down_w, m_down, v_down, MATRIX_RATE, WEIGHT_DECAY)
        + adam_step(f32(gains), grad_gains, m_gains, v_gains, GAIN_RATE, 0.0)
    )


def token_attention(x_own, pos_own, w_qkv, w_out, gains):
    tok = x_own.shape[0]
    q_width = HEADS * HEAD_DIM
    k_width = KV_HEADS * HEAD_DIM
    groups = HEADS // KV_HEADS
    qkv_full = gather(w_qkv, ALL)
    out_full = gather(w_out, ALL)
    gain_vals = f32(gather(gains, ALL, 1))
    normed = bf(rms_scale(f32(x_own), gain_vals[0]))
    qkv = mm(normed, qkv_full)
    cosine, sine = rotary_tables(pos_own)
    cosine, sine = (cosine[:, None, :], sine[:, None, :])
    query = rotary(qkv[:, :q_width].reshape(tok, HEADS, HEAD_DIM), cosine, sine)
    query = bf(query * HEAD_DIM ** (-0.5)).reshape(tok, KV_HEADS, groups, HEAD_DIM)
    key_own = qkv[:, q_width : q_width + k_width].reshape(tok, KV_HEADS, HEAD_DIM)
    key = gather(bf(rotary(key_own, cosine, sine)), PLANE)
    value = gather(bf(qkv[:, q_width + k_width :]).reshape(tok, KV_HEADS, HEAD_DIM), PLANE)
    pos_all = gather(pos_own, PLANE)
    count = pos_all.shape[0]
    scores = jnp.einsum("tgjd,sgd->gjts", query, key, preferred_element_type=jnp.float32)
    capped = SOFT_CAP * jnp.tanh(scores / SOFT_CAP)
    weights = jnp.where(pos_own[:, None] >= pos_all[None, :], jnp.exp(capped), 0.0)
    weights_b = bf(weights)
    total = jnp.sum(weights, axis=-1)
    attn = jnp.einsum("gjts,sgd->gjtd", weights_b, value, preferred_element_type=jnp.float32)
    attn = attn / total[..., None]
    attn_b = bf(jnp.transpose(attn, (2, 0, 1, 3)).reshape(tok, q_width))
    mixed = mm(attn_b, out_full)

    def backward(grad_mixed_b):
        grad_attn = mm_nt(grad_mixed_b, out_full).reshape(tok, KV_HEADS, groups, HEAD_DIM)
        grad_heads = jnp.transpose(grad_attn, (1, 2, 0, 3))
        rho = bf(grad_heads / total[..., None])
        delta = jnp.sum(grad_heads * attn, axis=-1) / total
        pulled = jnp.einsum("gjtd,sgd->gjts", rho, value, preferred_element_type=jnp.float32)
        grad_scores = bf(
            (pulled - delta[..., None]) * weights * (1.0 - (capped / SOFT_CAP) ** 2)
        )
        grad_query = jnp.einsum(
            "gjts,sgd->tgjd", grad_scores, key, preferred_element_type=jnp.float32
        ).reshape(tok, HEADS, HEAD_DIM)
        grad_key = jnp.einsum(
            "gjts,tgjd->sgd", grad_scores, query, preferred_element_type=jnp.float32
        ).reshape(count, k_width)
        grad_value = jnp.einsum(
            "gjts,gjtd->sgd", weights_b, rho, preferred_element_type=jnp.float32
        ).reshape(count, k_width)
        grad_kv = scatter_sum(jnp.concatenate([grad_key, grad_value], axis=1), PLANE)
        grad_query = unrotary(grad_query * HEAD_DIM ** (-0.5), cosine, sine)
        grad_key = unrotary(grad_kv[:, :k_width].reshape(tok, KV_HEADS, HEAD_DIM), cosine, sine)
        grad_qkv = bf(
            jnp.concatenate(
                [
                    grad_query.reshape(tok, q_width),
                    grad_key.reshape(tok, k_width),
                    grad_kv[:, k_width:],
                ],
                axis=1,
            )
        )
        grad_normed = mm_nt(grad_qkv, qkv_full)
        grad_qkv_w = f32(scatter_sum(bf(mm_tn(normed, grad_qkv)), ALL))
        grad_out_w = f32(scatter_sum(bf(mm_tn(attn_b, grad_mixed_b)), ALL))
        return grad_normed, grad_qkv_w, grad_out_w

    return mixed, gain_vals, backward


def wide_shards(
    hidden_in,
    positions,
    cotangent,
    w_qkv,
    w_out,
    w_gate_up,
    w_down,
    gains,
    m_qkv,
    v_qkv,
    m_out,
    v_out,
    m_gate_up,
    v_gate_up,
    m_down,
    v_down,
    m_gains,
    v_gains,
):
    x_own = hidden_in[0]
    rows, width = (w_qkv.shape[0], x_own.shape[1])
    group, across = (lax.axis_size(GROUP), lax.axis_size(ACROSS))
    ff_piece = w_down.shape[0]
    ff_own = across * ff_piece
    gu_pieces = w_gate_up.reshape(rows, 2, across, group, ff_piece)
    gu_pieces = jnp.transpose(gu_pieces, (3, 0, 1, 2, 4)).reshape(group * rows, 2 * ff_own)

    mixed, gain_vals, attention_back = token_attention(x_own, positions[0], w_qkv, w_out, gains)
    gu_own = gather(swap(gu_pieces, GROUP), ACROSS)
    down_own = gather(w_down, ACROSS)

    x_rows = f32(x_own)
    branch_one, pull_one = jax.vjp(rms_scale, mixed, gain_vals[1])
    resid = x_rows + branch_one
    normed_two, pull_two = jax.vjp(rms_scale, resid, gain_vals[2])
    tokens_b = gather(bf(normed_two), GROUP)
    gate_up = mm(tokens_b, gu_own)
    inner, pull_gelu = jax.vjp(
        lambda gate, up_part: jax.nn.gelu(gate, approximate=True) * up_part,
        gate_up[:, :ff_own],
        gate_up[:, ff_own:],
    )
    inner_b = bf(inner)
    down = f32(scatter_sum(bf(mm(inner_b, down_own)), GROUP))
    branch_two, pull_three = jax.vjp(rms_scale, down, gain_vals[3])
    block_out = bf(resid + branch_two)[None]
    grad_top = f32(cotangent[0])
    grad_down_in, gain_grad_three = pull_three(grad_top)
    grad_down_b = gather(bf(grad_down_in), GROUP)
    grad_gate, grad_up = pull_gelu(mm_nt(grad_down_b, down_own))
    grad_gu_b = bf(jnp.concatenate([grad_gate, grad_up], axis=1))
    grad_normed_two = f32(scatter_sum(bf(mm_nt(grad_gu_b, gu_own)), GROUP))
    grad_gate_up_w = scatter_sum(bf(mm_tn(tokens_b, grad_gu_b)), ACROSS)
    grad_down_w = f32(scatter_sum(bf(mm_tn(inner_b, grad_down_b)), ACROSS))

    grad_resid_two, gain_grad_two = pull_two(grad_normed_two)
    grad_resid = grad_top + grad_resid_two
    grad_mixed, gain_grad_one = pull_one(grad_resid)
    grad_normed, grad_qkv_w, grad_out_w = attention_back(bf(grad_mixed))
    _, pull_zero = jax.vjp(rms_scale, x_rows, gain_vals[0])
    grad_x_zero, gain_grad_zero = pull_zero(grad_normed)
    input_grad = (grad_resid + grad_x_zero)[None]

    grad_gate_up_w = swap(grad_gate_up_w, GROUP).reshape(group, rows, 2, across, ff_piece)
    grad_gate_up_w = f32(jnp.transpose(grad_gate_up_w, (1, 2, 3, 0, 4)).reshape(rows, -1))
    gain_term = jnp.stack([gain_grad_zero, gain_grad_one, gain_grad_two, gain_grad_three], axis=0)
    grad_gains = lax.psum_scatter(gain_term, ALL, scatter_dimension=1, tiled=True)

    return (
        (block_out, input_grad)
        + adam_step(f32(w_qkv), grad_qkv_w, m_qkv, v_qkv, MATRIX_RATE, WEIGHT_DECAY)
        + adam_step(f32(w_out), grad_out_w, m_out, v_out, MATRIX_RATE, WEIGHT_DECAY)
        + adam_step(f32(w_gate_up), grad_gate_up_w, m_gate_up, v_gate_up, MATRIX_RATE, WEIGHT_DECAY)
        + adam_step(f32(w_down), grad_down_w, m_down, v_down, MATRIX_RATE, WEIGHT_DECAY)
        + adam_step(f32(gains), grad_gains, m_gains, v_gains, GAIN_RATE, 0.0)
    )


def solution(mesh):
    sizes = dict(mesh.shape)
    fine = Mesh(
        mesh.devices.reshape(sizes["dp"] // 2, 2, sizes["ctx"], sizes["fsdp"] // 2, 2),
        ("dh", "dl", "ctx", "fy", "core"),
    )
    acts = P(DP, PLANE, None)
    mats = P(ALL, None)
    vecs = P(None, ALL)
    ladder = sizes["dp"] == 4 and sizes["ctx"] == 2 and sizes["fsdp"] == 4
    return jax.shard_map(
        ladder_shards if ladder else wide_shards,
        mesh=fine,
        in_specs=(acts, P(DP, PLANE), acts) + (mats,) * 4 + (vecs,) + (mats,) * 8 + (vecs,) * 2,
        out_specs=(acts, acts) + (mats,) * 12 + (vecs,) * 3,
        check_vma=False,
    )
```

```python
import jax
import jax.numpy as jnp
from jax import lax
from jax.sharding import Mesh, PartitionSpec as P

HEADS = 8
KV_HEADS = 4
HEAD_DIM = 256
STEP = 10

NORM_EPS = 1e-06
SOFT_CAP = 50.0
THETA = 10000.0
BETA_ONE = 0.9
BETA_TWO = 0.95
ADAM_EPS = 1e-08
MATRIX_RATE = 0.03
GAIN_RATE = 0.2
WEIGHT_DECAY = 0.1

DP = ("dh", "dl")
PLANE = ("ctx", "fy", "core")
ALL = DP + PLANE
LADDER = DP + ("ctx",)
GROUP = PLANE
ACROSS = DP


def f32(v):
    return v.astype(jnp.float32)


def bf(v):
    return v.astype(jnp.bfloat16)


def dot(left, right, dims):
    return lax.dot_general(left, right, (dims, ((), ())), preferred_element_type=jnp.float32)


def mm(left, right):
    return dot(left, right, ((1,), (0,)))


def mm_nt(left, right):
    return dot(left, right, ((1,), (1,)))


def mm_tn(left, right):
    return dot(left, right, ((0,), (0,)))


def rms_scale(values, gain):
    inverse = lax.rsqrt(jnp.mean(values * values, axis=-1, keepdims=True) + NORM_EPS)
    return values * inverse * (1.0 + gain)


def rotary_tables(places):
    half = HEAD_DIM // 2
    freqs = THETA ** (-(jnp.arange(half, dtype=jnp.float32) * 2.0 / HEAD_DIM))
    angles = f32(places)[:, None] * freqs[None, :]
    return (jnp.cos(angles), jnp.sin(angles))


def rotary(values, cosine, sine):
    half = HEAD_DIM // 2
    first = values[..., :half]
    second = values[..., half:]
    return jnp.concatenate(
        [first * cosine - second * sine, second * cosine + first * sine], axis=-1
    )


def unrotary(values, cosine, sine):
    return rotary(values, cosine, -sine)


def adam_step(weight, grad, first, second, rate, decay):
    first_new = BETA_ONE * first + (1.0 - BETA_ONE) * grad
    second_new = BETA_TWO * second + (1.0 - BETA_TWO) * grad * grad
    ratio = (
        first_new
        / (1.0 - BETA_ONE**STEP)
        / (jnp.sqrt(second_new / (1.0 - BETA_TWO**STEP)) + ADAM_EPS)
    )
    return (weight - rate * (ratio + decay * weight), first_new, second_new)


def gather(v, axes, axis=0):
    return lax.all_gather(v, axes, axis=axis, tiled=True)


def scatter_sum(v, axes):
    return lax.psum_scatter(v, axes, scatter_dimension=0, tiled=True)


def swap(v, axes):
    return lax.all_to_all(v, axes, split_axis=0, concat_axis=0, tiled=True)


def hold(v):
    return lax.optimization_barrier(v)


def flip(v, axis):
    return lax.ppermute(v, axis, [(0, 1), (1, 0)])


def plane_scatter(parts):
    size = parts.shape[0] // 8
    half = size // 2
    col, row, core = (lax.axis_index(axis) for axis in PLANE)
    parts = parts.reshape((4, 2, size) + parts.shape[1:])
    sent = lax.dynamic_index_in_dim(parts, 1 - core, 1, keepdims=False)
    kept = lax.dynamic_index_in_dim(parts, core, 1, keepdims=False)
    both = bf(f32(kept) + f32(flip(sent, "core")))
    own, over_y, over_x, corner = (
        lax.dynamic_index_in_dim(both, (2 * col + row) ^ bits, 0, keepdims=False) for bits in range(4)
    )
    got_y = flip(corner[:half], "ctx")
    got_x = flip(corner[half:], "fy")
    over_y = jnp.concatenate([bf(f32(over_y[:half]) + f32(got_y)), over_y[half:]], axis=0)
    over_x = jnp.concatenate([over_x[:half], bf(f32(over_x[half:]) + f32(got_x))], axis=0)
    return f32(own) + f32(flip(over_x, "ctx")) + f32(flip(over_y, "fy"))


def line_gather(own):
    count = lax.axis_size(DP)
    ups, downs = ([], [])
    up, down = (own, own)
    for step in range(1, count):
        up = lax.ppermute(up, DP, [(i, i + 1) for i in range(step - 1, count - 1)])
        down = lax.ppermute(down, DP, [(i + 1, i) for i in range(count - step)])
        ups.append(up)
        downs.append(down)
    row = jnp.stack(ups[::-1] + [own] + downs)
    return lax.dynamic_slice_in_dim(row, count - 1 - lax.axis_index(DP), count, axis=0)


def ring_pairs():
    count = lax.axis_size(DP)
    ring = [2 * z for z in range(count)] + [2 * z + 1 for z in reversed(range(count))]
    onward = [(ring[i], ring[(i + 1) % len(ring)]) for i in range(len(ring))]
    return onward, [(b, a) for a, b in onward]


def ring_gather(own):
    onward, back = ring_pairs()
    half = own.shape[0] // 2
    steps = [[own]]
    behind, ahead = (own, own)
    for _ in range(len(onward) // 2 - 1):
        behind = lax.ppermute(behind, LADDER, onward)
        ahead = lax.ppermute(ahead, LADDER, back)
        steps.append([behind, ahead])
    steps.append(
        [
            lax.ppermute(behind[:half], LADDER, onward),
            lax.ppermute(ahead[half:], LADDER, back),
        ]
    )
    return steps


def two_parts(steps):
    return [
        jnp.concatenate(sum(steps[:3], []), axis=0),
        jnp.concatenate(sum(steps[3:], []), axis=0),
    ]


def steps_of(parts, size):
    early, late = parts
    steps = [early[:size], early[size : 3 * size], early[3 * size :]]
    return steps + [late[: 2 * size], late[2 * size :]]


def ring_scatter(pieces):
    onward, back = ring_pairs()
    size = pieces[0].shape[0]
    half = size // 2
    ahead = lax.ppermute(pieces[-1][:half], LADDER, onward)
    behind = lax.ppermute(pieces[-1][half:], LADDER, back)
    for step in range(len(pieces) - 2, 0, -1):
        to_behind, to_ahead = (pieces[step][:size], pieces[step][size:])
        if step == len(pieces) - 2:
            to_ahead = jnp.concatenate(
                [bf(f32(to_ahead[:half]) + f32(ahead)), to_ahead[half:]], axis=0
            )
            to_behind = jnp.concatenate(
                [to_behind[:half], bf(f32(to_behind[half:]) + f32(behind))], axis=0
            )
        else:
            to_ahead = bf(f32(to_ahead) + f32(ahead))
            to_behind = bf(f32(to_behind) + f32(behind))
        to_ahead, to_behind = hold((to_ahead, to_behind))
        ahead = lax.ppermute(to_ahead, LADDER, onward)
        behind = lax.ppermute(to_behind, LADDER, back)
    return f32(pieces[0]) + f32(ahead) + f32(behind)


def quad_blocks(own, late=None):
    over_y = flip(own, "fy")
    if late is not None:
        over_y, _ = hold((over_y, late))
    return [own, flip(own, "core"), over_y, flip(over_y, "core")]


def quad_place(blocks, parts):
    me = lax.axis_index(("fy", "core"))
    count, rows, cols = blocks[0][0].shape
    whole = jnp.zeros((count, 4, rows, parts * cols), blocks[0][0].dtype)
    for part in range(parts):
        for bits, block in enumerate(blocks[part]):
            whole = lax.dynamic_update_slice(
                whole, block[:, None], (0, me ^ bits, 0, part * cols)
            )
    return whole


def core_sum(parts):
    core = lax.axis_index("core")
    parts = parts.reshape(parts.shape[:1] + (2, 2) + parts.shape[2:])
    sent = lax.dynamic_index_in_dim(parts, 1 - core, 2, keepdims=False)
    kept = lax.dynamic_index_in_dim(parts, core, 2, keepdims=False)
    return bf(f32(kept) + f32(flip(sent, "core")))


def row_sum(both):
    row = lax.axis_index("fy")
    sent = lax.dynamic_index_in_dim(both, 1 - row, 1, keepdims=False)
    kept = lax.dynamic_index_in_dim(both, row, 1, keepdims=False)
    return bf(f32(kept) + f32(flip(sent, "fy")))


def ladder_shards(
    hidden_in,
    positions,
    cotangent,
    w_qkv,
    w_out,
    w_gate_up,
    w_down,
    gains,
    m_qkv,
    v_qkv,
    m_out,
    v_out,
    m_gate_up,
    v_gate_up,
    m_down,
    v_down,
    m_gains,
    v_gains,
):
    x_own = hidden_in[0]
    tok, width = x_own.shape
    rows = w_qkv.shape[0]
    planes = lax.axis_size(DP)
    group = lax.axis_size(LADDER)
    q_width = HEADS * HEAD_DIM
    core = lax.axis_index("core")

    q_cols = w_qkv[:, :q_width].reshape(rows, HEADS, HEAD_DIM)
    kv_cols = w_qkv[:, q_width:].reshape(rows, 2, KV_HEADS, HEAD_DIM)
    kv_cols = jnp.swapaxes(kv_cols, 1, 2).reshape(rows, HEADS, HEAD_DIM)
    pieces = jnp.swapaxes(jnp.concatenate([q_cols, kv_cols], axis=2), 0, 1)
    first = jnp.stack([positions[0, 0] // 128, positions[0, 0] % 128])
    own_gains = jnp.concatenate([gains.reshape(4 * rows), bf(first)])[None, None]
    own_gains = jnp.pad(own_gains, ((0, 0), (0, 7), (0, 2 * HEAD_DIM - 4 * rows - 2)))
    pieces = jnp.concatenate(
        [pieces, jnp.broadcast_to(own_gains, (HEADS,) + own_gains.shape[1:])], axis=1
    )
    x_all = gather(x_own, PLANE)
    got, out_line = hold((swap(pieces, PLANE), w_out))
    out_line = line_gather(out_line)
    first = got[:, rows, 4 * rows : 4 * rows + 2].astype(jnp.int32)
    pos_all = first[:, :1] * 128 + first[:, 1:] + jnp.arange(tok, dtype=jnp.int32)[None]
    pos_all = pos_all.reshape(-1)
    cosine, sine = rotary_tables(pos_all)
    got = line_gather(got)
    ff_own = w_down.shape[0] * 4
    cols = []
    for part in range(2):
        piece = w_gate_up[:, part * group * ff_own : (part + 1) * group * ff_own]
        cols.append(jnp.swapaxes(piece.reshape(rows, group, ff_own), 0, 1))
    got, cols[0], w_down_late = hold((got, cols[0], w_down))
    w_own = got[:, :, :rows].reshape(width, 2 * HEAD_DIM)
    gain_vals = got[:, :, rows, : 4 * rows].reshape(planes * HEADS, 4, rows)
    gain_vals = f32(jnp.swapaxes(gain_vals, 0, 1).reshape(4, width))
    out_full = lax.all_gather(out_line, PLANE, axis=1, tiled=False).reshape(q_width, width)
    cols[0] = swap(cols[0], LADDER)

    normed_all = bf(rms_scale(f32(x_all), gain_vals[0]))
    qkv = mm(normed_all, w_own)
    query = bf(rotary(qkv[:, :HEAD_DIM], cosine, sine) * HEAD_DIM ** (-0.5))
    half = qkv[:, HEAD_DIM:]
    mine = jnp.where(core == 0, bf(rotary(half, cosine, sine)), bf(half))
    other = flip(mine, "core")
    key = jnp.where(core == 0, mine, other)
    value = jnp.where(core == 0, other, mine)
    scores = mm_nt(query, key)
    capped = SOFT_CAP * jnp.tanh(scores / SOFT_CAP)
    weights = jnp.where(pos_all[:, None] >= pos_all[None, :], jnp.exp(capped), 0.0)
    weights_b = bf(weights)
    total = jnp.sum(weights, axis=-1, keepdims=True)
    attn = mm(weights_b, value) / total
    cols[0], cols[1], _ = hold((cols[0], cols[1], attn))
    attn_own = swap(bf(attn).reshape(HEADS, tok, HEAD_DIM), PLANE)
    cols[1] = swap(cols[1], LADDER)
    attn_own = jnp.swapaxes(attn_own, 0, 1).reshape(tok, q_width)
    mixed = mm(attn_own, out_full)

    x_rows = f32(x_own)
    branch_one, pull_one = jax.vjp(rms_scale, mixed, gain_vals[1])
    resid = x_rows + branch_one
    normed_two, pull_two = jax.vjp(rms_scale, resid, gain_vals[2])

    tokens_own = bf(normed_two)
    cols[1], _ = hold((cols[1], tokens_own))
    down_own = quad_place([quad_blocks(w_down_late[None], tokens_own)], 1).reshape(ff_own, width)
    gate_up_own = [quad_blocks(cols[0], tokens_own), quad_blocks(cols[1])]
    gate_up_own = quad_place(gate_up_own, 2).reshape(width, 2 * ff_own)
    steps = ring_gather(tokens_own)
    tokens = jnp.concatenate(sum(steps, []), axis=0)
    gate_up = mm(tokens, gate_up_own)

    def gated(gate, up_part):
        return jax.nn.gelu(gate, approximate=True) * up_part

    inner = bf(gated(gate_up[:, :ff_own], gate_up[:, ff_own:]))
    late = tokens.shape[0] - 3 * tok
    down = bf(mm(inner, down_own))
    down = ring_scatter(steps_of((down[:late], down[late:]), tok))
    branch_two, pull_three = jax.vjp(rms_scale, down, gain_vals[3])
    block_out = bf(resid + branch_two)[None]
    grad_top = f32(cotangent[0])
    grad_down_in, gain_grad_three = pull_three(grad_top)
    steps = ring_gather(bf(grad_down_in))
    grad_downs = two_parts(steps)
    grad_gus, parts = ([], [])
    for piece, kept in zip(grad_downs, (gate_up[:late], gate_up[late:])):
        _, pull = jax.vjp(gated, kept[:, :ff_own], kept[:, ff_own:])
        grad_gus.append(bf(jnp.concatenate(pull(mm_nt(piece, down_own)), axis=1)))
        grad_gu, _ = hold((grad_gus[-1], steps[3][0]))
        parts.append(bf(mm_nt(grad_gu, gate_up_own)))
    tokens, inner, grad_downs, grad_gus, parts = hold(
        (tokens, inner, grad_downs, grad_gus, parts)
    )
    grad_normed_two = ring_scatter(steps_of(parts, tok))
    grad_gu_b = jnp.concatenate(grad_gus, axis=0)
    grad_halves = [bf(mm_tn(tokens, grad_gu_b[:, :ff_own])), bf(mm_tn(tokens, grad_gu_b[:, ff_own:]))]
    grad_down_w = bf(mm_tn(inner, jnp.concatenate(grad_downs, axis=0)))
    grad_normed_two, _, _ = hold((grad_normed_two, grad_halves, grad_down_w))
    grad_resid_two, _ = pull_two(grad_normed_two)
    grad_resid = grad_top + grad_resid_two
    grad_mixed, gain_grad_one = pull_one(grad_resid)
    grad_mixed_b = bf(grad_mixed)

    grad_attn = bf(mm_nt(grad_mixed_b, out_full)).reshape(tok, HEADS, HEAD_DIM)
    grad_head = swap(jnp.swapaxes(grad_attn, 0, 1), PLANE).reshape(HEADS * tok, HEAD_DIM)
    grad_head = f32(grad_head)
    rho = bf(grad_head / total)
    delta = jnp.sum(grad_head * attn, axis=-1, keepdims=True) / total
    pulled = mm_nt(rho, value)
    grad_scores = bf((pulled - delta) * weights * (1.0 - (capped / SOFT_CAP) ** 2))
    grad_query = mm(grad_scores, key) * HEAD_DIM ** (-0.5)
    grad_key = mm_tn(grad_scores, query)
    grad_value = mm_tn(weights_b, rho)
    sent = jnp.where(core == 0, grad_value, grad_key)
    grad_half = jnp.where(core == 0, grad_key, grad_value) + flip(sent, "core")
    grad_half = jnp.where(core == 0, unrotary(grad_half, cosine, sine), grad_half)
    grad_qkv = bf(jnp.concatenate([unrotary(grad_query, cosine, sine), grad_half], axis=1))
    attn_cols = attn_own.reshape(tok, planes, HEADS, w_out.shape[0])
    attn_cols = jnp.transpose(attn_cols, (2, 0, 1, 3)).reshape(HEADS, tok, HEAD_DIM)
    attn_cols = swap(attn_cols, PLANE).reshape(HEADS * tok, HEAD_DIM)
    grad_qkv, attn_cols, grad_mixed_all = hold(
        (grad_qkv, attn_cols, gather(grad_mixed_b, PLANE))
    )
    grad_normed = plane_scatter(bf(mm_nt(grad_qkv, w_own)))
    _, pull_zero = jax.vjp(rms_scale, x_rows, gain_vals[0])
    grad_x_zero, _ = pull_zero(grad_normed)
    input_grad = (grad_resid + grad_x_zero)[None]

    sums = [core_sum(v.reshape(group, 4, rows, ff_own)) for v in grad_halves]
    sums.append(core_sum(grad_down_w.reshape(1, 4, ff_own // 4, width)))
    sums, _ = hold((sums, grad_qkv))
    grad_halves = [row_sum(v) for v in sums[:2]]
    grad_down_w = f32(row_sum(sums[2])[0])
    grad_w = bf(mm_tn(normed_all, grad_qkv)).reshape(planes, -1, 2 * HEAD_DIM)
    grad_out_w = bf(mm_tn(attn_cols, grad_mixed_all)).reshape(planes, -1, 2 * HEAD_DIM)
    grad_w = scatter_sum(jnp.concatenate([grad_w, grad_out_w], axis=1), DP)[0]
    grad_out_w = f32(grad_w[HEADS * rows :].reshape(w_out.shape))
    grad_w = grad_w[: HEADS * rows].reshape(HEADS, rows, 2 * HEAD_DIM)
    for part in range(2):
        part_w = jnp.swapaxes(swap(grad_halves[part], LADDER), 0, 1)
        grad_halves[part] = part_w.reshape(rows, group * ff_own)
    grad_gate_up_w = f32(jnp.concatenate(grad_halves, axis=1))
    grad_w = f32(jnp.swapaxes(swap(grad_w, PLANE), 0, 1))
    grad_q_w = grad_w[:, :, :HEAD_DIM].reshape(rows, q_width)
    grad_kv_w = grad_w[:, :, HEAD_DIM:].reshape(rows, KV_HEADS, 2, HEAD_DIM)
    grad_kv_w = jnp.swapaxes(grad_kv_w, 1, 2).reshape(rows, q_width)
    grad_qkv_w = jnp.concatenate([grad_q_w, grad_kv_w], axis=1)

    gain_zero = jnp.sum(f32(w_qkv) * grad_qkv_w, axis=1) / (1.0 + f32(gains[0]))
    gain_two = jnp.sum(f32(w_gate_up) * grad_gate_up_w, axis=1) / (1.0 + f32(gains[2]))
    others = jnp.stack([gain_grad_one, gain_grad_three]).reshape(2, planes * HEADS, rows)
    others = jnp.sum(swap(jnp.swapaxes(others, 0, 1), ALL), axis=0)
    grad_gains = jnp.stack([gain_zero, others[0], gain_two, others[1]], axis=0)

    return (
        (block_out, input_grad)
        + adam_step(f32(w_qkv), grad_qkv_w, m_qkv, v_qkv, MATRIX_RATE, WEIGHT_DECAY)
        + adam_step(f32(w_out), grad_out_w, m_out, v_out, MATRIX_RATE, WEIGHT_DECAY)
        + adam_step(f32(w_gate_up), grad_gate_up_w, m_gate_up, v_gate_up, MATRIX_RATE, WEIGHT_DECAY)
        + adam_step(f32(w_down), grad_down_w, m_down, v_down, MATRIX_RATE, WEIGHT_DECAY)
        + adam_step(f32(gains), grad_gains, m_gains, v_gains, GAIN_RATE, 0.0)
    )


def token_attention(x_own, pos_own, w_qkv, w_out, gains):
    tok = x_own.shape[0]
    q_width = HEADS * HEAD_DIM
    k_width = KV_HEADS * HEAD_DIM
    groups = HEADS // KV_HEADS
    qkv_full = gather(w_qkv, ALL)
    out_full = gather(w_out, ALL)
    gain_vals = f32(gather(gains, ALL, 1))
    normed = bf(rms_scale(f32(x_own), gain_vals[0]))
    qkv = mm(normed, qkv_full)
    cosine, sine = rotary_tables(pos_own)
    cosine, sine = (cosine[:, None, :], sine[:, None, :])
    query = rotary(qkv[:, :q_width].reshape(tok, HEADS, HEAD_DIM), cosine, sine)
    query = bf(query * HEAD_DIM ** (-0.5)).reshape(tok, KV_HEADS, groups, HEAD_DIM)
    key_own = qkv[:, q_width : q_width + k_width].reshape(tok, KV_HEADS, HEAD_DIM)
    key = gather(bf(rotary(key_own, cosine, sine)), PLANE)
    value = gather(bf(qkv[:, q_width + k_width :]).reshape(tok, KV_HEADS, HEAD_DIM), PLANE)
    pos_all = gather(pos_own, PLANE)
    count = pos_all.shape[0]
    scores = jnp.einsum("tgjd,sgd->gjts", query, key, preferred_element_type=jnp.float32)
    capped = SOFT_CAP * jnp.tanh(scores / SOFT_CAP)
    weights = jnp.where(pos_own[:, None] >= pos_all[None, :], jnp.exp(capped), 0.0)
    weights_b = bf(weights)
    total = jnp.sum(weights, axis=-1)
    attn = jnp.einsum("gjts,sgd->gjtd", weights_b, value, preferred_element_type=jnp.float32)
    attn = attn / total[..., None]
    attn_b = bf(jnp.transpose(attn, (2, 0, 1, 3)).reshape(tok, q_width))
    mixed = mm(attn_b, out_full)

    def backward(grad_mixed_b):
        grad_attn = mm_nt(grad_mixed_b, out_full).reshape(tok, KV_HEADS, groups, HEAD_DIM)
        grad_heads = jnp.transpose(grad_attn, (1, 2, 0, 3))
        rho = bf(grad_heads / total[..., None])
        delta = jnp.sum(grad_heads * attn, axis=-1) / total
        pulled = jnp.einsum("gjtd,sgd->gjts", rho, value, preferred_element_type=jnp.float32)
        grad_scores = bf(
            (pulled - delta[..., None]) * weights * (1.0 - (capped / SOFT_CAP) ** 2)
        )
        grad_query = jnp.einsum(
            "gjts,sgd->tgjd", grad_scores, key, preferred_element_type=jnp.float32
        ).reshape(tok, HEADS, HEAD_DIM)
        grad_key = jnp.einsum(
            "gjts,tgjd->sgd", grad_scores, query, preferred_element_type=jnp.float32
        ).reshape(count, k_width)
        grad_value = jnp.einsum(
            "gjts,gjtd->sgd", weights_b, rho, preferred_element_type=jnp.float32
        ).reshape(count, k_width)
        grad_kv = scatter_sum(jnp.concatenate([grad_key, grad_value], axis=1), PLANE)
        grad_query = unrotary(grad_query * HEAD_DIM ** (-0.5), cosine, sine)
        grad_key = unrotary(grad_kv[:, :k_width].reshape(tok, KV_HEADS, HEAD_DIM), cosine, sine)
        grad_qkv = bf(
            jnp.concatenate(
                [
                    grad_query.reshape(tok, q_width),
                    grad_key.reshape(tok, k_width),
                    grad_kv[:, k_width:],
                ],
                axis=1,
            )
        )
        grad_normed = mm_nt(grad_qkv, qkv_full)
        grad_qkv_w = f32(scatter_sum(bf(mm_tn(normed, grad_qkv)), ALL))
        grad_out_w = f32(scatter_sum(bf(mm_tn(attn_b, grad_mixed_b)), ALL))
        return grad_normed, grad_qkv_w, grad_out_w

    return mixed, gain_vals, backward


def wide_shards(
    hidden_in,
    positions,
    cotangent,
    w_qkv,
    w_out,
    w_gate_up,
    w_down,
    gains,
    m_qkv,
    v_qkv,
    m_out,
    v_out,
    m_gate_up,
    v_gate_up,
    m_down,
    v_down,
    m_gains,
    v_gains,
):
    x_own = hidden_in[0]
    rows, width = (w_qkv.shape[0], x_own.shape[1])
    group, across = (lax.axis_size(GROUP), lax.axis_size(ACROSS))
    ff_piece = w_down.shape[0]
    ff_own = across * ff_piece
    gu_pieces = w_gate_up.reshape(rows, 2, across, group, ff_piece)
    gu_pieces = jnp.transpose(gu_pieces, (3, 0, 1, 2, 4)).reshape(group * rows, 2 * ff_own)

    mixed, gain_vals, attention_back = token_attention(x_own, positions[0], w_qkv, w_out, gains)
    gu_own = gather(swap(gu_pieces, GROUP), ACROSS)
    down_own = gather(w_down, ACROSS)

    x_rows = f32(x_own)
    branch_one, pull_one = jax.vjp(rms_scale, mixed, gain_vals[1])
    resid = x_rows + branch_one
    normed_two, pull_two = jax.vjp(rms_scale, resid, gain_vals[2])
    tokens_b = gather(bf(normed_two), GROUP)
    gate_up = mm(tokens_b, gu_own)
    inner, pull_gelu = jax.vjp(
        lambda gate, up_part: jax.nn.gelu(gate, approximate=True) * up_part,
        gate_up[:, :ff_own],
        gate_up[:, ff_own:],
    )
    inner_b = bf(inner)
    down = f32(scatter_sum(bf(mm(inner_b, down_own)), GROUP))
    branch_two, pull_three = jax.vjp(rms_scale, down, gain_vals[3])
    block_out = bf(resid + branch_two)[None]
    grad_top = f32(cotangent[0])
    grad_down_in, gain_grad_three = pull_three(grad_top)
    grad_down_b = gather(bf(grad_down_in), GROUP)
    grad_gate, grad_up = pull_gelu(mm_nt(grad_down_b, down_own))
    grad_gu_b = bf(jnp.concatenate([grad_gate, grad_up], axis=1))
    grad_normed_two = f32(scatter_sum(bf(mm_nt(grad_gu_b, gu_own)), GROUP))
    grad_gate_up_w = scatter_sum(bf(mm_tn(tokens_b, grad_gu_b)), ACROSS)
    grad_down_w = f32(scatter_sum(bf(mm_tn(inner_b, grad_down_b)), ACROSS))

    grad_resid_two, gain_grad_two = pull_two(grad_normed_two)
    grad_resid = grad_top + grad_resid_two
    grad_mixed, gain_grad_one = pull_one(grad_resid)
    grad_normed, grad_qkv_w, grad_out_w = attention_back(bf(grad_mixed))
    _, pull_zero = jax.vjp(rms_scale, x_rows, gain_vals[0])
    grad_x_zero, gain_grad_zero = pull_zero(grad_normed)
    input_grad = (grad_resid + grad_x_zero)[None]

    grad_gate_up_w = swap(grad_gate_up_w, GROUP).reshape(group, rows, 2, across, ff_piece)
    grad_gate_up_w = f32(jnp.transpose(grad_gate_up_w, (1, 2, 3, 0, 4)).reshape(rows, -1))
    gain_term = jnp.stack([gain_grad_zero, gain_grad_one, gain_grad_two, gain_grad_three], axis=0)
    grad_gains = lax.psum_scatter(gain_term, ALL, scatter_dimension=1, tiled=True)

    return (
        (block_out, input_grad)
        + adam_step(f32(w_qkv), grad_qkv_w, m_qkv, v_qkv, MATRIX_RATE, WEIGHT_DECAY)
        + adam_step(f32(w_out), grad_out_w, m_out, v_out, MATRIX_RATE, WEIGHT_DECAY)
        + adam_step(f32(w_gate_up), grad_gate_up_w, m_gate_up, v_gate_up, MATRIX_RATE, WEIGHT_DECAY)
        + adam_step(f32(w_down), grad_down_w, m_down, v_down, MATRIX_RATE, WEIGHT_DECAY)
        + adam_step(f32(gains), grad_gains, m_gains, v_gains, GAIN_RATE, 0.0)
    )


def solution(mesh):
    sizes = dict(mesh.shape)
    fine = Mesh(
        mesh.devices.reshape(sizes["dp"] // 2, 2, sizes["ctx"], sizes["fsdp"] // 2, 2),
        ("dh", "dl", "ctx", "fy", "core"),
    )
    acts = P(DP, PLANE, None)
    mats = P(ALL, None)
    vecs = P(None, ALL)
    ladder = sizes["dp"] == 4 and sizes["ctx"] == 2 and sizes["fsdp"] == 4
    return jax.shard_map(
        ladder_shards if ladder else wide_shards,
        mesh=fine,
        in_specs=(acts, P(DP, PLANE), acts) + (mats,) * 4 + (vecs,) + (mats,) * 8 + (vecs,) * 2,
        out_specs=(acts, acts) + (mats,) * 12 + (vecs,) * 3,
        check_vma=False,
    )
```

```python
import jax
import jax.numpy as jnp
from jax import lax
from jax.sharding import Mesh, PartitionSpec as P

HEADS = 8
KV_HEADS = 4
HEAD_DIM = 256
STEP = 10

NORM_EPS = 1e-06
SOFT_CAP = 50.0
THETA = 10000.0
BETA_ONE = 0.9
BETA_TWO = 0.95
ADAM_EPS = 1e-08
MATRIX_RATE = 0.03
GAIN_RATE = 0.2
WEIGHT_DECAY = 0.1

DP = ("dh", "dl")
PLANE = ("ctx", "fy", "core")
ALL = DP + PLANE
LADDER = DP + ("ctx",)
GROUP = PLANE
ACROSS = DP


def f32(v):
    return v.astype(jnp.float32)


def bf(v):
    return v.astype(jnp.bfloat16)


def dot(left, right, dims):
    return lax.dot_general(left, right, (dims, ((), ())), preferred_element_type=jnp.float32)


def mm(left, right):
    return dot(left, right, ((1,), (0,)))


def mm_nt(left, right):
    return dot(left, right, ((1,), (1,)))


def mm_tn(left, right):
    return dot(left, right, ((0,), (0,)))


def rms_scale(values, gain):
    inverse = lax.rsqrt(jnp.mean(values * values, axis=-1, keepdims=True) + NORM_EPS)
    return values * inverse * (1.0 + gain)


def rotary_tables(places):
    half = HEAD_DIM // 2
    freqs = THETA ** (-(jnp.arange(half, dtype=jnp.float32) * 2.0 / HEAD_DIM))
    angles = f32(places)[:, None] * freqs[None, :]
    return (jnp.cos(angles), jnp.sin(angles))


def rotary(values, cosine, sine):
    half = HEAD_DIM // 2
    first = values[..., :half]
    second = values[..., half:]
    return jnp.concatenate(
        [first * cosine - second * sine, second * cosine + first * sine], axis=-1
    )


def unrotary(values, cosine, sine):
    return rotary(values, cosine, -sine)


def adam_step(weight, grad, first, second, rate, decay):
    first_new = BETA_ONE * first + (1.0 - BETA_ONE) * grad
    second_new = BETA_TWO * second + (1.0 - BETA_TWO) * grad * grad
    ratio = (
        first_new
        / (1.0 - BETA_ONE**STEP)
        / (jnp.sqrt(second_new / (1.0 - BETA_TWO**STEP)) + ADAM_EPS)
    )
    return (weight - rate * (ratio + decay * weight), first_new, second_new)


def gather(v, axes, axis=0):
    return lax.all_gather(v, axes, axis=axis, tiled=True)


def scatter_sum(v, axes):
    return lax.psum_scatter(v, axes, scatter_dimension=0, tiled=True)


def swap(v, axes):
    return lax.all_to_all(v, axes, split_axis=0, concat_axis=0, tiled=True)


def hold(v):
    return lax.optimization_barrier(v)


def flip(v, axis):
    return lax.ppermute(v, axis, [(0, 1), (1, 0)])


def plane_scatter(parts):
    size = parts.shape[0] // 8
    half = size // 2
    col, row, core = (lax.axis_index(axis) for axis in PLANE)
    parts = parts.reshape((4, 2, size) + parts.shape[1:])
    sent = lax.dynamic_index_in_dim(parts, 1 - core, 1, keepdims=False)
    kept = lax.dynamic_index_in_dim(parts, core, 1, keepdims=False)
    both = bf(f32(kept) + f32(flip(sent, "core")))
    own, over_y, over_x, corner = (
        lax.dynamic_index_in_dim(both, (2 * col + row) ^ bits, 0, keepdims=False) for bits in range(4)
    )
    got_y = flip(corner[:half], "ctx")
    got_x = flip(corner[half:], "fy")
    over_y = jnp.concatenate([bf(f32(over_y[:half]) + f32(got_y)), over_y[half:]], axis=0)
    over_x = jnp.concatenate([over_x[:half], bf(f32(over_x[half:]) + f32(got_x))], axis=0)
    return f32(own) + f32(flip(over_x, "ctx")) + f32(flip(over_y, "fy"))


def line_gather(own, rider):
    count = lax.axis_size(DP)
    rows = [[own], [rider]]
    ends = [[own, own], [rider, rider]]
    for step in range(1, count + 1):
        for which in range(2):
            hop = step - which
            if 1 <= hop < count:
                up, down = ends[which]
                if which == 1 and hop == 1:
                    up, _ = hold((up, ends[0][0]))
                    down = up
                up = lax.ppermute(up, DP, [(i, i + 1) for i in range(hop - 1, count - 1)])
                down = lax.ppermute(down, DP, [(i + 1, i) for i in range(count - hop)])
                ends[which] = [up, down]
                rows[which] = [up] + rows[which] + [down]
    start = count - 1 - lax.axis_index(DP)
    return [lax.dynamic_slice_in_dim(jnp.stack(row), start, count, axis=0) for row in rows]


def exchange(v, axes):
    count = lax.axis_size(axes)
    me = lax.axis_index(axes)
    sent = jnp.take(v, jnp.arange(count) ^ me, axis=0)
    got = [sent[0]]
    for bits in range(1, count):
        got.append(lax.ppermute(sent[bits], axes, [(i, i ^ bits) for i in range(count)]))
    return jnp.take(jnp.stack(got), jnp.arange(count) ^ me, axis=0)


def ring_pairs():
    count = lax.axis_size(DP)
    ring = [2 * z for z in range(count)] + [2 * z + 1 for z in reversed(range(count))]
    onward = [(ring[i], ring[(i + 1) % len(ring)]) for i in range(len(ring))]
    return onward, [(b, a) for a, b in onward]


def ring_gather(own):
    onward, back = ring_pairs()
    half = own.shape[0] // 2
    steps = [[own]]
    behind, ahead = (own, own)
    for _ in range(len(onward) // 2 - 1):
        behind = lax.ppermute(behind, LADDER, onward)
        ahead = lax.ppermute(ahead, LADDER, back)
        steps.append([behind, ahead])
    steps.append(
        [
            lax.ppermute(behind[:half], LADDER, onward),
            lax.ppermute(ahead[half:], LADDER, back),
        ]
    )
    return steps


def two_parts(steps):
    return [
        jnp.concatenate(sum(steps[:3], []), axis=0),
        jnp.concatenate(sum(steps[3:], []), axis=0),
    ]


def steps_of(parts, size):
    early, late = parts
    steps = [early[:size], early[size : 3 * size], early[3 * size :]]
    return steps + [late[: 2 * size], late[2 * size :]]


def ring_scatter(pieces):
    onward, back = ring_pairs()
    size = pieces[0].shape[0]
    half = size // 2
    ahead = lax.ppermute(pieces[-1][:half], LADDER, onward)
    behind = lax.ppermute(pieces[-1][half:], LADDER, back)
    for step in range(len(pieces) - 2, 0, -1):
        to_behind, to_ahead = (pieces[step][:size], pieces[step][size:])
        if step == len(pieces) - 2:
            to_ahead = jnp.concatenate(
                [bf(f32(to_ahead[:half]) + f32(ahead)), to_ahead[half:]], axis=0
            )
            to_behind = jnp.concatenate(
                [to_behind[:half], bf(f32(to_behind[half:]) + f32(behind))], axis=0
            )
        else:
            to_ahead = bf(f32(to_ahead) + f32(ahead))
            to_behind = bf(f32(to_behind) + f32(behind))
        to_ahead, to_behind = hold((to_ahead, to_behind))
        ahead = lax.ppermute(to_ahead, LADDER, onward)
        behind = lax.ppermute(to_behind, LADDER, back)
    return f32(pieces[0]) + f32(ahead) + f32(behind)


def quad_blocks(own, late=None):
    over_y = flip(own, "fy")
    if late is not None:
        over_y, _ = hold((over_y, late))
    return [own, flip(own, "core"), over_y, flip(over_y, "core")]


def quad_place(blocks, parts):
    me = lax.axis_index(("fy", "core"))
    count, rows, cols = blocks[0][0].shape
    whole = jnp.zeros((count, 4, rows, parts * cols), blocks[0][0].dtype)
    for part in range(parts):
        for bits, block in enumerate(blocks[part]):
            whole = lax.dynamic_update_slice(
                whole, block[:, None], (0, me ^ bits, 0, part * cols)
            )
    return whole


def core_sum(parts):
    core = lax.axis_index("core")
    parts = parts.reshape(parts.shape[:1] + (2, 2) + parts.shape[2:])
    sent = lax.dynamic_index_in_dim(parts, 1 - core, 2, keepdims=False)
    kept = lax.dynamic_index_in_dim(parts, core, 2, keepdims=False)
    return bf(f32(kept) + f32(flip(sent, "core")))


def row_sum(both):
    row = lax.axis_index("fy")
    sent = lax.dynamic_index_in_dim(both, 1 - row, 1, keepdims=False)
    kept = lax.dynamic_index_in_dim(both, row, 1, keepdims=False)
    return bf(f32(kept) + f32(flip(sent, "fy")))


def ladder_shards(
    hidden_in,
    positions,
    cotangent,
    w_qkv,
    w_out,
    w_gate_up,
    w_down,
    gains,
    m_qkv,
    v_qkv,
    m_out,
    v_out,
    m_gate_up,
    v_gate_up,
    m_down,
    v_down,
    m_gains,
    v_gains,
):
    x_own = hidden_in[0]
    tok, width = x_own.shape
    rows = w_qkv.shape[0]
    planes = lax.axis_size(DP)
    group = lax.axis_size(LADDER)
    q_width = HEADS * HEAD_DIM
    core = lax.axis_index("core")

    q_cols = w_qkv[:, :q_width].reshape(rows, HEADS, HEAD_DIM)
    kv_cols = w_qkv[:, q_width:].reshape(rows, 2, KV_HEADS, HEAD_DIM)
    kv_cols = jnp.swapaxes(kv_cols, 1, 2).reshape(rows, HEADS, HEAD_DIM)
    pieces = jnp.swapaxes(jnp.concatenate([q_cols, kv_cols], axis=2), 0, 1)
    first = jnp.stack([positions[0, 0] // 128, positions[0, 0] % 128])
    own_gains = jnp.concatenate([gains.reshape(4 * rows), bf(first)])[None, None]
    own_gains = jnp.pad(own_gains, ((0, 0), (0, 7), (0, 2 * HEAD_DIM - 4 * rows - 2)))
    pieces = jnp.concatenate(
        [pieces, jnp.broadcast_to(own_gains, (HEADS,) + own_gains.shape[1:])], axis=1
    )
    x_all = gather(x_own, PLANE)
    got = swap(pieces, PLANE)
    first = got[:, rows, 4 * rows : 4 * rows + 2].astype(jnp.int32)
    pos_all = first[:, :1] * 128 + first[:, 1:] + jnp.arange(tok, dtype=jnp.int32)[None]
    pos_all = pos_all.reshape(-1)
    cosine, sine = rotary_tables(pos_all)
    got, out_line = line_gather(got, w_out)
    ff_own = w_down.shape[0] * 4
    cols = []
    for part in range(2):
        piece = w_gate_up[:, part * group * ff_own : (part + 1) * group * ff_own]
        cols.append(jnp.swapaxes(piece.reshape(rows, group, ff_own), 0, 1))
    got, cols[0], w_down_late = hold((got, cols[0], w_down))
    w_own = got[:, :, :rows].reshape(width, 2 * HEAD_DIM)
    gain_vals = got[:, :, rows, : 4 * rows].reshape(planes * HEADS, 4, rows)
    gain_vals = f32(jnp.swapaxes(gain_vals, 0, 1).reshape(4, width))
    out_full = lax.all_gather(out_line, PLANE, axis=1, tiled=False).reshape(q_width, width)
    cols[0] = swap(cols[0], LADDER)

    normed_all = bf(rms_scale(f32(x_all), gain_vals[0]))
    qkv = mm(normed_all, w_own)
    query = bf(rotary(qkv[:, :HEAD_DIM], cosine, sine) * HEAD_DIM ** (-0.5))
    half = qkv[:, HEAD_DIM:]
    mine = jnp.where(core == 0, bf(rotary(half, cosine, sine)), bf(half))
    other = flip(mine, "core")
    key = jnp.where(core == 0, mine, other)
    value = jnp.where(core == 0, other, mine)
    scores = mm_nt(query, key)
    capped = SOFT_CAP * jnp.tanh(scores / SOFT_CAP)
    weights = jnp.where(pos_all[:, None] >= pos_all[None, :], jnp.exp(capped), 0.0)
    weights_b = bf(weights)
    total = jnp.sum(weights, axis=-1, keepdims=True)
    attn = mm(weights_b, value) / total
    cols[0], cols[1] = hold((cols[0], cols[1]))
    cols[1] = swap(cols[1], LADDER)
    attn_own = exchange(bf(attn).reshape(HEADS, tok, HEAD_DIM), PLANE)
    attn_own = jnp.swapaxes(attn_own, 0, 1).reshape(tok, q_width)
    mixed = mm(attn_own, out_full)

    x_rows = f32(x_own)
    branch_one, pull_one = jax.vjp(rms_scale, mixed, gain_vals[1])
    resid = x_rows + branch_one
    normed_two, pull_two = jax.vjp(rms_scale, resid, gain_vals[2])

    tokens_own = bf(normed_two)
    steps = ring_gather(tokens_own)
    cols, _ = hold((cols, tokens_own))
    down_own = quad_place([quad_blocks(w_down_late[None], tokens_own)], 1).reshape(ff_own, width)
    gate_up_own = quad_place([quad_blocks(v) for v in cols], 2).reshape(width, 2 * ff_own)
    tokens = jnp.concatenate(sum(steps, []), axis=0)
    gate_up = mm(tokens, gate_up_own)

    def gated(gate, up_part):
        return jax.nn.gelu(gate, approximate=True) * up_part

    inner = bf(gated(gate_up[:, :ff_own], gate_up[:, ff_own:]))
    late = tokens.shape[0] - 3 * tok
    down = bf(mm(inner, down_own))
    attn_cols = attn_own.reshape(tok, planes, HEADS, w_out.shape[0])
    attn_cols = jnp.transpose(attn_cols, (2, 0, 1, 3)).reshape(HEADS, tok, HEAD_DIM)
    attn_cols, down = hold((attn_cols, down))
    attn_cols = swap(attn_cols, PLANE).reshape(HEADS * tok, HEAD_DIM)
    down = ring_scatter(steps_of((down[:late], down[late:]), tok))
    down, attn_cols = hold((down, attn_cols))
    branch_two, pull_three = jax.vjp(rms_scale, down, gain_vals[3])
    block_out = bf(resid + branch_two)[None]
    grad_top = f32(cotangent[0])
    grad_down_in, gain_grad_three = pull_three(grad_top)
    steps = ring_gather(bf(grad_down_in))
    grad_downs = two_parts(steps)
    grad_gus, parts = ([], [])
    for piece, kept in zip(grad_downs, (gate_up[:late], gate_up[late:])):
        _, pull = jax.vjp(gated, kept[:, :ff_own], kept[:, ff_own:])
        grad_gus.append(bf(jnp.concatenate(pull(mm_nt(piece, down_own)), axis=1)))
        grad_gu, _ = hold((grad_gus[-1], steps[3][0]))
        parts.append(bf(mm_nt(grad_gu, gate_up_own)))
    tokens, inner, grad_downs, grad_gus, parts = hold(
        (tokens, inner, grad_downs, grad_gus, parts)
    )
    grad_normed_two = ring_scatter(steps_of(parts, tok))
    grad_gu_b = jnp.concatenate(grad_gus, axis=0)
    grad_halves = [bf(mm_tn(tokens, grad_gu_b[:, :ff_own])), bf(mm_tn(tokens, grad_gu_b[:, ff_own:]))]
    grad_down_w = bf(mm_tn(inner, jnp.concatenate(grad_downs, axis=0)))
    grad_normed_two, _, _ = hold((grad_normed_two, grad_halves, grad_down_w))
    grad_resid_two, _ = pull_two(grad_normed_two)
    grad_resid = grad_top + grad_resid_two
    grad_mixed, gain_grad_one = pull_one(grad_resid)
    grad_mixed_b = bf(grad_mixed)

    grad_attn = bf(mm_nt(grad_mixed_b, out_full)).reshape(tok, HEADS, HEAD_DIM)
    grad_head = swap(jnp.swapaxes(grad_attn, 0, 1), PLANE).reshape(HEADS * tok, HEAD_DIM)
    grad_head = f32(grad_head)
    rho = bf(grad_head / total)
    delta = jnp.sum(grad_head * attn, axis=-1, keepdims=True) / total
    pulled = mm_nt(rho, value)
    grad_scores = bf((pulled - delta) * weights * (1.0 - (capped / SOFT_CAP) ** 2))
    grad_query = mm(grad_scores, key) * HEAD_DIM ** (-0.5)
    grad_key = mm_tn(grad_scores, query)
    grad_value = mm_tn(weights_b, rho)
    sent = jnp.where(core == 0, grad_value, grad_key)
    grad_half = jnp.where(core == 0, grad_key, grad_value) + flip(sent, "core")
    grad_half = jnp.where(core == 0, unrotary(grad_half, cosine, sine), grad_half)
    grad_qkv = bf(jnp.concatenate([unrotary(grad_query, cosine, sine), grad_half], axis=1))
    grad_qkv, grad_mixed_all = hold((grad_qkv, gather(grad_mixed_b, PLANE)))
    grad_w = bf(mm_tn(normed_all, grad_qkv))
    grad_qkv, grad_w = hold((grad_qkv, grad_w))
    grad_normed = plane_scatter(bf(mm_nt(grad_qkv, w_own)))
    _, pull_zero = jax.vjp(rms_scale, x_rows, gain_vals[0])
    grad_x_zero, _ = pull_zero(grad_normed)
    input_grad = (grad_resid + grad_x_zero)[None]

    sums = [core_sum(v.reshape(group, 4, rows, ff_own)) for v in grad_halves]
    sums.append(core_sum(grad_down_w.reshape(1, 4, ff_own // 4, width)))
    sums, _ = hold((sums, grad_qkv))
    grad_halves = [row_sum(v) for v in sums[:2]]
    grad_down_w, grad_halves[1] = hold((sums[2], grad_halves[1]))
    grad_down_w = f32(row_sum(grad_down_w)[0])
    grad_w = grad_w.reshape(planes, -1, 2 * HEAD_DIM)
    grad_out_w = bf(mm_tn(attn_cols, grad_mixed_all)).reshape(planes, -1, 2 * HEAD_DIM)
    grad_w = scatter_sum(jnp.concatenate([grad_w, grad_out_w], axis=1), DP)[0]
    grad_out_w = f32(grad_w[HEADS * rows :].reshape(w_out.shape))
    grad_w = grad_w[: HEADS * rows].reshape(HEADS, rows, 2 * HEAD_DIM)
    gain_grad_one, _ = hold((gain_grad_one, grad_w))
    others = jnp.stack([gain_grad_one, gain_grad_three]).reshape(2, planes * HEADS, rows)
    others = jnp.sum(swap(jnp.swapaxes(others, 0, 1), ALL), axis=0)
    grad_halves[0], others = hold((grad_halves[0], others))
    for part in range(2):
        part_w = jnp.swapaxes(swap(grad_halves[part], LADDER), 0, 1)
        grad_halves[part] = part_w.reshape(rows, group * ff_own)
    grad_gate_up_w = f32(jnp.concatenate(grad_halves, axis=1))
    grad_w = f32(jnp.swapaxes(swap(grad_w, PLANE), 0, 1))
    grad_q_w = grad_w[:, :, :HEAD_DIM].reshape(rows, q_width)
    grad_kv_w = grad_w[:, :, HEAD_DIM:].reshape(rows, KV_HEADS, 2, HEAD_DIM)
    grad_kv_w = jnp.swapaxes(grad_kv_w, 1, 2).reshape(rows, q_width)
    grad_qkv_w = jnp.concatenate([grad_q_w, grad_kv_w], axis=1)

    gain_zero = jnp.sum(f32(w_qkv) * grad_qkv_w, axis=1) / (1.0 + f32(gains[0]))
    gain_two = jnp.sum(f32(w_gate_up) * grad_gate_up_w, axis=1) / (1.0 + f32(gains[2]))
    grad_gains = jnp.stack([gain_zero, others[0], gain_two, others[1]], axis=0)

    return (
        (block_out, input_grad)
        + adam_step(f32(w_qkv), grad_qkv_w, m_qkv, v_qkv, MATRIX_RATE, WEIGHT_DECAY)
        + adam_step(f32(w_out), grad_out_w, m_out, v_out, MATRIX_RATE, WEIGHT_DECAY)
        + adam_step(f32(w_gate_up), grad_gate_up_w, m_gate_up, v_gate_up, MATRIX_RATE, WEIGHT_DECAY)
        + adam_step(f32(w_down), grad_down_w, m_down, v_down, MATRIX_RATE, WEIGHT_DECAY)
        + adam_step(f32(gains), grad_gains, m_gains, v_gains, GAIN_RATE, 0.0)
    )


def token_attention(x_own, pos_own, w_qkv, w_out, gains):
    tok = x_own.shape[0]
    q_width = HEADS * HEAD_DIM
    k_width = KV_HEADS * HEAD_DIM
    groups = HEADS // KV_HEADS
    qkv_full = gather(w_qkv, ALL)
    out_full = gather(w_out, ALL)
    gain_vals = f32(gather(gains, ALL, 1))
    normed = bf(rms_scale(f32(x_own), gain_vals[0]))
    qkv = mm(normed, qkv_full)
    cosine, sine = rotary_tables(pos_own)
    cosine, sine = (cosine[:, None, :], sine[:, None, :])
    query = rotary(qkv[:, :q_width].reshape(tok, HEADS, HEAD_DIM), cosine, sine)
    query = bf(query * HEAD_DIM ** (-0.5)).reshape(tok, KV_HEADS, groups, HEAD_DIM)
    key_own = qkv[:, q_width : q_width + k_width].reshape(tok, KV_HEADS, HEAD_DIM)
    key = gather(bf(rotary(key_own, cosine, sine)), PLANE)
    value = gather(bf(qkv[:, q_width + k_width :]).reshape(tok, KV_HEADS, HEAD_DIM), PLANE)
    pos_all = gather(pos_own, PLANE)
    count = pos_all.shape[0]
    scores = jnp.einsum("tgjd,sgd->gjts", query, key, preferred_element_type=jnp.float32)
    capped = SOFT_CAP * jnp.tanh(scores / SOFT_CAP)
    weights = jnp.where(pos_own[:, None] >= pos_all[None, :], jnp.exp(capped), 0.0)
    weights_b = bf(weights)
    total = jnp.sum(weights, axis=-1)
    attn = jnp.einsum("gjts,sgd->gjtd", weights_b, value, preferred_element_type=jnp.float32)
    attn = attn / total[..., None]
    attn_b = bf(jnp.transpose(attn, (2, 0, 1, 3)).reshape(tok, q_width))
    mixed = mm(attn_b, out_full)

    def backward(grad_mixed_b):
        grad_attn = mm_nt(grad_mixed_b, out_full).reshape(tok, KV_HEADS, groups, HEAD_DIM)
        grad_heads = jnp.transpose(grad_attn, (1, 2, 0, 3))
        rho = bf(grad_heads / total[..., None])
        delta = jnp.sum(grad_heads * attn, axis=-1) / total
        pulled = jnp.einsum("gjtd,sgd->gjts", rho, value, preferred_element_type=jnp.float32)
        grad_scores = bf(
            (pulled - delta[..., None]) * weights * (1.0 - (capped / SOFT_CAP) ** 2)
        )
        grad_query = jnp.einsum(
            "gjts,sgd->tgjd", grad_scores, key, preferred_element_type=jnp.float32
        ).reshape(tok, HEADS, HEAD_DIM)
        grad_key = jnp.einsum(
            "gjts,tgjd->sgd", grad_scores, query, preferred_element_type=jnp.float32
        ).reshape(count, k_width)
        grad_value = jnp.einsum(
            "gjts,gjtd->sgd", weights_b, rho, preferred_element_type=jnp.float32
        ).reshape(count, k_width)
        grad_kv = scatter_sum(jnp.concatenate([grad_key, grad_value], axis=1), PLANE)
        grad_query = unrotary(grad_query * HEAD_DIM ** (-0.5), cosine, sine)
        grad_key = unrotary(grad_kv[:, :k_width].reshape(tok, KV_HEADS, HEAD_DIM), cosine, sine)
        grad_qkv = bf(
            jnp.concatenate(
                [
                    grad_query.reshape(tok, q_width),
                    grad_key.reshape(tok, k_width),
                    grad_kv[:, k_width:],
                ],
                axis=1,
            )
        )
        grad_normed = mm_nt(grad_qkv, qkv_full)
        grad_qkv_w = f32(scatter_sum(bf(mm_tn(normed, grad_qkv)), ALL))
        grad_out_w = f32(scatter_sum(bf(mm_tn(attn_b, grad_mixed_b)), ALL))
        return grad_normed, grad_qkv_w, grad_out_w

    return mixed, gain_vals, backward


def wide_shards(
    hidden_in,
    positions,
    cotangent,
    w_qkv,
    w_out,
    w_gate_up,
    w_down,
    gains,
    m_qkv,
    v_qkv,
    m_out,
    v_out,
    m_gate_up,
    v_gate_up,
    m_down,
    v_down,
    m_gains,
    v_gains,
):
    x_own = hidden_in[0]
    rows, width = (w_qkv.shape[0], x_own.shape[1])
    group, across = (lax.axis_size(GROUP), lax.axis_size(ACROSS))
    ff_piece = w_down.shape[0]
    ff_own = across * ff_piece
    gu_pieces = w_gate_up.reshape(rows, 2, across, group, ff_piece)
    gu_pieces = jnp.transpose(gu_pieces, (3, 0, 1, 2, 4)).reshape(group * rows, 2 * ff_own)

    mixed, gain_vals, attention_back = token_attention(x_own, positions[0], w_qkv, w_out, gains)
    gu_own = gather(swap(gu_pieces, GROUP), ACROSS)
    down_own = gather(w_down, ACROSS)

    x_rows = f32(x_own)
    branch_one, pull_one = jax.vjp(rms_scale, mixed, gain_vals[1])
    resid = x_rows + branch_one
    normed_two, pull_two = jax.vjp(rms_scale, resid, gain_vals[2])
    tokens_b = gather(bf(normed_two), GROUP)
    gate_up = mm(tokens_b, gu_own)
    inner, pull_gelu = jax.vjp(
        lambda gate, up_part: jax.nn.gelu(gate, approximate=True) * up_part,
        gate_up[:, :ff_own],
        gate_up[:, ff_own:],
    )
    inner_b = bf(inner)
    down = f32(scatter_sum(bf(mm(inner_b, down_own)), GROUP))
    branch_two, pull_three = jax.vjp(rms_scale, down, gain_vals[3])
    block_out = bf(resid + branch_two)[None]
    grad_top = f32(cotangent[0])
    grad_down_in, gain_grad_three = pull_three(grad_top)
    grad_down_b = gather(bf(grad_down_in), GROUP)
    grad_gate, grad_up = pull_gelu(mm_nt(grad_down_b, down_own))
    grad_gu_b = bf(jnp.concatenate([grad_gate, grad_up], axis=1))
    grad_normed_two = f32(scatter_sum(bf(mm_nt(grad_gu_b, gu_own)), GROUP))
    grad_gate_up_w = scatter_sum(bf(mm_tn(tokens_b, grad_gu_b)), ACROSS)
    grad_down_w = f32(scatter_sum(bf(mm_tn(inner_b, grad_down_b)), ACROSS))

    grad_resid_two, gain_grad_two = pull_two(grad_normed_two)
    grad_resid = grad_top + grad_resid_two
    grad_mixed, gain_grad_one = pull_one(grad_resid)
    grad_normed, grad_qkv_w, grad_out_w = attention_back(bf(grad_mixed))
    _, pull_zero = jax.vjp(rms_scale, x_rows, gain_vals[0])
    grad_x_zero, gain_grad_zero = pull_zero(grad_normed)
    input_grad = (grad_resid + grad_x_zero)[None]

    grad_gate_up_w = swap(grad_gate_up_w, GROUP).reshape(group, rows, 2, across, ff_piece)
    grad_gate_up_w = f32(jnp.transpose(grad_gate_up_w, (1, 2, 3, 0, 4)).reshape(rows, -1))
    gain_term = jnp.stack([gain_grad_zero, gain_grad_one, gain_grad_two, gain_grad_three], axis=0)
    grad_gains = lax.psum_scatter(gain_term, ALL, scatter_dimension=1, tiled=True)

    return (
        (block_out, input_grad)
        + adam_step(f32(w_qkv), grad_qkv_w, m_qkv, v_qkv, MATRIX_RATE, WEIGHT_DECAY)
        + adam_step(f32(w_out), grad_out_w, m_out, v_out, MATRIX_RATE, WEIGHT_DECAY)
        + adam_step(f32(w_gate_up), grad_gate_up_w, m_gate_up, v_gate_up, MATRIX_RATE, WEIGHT_DECAY)
        + adam_step(f32(w_down), grad_down_w, m_down, v_down, MATRIX_RATE, WEIGHT_DECAY)
        + adam_step(f32(gains), grad_gains, m_gains, v_gains, GAIN_RATE, 0.0)
    )


def solution(mesh):
    sizes = dict(mesh.shape)
    fine = Mesh(
        mesh.devices.reshape(sizes["dp"] // 2, 2, sizes["ctx"], sizes["fsdp"] // 2, 2),
        ("dh", "dl", "ctx", "fy", "core"),
    )
    acts = P(DP, PLANE, None)
    mats = P(ALL, None)
    vecs = P(None, ALL)
    ladder = sizes["dp"] == 4 and sizes["ctx"] == 2 and sizes["fsdp"] == 4
    return jax.shard_map(
        ladder_shards if ladder else wide_shards,
        mesh=fine,
        in_specs=(acts, P(DP, PLANE), acts) + (mats,) * 4 + (vecs,) + (mats,) * 8 + (vecs,) * 2,
        out_specs=(acts, acts) + (mats,) * 12 + (vecs,) * 3,
        check_vma=False,
    )
```

```python
import functools

import jax
import jax.numpy as jnp
from jax import lax
from jax.experimental import pallas as pl
from jax.experimental.pallas import tpu as pltpu
from jax.sharding import Mesh, PartitionSpec as P

HEADS = 8
KV_HEADS = 4
HEAD_DIM = 256
STEP = 10

NORM_EPS = 1e-06
SOFT_CAP = 50.0
THETA = 10000.0
BETA_ONE = 0.9
BETA_TWO = 0.95
ADAM_EPS = 1e-08
MATRIX_RATE = 0.03
GAIN_RATE = 0.2
WEIGHT_DECAY = 0.1

DP = ("dh", "dl")
PLANE = ("ctx", "fy", "core")
ALL = DP + PLANE
LADDER = DP + ("ctx",)
GROUP = PLANE
ACROSS = DP


def f32(v):
    return v.astype(jnp.float32)


def bf(v):
    return v.astype(jnp.bfloat16)


def dot(left, right, dims):
    return lax.dot_general(left, right, (dims, ((), ())), preferred_element_type=jnp.float32)


def mm(left, right):
    return dot(left, right, ((1,), (0,)))


def mm_nt(left, right):
    return dot(left, right, ((1,), (1,)))


def mm_tn(left, right):
    return dot(left, right, ((0,), (0,)))


def rms_scale(values, gain):
    inverse = lax.rsqrt(jnp.mean(values * values, axis=-1, keepdims=True) + NORM_EPS)
    return values * inverse * (1.0 + gain)


def rotary_tables(places):
    half = HEAD_DIM // 2
    freqs = THETA ** (-(jnp.arange(half, dtype=jnp.float32) * 2.0 / HEAD_DIM))
    angles = f32(places)[:, None] * freqs[None, :]
    return (jnp.cos(angles), jnp.sin(angles))


def rotary(values, cosine, sine):
    half = HEAD_DIM // 2
    first = values[..., :half]
    second = values[..., half:]
    return jnp.concatenate(
        [first * cosine - second * sine, second * cosine + first * sine], axis=-1
    )


def unrotary(values, cosine, sine):
    return rotary(values, cosine, -sine)


def adam_step(weight, grad, first, second, rate, decay):
    first_new = BETA_ONE * first + (1.0 - BETA_ONE) * grad
    second_new = BETA_TWO * second + (1.0 - BETA_TWO) * grad * grad
    ratio = (
        first_new
        / (1.0 - BETA_ONE**STEP)
        / (jnp.sqrt(second_new / (1.0 - BETA_TWO**STEP)) + ADAM_EPS)
    )
    return (weight - rate * (ratio + decay * weight), first_new, second_new)


def gather(v, axes, axis=0):
    return lax.all_gather(v, axes, axis=axis, tiled=True)


def scatter_sum(v, axes):
    return lax.psum_scatter(v, axes, scatter_dimension=0, tiled=True)


def swap(v, axes):
    return lax.all_to_all(v, axes, split_axis=0, concat_axis=0, tiled=True)


def hold(v):
    return lax.optimization_barrier(v)


def flip(v, axis):
    return lax.ppermute(v, axis, [(0, 1), (1, 0)])


def plane_scatter(parts):
    size = parts.shape[0] // 8
    half = size // 2
    col, row, core = (lax.axis_index(axis) for axis in PLANE)
    parts = parts.reshape((4, 2, size) + parts.shape[1:])
    sent = lax.dynamic_index_in_dim(parts, 1 - core, 1, keepdims=False)
    kept = lax.dynamic_index_in_dim(parts, core, 1, keepdims=False)
    both = bf(f32(kept) + f32(flip(sent, "core")))
    own, over_y, over_x, corner = (
        lax.dynamic_index_in_dim(both, (2 * col + row) ^ bits, 0, keepdims=False) for bits in range(4)
    )
    got_y = flip(corner[:half], "ctx")
    got_x = flip(corner[half:], "fy")
    over_y = jnp.concatenate([bf(f32(over_y[:half]) + f32(got_y)), over_y[half:]], axis=0)
    over_x = jnp.concatenate([over_x[:half], bf(f32(over_x[half:]) + f32(got_x))], axis=0)
    return f32(own) + f32(flip(over_x, "ctx")) + f32(flip(over_y, "fy"))


def line_gather(own, rider):
    count = lax.axis_size(DP)
    rows = [[own], [rider]]
    ends = [[own, own], [rider, rider]]
    for step in range(1, count + 1):
        for which in range(2):
            hop = step - which
            if 1 <= hop < count:
                up, down = ends[which]
                up = lax.ppermute(up, DP, [(i, i + 1) for i in range(hop - 1, count - 1)])
                down = lax.ppermute(down, DP, [(i + 1, i) for i in range(count - hop)])
                ends[which] = [up, down]
                rows[which] = [up] + rows[which] + [down]
        if step < count - 1:
            ends = hold(ends)
    start = count - 1 - lax.axis_index(DP)
    return [lax.dynamic_slice_in_dim(jnp.stack(row), start, count, axis=0) for row in rows]


def ring_pairs():
    count = lax.axis_size(DP)
    ring = [2 * z for z in range(count)] + [2 * z + 1 for z in reversed(range(count))]
    onward = [(ring[i], ring[(i + 1) % len(ring)]) for i in range(len(ring))]
    return onward, [(b, a) for a, b in onward]


def ring_gather(own):
    onward, back = ring_pairs()
    half = own.shape[0] // 2
    steps = [[own]]
    behind, ahead = (own, own)
    for _ in range(len(onward) // 2 - 1):
        behind = lax.ppermute(behind, LADDER, onward)
        ahead = lax.ppermute(ahead, LADDER, back)
        steps.append([behind, ahead])
    steps.append(
        [
            lax.ppermute(behind[:half], LADDER, onward),
            lax.ppermute(ahead[half:], LADDER, back),
        ]
    )
    return steps


def two_parts(steps):
    return [
        jnp.concatenate(sum(steps[:3], []), axis=0),
        jnp.concatenate(sum(steps[3:], []), axis=0),
    ]


def steps_of(parts, size):
    early, late = parts
    steps = [early[:size], early[size : 3 * size], early[3 * size :]]
    return steps + [late[: 2 * size], late[2 * size :]]


def ring_scatter(pieces):
    onward, back = ring_pairs()
    size = pieces[0].shape[0]
    half = size // 2
    ahead = lax.ppermute(pieces[-1][:half], LADDER, onward)
    behind = lax.ppermute(pieces[-1][half:], LADDER, back)
    for step in range(len(pieces) - 2, 0, -1):
        to_behind, to_ahead = (pieces[step][:size], pieces[step][size:])
        if step == len(pieces) - 2:
            to_ahead = jnp.concatenate(
                [bf(f32(to_ahead[:half]) + f32(ahead)), to_ahead[half:]], axis=0
            )
            to_behind = jnp.concatenate(
                [to_behind[:half], bf(f32(to_behind[half:]) + f32(behind))], axis=0
            )
        else:
            to_ahead = bf(f32(to_ahead) + f32(ahead))
            to_behind = bf(f32(to_behind) + f32(behind))
        to_ahead, to_behind = hold((to_ahead, to_behind))
        ahead = lax.ppermute(to_ahead, LADDER, onward)
        behind = lax.ppermute(to_behind, LADDER, back)
    return f32(pieces[0]) + f32(ahead) + f32(behind)


def quad_blocks(own, late=None):
    over_y = flip(own, "fy")
    if late is not None:
        over_y, _ = hold((over_y, late))
    return [own, flip(own, "core"), over_y, flip(over_y, "core")]


def quad_place(blocks, parts):
    me = lax.axis_index(("fy", "core"))
    count, rows, cols = blocks[0][0].shape
    whole = jnp.zeros((count, 4, rows, parts * cols), blocks[0][0].dtype)
    for part in range(parts):
        for bits, block in enumerate(blocks[part]):
            whole = lax.dynamic_update_slice(
                whole, block[:, None], (0, me ^ bits, 0, part * cols)
            )
    return whole


def core_sum(parts):
    core = lax.axis_index("core")
    parts = parts.reshape(parts.shape[:1] + (2, 2) + parts.shape[2:])
    sent = lax.dynamic_index_in_dim(parts, 1 - core, 2, keepdims=False)
    kept = lax.dynamic_index_in_dim(parts, core, 2, keepdims=False)
    return bf(f32(kept) + f32(flip(sent, "core")))


def row_sum(both):
    row = lax.axis_index("fy")
    sent = lax.dynamic_index_in_dim(both, 1 - row, 1, keepdims=False)
    kept = lax.dynamic_index_in_dim(both, row, 1, keepdims=False)
    return bf(f32(kept) + f32(flip(sent, "fy")))


def kernel_params():
    return pltpu.CompilerParams(vmem_limit_bytes=32 * 1024 * 1024)


LIGHT = pl.CostEstimate(flops=1, bytes_accessed=1, transcendentals=0)


def scores_of(q_ref, k_ref, at_ref, all_ref):
    scores = mm_nt(q_ref[...], k_ref[...])
    capped = jnp.tanh(scores * (1.0 / SOFT_CAP))
    weights = jnp.where(at_ref[...] >= all_ref[...], jnp.exp(SOFT_CAP * capped), 0.0)
    return capped, weights


def attend_kernel(q_ref, k_ref, v_ref, at_ref, all_ref, attn_ref, total_ref):
    _, weights = scores_of(q_ref, k_ref, at_ref, all_ref)
    total = jnp.sum(weights, axis=-1, keepdims=True)
    attn_ref[...] = mm(bf(weights), v_ref[...]) / total
    total_ref[...] = total


def attend_back_kernel(
    q_ref, k_ref, v_ref, at_ref, all_ref, attn_ref, total_ref, grad_ref, dq_ref, dk_ref, dv_ref
):
    @pl.when(pl.program_id(0) == 0)
    def _():
        dk_ref[...] = jnp.zeros_like(dk_ref)
        dv_ref[...] = jnp.zeros_like(dv_ref)

    capped, weights = scores_of(q_ref, k_ref, at_ref, all_ref)
    inverse = 1.0 / total_ref[...]
    grad = f32(grad_ref[...])
    rho = bf(grad * inverse)
    delta = jnp.sum(grad * attn_ref[...], axis=-1, keepdims=True) * inverse
    pulled = mm_nt(rho, v_ref[...])
    grad_scores = bf((pulled - delta) * weights * (1.0 - capped * capped))
    dq_ref[...] = mm(grad_scores, k_ref[...]) * HEAD_DIM ** (-0.5)
    dk_ref[...] += mm_tn(grad_scores, q_ref[...])
    dv_ref[...] += mm_tn(bf(weights), rho)


def attend(query, key, value, places):
    count, depth = query.shape
    block = min(256, count)
    part = pl.BlockSpec((block, depth), lambda i: (i, 0))
    whole = pl.BlockSpec((count, depth), lambda i: (0, 0))
    column = pl.BlockSpec((block, 1), lambda i: (i, 0))
    row = pl.BlockSpec((1, count), lambda i: (0, 0))
    wide = jax.ShapeDtypeStruct((count, depth), jnp.float32)
    places = (places[:, None], places[None, :])
    attn, total = pl.pallas_call(
        attend_kernel,
        grid=(count // block,),
        in_specs=[part, whole, whole, column, row],
        out_specs=[part, column],
        out_shape=[wide, jax.ShapeDtypeStruct((count, 1), jnp.float32)],
        compiler_params=kernel_params(),
        cost_estimate=LIGHT,
        name="attend",
    )(query, key, value, *places)

    def backward(grad):
        return pl.pallas_call(
            attend_back_kernel,
            grid=(count // block,),
            in_specs=[part, whole, whole, column, row, part, column, part],
            out_specs=[part, whole, whole],
            out_shape=[wide] * 3,
            compiler_params=kernel_params(),
            cost_estimate=LIGHT,
            name="attend_back",
        )(query, key, value, *places, attn, total, grad)

    return attn, backward


def product_kernel(contract, left_ref, right_ref, out_ref):
    out_ref[...] = bf(dot(left_ref[...], right_ref[...], contract))


def product(left, right, contract, by_left):
    free = (1 - contract[0], 1 - contract[1])
    rows, cols = (left.shape[free[0]], right.shape[free[1]])
    split = rows if by_left else cols
    block = 256 if split % 256 == 0 else split

    def spec(operand, dim, moves):
        shape = list(operand.shape)
        if moves:
            shape[dim] = block
        where = (lambda i: (i, 0)) if dim == 0 else (lambda i: (0, i))
        return pl.BlockSpec(tuple(shape), where if moves else (lambda i: (0, 0)))

    out = (block, cols) if by_left else (rows, block)
    return pl.pallas_call(
        functools.partial(product_kernel, ((contract[0],), (contract[1],))),
        grid=(split // block,),
        in_specs=[
            spec(left, free[0], by_left),
            spec(right, free[1], not by_left),
        ],
        out_specs=pl.BlockSpec(out, (lambda i: (i, 0)) if by_left else (lambda i: (0, i))),
        out_shape=jax.ShapeDtypeStruct((rows, cols), jnp.bfloat16),
        compiler_params=kernel_params(),
        cost_estimate=LIGHT,
        name="product",
    )(left, right)


def ladder_shards(
    hidden_in,
    positions,
    cotangent,
    w_qkv,
    w_out,
    w_gate_up,
    w_down,
    gains,
    m_qkv,
    v_qkv,
    m_out,
    v_out,
    m_gate_up,
    v_gate_up,
    m_down,
    v_down,
    m_gains,
    v_gains,
):
    x_own = hidden_in[0]
    tok, width = x_own.shape
    rows = w_qkv.shape[0]
    planes = lax.axis_size(DP)
    group = lax.axis_size(LADDER)
    q_width = HEADS * HEAD_DIM
    core = lax.axis_index("core")

    q_cols = w_qkv[:, :q_width].reshape(rows, HEADS, HEAD_DIM)
    kv_cols = w_qkv[:, q_width:].reshape(rows, 2, KV_HEADS, HEAD_DIM)
    kv_cols = jnp.swapaxes(kv_cols, 1, 2).reshape(rows, HEADS, HEAD_DIM)
    pieces = jnp.swapaxes(jnp.concatenate([q_cols, kv_cols], axis=2), 0, 1)
    first = jnp.stack([positions[0, 0] // 128, positions[0, 0] % 128])
    own_gains = jnp.concatenate([gains.reshape(4 * rows), bf(first)])[None, None]
    own_gains = jnp.pad(own_gains, ((0, 0), (0, 7), (0, 2 * HEAD_DIM - 4 * rows - 2)))
    pieces = jnp.concatenate(
        [pieces, jnp.broadcast_to(own_gains, (HEADS,) + own_gains.shape[1:])], axis=1
    )
    x_all = gather(x_own, PLANE)
    got = swap(pieces, PLANE)
    first = got[:, rows, 4 * rows : 4 * rows + 2].astype(jnp.int32)
    pos_all = first[:, :1] * 128 + first[:, 1:] + jnp.arange(tok, dtype=jnp.int32)[None]
    pos_all = pos_all.reshape(-1)
    cosine, sine = rotary_tables(pos_all)
    got, out_line = line_gather(got, w_out)
    ff_own = w_down.shape[0] * 4
    cols = []
    for part in range(2):
        piece = w_gate_up[:, part * group * ff_own : (part + 1) * group * ff_own]
        cols.append(jnp.swapaxes(piece.reshape(rows, group, ff_own), 0, 1))
    got, cols[0], w_down_late = hold((got, cols[0], w_down))
    w_own = got[:, :, :rows].reshape(width, 2 * HEAD_DIM)
    gain_vals = got[:, :, rows, : 4 * rows].reshape(planes * HEADS, 4, rows)
    gain_vals = f32(jnp.swapaxes(gain_vals, 0, 1).reshape(4, width))
    out_full = lax.all_gather(out_line, PLANE, axis=1, tiled=False).reshape(q_width, width)
    cols[0] = swap(cols[0], LADDER)

    normed_all = bf(rms_scale(f32(x_all), gain_vals[0]))
    qkv = mm(normed_all, w_own)
    query = bf(rotary(qkv[:, :HEAD_DIM], cosine, sine) * HEAD_DIM ** (-0.5))
    half = qkv[:, HEAD_DIM:]
    mine = jnp.where(core == 0, bf(rotary(half, cosine, sine)), bf(half))
    other = flip(mine, "core")
    key = jnp.where(core == 0, mine, other)
    value = jnp.where(core == 0, other, mine)
    attn, attn_back = attend(query, key, value, pos_all)
    attn_own = swap(bf(attn).reshape(HEADS, tok, HEAD_DIM), PLANE)
    cols[0], cols[1], attn_own = hold((cols[0], cols[1], attn_own))
    cols[1] = swap(cols[1], LADDER)
    attn_own = jnp.swapaxes(attn_own, 0, 1).reshape(tok, q_width)
    mixed = mm(attn_own, out_full)

    x_rows = f32(x_own)
    branch_one, pull_one = jax.vjp(rms_scale, mixed, gain_vals[1])
    resid = x_rows + branch_one
    normed_two, pull_two = jax.vjp(rms_scale, resid, gain_vals[2])

    tokens_own = bf(normed_two)
    steps = ring_gather(tokens_own)
    cols[1], _ = hold((cols[1], tokens_own))
    down_own = quad_place([quad_blocks(w_down_late[None], tokens_own)], 1).reshape(ff_own, width)
    gate_up_own = [quad_blocks(cols[0], tokens_own), quad_blocks(cols[1])]
    gate_up_own = quad_place(gate_up_own, 2).reshape(width, 2 * ff_own)
    tokens = jnp.concatenate(sum(steps, []), axis=0)
    gate_up = mm(tokens, gate_up_own)

    def gated(gate, up_part):
        return jax.nn.gelu(gate, approximate=True) * up_part

    inner = bf(gated(gate_up[:, :ff_own], gate_up[:, ff_own:]))
    late = tokens.shape[0] - 3 * tok
    down = bf(mm(inner, down_own))
    attn_cols = attn_own.reshape(tok, planes, HEADS, w_out.shape[0])
    attn_cols = jnp.transpose(attn_cols, (2, 0, 1, 3)).reshape(HEADS, tok, HEAD_DIM)
    attn_cols, down = hold((attn_cols, down))
    attn_cols = swap(attn_cols, PLANE).reshape(HEADS * tok, HEAD_DIM)
    down = ring_scatter(steps_of((down[:late], down[late:]), tok))
    down, attn_cols = hold((down, attn_cols))
    branch_two, pull_three = jax.vjp(rms_scale, down, gain_vals[3])
    block_out = bf(resid + branch_two)[None]
    grad_top = f32(cotangent[0])
    grad_down_in, gain_grad_three = pull_three(grad_top)
    steps = ring_gather(bf(grad_down_in))
    grad_downs = two_parts(steps)
    grad_gus, parts = ([], [])
    for piece, kept in zip(grad_downs, (gate_up[:late], gate_up[late:])):
        _, pull = jax.vjp(gated, kept[:, :ff_own], kept[:, ff_own:])
        grad_gus.append(bf(jnp.concatenate(pull(mm_nt(piece, down_own)), axis=1)))
        grad_gu, _ = hold((grad_gus[-1], steps[3][0]))
        parts.append(bf(mm_nt(grad_gu, gate_up_own)))
    tokens, inner, grad_downs, grad_gus, parts = hold(
        (tokens, inner, grad_downs, grad_gus, parts)
    )
    grad_normed_two = ring_scatter(steps_of(parts, tok))
    grad_gu_b = jnp.concatenate(grad_gus, axis=0)
    grad_halves = [bf(mm_tn(tokens, grad_gu_b[:, :ff_own])), bf(mm_tn(tokens, grad_gu_b[:, ff_own:]))]
    grad_down_w = bf(mm_tn(inner, jnp.concatenate(grad_downs, axis=0)))
    grad_normed_two, _, _ = hold((grad_normed_two, grad_halves, grad_down_w))
    grad_resid_two, _ = pull_two(grad_normed_two)
    grad_resid = grad_top + grad_resid_two
    grad_mixed, gain_grad_one = pull_one(grad_resid)
    grad_mixed_b = bf(grad_mixed)

    grad_attn = bf(mm_nt(grad_mixed_b, out_full)).reshape(tok, HEADS, HEAD_DIM)
    grad_head = swap(jnp.swapaxes(grad_attn, 0, 1), PLANE).reshape(HEADS * tok, HEAD_DIM)
    gain_grad_one, _ = hold((gain_grad_one, grad_head))
    others = jnp.stack([gain_grad_one, gain_grad_three]).reshape(2, planes * HEADS, rows)
    others = jnp.sum(swap(jnp.swapaxes(others, 0, 1), ALL), axis=0)
    grad_query, grad_key, grad_value = attn_back(grad_head)
    sent = jnp.where(core == 0, grad_value, grad_key)
    grad_half = jnp.where(core == 0, grad_key, grad_value) + flip(sent, "core")
    grad_half = jnp.where(core == 0, unrotary(grad_half, cosine, sine), grad_half)
    grad_qkv = bf(jnp.concatenate([unrotary(grad_query, cosine, sine), grad_half], axis=1))
    grad_qkv, others, grad_mixed_all = hold((grad_qkv, others, gather(grad_mixed_b, PLANE)))
    grad_w = product(normed_all, grad_qkv, (0, 0), True)
    grad_qkv, grad_w = hold((grad_qkv, grad_w))
    grad_normed = plane_scatter(product(grad_qkv, w_own, (1, 1), False))
    _, pull_zero = jax.vjp(rms_scale, x_rows, gain_vals[0])
    grad_x_zero, _ = pull_zero(grad_normed)
    input_grad = (grad_resid + grad_x_zero)[None]

    sums = [core_sum(v.reshape(group, 4, rows, ff_own)) for v in grad_halves]
    sums.append(core_sum(grad_down_w.reshape(1, 4, ff_own // 4, width)))
    sums, _ = hold((sums, grad_qkv))
    grad_halves = [row_sum(v) for v in sums[:2]]
    grad_down_w, grad_halves[1] = hold((sums[2], grad_halves[1]))
    grad_down_w = f32(row_sum(grad_down_w)[0])
    grad_w = grad_w.reshape(planes, -1, 2 * HEAD_DIM)
    grad_out_w = product(attn_cols, grad_mixed_all, (0, 0), False).reshape(planes, -1, 2 * HEAD_DIM)
    grad_w = scatter_sum(jnp.concatenate([grad_w, grad_out_w], axis=1), DP)[0]
    grad_out_w = f32(grad_w[HEADS * rows :].reshape(w_out.shape))
    grad_w = grad_w[: HEADS * rows].reshape(HEADS, rows, 2 * HEAD_DIM)
    for part in range(2):
        part_w = jnp.swapaxes(swap(grad_halves[part], LADDER), 0, 1)
        grad_halves[part] = part_w.reshape(rows, group * ff_own)
    grad_gate_up_w = f32(jnp.concatenate(grad_halves, axis=1))
    grad_w, grad_halves[1] = hold((grad_w, grad_halves[1]))
    grad_w = f32(jnp.swapaxes(swap(grad_w, PLANE), 0, 1))
    grad_q_w = grad_w[:, :, :HEAD_DIM].reshape(rows, q_width)
    grad_kv_w = grad_w[:, :, HEAD_DIM:].reshape(rows, KV_HEADS, 2, HEAD_DIM)
    grad_kv_w = jnp.swapaxes(grad_kv_w, 1, 2).reshape(rows, q_width)
    grad_qkv_w = jnp.concatenate([grad_q_w, grad_kv_w], axis=1)

    gain_zero = jnp.sum(f32(w_qkv) * grad_qkv_w, axis=1) / (1.0 + f32(gains[0]))
    gain_two = jnp.sum(f32(w_gate_up) * grad_gate_up_w, axis=1) / (1.0 + f32(gains[2]))
    grad_gains = jnp.stack([gain_zero, others[0], gain_two, others[1]], axis=0)

    return (
        (block_out, input_grad)
        + adam_step(f32(w_qkv), grad_qkv_w, m_qkv, v_qkv, MATRIX_RATE, WEIGHT_DECAY)
        + adam_step(f32(w_out), grad_out_w, m_out, v_out, MATRIX_RATE, WEIGHT_DECAY)
        + adam_step(f32(w_gate_up), grad_gate_up_w, m_gate_up, v_gate_up, MATRIX_RATE, WEIGHT_DECAY)
        + adam_step(f32(w_down), grad_down_w, m_down, v_down, MATRIX_RATE, WEIGHT_DECAY)
        + adam_step(f32(gains), grad_gains, m_gains, v_gains, GAIN_RATE, 0.0)
    )


def token_attention(x_own, pos_own, w_qkv, w_out, gains):
    tok = x_own.shape[0]
    q_width = HEADS * HEAD_DIM
    k_width = KV_HEADS * HEAD_DIM
    groups = HEADS // KV_HEADS
    qkv_full = gather(w_qkv, ALL)
    out_full = gather(w_out, ALL)
    gain_vals = f32(gather(gains, ALL, 1))
    normed = bf(rms_scale(f32(x_own), gain_vals[0]))
    qkv = mm(normed, qkv_full)
    cosine, sine = rotary_tables(pos_own)
    cosine, sine = (cosine[:, None, :], sine[:, None, :])
    query = rotary(qkv[:, :q_width].reshape(tok, HEADS, HEAD_DIM), cosine, sine)
    query = bf(query * HEAD_DIM ** (-0.5)).reshape(tok, KV_HEADS, groups, HEAD_DIM)
    key_own = qkv[:, q_width : q_width + k_width].reshape(tok, KV_HEADS, HEAD_DIM)
    key = gather(bf(rotary(key_own, cosine, sine)), PLANE)
    value = gather(bf(qkv[:, q_width + k_width :]).reshape(tok, KV_HEADS, HEAD_DIM), PLANE)
    pos_all = gather(pos_own, PLANE)
    count = pos_all.shape[0]
    scores = jnp.einsum("tgjd,sgd->gjts", query, key, preferred_element_type=jnp.float32)
    capped = SOFT_CAP * jnp.tanh(scores / SOFT_CAP)
    weights = jnp.where(pos_own[:, None] >= pos_all[None, :], jnp.exp(capped), 0.0)
    weights_b = bf(weights)
    total = jnp.sum(weights, axis=-1)
    attn = jnp.einsum("gjts,sgd->gjtd", weights_b, value, preferred_element_type=jnp.float32)
    attn = attn / total[..., None]
    attn_b = bf(jnp.transpose(attn, (2, 0, 1, 3)).reshape(tok, q_width))
    mixed = mm(attn_b, out_full)

    def backward(grad_mixed_b):
        grad_attn = mm_nt(grad_mixed_b, out_full).reshape(tok, KV_HEADS, groups, HEAD_DIM)
        grad_heads = jnp.transpose(grad_attn, (1, 2, 0, 3))
        rho = bf(grad_heads / total[..., None])
        delta = jnp.sum(grad_heads * attn, axis=-1) / total
        pulled = jnp.einsum("gjtd,sgd->gjts", rho, value, preferred_element_type=jnp.float32)
        grad_scores = bf(
            (pulled - delta[..., None]) * weights * (1.0 - (capped / SOFT_CAP) ** 2)
        )
        grad_query = jnp.einsum(
            "gjts,sgd->tgjd", grad_scores, key, preferred_element_type=jnp.float32
        ).reshape(tok, HEADS, HEAD_DIM)
        grad_key = jnp.einsum(
            "gjts,tgjd->sgd", grad_scores, query, preferred_element_type=jnp.float32
        ).reshape(count, k_width)
        grad_value = jnp.einsum(
            "gjts,gjtd->sgd", weights_b, rho, preferred_element_type=jnp.float32
        ).reshape(count, k_width)
        grad_kv = scatter_sum(jnp.concatenate([grad_key, grad_value], axis=1), PLANE)
        grad_query = unrotary(grad_query * HEAD_DIM ** (-0.5), cosine, sine)
        grad_key = unrotary(grad_kv[:, :k_width].reshape(tok, KV_HEADS, HEAD_DIM), cosine, sine)
        grad_qkv = bf(
            jnp.concatenate(
                [
                    grad_query.reshape(tok, q_width),
                    grad_key.reshape(tok, k_width),
                    grad_kv[:, k_width:],
                ],
                axis=1,
            )
        )
        grad_normed = mm_nt(grad_qkv, qkv_full)
        grad_qkv_w = f32(scatter_sum(bf(mm_tn(normed, grad_qkv)), ALL))
        grad_out_w = f32(scatter_sum(bf(mm_tn(attn_b, grad_mixed_b)), ALL))
        return grad_normed, grad_qkv_w, grad_out_w

    return mixed, gain_vals, backward


def wide_shards(
    hidden_in,
    positions,
    cotangent,
    w_qkv,
    w_out,
    w_gate_up,
    w_down,
    gains,
    m_qkv,
    v_qkv,
    m_out,
    v_out,
    m_gate_up,
    v_gate_up,
    m_down,
    v_down,
    m_gains,
    v_gains,
):
    x_own = hidden_in[0]
    rows, width = (w_qkv.shape[0], x_own.shape[1])
    group, across = (lax.axis_size(GROUP), lax.axis_size(ACROSS))
    ff_piece = w_down.shape[0]
    ff_own = across * ff_piece
    gu_pieces = w_gate_up.reshape(rows, 2, across, group, ff_piece)
    gu_pieces = jnp.transpose(gu_pieces, (3, 0, 1, 2, 4)).reshape(group * rows, 2 * ff_own)

    mixed, gain_vals, attention_back = token_attention(x_own, positions[0], w_qkv, w_out, gains)
    gu_own = gather(swap(gu_pieces, GROUP), ACROSS)
    down_own = gather(w_down, ACROSS)

    x_rows = f32(x_own)
    branch_one, pull_one = jax.vjp(rms_scale, mixed, gain_vals[1])
    resid = x_rows + branch_one
    normed_two, pull_two = jax.vjp(rms_scale, resid, gain_vals[2])
    tokens_b = gather(bf(normed_two), GROUP)
    gate_up = mm(tokens_b, gu_own)
    inner, pull_gelu = jax.vjp(
        lambda gate, up_part: jax.nn.gelu(gate, approximate=True) * up_part,
        gate_up[:, :ff_own],
        gate_up[:, ff_own:],
    )
    inner_b = bf(inner)
    down = f32(scatter_sum(bf(mm(inner_b, down_own)), GROUP))
    branch_two, pull_three = jax.vjp(rms_scale, down, gain_vals[3])
    block_out = bf(resid + branch_two)[None]
    grad_top = f32(cotangent[0])
    grad_down_in, gain_grad_three = pull_three(grad_top)
    grad_down_b = gather(bf(grad_down_in), GROUP)
    grad_gate, grad_up = pull_gelu(mm_nt(grad_down_b, down_own))
    grad_gu_b = bf(jnp.concatenate([grad_gate, grad_up], axis=1))
    grad_normed_two = f32(scatter_sum(bf(mm_nt(grad_gu_b, gu_own)), GROUP))
    grad_gate_up_w = scatter_sum(bf(mm_tn(tokens_b, grad_gu_b)), ACROSS)
    grad_down_w = f32(scatter_sum(bf(mm_tn(inner_b, grad_down_b)), ACROSS))

    grad_resid_two, gain_grad_two = pull_two(grad_normed_two)
    grad_resid = grad_top + grad_resid_two
    grad_mixed, gain_grad_one = pull_one(grad_resid)
    grad_normed, grad_qkv_w, grad_out_w = attention_back(bf(grad_mixed))
    _, pull_zero = jax.vjp(rms_scale, x_rows, gain_vals[0])
    grad_x_zero, gain_grad_zero = pull_zero(grad_normed)
    input_grad = (grad_resid + grad_x_zero)[None]

    grad_gate_up_w = swap(grad_gate_up_w, GROUP).reshape(group, rows, 2, across, ff_piece)
    grad_gate_up_w = f32(jnp.transpose(grad_gate_up_w, (1, 2, 3, 0, 4)).reshape(rows, -1))
    gain_term = jnp.stack([gain_grad_zero, gain_grad_one, gain_grad_two, gain_grad_three], axis=0)
    grad_gains = lax.psum_scatter(gain_term, ALL, scatter_dimension=1, tiled=True)

    return (
        (block_out, input_grad)
        + adam_step(f32(w_qkv), grad_qkv_w, m_qkv, v_qkv, MATRIX_RATE, WEIGHT_DECAY)
        + adam_step(f32(w_out), grad_out_w, m_out, v_out, MATRIX_RATE, WEIGHT_DECAY)
        + adam_step(f32(w_gate_up), grad_gate_up_w, m_gate_up, v_gate_up, MATRIX_RATE, WEIGHT_DECAY)
        + adam_step(f32(w_down), grad_down_w, m_down, v_down, MATRIX_RATE, WEIGHT_DECAY)
        + adam_step(f32(gains), grad_gains, m_gains, v_gains, GAIN_RATE, 0.0)
    )


def solution(mesh):
    sizes = dict(mesh.shape)
    fine = Mesh(
        mesh.devices.reshape(sizes["dp"] // 2, 2, sizes["ctx"], sizes["fsdp"] // 2, 2),
        ("dh", "dl", "ctx", "fy", "core"),
    )
    acts = P(DP, PLANE, None)
    mats = P(ALL, None)
    vecs = P(None, ALL)
    ladder = sizes["dp"] == 4 and sizes["ctx"] == 2 and sizes["fsdp"] == 4
    return jax.shard_map(
        ladder_shards if ladder else wide_shards,
        mesh=fine,
        in_specs=(acts, P(DP, PLANE), acts) + (mats,) * 4 + (vecs,) + (mats,) * 8 + (vecs,) * 2,
        out_specs=(acts, acts) + (mats,) * 12 + (vecs,) * 3,
        check_vma=False,
    )
```

```python
import jax
import jax.numpy as jnp
from jax import lax
from jax.sharding import Mesh, PartitionSpec as P

HEADS = 8
KV_HEADS = 4
HEAD_DIM = 256
STEP = 10

NORM_EPS = 1e-06
SOFT_CAP = 50.0
THETA = 10000.0
BETA_ONE = 0.9
BETA_TWO = 0.95
ADAM_EPS = 1e-08
MATRIX_RATE = 0.03
GAIN_RATE = 0.2
WEIGHT_DECAY = 0.1

DP = ("dh", "dl")
PLANE = ("ctx", "fy", "core")
ALL = DP + PLANE
LADDER = DP + ("ctx",)
GROUP = PLANE
ACROSS = DP


def f32(v):
    return v.astype(jnp.float32)


def bf(v):
    return v.astype(jnp.bfloat16)


def dot(left, right, dims):
    return lax.dot_general(left, right, (dims, ((), ())), preferred_element_type=jnp.float32)


def mm(left, right):
    return dot(left, right, ((1,), (0,)))


def mm_nt(left, right):
    return dot(left, right, ((1,), (1,)))


def mm_tn(left, right):
    return dot(left, right, ((0,), (0,)))


def rms_scale(values, gain):
    inverse = lax.rsqrt(jnp.mean(values * values, axis=-1, keepdims=True) + NORM_EPS)
    return values * inverse * (1.0 + gain)


def rotary_tables(places):
    half = HEAD_DIM // 2
    freqs = THETA ** (-(jnp.arange(half, dtype=jnp.float32) * 2.0 / HEAD_DIM))
    angles = f32(places)[:, None] * freqs[None, :]
    return (jnp.cos(angles), jnp.sin(angles))


def rotary(values, cosine, sine):
    half = HEAD_DIM // 2
    first = values[..., :half]
    second = values[..., half:]
    return jnp.concatenate(
        [first * cosine - second * sine, second * cosine + first * sine], axis=-1
    )


def unrotary(values, cosine, sine):
    return rotary(values, cosine, -sine)


def adam_step(weight, grad, first, second, rate, decay):
    first_new = BETA_ONE * first + (1.0 - BETA_ONE) * grad
    second_new = BETA_TWO * second + (1.0 - BETA_TWO) * grad * grad
    ratio = (
        first_new
        / (1.0 - BETA_ONE**STEP)
        / (jnp.sqrt(second_new / (1.0 - BETA_TWO**STEP)) + ADAM_EPS)
    )
    return (weight - rate * (ratio + decay * weight), first_new, second_new)


def gather(v, axes, axis=0):
    return lax.all_gather(v, axes, axis=axis, tiled=True)


def scatter_sum(v, axes):
    return lax.psum_scatter(v, axes, scatter_dimension=0, tiled=True)


def swap(v, axes):
    return lax.all_to_all(v, axes, split_axis=0, concat_axis=0, tiled=True)


def hold(v):
    return lax.optimization_barrier(v)


def flip(v, axis):
    return lax.ppermute(v, axis, [(0, 1), (1, 0)])


def plane_scatter(parts):
    size = parts.shape[0] // 8
    half = size // 2
    col, row, core = (lax.axis_index(axis) for axis in PLANE)
    parts = parts.reshape((4, 2, size) + parts.shape[1:])
    sent = lax.dynamic_index_in_dim(parts, 1 - core, 1, keepdims=False)
    kept = lax.dynamic_index_in_dim(parts, core, 1, keepdims=False)
    both = bf(f32(kept) + f32(flip(sent, "core")))
    own, over_y, over_x, corner = (
        lax.dynamic_index_in_dim(both, (2 * col + row) ^ bits, 0, keepdims=False) for bits in range(4)
    )
    got_y = flip(corner[:half], "ctx")
    got_x = flip(corner[half:], "fy")
    over_y = jnp.concatenate([bf(f32(over_y[:half]) + f32(got_y)), over_y[half:]], axis=0)
    over_x = jnp.concatenate([over_x[:half], bf(f32(over_x[half:]) + f32(got_x))], axis=0)
    return f32(own) + f32(flip(over_x, "ctx")) + f32(flip(over_y, "fy"))


def line_gather(own):
    count = lax.axis_size(DP)
    row = [own]
    up, down = (own, own)
    for step in range(1, count):
        up = lax.ppermute(up, DP, [(i, i + 1) for i in range(step - 1, count - 1)])
        down = lax.ppermute(down, DP, [(i + 1, i) for i in range(count - step)])
        row = [up] + row + [down]
        up, down = hold((up, down))
    return lax.dynamic_slice_in_dim(jnp.stack(row), count - 1 - lax.axis_index(DP), count, axis=0)


def ring_pairs():
    count = lax.axis_size(DP)
    ring = [2 * z for z in range(count)] + [2 * z + 1 for z in reversed(range(count))]
    onward = [(ring[i], ring[(i + 1) % len(ring)]) for i in range(len(ring))]
    return onward, [(b, a) for a, b in onward]


def ring_gather(own):
    onward, back = ring_pairs()
    half = own.shape[0] // 2
    steps = [[own]]
    behind, ahead = (own, own)
    for _ in range(len(onward) // 2 - 1):
        behind = lax.ppermute(behind, LADDER, onward)
        ahead = lax.ppermute(ahead, LADDER, back)
        steps.append([behind, ahead])
    steps.append(
        [
            lax.ppermute(behind[:half], LADDER, onward),
            lax.ppermute(ahead[half:], LADDER, back),
        ]
    )
    return steps


def two_parts(steps):
    return [
        jnp.concatenate(sum(steps[:3], []), axis=0),
        jnp.concatenate(sum(steps[3:], []), axis=0),
    ]


def steps_of(parts, size):
    early, late = parts
    steps = [early[:size], early[size : 3 * size], early[3 * size :]]
    return steps + [late[: 2 * size], late[2 * size :]]


def ring_scatter(pieces):
    onward, back = ring_pairs()
    size = pieces[0].shape[0]
    half = size // 2
    ahead = lax.ppermute(pieces[-1][:half], LADDER, onward)
    behind = lax.ppermute(pieces[-1][half:], LADDER, back)
    for step in range(len(pieces) - 2, 0, -1):
        to_behind, to_ahead = (pieces[step][:size], pieces[step][size:])
        if step == len(pieces) - 2:
            to_ahead = jnp.concatenate(
                [bf(f32(to_ahead[:half]) + f32(ahead)), to_ahead[half:]], axis=0
            )
            to_behind = jnp.concatenate(
                [to_behind[:half], bf(f32(to_behind[half:]) + f32(behind))], axis=0
            )
        else:
            to_ahead = bf(f32(to_ahead) + f32(ahead))
            to_behind = bf(f32(to_behind) + f32(behind))
        to_ahead, to_behind = hold((to_ahead, to_behind))
        ahead = lax.ppermute(to_ahead, LADDER, onward)
        behind = lax.ppermute(to_behind, LADDER, back)
    return f32(pieces[0]) + f32(ahead) + f32(behind)


def quad_blocks(own, late=None):
    over_y = flip(own, "fy")
    if late is not None:
        over_y, _ = hold((over_y, late))
    return [own, flip(own, "core"), over_y, flip(over_y, "core")]


def quad_place(blocks, parts):
    me = lax.axis_index(("fy", "core"))
    count, rows, cols = blocks[0][0].shape
    whole = jnp.zeros((count, 4, rows, parts * cols), blocks[0][0].dtype)
    for part in range(parts):
        for bits, block in enumerate(blocks[part]):
            whole = lax.dynamic_update_slice(
                whole, block[:, None], (0, me ^ bits, 0, part * cols)
            )
    return whole


def core_sum(parts):
    core = lax.axis_index("core")
    parts = parts.reshape(parts.shape[:1] + (2, 2) + parts.shape[2:])
    sent = lax.dynamic_index_in_dim(parts, 1 - core, 2, keepdims=False)
    kept = lax.dynamic_index_in_dim(parts, core, 2, keepdims=False)
    return bf(f32(kept) + f32(flip(sent, "core")))


def row_sum(both):
    row = lax.axis_index("fy")
    sent = lax.dynamic_index_in_dim(both, 1 - row, 1, keepdims=False)
    kept = lax.dynamic_index_in_dim(both, row, 1, keepdims=False)
    return bf(f32(kept) + f32(flip(sent, "fy")))


def ladder_shards(
    hidden_in,
    positions,
    cotangent,
    w_qkv,
    w_out,
    w_gate_up,
    w_down,
    gains,
    m_qkv,
    v_qkv,
    m_out,
    v_out,
    m_gate_up,
    v_gate_up,
    m_down,
    v_down,
    m_gains,
    v_gains,
):
    x_own = hidden_in[0]
    tok, width = x_own.shape
    rows = w_qkv.shape[0]
    planes = lax.axis_size(DP)
    group = lax.axis_size(LADDER)
    q_width = HEADS * HEAD_DIM
    core = lax.axis_index("core")

    q_cols = w_qkv[:, :q_width].reshape(rows, HEADS, HEAD_DIM)
    kv_cols = w_qkv[:, q_width:].reshape(rows, 2, KV_HEADS, HEAD_DIM)
    kv_cols = jnp.swapaxes(kv_cols, 1, 2).reshape(rows, HEADS, HEAD_DIM)
    pieces = jnp.swapaxes(jnp.concatenate([q_cols, kv_cols], axis=2), 0, 1)
    first = jnp.stack([positions[0, 0] // 128, positions[0, 0] % 128])
    own_gains = jnp.concatenate([gains.reshape(4 * rows), bf(first)])[None, None]
    own_gains = jnp.pad(own_gains, ((0, 0), (0, 7), (0, 2 * HEAD_DIM - 4 * rows - 2)))
    pieces = jnp.concatenate(
        [pieces, jnp.broadcast_to(own_gains, (HEADS,) + own_gains.shape[1:])], axis=1
    )
    x_all = gather(x_own, PLANE)
    got = swap(pieces, PLANE)
    first = got[:, rows, 4 * rows : 4 * rows + 2].astype(jnp.int32)
    pos_all = first[:, :1] * 128 + first[:, 1:] + jnp.arange(tok, dtype=jnp.int32)[None]
    pos_all = pos_all.reshape(-1)
    cosine, sine = rotary_tables(pos_all)
    shape = got.shape
    got = jnp.concatenate([got.reshape(-1, shape[2]), w_out.reshape(-1, shape[2])], axis=0)
    got = line_gather(got)
    out_line = got[:, shape[0] * shape[1] :].reshape((planes,) + w_out.shape)
    got = got[:, : shape[0] * shape[1]].reshape((planes,) + shape)
    ff_own = w_down.shape[0] * 4
    cols = []
    for part in range(2):
        piece = w_gate_up[:, part * group * ff_own : (part + 1) * group * ff_own]
        cols.append(jnp.swapaxes(piece.reshape(rows, group, ff_own), 0, 1))
    got, cols[0] = hold((got, cols[0]))
    w_own = got[:, :, :rows].reshape(width, 2 * HEAD_DIM)
    gain_vals = got[:, :, rows, : 4 * rows].reshape(planes * HEADS, 4, rows)
    gain_vals = f32(jnp.swapaxes(gain_vals, 0, 1).reshape(4, width))
    out_full = lax.all_gather(out_line, PLANE, axis=1, tiled=False).reshape(q_width, width)
    cols[0] = swap(cols[0], LADDER)

    normed_all = bf(rms_scale(f32(x_all), gain_vals[0]))
    qkv = mm(normed_all, w_own)
    query = bf(rotary(qkv[:, :HEAD_DIM], cosine, sine) * HEAD_DIM ** (-0.5))
    half = qkv[:, HEAD_DIM:]
    mine = jnp.where(core == 0, bf(rotary(half, cosine, sine)), bf(half))
    other = flip(mine, "core")
    key = jnp.where(core == 0, mine, other)
    value = jnp.where(core == 0, other, mine)
    scores = mm_nt(query, key)
    capped = SOFT_CAP * jnp.tanh(scores / SOFT_CAP)
    weights = jnp.where(pos_all[:, None] >= pos_all[None, :], jnp.exp(capped), 0.0)
    weights_b = bf(weights)
    total = jnp.sum(weights, axis=-1, keepdims=True)
    attn = mm(weights_b, value) / total
    attn_own = swap(bf(attn).reshape(HEADS, tok, HEAD_DIM), PLANE)
    cols[0], cols[1], w_down_late, attn_own = hold((cols[0], cols[1], w_down, attn_own))
    cols[1] = swap(cols[1], LADDER)
    attn_own = jnp.swapaxes(attn_own, 0, 1).reshape(tok, q_width)
    mixed = mm(attn_own, out_full)

    x_rows = f32(x_own)
    branch_one, pull_one = jax.vjp(rms_scale, mixed, gain_vals[1])
    resid = x_rows + branch_one
    normed_two, pull_two = jax.vjp(rms_scale, resid, gain_vals[2])

    tokens_own = bf(normed_two)
    steps = ring_gather(tokens_own)
    cols[1], _ = hold((cols[1], tokens_own))
    down_own = quad_place([quad_blocks(w_down_late[None], tokens_own)], 1).reshape(ff_own, width)
    gate_up_own = [quad_blocks(cols[0], tokens_own), quad_blocks(cols[1])]
    gate_up_own = quad_place(gate_up_own, 2).reshape(width, 2 * ff_own)
    tokens = jnp.concatenate(sum(steps, []), axis=0)
    gate_up = mm(tokens, gate_up_own)

    def gated(gate, up_part):
        return jax.nn.gelu(gate, approximate=True) * up_part

    inner = bf(gated(gate_up[:, :ff_own], gate_up[:, ff_own:]))
    late = tokens.shape[0] - 3 * tok
    down = bf(mm(inner, down_own))
    attn_cols = attn_own.reshape(tok, planes, HEADS, w_out.shape[0])
    attn_cols = jnp.transpose(attn_cols, (2, 0, 1, 3)).reshape(HEADS, tok, HEAD_DIM)
    attn_cols, down = hold((attn_cols, down))
    attn_cols = swap(attn_cols, PLANE).reshape(HEADS * tok, HEAD_DIM)
    down = ring_scatter(steps_of((down[:late], down[late:]), tok))
    down, attn_cols = hold((down, attn_cols))
    branch_two, pull_three = jax.vjp(rms_scale, down, gain_vals[3])
    block_out = bf(resid + branch_two)[None]
    grad_top = f32(cotangent[0])
    grad_down_in, gain_grad_three = pull_three(grad_top)
    steps = ring_gather(bf(grad_down_in))
    grad_downs = two_parts(steps)
    grad_gus, parts = ([], [])
    for piece, kept in zip(grad_downs, (gate_up[:late], gate_up[late:])):
        _, pull = jax.vjp(gated, kept[:, :ff_own], kept[:, ff_own:])
        grad_gus.append(bf(jnp.concatenate(pull(mm_nt(piece, down_own)), axis=1)))
        grad_gu, _ = hold((grad_gus[-1], steps[3][0]))
        parts.append(bf(mm_nt(grad_gu, gate_up_own)))
    tokens, inner, grad_downs, grad_gus, parts = hold(
        (tokens, inner, grad_downs, grad_gus, parts)
    )
    grad_normed_two = ring_scatter(steps_of(parts, tok))
    grad_gu_b = jnp.concatenate(grad_gus, axis=0)
    grad_halves = [bf(mm_tn(tokens, grad_gu_b[:, :ff_own])), bf(mm_tn(tokens, grad_gu_b[:, ff_own:]))]
    grad_down_w = bf(mm_tn(inner, jnp.concatenate(grad_downs, axis=0)))
    grad_normed_two, _, _ = hold((grad_normed_two, grad_halves, grad_down_w))
    grad_resid_two, _ = pull_two(grad_normed_two)
    grad_resid = grad_top + grad_resid_two
    grad_mixed, gain_grad_one = pull_one(grad_resid)
    grad_mixed_b = bf(grad_mixed)

    grad_attn = bf(mm_nt(grad_mixed_b, out_full)).reshape(tok, HEADS, HEAD_DIM)
    grad_head = swap(jnp.swapaxes(grad_attn, 0, 1), PLANE).reshape(HEADS * tok, HEAD_DIM)
    grad_head = f32(grad_head)
    rho = bf(grad_head / total)
    delta = jnp.sum(grad_head * attn, axis=-1, keepdims=True) / total
    pulled = mm_nt(rho, value)
    grad_scores = bf((pulled - delta) * weights * (1.0 - (capped / SOFT_CAP) ** 2))
    grad_query = mm(grad_scores, key) * HEAD_DIM ** (-0.5)
    grad_key = mm_tn(grad_scores, query)
    grad_value = mm_tn(weights_b, rho)
    sent = jnp.where(core == 0, grad_value, grad_key)
    grad_half = jnp.where(core == 0, grad_key, grad_value) + flip(sent, "core")
    grad_half = jnp.where(core == 0, unrotary(grad_half, cosine, sine), grad_half)
    grad_qkv = bf(jnp.concatenate([unrotary(grad_query, cosine, sine), grad_half], axis=1))
    grad_qkv, grad_mixed_all = hold((grad_qkv, gather(grad_mixed_b, PLANE)))
    grad_w = bf(mm_tn(normed_all, grad_qkv))
    grad_qkv, grad_w = hold((grad_qkv, grad_w))
    sums = [core_sum(v.reshape(group, 4, rows, ff_own)) for v in grad_halves]
    sums.append(core_sum(grad_down_w.reshape(1, 4, ff_own // 4, width)))
    sums, gain_grad_one, _ = hold((sums, gain_grad_one, grad_qkv))
    others = jnp.stack([gain_grad_one, gain_grad_three]).reshape(2, planes * HEADS, rows)
    others = jnp.sum(swap(jnp.swapaxes(others, 0, 1), ALL), axis=0)
    grad_halves = [row_sum(v) for v in sums[:2]]
    grad_w = grad_w.reshape(planes, -1, 2 * HEAD_DIM)
    grad_out_w = bf(mm_tn(attn_cols, grad_mixed_all)).reshape(planes, -1, 2 * HEAD_DIM)
    grad_w = scatter_sum(jnp.concatenate([grad_w, grad_out_w], axis=1), DP)[0]
    grad_out_w = f32(grad_w[HEADS * rows :].reshape(w_out.shape))
    grad_w = grad_w[: HEADS * rows].reshape(HEADS, rows, 2 * HEAD_DIM)
    grad_halves[0], others, grad_qkv = hold((grad_halves[0], others, grad_qkv))
    grad_halves[0] = swap(grad_halves[0], LADDER)
    grad_normed = plane_scatter(bf(mm_nt(grad_qkv, w_own)))
    grad_down_w, grad_halves[1] = hold((sums[2], grad_halves[1]))
    grad_down_w = f32(row_sum(grad_down_w)[0])
    grad_halves[1] = swap(grad_halves[1], LADDER)
    grad_w, grad_halves[1], grad_normed = hold((grad_w, grad_halves[1], grad_normed))
    _, pull_zero = jax.vjp(rms_scale, x_rows, gain_vals[0])
    grad_x_zero, _ = pull_zero(grad_normed)
    input_grad = (grad_resid + grad_x_zero)[None]
    grad_halves = [jnp.swapaxes(v, 0, 1).reshape(rows, group * ff_own) for v in grad_halves]
    grad_gate_up_w = f32(jnp.concatenate(grad_halves, axis=1))
    grad_w = f32(jnp.swapaxes(swap(grad_w, PLANE), 0, 1))
    grad_q_w = grad_w[:, :, :HEAD_DIM].reshape(rows, q_width)
    grad_kv_w = grad_w[:, :, HEAD_DIM:].reshape(rows, KV_HEADS, 2, HEAD_DIM)
    grad_kv_w = jnp.swapaxes(grad_kv_w, 1, 2).reshape(rows, q_width)
    grad_qkv_w = jnp.concatenate([grad_q_w, grad_kv_w], axis=1)

    gain_zero = jnp.sum(f32(w_qkv) * grad_qkv_w, axis=1) / (1.0 + f32(gains[0]))
    gain_two = jnp.sum(f32(w_gate_up) * grad_gate_up_w, axis=1) / (1.0 + f32(gains[2]))
    grad_gains = jnp.stack([gain_zero, others[0], gain_two, others[1]], axis=0)

    return (
        (block_out, input_grad)
        + adam_step(f32(w_qkv), grad_qkv_w, m_qkv, v_qkv, MATRIX_RATE, WEIGHT_DECAY)
        + adam_step(f32(w_out), grad_out_w, m_out, v_out, MATRIX_RATE, WEIGHT_DECAY)
        + adam_step(f32(w_gate_up), grad_gate_up_w, m_gate_up, v_gate_up, MATRIX_RATE, WEIGHT_DECAY)
        + adam_step(f32(w_down), grad_down_w, m_down, v_down, MATRIX_RATE, WEIGHT_DECAY)
        + adam_step(f32(gains), grad_gains, m_gains, v_gains, GAIN_RATE, 0.0)
    )


def token_attention(x_own, pos_own, w_qkv, w_out, gains):
    tok = x_own.shape[0]
    q_width = HEADS * HEAD_DIM
    k_width = KV_HEADS * HEAD_DIM
    groups = HEADS // KV_HEADS
    qkv_full = gather(w_qkv, ALL)
    out_full = gather(w_out, ALL)
    gain_vals = f32(gather(gains, ALL, 1))
    normed = bf(rms_scale(f32(x_own), gain_vals[0]))
    qkv = mm(normed, qkv_full)
    cosine, sine = rotary_tables(pos_own)
    cosine, sine = (cosine[:, None, :], sine[:, None, :])
    query = rotary(qkv[:, :q_width].reshape(tok, HEADS, HEAD_DIM), cosine, sine)
    query = bf(query * HEAD_DIM ** (-0.5)).reshape(tok, KV_HEADS, groups, HEAD_DIM)
    key_own = qkv[:, q_width : q_width + k_width].reshape(tok, KV_HEADS, HEAD_DIM)
    key = gather(bf(rotary(key_own, cosine, sine)), PLANE)
    value = gather(bf(qkv[:, q_width + k_width :]).reshape(tok, KV_HEADS, HEAD_DIM), PLANE)
    pos_all = gather(pos_own, PLANE)
    count = pos_all.shape[0]
    scores = jnp.einsum("tgjd,sgd->gjts", query, key, preferred_element_type=jnp.float32)
    capped = SOFT_CAP * jnp.tanh(scores / SOFT_CAP)
    weights = jnp.where(pos_own[:, None] >= pos_all[None, :], jnp.exp(capped), 0.0)
    weights_b = bf(weights)
    total = jnp.sum(weights, axis=-1)
    attn = jnp.einsum("gjts,sgd->gjtd", weights_b, value, preferred_element_type=jnp.float32)
    attn = attn / total[..., None]
    attn_b = bf(jnp.transpose(attn, (2, 0, 1, 3)).reshape(tok, q_width))
    mixed = mm(attn_b, out_full)

    def backward(grad_mixed_b):
        grad_attn = mm_nt(grad_mixed_b, out_full).reshape(tok, KV_HEADS, groups, HEAD_DIM)
        grad_heads = jnp.transpose(grad_attn, (1, 2, 0, 3))
        rho = bf(grad_heads / total[..., None])
        delta = jnp.sum(grad_heads * attn, axis=-1) / total
        pulled = jnp.einsum("gjtd,sgd->gjts", rho, value, preferred_element_type=jnp.float32)
        grad_scores = bf(
            (pulled - delta[..., None]) * weights * (1.0 - (capped / SOFT_CAP) ** 2)
        )
        grad_query = jnp.einsum(
            "gjts,sgd->tgjd", grad_scores, key, preferred_element_type=jnp.float32
        ).reshape(tok, HEADS, HEAD_DIM)
        grad_key = jnp.einsum(
            "gjts,tgjd->sgd", grad_scores, query, preferred_element_type=jnp.float32
        ).reshape(count, k_width)
        grad_value = jnp.einsum(
            "gjts,gjtd->sgd", weights_b, rho, preferred_element_type=jnp.float32
        ).reshape(count, k_width)
        grad_kv = scatter_sum(jnp.concatenate([grad_key, grad_value], axis=1), PLANE)
        grad_query = unrotary(grad_query * HEAD_DIM ** (-0.5), cosine, sine)
        grad_key = unrotary(grad_kv[:, :k_width].reshape(tok, KV_HEADS, HEAD_DIM), cosine, sine)
        grad_qkv = bf(
            jnp.concatenate(
                [
                    grad_query.reshape(tok, q_width),
                    grad_key.reshape(tok, k_width),
                    grad_kv[:, k_width:],
                ],
                axis=1,
            )
        )
        grad_normed = mm_nt(grad_qkv, qkv_full)
        grad_qkv_w = f32(scatter_sum(bf(mm_tn(normed, grad_qkv)), ALL))
        grad_out_w = f32(scatter_sum(bf(mm_tn(attn_b, grad_mixed_b)), ALL))
        return grad_normed, grad_qkv_w, grad_out_w

    return mixed, gain_vals, backward


def wide_shards(
    hidden_in,
    positions,
    cotangent,
    w_qkv,
    w_out,
    w_gate_up,
    w_down,
    gains,
    m_qkv,
    v_qkv,
    m_out,
    v_out,
    m_gate_up,
    v_gate_up,
    m_down,
    v_down,
    m_gains,
    v_gains,
):
    x_own = hidden_in[0]
    rows, width = (w_qkv.shape[0], x_own.shape[1])
    group, across = (lax.axis_size(GROUP), lax.axis_size(ACROSS))
    ff_piece = w_down.shape[0]
    ff_own = across * ff_piece
    gu_pieces = w_gate_up.reshape(rows, 2, across, group, ff_piece)
    gu_pieces = jnp.transpose(gu_pieces, (3, 0, 1, 2, 4)).reshape(group * rows, 2 * ff_own)

    mixed, gain_vals, attention_back = token_attention(x_own, positions[0], w_qkv, w_out, gains)
    gu_own = gather(swap(gu_pieces, GROUP), ACROSS)
    down_own = gather(w_down, ACROSS)

    x_rows = f32(x_own)
    branch_one, pull_one = jax.vjp(rms_scale, mixed, gain_vals[1])
    resid = x_rows + branch_one
    normed_two, pull_two = jax.vjp(rms_scale, resid, gain_vals[2])
    tokens_b = gather(bf(normed_two), GROUP)
    gate_up = mm(tokens_b, gu_own)
    inner, pull_gelu = jax.vjp(
        lambda gate, up_part: jax.nn.gelu(gate, approximate=True) * up_part,
        gate_up[:, :ff_own],
        gate_up[:, ff_own:],
    )
    inner_b = bf(inner)
    down = f32(scatter_sum(bf(mm(inner_b, down_own)), GROUP))
    branch_two, pull_three = jax.vjp(rms_scale, down, gain_vals[3])
    block_out = bf(resid + branch_two)[None]
    grad_top = f32(cotangent[0])
    grad_down_in, gain_grad_three = pull_three(grad_top)
    grad_down_b = gather(bf(grad_down_in), GROUP)
    grad_gate, grad_up = pull_gelu(mm_nt(grad_down_b, down_own))
    grad_gu_b = bf(jnp.concatenate([grad_gate, grad_up], axis=1))
    grad_normed_two = f32(scatter_sum(bf(mm_nt(grad_gu_b, gu_own)), GROUP))
    grad_gate_up_w = scatter_sum(bf(mm_tn(tokens_b, grad_gu_b)), ACROSS)
    grad_down_w = f32(scatter_sum(bf(mm_tn(inner_b, grad_down_b)), ACROSS))

    grad_resid_two, gain_grad_two = pull_two(grad_normed_two)
    grad_resid = grad_top + grad_resid_two
    grad_mixed, gain_grad_one = pull_one(grad_resid)
    grad_normed, grad_qkv_w, grad_out_w = attention_back(bf(grad_mixed))
    _, pull_zero = jax.vjp(rms_scale, x_rows, gain_vals[0])
    grad_x_zero, gain_grad_zero = pull_zero(grad_normed)
    input_grad = (grad_resid + grad_x_zero)[None]

    grad_gate_up_w = swap(grad_gate_up_w, GROUP).reshape(group, rows, 2, across, ff_piece)
    grad_gate_up_w = f32(jnp.transpose(grad_gate_up_w, (1, 2, 3, 0, 4)).reshape(rows, -1))
    gain_term = jnp.stack([gain_grad_zero, gain_grad_one, gain_grad_two, gain_grad_three], axis=0)
    grad_gains = lax.psum_scatter(gain_term, ALL, scatter_dimension=1, tiled=True)

    return (
        (block_out, input_grad)
        + adam_step(f32(w_qkv), grad_qkv_w, m_qkv, v_qkv, MATRIX_RATE, WEIGHT_DECAY)
        + adam_step(f32(w_out), grad_out_w, m_out, v_out, MATRIX_RATE, WEIGHT_DECAY)
        + adam_step(f32(w_gate_up), grad_gate_up_w, m_gate_up, v_gate_up, MATRIX_RATE, WEIGHT_DECAY)
        + adam_step(f32(w_down), grad_down_w, m_down, v_down, MATRIX_RATE, WEIGHT_DECAY)
        + adam_step(f32(gains), grad_gains, m_gains, v_gains, GAIN_RATE, 0.0)
    )


def solution(mesh):
    sizes = dict(mesh.shape)
    fine = Mesh(
        mesh.devices.reshape(sizes["dp"] // 2, 2, sizes["ctx"], sizes["fsdp"] // 2, 2),
        ("dh", "dl", "ctx", "fy", "core"),
    )
    acts = P(DP, PLANE, None)
    mats = P(ALL, None)
    vecs = P(None, ALL)
    ladder = sizes["dp"] == 4 and sizes["ctx"] == 2 and sizes["fsdp"] == 4
    return jax.shard_map(
        ladder_shards if ladder else wide_shards,
        mesh=fine,
        in_specs=(acts, P(DP, PLANE), acts) + (mats,) * 4 + (vecs,) + (mats,) * 8 + (vecs,) * 2,
        out_specs=(acts, acts) + (mats,) * 12 + (vecs,) * 3,
        check_vma=False,
    )
```

```python
import jax
import jax.numpy as jnp
from jax import lax
from jax.sharding import Mesh, PartitionSpec as P

HEADS = 8
KV_HEADS = 4
HEAD_DIM = 256
STEP = 10

NORM_EPS = 1e-06
SOFT_CAP = 50.0
THETA = 10000.0
BETA_ONE = 0.9
BETA_TWO = 0.95
ADAM_EPS = 1e-08
MATRIX_RATE = 0.03
GAIN_RATE = 0.2
WEIGHT_DECAY = 0.1

DP = ("dh", "dl")
PLANE = ("ctx", "fy", "core")
ALL = DP + PLANE
LADDER = DP + ("ctx",)
GROUP = PLANE
ACROSS = DP


def f32(v):
    return v.astype(jnp.float32)


def bf(v):
    return v.astype(jnp.bfloat16)


def dot(left, right, dims):
    return lax.dot_general(left, right, (dims, ((), ())), preferred_element_type=jnp.float32)


def mm(left, right):
    return dot(left, right, ((1,), (0,)))


def mm_nt(left, right):
    return dot(left, right, ((1,), (1,)))


def mm_tn(left, right):
    return dot(left, right, ((0,), (0,)))


def rms_scale(values, gain):
    inverse = lax.rsqrt(jnp.mean(values * values, axis=-1, keepdims=True) + NORM_EPS)
    return values * inverse * (1.0 + gain)


def rotary_tables(places):
    half = HEAD_DIM // 2
    freqs = THETA ** (-(jnp.arange(half, dtype=jnp.float32) * 2.0 / HEAD_DIM))
    angles = f32(places)[:, None] * freqs[None, :]
    return (jnp.cos(angles), jnp.sin(angles))


def rotary(values, cosine, sine):
    half = HEAD_DIM // 2
    first = values[..., :half]
    second = values[..., half:]
    return jnp.concatenate(
        [first * cosine - second * sine, second * cosine + first * sine], axis=-1
    )


def unrotary(values, cosine, sine):
    return rotary(values, cosine, -sine)


def adam_step(weight, grad, first, second, rate, decay):
    first_new = BETA_ONE * first + (1.0 - BETA_ONE) * grad
    second_new = BETA_TWO * second + (1.0 - BETA_TWO) * grad * grad
    ratio = (
        first_new
        / (1.0 - BETA_ONE**STEP)
        / (jnp.sqrt(second_new / (1.0 - BETA_TWO**STEP)) + ADAM_EPS)
    )
    return (weight - rate * (ratio + decay * weight), first_new, second_new)


def gather(v, axes, axis=0):
    return lax.all_gather(v, axes, axis=axis, tiled=True)


def scatter_sum(v, axes):
    return lax.psum_scatter(v, axes, scatter_dimension=0, tiled=True)


def swap(v, axes):
    return lax.all_to_all(v, axes, split_axis=0, concat_axis=0, tiled=True)


def hold(v):
    return lax.optimization_barrier(v)


def flip(v, axis):
    return lax.ppermute(v, axis, [(0, 1), (1, 0)])


def plane_scatter(parts):
    size = parts.shape[0] // 8
    half = size // 2
    col, row, core = (lax.axis_index(axis) for axis in PLANE)
    parts = parts.reshape((4, 2, size) + parts.shape[1:])
    sent = lax.dynamic_index_in_dim(parts, 1 - core, 1, keepdims=False)
    kept = lax.dynamic_index_in_dim(parts, core, 1, keepdims=False)
    both = bf(f32(kept) + f32(flip(sent, "core")))
    own, over_y, over_x, corner = (
        lax.dynamic_index_in_dim(both, (2 * col + row) ^ bits, 0, keepdims=False) for bits in range(4)
    )
    got_y = flip(corner[:half], "ctx")
    got_x = flip(corner[half:], "fy")
    over_y = jnp.concatenate([bf(f32(over_y[:half]) + f32(got_y)), over_y[half:]], axis=0)
    over_x = jnp.concatenate([over_x[:half], bf(f32(over_x[half:]) + f32(got_x))], axis=0)
    return f32(own) + f32(flip(over_x, "ctx")) + f32(flip(over_y, "fy"))


def line_gather(own):
    count = lax.axis_size(DP)
    row = [own]
    up, down = (own, own)
    for step in range(1, count):
        up = lax.ppermute(up, DP, [(i, i + 1) for i in range(step - 1, count - 1)])
        down = lax.ppermute(down, DP, [(i + 1, i) for i in range(count - step)])
        row = [up] + row + [down]
    return lax.dynamic_slice_in_dim(jnp.stack(row), count - 1 - lax.axis_index(DP), count, axis=0)


def ring_pairs():
    count = lax.axis_size(DP)
    ring = [2 * z for z in range(count)] + [2 * z + 1 for z in reversed(range(count))]
    onward = [(ring[i], ring[(i + 1) % len(ring)]) for i in range(len(ring))]
    return onward, [(b, a) for a, b in onward]


def ring_gather(own):
    onward, back = ring_pairs()
    half = own.shape[0] // 2
    steps = [[own]]
    behind, ahead = (own, own)
    for _ in range(len(onward) // 2 - 1):
        behind = lax.ppermute(behind, LADDER, onward)
        ahead = lax.ppermute(ahead, LADDER, back)
        steps.append([behind, ahead])
    steps.append(
        [
            lax.ppermute(behind[:half], LADDER, onward),
            lax.ppermute(ahead[half:], LADDER, back),
        ]
    )
    return steps


def two_parts(steps):
    return [
        jnp.concatenate(sum(steps[:3], []), axis=0),
        jnp.concatenate(sum(steps[3:], []), axis=0),
    ]


def steps_of(parts, size):
    early, late = parts
    steps = [early[:size], early[size : 3 * size], early[3 * size :]]
    return steps + [late[: 2 * size], late[2 * size :]]


def ring_scatter(pieces):
    onward, back = ring_pairs()
    size = pieces[0].shape[0]
    half = size // 2
    ahead = lax.ppermute(pieces[-1][:half], LADDER, onward)
    behind = lax.ppermute(pieces[-1][half:], LADDER, back)
    for step in range(len(pieces) - 2, 0, -1):
        to_behind, to_ahead = (pieces[step][:size], pieces[step][size:])
        if step == len(pieces) - 2:
            to_ahead = jnp.concatenate(
                [bf(f32(to_ahead[:half]) + f32(ahead)), to_ahead[half:]], axis=0
            )
            to_behind = jnp.concatenate(
                [to_behind[:half], bf(f32(to_behind[half:]) + f32(behind))], axis=0
            )
        else:
            to_ahead = bf(f32(to_ahead) + f32(ahead))
            to_behind = bf(f32(to_behind) + f32(behind))
        to_ahead, to_behind = hold((to_ahead, to_behind))
        ahead = lax.ppermute(to_ahead, LADDER, onward)
        behind = lax.ppermute(to_behind, LADDER, back)
    return f32(pieces[0]) + f32(ahead) + f32(behind)


def quad_blocks(own, late=None):
    over_y = flip(own, "fy")
    if late is not None:
        over_y, _ = hold((over_y, late))
    return [own, flip(own, "core"), over_y, flip(over_y, "core")]


def quad_place(blocks, parts):
    me = lax.axis_index(("fy", "core"))
    count, rows, cols = blocks[0][0].shape
    whole = jnp.zeros((count, 4, rows, parts * cols), blocks[0][0].dtype)
    for part in range(parts):
        for bits, block in enumerate(blocks[part]):
            whole = lax.dynamic_update_slice(
                whole, block[:, None], (0, me ^ bits, 0, part * cols)
            )
    return whole


def core_sum(parts):
    core = lax.axis_index("core")
    parts = parts.reshape(parts.shape[:1] + (2, 2) + parts.shape[2:])
    sent = lax.dynamic_index_in_dim(parts, 1 - core, 2, keepdims=False)
    kept = lax.dynamic_index_in_dim(parts, core, 2, keepdims=False)
    return bf(f32(kept) + f32(flip(sent, "core")))


def row_sum(both):
    row = lax.axis_index("fy")
    sent = lax.dynamic_index_in_dim(both, 1 - row, 1, keepdims=False)
    kept = lax.dynamic_index_in_dim(both, row, 1, keepdims=False)
    return bf(f32(kept) + f32(flip(sent, "fy")))


def ladder_shards(
    hidden_in,
    positions,
    cotangent,
    w_qkv,
    w_out,
    w_gate_up,
    w_down,
    gains,
    m_qkv,
    v_qkv,
    m_out,
    v_out,
    m_gate_up,
    v_gate_up,
    m_down,
    v_down,
    m_gains,
    v_gains,
):
    x_own = hidden_in[0]
    tok, width = x_own.shape
    rows = w_qkv.shape[0]
    planes = lax.axis_size(DP)
    group = lax.axis_size(LADDER)
    q_width = HEADS * HEAD_DIM
    core = lax.axis_index("core")

    q_cols = w_qkv[:, :q_width].reshape(rows, HEADS, HEAD_DIM)
    kv_cols = w_qkv[:, q_width:].reshape(rows, 2, KV_HEADS, HEAD_DIM)
    kv_cols = jnp.swapaxes(kv_cols, 1, 2).reshape(rows, HEADS, HEAD_DIM)
    pieces = jnp.swapaxes(jnp.concatenate([q_cols, kv_cols], axis=2), 0, 1)
    first = jnp.stack([positions[0, 0] // 128, positions[0, 0] % 128])
    own_gains = jnp.concatenate([gains.reshape(4 * rows), bf(first)])[None, None]
    own_gains = jnp.pad(own_gains, ((0, 0), (0, 7), (0, 2 * HEAD_DIM - 4 * rows - 2)))
    pieces = jnp.concatenate(
        [pieces, jnp.broadcast_to(own_gains, (HEADS,) + own_gains.shape[1:])], axis=1
    )
    got = swap(pieces, PLANE)
    got, x_sent, out_line = hold((got, x_own, w_out))
    x_sent = jnp.broadcast_to(x_sent[None], (HEADS,) + x_own.shape)
    x_all = swap(x_sent, PLANE).reshape(HEADS * tok, width)
    out_line = line_gather(out_line)
    first = got[:, rows, 4 * rows : 4 * rows + 2].astype(jnp.int32)
    pos_all = first[:, :1] * 128 + first[:, 1:] + jnp.arange(tok, dtype=jnp.int32)[None]
    pos_all = pos_all.reshape(-1)
    cosine, sine = rotary_tables(pos_all)
    got = lax.all_gather(got, DP)
    ff_own = w_down.shape[0] * 4
    cols = []
    for part in range(2):
        piece = w_gate_up[:, part * group * ff_own : (part + 1) * group * ff_own]
        cols.append(jnp.swapaxes(piece.reshape(rows, group, ff_own), 0, 1))
    got, cols[0], w_down_late = hold((got, cols[0], w_down))
    w_own = got[:, :, :rows].reshape(width, 2 * HEAD_DIM)
    gain_vals = got[:, :, rows, : 4 * rows].reshape(planes * HEADS, 4, rows)
    gain_vals = f32(jnp.swapaxes(gain_vals, 0, 1).reshape(4, width))
    out_full = lax.all_gather(out_line, PLANE, axis=1, tiled=False).reshape(q_width, width)
    cols[0] = swap(cols[0], LADDER)

    normed_all = bf(rms_scale(f32(x_all), gain_vals[0]))
    qkv = mm(normed_all, w_own)
    query = bf(rotary(qkv[:, :HEAD_DIM], cosine, sine) * HEAD_DIM ** (-0.5))
    half = qkv[:, HEAD_DIM:]
    mine = jnp.where(core == 0, bf(rotary(half, cosine, sine)), bf(half))
    other = flip(mine, "core")
    key = jnp.where(core == 0, mine, other)
    value = jnp.where(core == 0, other, mine)
    scores = mm_nt(query, key)
    capped = SOFT_CAP * jnp.tanh(scores / SOFT_CAP)
    weights = jnp.where(pos_all[:, None] >= pos_all[None, :], jnp.exp(capped), 0.0)
    weights_b = bf(weights)
    total = jnp.sum(weights, axis=-1, keepdims=True)
    attn = mm(weights_b, value) / total
    attn_own = swap(bf(attn).reshape(HEADS, tok, HEAD_DIM), PLANE)
    cols[0], cols[1], attn_own = hold((cols[0], cols[1], attn_own))
    cols[1] = swap(cols[1], LADDER)
    attn_own = jnp.swapaxes(attn_own, 0, 1).reshape(tok, q_width)
    mixed = mm(attn_own, out_full)

    x_rows = f32(x_own)
    branch_one, pull_one = jax.vjp(rms_scale, mixed, gain_vals[1])
    resid = x_rows + branch_one
    normed_two, pull_two = jax.vjp(rms_scale, resid, gain_vals[2])

    tokens_own = bf(normed_two)
    steps = ring_gather(tokens_own)
    cols[1], _ = hold((cols[1], tokens_own))
    down_own = quad_place([quad_blocks(w_down_late[None], tokens_own)], 1).reshape(ff_own, width)
    gate_up_own = [quad_blocks(cols[0], tokens_own), quad_blocks(cols[1])]
    gate_up_own = quad_place(gate_up_own, 2).reshape(width, 2 * ff_own)
    tokens = jnp.concatenate(sum(steps, []), axis=0)
    gate_up = mm(tokens, gate_up_own)

    def gated(gate, up_part):
        return jax.nn.gelu(gate, approximate=True) * up_part

    inner = bf(gated(gate_up[:, :ff_own], gate_up[:, ff_own:]))
    late = tokens.shape[0] - 3 * tok
    down = bf(mm(inner, down_own))
    attn_cols = attn_own.reshape(tok, planes, HEADS, w_out.shape[0])
    attn_cols = jnp.transpose(attn_cols, (2, 0, 1, 3)).reshape(HEADS, tok, HEAD_DIM)
    attn_cols, down = hold((attn_cols, down))
    attn_cols = swap(attn_cols, PLANE).reshape(HEADS * tok, HEAD_DIM)
    down = ring_scatter(steps_of((down[:late], down[late:]), tok))
    down, attn_cols = hold((down, attn_cols))
    branch_two, pull_three = jax.vjp(rms_scale, down, gain_vals[3])
    block_out = bf(resid + branch_two)[None]
    grad_top = f32(cotangent[0])
    grad_down_in, gain_grad_three = pull_three(grad_top)
    steps = ring_gather(bf(grad_down_in))
    grad_downs = two_parts(steps)
    grad_gus, parts = ([], [])
    for piece, kept in zip(grad_downs, (gate_up[:late], gate_up[late:])):
        _, pull = jax.vjp(gated, kept[:, :ff_own], kept[:, ff_own:])
        grad_gus.append(bf(jnp.concatenate(pull(mm_nt(piece, down_own)), axis=1)))
        grad_gu, _ = hold((grad_gus[-1], steps[3][0]))
        parts.append(bf(mm_nt(grad_gu, gate_up_own)))
    tokens, inner, grad_downs, grad_gus, parts = hold(
        (tokens, inner, grad_downs, grad_gus, parts)
    )
    grad_normed_two = ring_scatter(steps_of(parts, tok))
    grad_gu_b = jnp.concatenate(grad_gus, axis=0)
    grad_halves = [bf(mm_tn(tokens, grad_gu_b[:, :ff_own])), bf(mm_tn(tokens, grad_gu_b[:, ff_own:]))]
    grad_down_w = bf(mm_tn(inner, jnp.concatenate(grad_downs, axis=0)))
    grad_normed_two, _, _ = hold((grad_normed_two, grad_halves, grad_down_w))
    grad_resid_two, _ = pull_two(grad_normed_two)
    grad_resid = grad_top + grad_resid_two
    grad_mixed, gain_grad_one = pull_one(grad_resid)
    grad_mixed_b = bf(grad_mixed)

    grad_attn = bf(mm_nt(grad_mixed_b, out_full)).reshape(tok, HEADS, HEAD_DIM)
    grad_head = swap(jnp.swapaxes(grad_attn, 0, 1), PLANE).reshape(HEADS * tok, HEAD_DIM)
    grad_head = f32(grad_head)
    rho = bf(grad_head / total)
    delta = jnp.sum(grad_head * attn, axis=-1, keepdims=True) / total
    pulled = mm_nt(rho, value)
    grad_scores = bf((pulled - delta) * weights * (1.0 - (capped / SOFT_CAP) ** 2))
    grad_query = mm(grad_scores, key) * HEAD_DIM ** (-0.5)
    grad_key = mm_tn(grad_scores, query)
    grad_value = mm_tn(weights_b, rho)
    sent = jnp.where(core == 0, grad_value, grad_key)
    grad_half = jnp.where(core == 0, grad_key, grad_value) + flip(sent, "core")
    grad_half = jnp.where(core == 0, unrotary(grad_half, cosine, sine), grad_half)
    grad_qkv = bf(jnp.concatenate([unrotary(grad_query, cosine, sine), grad_half], axis=1))
    others = bf(jnp.stack([gain_grad_one, gain_grad_three]))
    others = jnp.concatenate([grad_mixed_b, jnp.pad(others, ((0, 14), (0, 0)))], axis=0)
    others = lax.all_gather(others, PLANE)
    grad_qkv, others = hold((grad_qkv, others))
    grad_mixed_all = others[:, :tok].reshape(HEADS * tok, width)
    others = jnp.sum(f32(others[:, tok : tok + 2]), axis=0).reshape(2, planes, HEADS, rows)
    others = lax.dynamic_index_in_dim(others, lax.axis_index(PLANE), 2, keepdims=False)
    others = jnp.swapaxes(others, 0, 1).reshape(planes, 1, 2 * rows)
    others = bf(jnp.pad(others, ((0, 0), (0, 7), (0, 2 * HEAD_DIM - 2 * rows))))
    grad_w = bf(mm_tn(normed_all, grad_qkv))
    grad_qkv, grad_w = hold((grad_qkv, grad_w))
    grad_normed = plane_scatter(bf(mm_nt(grad_qkv, w_own)))
    sums = [core_sum(v.reshape(group, 4, rows, ff_own)) for v in grad_halves]
    sums.append(core_sum(grad_down_w.reshape(1, 4, ff_own // 4, width)))
    sums, _ = hold((sums, grad_qkv))
    grad_halves = [row_sum(v) for v in sums[:2]]
    grad_down_w, grad_halves[1] = hold((sums[2], grad_halves[1]))
    grad_down_w = f32(row_sum(grad_down_w)[0])
    grad_w = grad_w.reshape(planes, -1, 2 * HEAD_DIM)
    grad_out_w = bf(mm_tn(attn_cols, grad_mixed_all)).reshape(planes, -1, 2 * HEAD_DIM)
    grad_w = scatter_sum(jnp.concatenate([grad_w, grad_out_w, others], axis=1), DP)[0]
    others = f32(grad_w[-8, : 2 * rows]).reshape(2, rows)
    grad_out_w = f32(grad_w[HEADS * rows : -8].reshape(w_out.shape))
    grad_w = grad_w[: HEADS * rows].reshape(HEADS, rows, 2 * HEAD_DIM)
    grad_halves = [swap(v, LADDER) for v in grad_halves]
    grad_w, grad_halves[1], grad_normed = hold((grad_w, grad_halves[1], grad_normed))
    grad_halves = [jnp.swapaxes(v, 0, 1).reshape(rows, group * ff_own) for v in grad_halves]
    grad_gate_up_w = f32(jnp.concatenate(grad_halves, axis=1))
    _, pull_zero = jax.vjp(rms_scale, x_rows, gain_vals[0])
    grad_x_zero, _ = pull_zero(grad_normed)
    input_grad = (grad_resid + grad_x_zero)[None]
    grad_w = f32(jnp.swapaxes(swap(grad_w, PLANE), 0, 1))
    grad_q_w = grad_w[:, :, :HEAD_DIM].reshape(rows, q_width)
    grad_kv_w = grad_w[:, :, HEAD_DIM:].reshape(rows, KV_HEADS, 2, HEAD_DIM)
    grad_kv_w = jnp.swapaxes(grad_kv_w, 1, 2).reshape(rows, q_width)
    grad_qkv_w = jnp.concatenate([grad_q_w, grad_kv_w], axis=1)

    gain_zero = jnp.sum(f32(w_qkv) * grad_qkv_w, axis=1) / (1.0 + f32(gains[0]))
    gain_two = jnp.sum(f32(w_gate_up) * grad_gate_up_w, axis=1) / (1.0 + f32(gains[2]))
    grad_gains = jnp.stack([gain_zero, others[0], gain_two, others[1]], axis=0)

    return (
        (block_out, input_grad)
        + adam_step(f32(w_qkv), grad_qkv_w, m_qkv, v_qkv, MATRIX_RATE, WEIGHT_DECAY)
        + adam_step(f32(w_out), grad_out_w, m_out, v_out, MATRIX_RATE, WEIGHT_DECAY)
        + adam_step(f32(w_gate_up), grad_gate_up_w, m_gate_up, v_gate_up, MATRIX_RATE, WEIGHT_DECAY)
        + adam_step(f32(w_down), grad_down_w, m_down, v_down, MATRIX_RATE, WEIGHT_DECAY)
        + adam_step(f32(gains), grad_gains, m_gains, v_gains, GAIN_RATE, 0.0)
    )


def token_attention(x_own, pos_own, w_qkv, w_out, gains):
    tok = x_own.shape[0]
    q_width = HEADS * HEAD_DIM
    k_width = KV_HEADS * HEAD_DIM
    groups = HEADS // KV_HEADS
    qkv_full = gather(w_qkv, ALL)
    out_full = gather(w_out, ALL)
    gain_vals = f32(gather(gains, ALL, 1))
    normed = bf(rms_scale(f32(x_own), gain_vals[0]))
    qkv = mm(normed, qkv_full)
    cosine, sine = rotary_tables(pos_own)
    cosine, sine = (cosine[:, None, :], sine[:, None, :])
    query = rotary(qkv[:, :q_width].reshape(tok, HEADS, HEAD_DIM), cosine, sine)
    query = bf(query * HEAD_DIM ** (-0.5)).reshape(tok, KV_HEADS, groups, HEAD_DIM)
    key_own = qkv[:, q_width : q_width + k_width].reshape(tok, KV_HEADS, HEAD_DIM)
    key = gather(bf(rotary(key_own, cosine, sine)), PLANE)
    value = gather(bf(qkv[:, q_width + k_width :]).reshape(tok, KV_HEADS, HEAD_DIM), PLANE)
    pos_all = gather(pos_own, PLANE)
    count = pos_all.shape[0]
    scores = jnp.einsum("tgjd,sgd->gjts", query, key, preferred_element_type=jnp.float32)
    capped = SOFT_CAP * jnp.tanh(scores / SOFT_CAP)
    weights = jnp.where(pos_own[:, None] >= pos_all[None, :], jnp.exp(capped), 0.0)
    weights_b = bf(weights)
    total = jnp.sum(weights, axis=-1)
    attn = jnp.einsum("gjts,sgd->gjtd", weights_b, value, preferred_element_type=jnp.float32)
    attn = attn / total[..., None]
    attn_b = bf(jnp.transpose(attn, (2, 0, 1, 3)).reshape(tok, q_width))
    mixed = mm(attn_b, out_full)

    def backward(grad_mixed_b):
        grad_attn = mm_nt(grad_mixed_b, out_full).reshape(tok, KV_HEADS, groups, HEAD_DIM)
        grad_heads = jnp.transpose(grad_attn, (1, 2, 0, 3))
        rho = bf(grad_heads / total[..., None])
        delta = jnp.sum(grad_heads * attn, axis=-1) / total
        pulled = jnp.einsum("gjtd,sgd->gjts", rho, value, preferred_element_type=jnp.float32)
        grad_scores = bf(
            (pulled - delta[..., None]) * weights * (1.0 - (capped / SOFT_CAP) ** 2)
        )
        grad_query = jnp.einsum(
            "gjts,sgd->tgjd", grad_scores, key, preferred_element_type=jnp.float32
        ).reshape(tok, HEADS, HEAD_DIM)
        grad_key = jnp.einsum(
            "gjts,tgjd->sgd", grad_scores, query, preferred_element_type=jnp.float32
        ).reshape(count, k_width)
        grad_value = jnp.einsum(
            "gjts,gjtd->sgd", weights_b, rho, preferred_element_type=jnp.float32
        ).reshape(count, k_width)
        grad_kv = scatter_sum(jnp.concatenate([grad_key, grad_value], axis=1), PLANE)
        grad_query = unrotary(grad_query * HEAD_DIM ** (-0.5), cosine, sine)
        grad_key = unrotary(grad_kv[:, :k_width].reshape(tok, KV_HEADS, HEAD_DIM), cosine, sine)
        grad_qkv = bf(
            jnp.concatenate(
                [
                    grad_query.reshape(tok, q_width),
                    grad_key.reshape(tok, k_width),
                    grad_kv[:, k_width:],
                ],
                axis=1,
            )
        )
        grad_normed = mm_nt(grad_qkv, qkv_full)
        grad_qkv_w = f32(scatter_sum(bf(mm_tn(normed, grad_qkv)), ALL))
        grad_out_w = f32(scatter_sum(bf(mm_tn(attn_b, grad_mixed_b)), ALL))
        return grad_normed, grad_qkv_w, grad_out_w

    return mixed, gain_vals, backward


def wide_shards(
    hidden_in,
    positions,
    cotangent,
    w_qkv,
    w_out,
    w_gate_up,
    w_down,
    gains,
    m_qkv,
    v_qkv,
    m_out,
    v_out,
    m_gate_up,
    v_gate_up,
    m_down,
    v_down,
    m_gains,
    v_gains,
):
    x_own = hidden_in[0]
    rows, width = (w_qkv.shape[0], x_own.shape[1])
    group, across = (lax.axis_size(GROUP), lax.axis_size(ACROSS))
    ff_piece = w_down.shape[0]
    ff_own = across * ff_piece
    gu_pieces = w_gate_up.reshape(rows, 2, across, group, ff_piece)
    gu_pieces = jnp.transpose(gu_pieces, (3, 0, 1, 2, 4)).reshape(group * rows, 2 * ff_own)

    mixed, gain_vals, attention_back = token_attention(x_own, positions[0], w_qkv, w_out, gains)
    gu_own = gather(swap(gu_pieces, GROUP), ACROSS)
    down_own = gather(w_down, ACROSS)

    x_rows = f32(x_own)
    branch_one, pull_one = jax.vjp(rms_scale, mixed, gain_vals[1])
    resid = x_rows + branch_one
    normed_two, pull_two = jax.vjp(rms_scale, resid, gain_vals[2])
    tokens_b = gather(bf(normed_two), GROUP)
    gate_up = mm(tokens_b, gu_own)
    inner, pull_gelu = jax.vjp(
        lambda gate, up_part: jax.nn.gelu(gate, approximate=True) * up_part,
        gate_up[:, :ff_own],
        gate_up[:, ff_own:],
    )
    inner_b = bf(inner)
    down = f32(scatter_sum(bf(mm(inner_b, down_own)), GROUP))
    branch_two, pull_three = jax.vjp(rms_scale, down, gain_vals[3])
    block_out = bf(resid + branch_two)[None]
    grad_top = f32(cotangent[0])
    grad_down_in, gain_grad_three = pull_three(grad_top)
    grad_down_b = gather(bf(grad_down_in), GROUP)
    grad_gate, grad_up = pull_gelu(mm_nt(grad_down_b, down_own))
    grad_gu_b = bf(jnp.concatenate([grad_gate, grad_up], axis=1))
    grad_normed_two = f32(scatter_sum(bf(mm_nt(grad_gu_b, gu_own)), GROUP))
    grad_gate_up_w = scatter_sum(bf(mm_tn(tokens_b, grad_gu_b)), ACROSS)
    grad_down_w = f32(scatter_sum(bf(mm_tn(inner_b, grad_down_b)), ACROSS))

    grad_resid_two, gain_grad_two = pull_two(grad_normed_two)
    grad_resid = grad_top + grad_resid_two
    grad_mixed, gain_grad_one = pull_one(grad_resid)
    grad_normed, grad_qkv_w, grad_out_w = attention_back(bf(grad_mixed))
    _, pull_zero = jax.vjp(rms_scale, x_rows, gain_vals[0])
    grad_x_zero, gain_grad_zero = pull_zero(grad_normed)
    input_grad = (grad_resid + grad_x_zero)[None]

    grad_gate_up_w = swap(grad_gate_up_w, GROUP).reshape(group, rows, 2, across, ff_piece)
    grad_gate_up_w = f32(jnp.transpose(grad_gate_up_w, (1, 2, 3, 0, 4)).reshape(rows, -1))
    gain_term = jnp.stack([gain_grad_zero, gain_grad_one, gain_grad_two, gain_grad_three], axis=0)
    grad_gains = lax.psum_scatter(gain_term, ALL, scatter_dimension=1, tiled=True)

    return (
        (block_out, input_grad)
        + adam_step(f32(w_qkv), grad_qkv_w, m_qkv, v_qkv, MATRIX_RATE, WEIGHT_DECAY)
        + adam_step(f32(w_out), grad_out_w, m_out, v_out, MATRIX_RATE, WEIGHT_DECAY)
        + adam_step(f32(w_gate_up), grad_gate_up_w, m_gate_up, v_gate_up, MATRIX_RATE, WEIGHT_DECAY)
        + adam_step(f32(w_down), grad_down_w, m_down, v_down, MATRIX_RATE, WEIGHT_DECAY)
        + adam_step(f32(gains), grad_gains, m_gains, v_gains, GAIN_RATE, 0.0)
    )


def solution(mesh):
    sizes = dict(mesh.shape)
    fine = Mesh(
        mesh.devices.reshape(sizes["dp"] // 2, 2, sizes["ctx"], sizes["fsdp"] // 2, 2),
        ("dh", "dl", "ctx", "fy", "core"),
    )
    acts = P(DP, PLANE, None)
    mats = P(ALL, None)
    vecs = P(None, ALL)
    ladder = sizes["dp"] == 4 and sizes["ctx"] == 2 and sizes["fsdp"] == 4
    return jax.shard_map(
        ladder_shards if ladder else wide_shards,
        mesh=fine,
        in_specs=(acts, P(DP, PLANE), acts) + (mats,) * 4 + (vecs,) + (mats,) * 8 + (vecs,) * 2,
        out_specs=(acts, acts) + (mats,) * 12 + (vecs,) * 3,
        check_vma=False,
    )
```

```python
import jax
import jax.numpy as jnp
from jax import lax
from jax.sharding import Mesh, PartitionSpec as P

HEADS = 8
KV_HEADS = 4
HEAD_DIM = 256
STEP = 10

NORM_EPS = 1e-06
SOFT_CAP = 50.0
THETA = 10000.0
BETA_ONE = 0.9
BETA_TWO = 0.95
ADAM_EPS = 1e-08
MATRIX_RATE = 0.03
GAIN_RATE = 0.2
WEIGHT_DECAY = 0.1

DP = ("dh", "dl")
PLANE = ("ctx", "fy", "core")
ALL = DP + PLANE
LADDER = DP + ("ctx",)
GROUP = PLANE
ACROSS = DP


def f32(v):
    return v.astype(jnp.float32)


def bf(v):
    return v.astype(jnp.bfloat16)


def dot(left, right, dims):
    return lax.dot_general(left, right, (dims, ((), ())), preferred_element_type=jnp.float32)


def mm(left, right):
    return dot(left, right, ((1,), (0,)))


def mm_nt(left, right):
    return dot(left, right, ((1,), (1,)))


def mm_tn(left, right):
    return dot(left, right, ((0,), (0,)))


def rms_scale(values, gain):
    inverse = lax.rsqrt(jnp.mean(values * values, axis=-1, keepdims=True) + NORM_EPS)
    return values * inverse * (1.0 + gain)


def rotary_tables(places):
    half = HEAD_DIM // 2
    freqs = THETA ** (-(jnp.arange(half, dtype=jnp.float32) * 2.0 / HEAD_DIM))
    angles = f32(places)[:, None] * freqs[None, :]
    return (jnp.cos(angles), jnp.sin(angles))


def rotary(values, cosine, sine):
    half = HEAD_DIM // 2
    first = values[..., :half]
    second = values[..., half:]
    return jnp.concatenate(
        [first * cosine - second * sine, second * cosine + first * sine], axis=-1
    )


def unrotary(values, cosine, sine):
    return rotary(values, cosine, -sine)


def adam_step(weight, grad, first, second, rate, decay):
    first_new = BETA_ONE * first + (1.0 - BETA_ONE) * grad
    second_new = BETA_TWO * second + (1.0 - BETA_TWO) * grad * grad
    ratio = (
        first_new
        / (1.0 - BETA_ONE**STEP)
        / (jnp.sqrt(second_new / (1.0 - BETA_TWO**STEP)) + ADAM_EPS)
    )
    return (weight - rate * (ratio + decay * weight), first_new, second_new)


def gather(v, axes, axis=0):
    return lax.all_gather(v, axes, axis=axis, tiled=True)


def scatter_sum(v, axes):
    return lax.psum_scatter(v, axes, scatter_dimension=0, tiled=True)


def swap(v, axes):
    return lax.all_to_all(v, axes, split_axis=0, concat_axis=0, tiled=True)


def hold(v):
    return lax.optimization_barrier(v)


def flip(v, axis):
    return lax.ppermute(v, axis, [(0, 1), (1, 0)])


def plane_gather(own):
    me = lax.axis_index(PLANE)
    over_y = flip(own, "fy")
    over_x = flip(own, "ctx")
    blocks = [own, over_y, over_x, flip(over_y, "ctx")]
    whole = jnp.zeros((8,) + own.shape, own.dtype)
    for bits, block in enumerate(blocks):
        whole = lax.dynamic_update_index_in_dim(whole, block, me ^ (2 * bits), 0)
        whole = lax.dynamic_update_index_in_dim(whole, flip(block, "core"), me ^ (2 * bits + 1), 0)
    return whole.reshape((-1,) + own.shape[1:])


def plane_scatter(parts):
    size = parts.shape[0] // 8
    half = size // 2
    col, row, core = (lax.axis_index(axis) for axis in PLANE)
    parts = parts.reshape((4, 2, size) + parts.shape[1:])
    sent = lax.dynamic_index_in_dim(parts, 1 - core, 1, keepdims=False)
    kept = lax.dynamic_index_in_dim(parts, core, 1, keepdims=False)
    both = bf(f32(kept) + f32(flip(sent, "core")))
    own, over_y, over_x, corner = (
        lax.dynamic_index_in_dim(both, (2 * col + row) ^ bits, 0, keepdims=False) for bits in range(4)
    )
    got_y = flip(corner[:half], "ctx")
    got_x = flip(corner[half:], "fy")
    over_y = jnp.concatenate([bf(f32(over_y[:half]) + f32(got_y)), over_y[half:]], axis=0)
    over_x = jnp.concatenate([over_x[:half], bf(f32(over_x[half:]) + f32(got_x))], axis=0)
    return f32(own) + f32(flip(over_x, "ctx")) + f32(flip(over_y, "fy"))


def line_gather(own):
    count = lax.axis_size(DP)
    row = [own]
    up, down = (own, own)
    for step in range(1, count):
        up = lax.ppermute(up, DP, [(i, i + 1) for i in range(step - 1, count - 1)])
        down = lax.ppermute(down, DP, [(i + 1, i) for i in range(count - step)])
        row = [up] + row + [down]
    return lax.dynamic_slice_in_dim(jnp.stack(row), count - 1 - lax.axis_index(DP), count, axis=0)


def ring_pairs():
    count = lax.axis_size(DP)
    ring = [2 * z for z in range(count)] + [2 * z + 1 for z in reversed(range(count))]
    onward = [(ring[i], ring[(i + 1) % len(ring)]) for i in range(len(ring))]
    return onward, [(b, a) for a, b in onward]


def ring_gather(own):
    onward, back = ring_pairs()
    half = own.shape[0] // 2
    steps = [[own]]
    behind, ahead = (own, own)
    for _ in range(len(onward) // 2 - 1):
        behind = lax.ppermute(behind, LADDER, onward)
        ahead = lax.ppermute(ahead, LADDER, back)
        steps.append([behind, ahead])
    steps.append(
        [
            lax.ppermute(behind[:half], LADDER, onward),
            lax.ppermute(ahead[half:], LADDER, back),
        ]
    )
    return steps


def two_parts(steps):
    return [
        jnp.concatenate(sum(steps[:3], []), axis=0),
        jnp.concatenate(sum(steps[3:], []), axis=0),
    ]


def steps_of(parts, size):
    early, late = parts
    steps = [early[:size], early[size : 3 * size], early[3 * size :]]
    return steps + [late[: 2 * size], late[2 * size :]]


def ring_scatter(pieces, beside=None):
    onward, back = ring_pairs()
    size = pieces[0].shape[0]
    half = size // 2
    ahead = lax.ppermute(pieces[-1][:half], LADDER, onward)
    behind = lax.ppermute(pieces[-1][half:], LADDER, back)
    riders = {} if beside is None else beside(ahead)
    for step in range(len(pieces) - 2, 0, -1):
        to_behind, to_ahead = (pieces[step][:size], pieces[step][size:])
        if step == len(pieces) - 2:
            to_ahead = jnp.concatenate(
                [bf(f32(to_ahead[:half]) + f32(ahead)), to_ahead[half:]], axis=0
            )
            to_behind = jnp.concatenate(
                [to_behind[:half], bf(f32(to_behind[half:]) + f32(behind))], axis=0
            )
        else:
            to_ahead = bf(f32(to_ahead) + f32(ahead))
            to_behind = bf(f32(to_behind) + f32(behind))
        to_ahead, to_behind, _ = hold((to_ahead, to_behind, riders.get(step, ())))
        ahead = lax.ppermute(to_ahead, LADDER, onward)
        behind = lax.ppermute(to_behind, LADDER, back)
    return f32(pieces[0]) + f32(ahead) + f32(behind)


def quad_blocks(own, late=None):
    over_y = flip(own, "fy")
    if late is not None:
        over_y, _ = hold((over_y, late))
    return [own, flip(own, "core"), over_y, flip(over_y, "core")]


def quad_place(blocks, parts):
    me = lax.axis_index(("fy", "core"))
    count, rows, cols = blocks[0][0].shape
    whole = jnp.zeros((count, 4, rows, parts * cols), blocks[0][0].dtype)
    for part in range(parts):
        for bits, block in enumerate(blocks[part]):
            whole = lax.dynamic_update_slice(
                whole, block[:, None], (0, me ^ bits, 0, part * cols)
            )
    return whole


def core_sum(parts):
    core = lax.axis_index("core")
    parts = parts.reshape(parts.shape[:1] + (2, 2) + parts.shape[2:])
    sent = lax.dynamic_index_in_dim(parts, 1 - core, 2, keepdims=False)
    kept = lax.dynamic_index_in_dim(parts, core, 2, keepdims=False)
    return bf(f32(kept) + f32(flip(sent, "core")))


def row_sum(both):
    row = lax.axis_index("fy")
    sent = lax.dynamic_index_in_dim(both, 1 - row, 1, keepdims=False)
    kept = lax.dynamic_index_in_dim(both, row, 1, keepdims=False)
    return bf(f32(kept) + f32(flip(sent, "fy")))


def ladder_shards(
    hidden_in,
    positions,
    cotangent,
    w_qkv,
    w_out,
    w_gate_up,
    w_down,
    gains,
    m_qkv,
    v_qkv,
    m_out,
    v_out,
    m_gate_up,
    v_gate_up,
    m_down,
    v_down,
    m_gains,
    v_gains,
):
    x_own = hidden_in[0]
    tok, width = x_own.shape
    rows = w_qkv.shape[0]
    planes = lax.axis_size(DP)
    group = lax.axis_size(LADDER)
    q_width = HEADS * HEAD_DIM
    core = lax.axis_index("core")

    q_cols = w_qkv[:, :q_width].reshape(rows, HEADS, HEAD_DIM)
    kv_cols = w_qkv[:, q_width:].reshape(rows, 2, KV_HEADS, HEAD_DIM)
    kv_cols = jnp.swapaxes(kv_cols, 1, 2).reshape(rows, HEADS, HEAD_DIM)
    pieces = jnp.swapaxes(jnp.concatenate([q_cols, kv_cols], axis=2), 0, 1)
    first = jnp.stack([positions[0, 0] // 128, positions[0, 0] % 128])
    own_gains = jnp.concatenate([gains.reshape(4 * rows), bf(first)])[None, None]
    own_gains = jnp.pad(own_gains, ((0, 0), (0, 7), (0, 2 * HEAD_DIM - 4 * rows - 2)))
    pieces = jnp.concatenate(
        [pieces, jnp.broadcast_to(own_gains, (HEADS,) + own_gains.shape[1:])], axis=1
    )
    got = swap(pieces, PLANE)
    got, x_sent, out_line = hold((got, x_own, w_out))
    x_all = plane_gather(x_sent)
    out_line = line_gather(out_line)
    first = got[:, rows, 4 * rows : 4 * rows + 2].astype(jnp.int32)
    pos_all = first[:, :1] * 128 + first[:, 1:] + jnp.arange(tok, dtype=jnp.int32)[None]
    pos_all = pos_all.reshape(-1)
    cosine, sine = rotary_tables(pos_all)
    got = lax.all_gather(got, DP)
    ff_own = w_down.shape[0] * 4
    cols = []
    for part in range(2):
        piece = w_gate_up[:, part * group * ff_own : (part + 1) * group * ff_own]
        cols.append(jnp.swapaxes(piece.reshape(rows, group, ff_own), 0, 1))
    got, cols[0], w_down_late = hold((got, cols[0], w_down))
    w_own = got[:, :, :rows].reshape(width, 2 * HEAD_DIM)
    gain_vals = got[:, :, rows, : 4 * rows].reshape(planes * HEADS, 4, rows)
    gain_vals = f32(jnp.swapaxes(gain_vals, 0, 1).reshape(4, width))
    out_full = lax.all_gather(out_line, PLANE, axis=1, tiled=False).reshape(q_width, width)
    cols[0] = swap(cols[0], LADDER)

    normed_all = bf(rms_scale(f32(x_all), gain_vals[0]))
    qkv = mm(normed_all, w_own)
    query = bf(rotary(qkv[:, :HEAD_DIM], cosine, sine) * HEAD_DIM ** (-0.5))
    half = qkv[:, HEAD_DIM:]
    mine = jnp.where(core == 0, bf(rotary(half, cosine, sine)), bf(half))
    other = flip(mine, "core")
    key = jnp.where(core == 0, mine, other)
    value = jnp.where(core == 0, other, mine)
    scores = mm_nt(query, key)
    capped = SOFT_CAP * jnp.tanh(scores / SOFT_CAP)
    weights = jnp.where(pos_all[:, None] >= pos_all[None, :], jnp.exp(capped), 0.0)
    weights_b = bf(weights)
    total = jnp.sum(weights, axis=-1, keepdims=True)
    attn = mm(weights_b, value) / total
    attn_own = swap(bf(attn).reshape(HEADS, tok, HEAD_DIM), PLANE)
    cols[0], cols[1], _ = hold((cols[0], cols[1], attn_own))
    cols[1] = swap(cols[1], LADDER)
    attn_own = jnp.swapaxes(attn_own, 0, 1).reshape(tok, q_width)
    mixed = mm(attn_own, out_full)

    x_rows = f32(x_own)
    branch_one, pull_one = jax.vjp(rms_scale, mixed, gain_vals[1])
    resid = x_rows + branch_one
    normed_two, pull_two = jax.vjp(rms_scale, resid, gain_vals[2])

    tokens_own = bf(normed_two)
    steps = ring_gather(tokens_own)
    cols[1], _ = hold((cols[1], tokens_own))
    down_own = quad_place([quad_blocks(w_down_late[None], tokens_own)], 1).reshape(ff_own, width)
    gate_up_own = [quad_blocks(cols[0], tokens_own), quad_blocks(cols[1])]
    gate_up_own = quad_place(gate_up_own, 2).reshape(width, 2 * ff_own)
    tokens = jnp.concatenate(sum(steps, []), axis=0)
    gate_up = mm(tokens, gate_up_own)

    def gated(gate, up_part):
        return jax.nn.gelu(gate, approximate=True) * up_part

    inner = bf(gated(gate_up[:, :ff_own], gate_up[:, ff_own:]))
    late = tokens.shape[0] - 3 * tok
    down = bf(mm(inner, down_own))
    attn_cols = attn_own.reshape(tok, planes, HEADS, w_out.shape[0])
    attn_cols = jnp.transpose(attn_cols, (2, 0, 1, 3)).reshape(HEADS, tok, HEAD_DIM)
    attn_cols, down = hold((attn_cols, down))
    attn_cols = swap(attn_cols, PLANE).reshape(HEADS * tok, HEAD_DIM)
    down = ring_scatter(steps_of((down[:late], down[late:]), tok))
    down, attn_cols = hold((down, attn_cols))
    branch_two, pull_three = jax.vjp(rms_scale, down, gain_vals[3])
    block_out = bf(resid + branch_two)[None]
    grad_top = f32(cotangent[0])
    grad_down_in, gain_grad_three = pull_three(grad_top)
    steps = ring_gather(bf(grad_down_in))
    grad_downs = two_parts(steps)
    grad_gus, parts = ([], [])
    for piece, kept in zip(grad_downs, (gate_up[:late], gate_up[late:])):
        _, pull = jax.vjp(gated, kept[:, :ff_own], kept[:, ff_own:])
        grad_gus.append(bf(jnp.concatenate(pull(mm_nt(piece, down_own)), axis=1)))
        grad_gu, _ = hold((grad_gus[-1], steps[3][0]))
        parts.append(bf(mm_nt(grad_gu, gate_up_own)))
    tokens, inner, grad_downs, grad_gus, parts = hold(
        (tokens, inner, grad_downs, grad_gus, parts)
    )
    grad_gu_b = jnp.concatenate(grad_gus, axis=0)
    grad_halves, sums = ([], [])

    def beside(arrived):
        left, right, _ = hold((tokens, grad_gu_b, arrived))
        for part in range(2):
            product = bf(mm_tn(left, right[:, part * ff_own : (part + 1) * ff_own]))
            grad_halves.append(product)
            sums.append(core_sum(product.reshape(group, 4, rows, ff_own)))
        return {2: grad_halves[0], 1: (grad_halves[1], sums[0])}

    grad_normed_two = ring_scatter(steps_of(parts, tok), beside)
    grad_down_w = bf(mm_tn(inner, jnp.concatenate(grad_downs, axis=0)))
    grad_normed_two, sums[1] = hold((grad_normed_two, sums[1]))
    grad_resid_two, _ = pull_two(grad_normed_two)
    grad_resid = grad_top + grad_resid_two
    grad_mixed, gain_grad_one = pull_one(grad_resid)
    grad_mixed_b = bf(grad_mixed)

    grad_attn = bf(mm_nt(grad_mixed_b, out_full)).reshape(tok, HEADS, HEAD_DIM)
    grad_head = swap(jnp.swapaxes(grad_attn, 0, 1), PLANE).reshape(HEADS * tok, HEAD_DIM)
    grad_head = f32(grad_head)
    rho = bf(grad_head / total)
    delta = jnp.sum(grad_head * attn, axis=-1, keepdims=True) / total
    pulled = mm_nt(rho, value)
    grad_scores = bf((pulled - delta) * weights * (1.0 - (capped / SOFT_CAP) ** 2))
    grad_query = mm(grad_scores, key) * HEAD_DIM ** (-0.5)
    grad_key = mm_tn(grad_scores, query)
    grad_value = mm_tn(weights_b, rho)
    sent = jnp.where(core == 0, grad_value, grad_key)
    grad_half = jnp.where(core == 0, grad_key, grad_value) + flip(sent, "core")
    grad_half = jnp.where(core == 0, unrotary(grad_half, cosine, sine), grad_half)
    grad_qkv = bf(jnp.concatenate([unrotary(grad_query, cosine, sine), grad_half], axis=1))
    others = bf(jnp.stack([gain_grad_one, gain_grad_three]))
    others = jnp.concatenate([grad_mixed_b, jnp.pad(others, ((0, 14), (0, 0)))], axis=0)
    others = lax.all_gather(others, PLANE)
    grad_qkv, others = hold((grad_qkv, others))
    grad_mixed_all = others[:, :tok].reshape(HEADS * tok, width)
    others = jnp.sum(f32(others[:, tok : tok + 2]), axis=0).reshape(2, planes, HEADS, rows)
    others = lax.dynamic_index_in_dim(others, lax.axis_index(PLANE), 2, keepdims=False)
    others = jnp.swapaxes(others, 0, 1).reshape(planes, 1, 2 * rows)
    others = bf(jnp.pad(others, ((0, 0), (0, 7), (0, 2 * HEAD_DIM - 2 * rows))))
    grad_w = bf(mm_tn(normed_all, grad_qkv))
    grad_qkv, grad_w = hold((grad_qkv, grad_w))
    sums.append(core_sum(grad_down_w.reshape(1, 4, ff_own // 4, width)))
    sums[1:], _ = hold((sums[1:], grad_qkv))
    grad_halves = [row_sum(v) for v in sums[:2]]
    grad_qkv, _ = hold((grad_qkv, grad_halves[0]))
    grad_normed = plane_scatter(bf(mm_nt(grad_qkv, w_own)))
    grad_down_w, grad_halves[1] = hold((sums[2], grad_halves[1]))
    grad_down_w = f32(row_sum(grad_down_w)[0])
    grad_w = grad_w.reshape(planes, -1, 2 * HEAD_DIM)
    grad_out_w = bf(mm_tn(attn_cols, grad_mixed_all)).reshape(planes, -1, 2 * HEAD_DIM)
    grad_w = scatter_sum(jnp.concatenate([grad_w, grad_out_w, others], axis=1), DP)[0]
    others = f32(grad_w[-8, : 2 * rows]).reshape(2, rows)
    grad_out_w = f32(grad_w[HEADS * rows : -8].reshape(w_out.shape))
    grad_w = grad_w[: HEADS * rows].reshape(HEADS, rows, 2 * HEAD_DIM)
    grad_halves = [swap(v, LADDER) for v in grad_halves]
    grad_w, grad_halves[1], grad_normed = hold((grad_w, grad_halves[1], grad_normed))
    grad_halves = [jnp.swapaxes(v, 0, 1).reshape(rows, group * ff_own) for v in grad_halves]
    grad_gate_up_w = f32(jnp.concatenate(grad_halves, axis=1))
    _, pull_zero = jax.vjp(rms_scale, x_rows, gain_vals[0])
    grad_x_zero, _ = pull_zero(grad_normed)
    input_grad = (grad_resid + grad_x_zero)[None]
    grad_w = f32(jnp.swapaxes(swap(grad_w, PLANE), 0, 1))
    grad_q_w = grad_w[:, :, :HEAD_DIM].reshape(rows, q_width)
    grad_kv_w = grad_w[:, :, HEAD_DIM:].reshape(rows, KV_HEADS, 2, HEAD_DIM)
    grad_kv_w = jnp.swapaxes(grad_kv_w, 1, 2).reshape(rows, q_width)
    grad_qkv_w = jnp.concatenate([grad_q_w, grad_kv_w], axis=1)

    gain_zero = jnp.sum(f32(w_qkv) * grad_qkv_w, axis=1) / (1.0 + f32(gains[0]))
    gain_two = jnp.sum(f32(w_gate_up) * grad_gate_up_w, axis=1) / (1.0 + f32(gains[2]))
    grad_gains = jnp.stack([gain_zero, others[0], gain_two, others[1]], axis=0)

    return (
        (block_out, input_grad)
        + adam_step(f32(w_qkv), grad_qkv_w, m_qkv, v_qkv, MATRIX_RATE, WEIGHT_DECAY)
        + adam_step(f32(w_out), grad_out_w, m_out, v_out, MATRIX_RATE, WEIGHT_DECAY)
        + adam_step(f32(w_gate_up), grad_gate_up_w, m_gate_up, v_gate_up, MATRIX_RATE, WEIGHT_DECAY)
        + adam_step(f32(w_down), grad_down_w, m_down, v_down, MATRIX_RATE, WEIGHT_DECAY)
        + adam_step(f32(gains), grad_gains, m_gains, v_gains, GAIN_RATE, 0.0)
    )


def token_attention(x_own, pos_own, w_qkv, w_out, gains):
    tok = x_own.shape[0]
    q_width = HEADS * HEAD_DIM
    k_width = KV_HEADS * HEAD_DIM
    groups = HEADS // KV_HEADS
    qkv_full = gather(w_qkv, ALL)
    out_full = gather(w_out, ALL)
    gain_vals = f32(gather(gains, ALL, 1))
    normed = bf(rms_scale(f32(x_own), gain_vals[0]))
    qkv = mm(normed, qkv_full)
    cosine, sine = rotary_tables(pos_own)
    cosine, sine = (cosine[:, None, :], sine[:, None, :])
    query = rotary(qkv[:, :q_width].reshape(tok, HEADS, HEAD_DIM), cosine, sine)
    query = bf(query * HEAD_DIM ** (-0.5)).reshape(tok, KV_HEADS, groups, HEAD_DIM)
    key_own = qkv[:, q_width : q_width + k_width].reshape(tok, KV_HEADS, HEAD_DIM)
    key = gather(bf(rotary(key_own, cosine, sine)), PLANE)
    value = gather(bf(qkv[:, q_width + k_width :]).reshape(tok, KV_HEADS, HEAD_DIM), PLANE)
    pos_all = gather(pos_own, PLANE)
    count = pos_all.shape[0]
    scores = jnp.einsum("tgjd,sgd->gjts", query, key, preferred_element_type=jnp.float32)
    capped = SOFT_CAP * jnp.tanh(scores / SOFT_CAP)
    weights = jnp.where(pos_own[:, None] >= pos_all[None, :], jnp.exp(capped), 0.0)
    weights_b = bf(weights)
    total = jnp.sum(weights, axis=-1)
    attn = jnp.einsum("gjts,sgd->gjtd", weights_b, value, preferred_element_type=jnp.float32)
    attn = attn / total[..., None]
    attn_b = bf(jnp.transpose(attn, (2, 0, 1, 3)).reshape(tok, q_width))
    mixed = mm(attn_b, out_full)

    def backward(grad_mixed_b):
        grad_attn = mm_nt(grad_mixed_b, out_full).reshape(tok, KV_HEADS, groups, HEAD_DIM)
        grad_heads = jnp.transpose(grad_attn, (1, 2, 0, 3))
        rho = bf(grad_heads / total[..., None])
        delta = jnp.sum(grad_heads * attn, axis=-1) / total
        pulled = jnp.einsum("gjtd,sgd->gjts", rho, value, preferred_element_type=jnp.float32)
        grad_scores = bf(
            (pulled - delta[..., None]) * weights * (1.0 - (capped / SOFT_CAP) ** 2)
        )
        grad_query = jnp.einsum(
            "gjts,sgd->tgjd", grad_scores, key, preferred_element_type=jnp.float32
        ).reshape(tok, HEADS, HEAD_DIM)
        grad_key = jnp.einsum(
            "gjts,tgjd->sgd", grad_scores, query, preferred_element_type=jnp.float32
        ).reshape(count, k_width)
        grad_value = jnp.einsum(
            "gjts,gjtd->sgd", weights_b, rho, preferred_element_type=jnp.float32
        ).reshape(count, k_width)
        grad_kv = scatter_sum(jnp.concatenate([grad_key, grad_value], axis=1), PLANE)
        grad_query = unrotary(grad_query * HEAD_DIM ** (-0.5), cosine, sine)
        grad_key = unrotary(grad_kv[:, :k_width].reshape(tok, KV_HEADS, HEAD_DIM), cosine, sine)
        grad_qkv = bf(
            jnp.concatenate(
                [
                    grad_query.reshape(tok, q_width),
                    grad_key.reshape(tok, k_width),
                    grad_kv[:, k_width:],
                ],
                axis=1,
            )
        )
        grad_normed = mm_nt(grad_qkv, qkv_full)
        grad_qkv_w = f32(scatter_sum(bf(mm_tn(normed, grad_qkv)), ALL))
        grad_out_w = f32(scatter_sum(bf(mm_tn(attn_b, grad_mixed_b)), ALL))
        return grad_normed, grad_qkv_w, grad_out_w

    return mixed, gain_vals, backward


def wide_shards(
    hidden_in,
    positions,
    cotangent,
    w_qkv,
    w_out,
    w_gate_up,
    w_down,
    gains,
    m_qkv,
    v_qkv,
    m_out,
    v_out,
    m_gate_up,
    v_gate_up,
    m_down,
    v_down,
    m_gains,
    v_gains,
):
    x_own = hidden_in[0]
    rows, width = (w_qkv.shape[0], x_own.shape[1])
    group, across = (lax.axis_size(GROUP), lax.axis_size(ACROSS))
    ff_piece = w_down.shape[0]
    ff_own = across * ff_piece
    gu_pieces = w_gate_up.reshape(rows, 2, across, group, ff_piece)
    gu_pieces = jnp.transpose(gu_pieces, (3, 0, 1, 2, 4)).reshape(group * rows, 2 * ff_own)

    mixed, gain_vals, attention_back = token_attention(x_own, positions[0], w_qkv, w_out, gains)
    gu_own = gather(swap(gu_pieces, GROUP), ACROSS)
    down_own = gather(w_down, ACROSS)

    x_rows = f32(x_own)
    branch_one, pull_one = jax.vjp(rms_scale, mixed, gain_vals[1])
    resid = x_rows + branch_one
    normed_two, pull_two = jax.vjp(rms_scale, resid, gain_vals[2])
    tokens_b = gather(bf(normed_two), GROUP)
    gate_up = mm(tokens_b, gu_own)
    inner, pull_gelu = jax.vjp(
        lambda gate, up_part: jax.nn.gelu(gate, approximate=True) * up_part,
        gate_up[:, :ff_own],
        gate_up[:, ff_own:],
    )
    inner_b = bf(inner)
    down = f32(scatter_sum(bf(mm(inner_b, down_own)), GROUP))
    branch_two, pull_three = jax.vjp(rms_scale, down, gain_vals[3])
    block_out = bf(resid + branch_two)[None]
    grad_top = f32(cotangent[0])
    grad_down_in, gain_grad_three = pull_three(grad_top)
    grad_down_b = gather(bf(grad_down_in), GROUP)
    grad_gate, grad_up = pull_gelu(mm_nt(grad_down_b, down_own))
    grad_gu_b = bf(jnp.concatenate([grad_gate, grad_up], axis=1))
    grad_normed_two = f32(scatter_sum(bf(mm_nt(grad_gu_b, gu_own)), GROUP))
    grad_gate_up_w = scatter_sum(bf(mm_tn(tokens_b, grad_gu_b)), ACROSS)
    grad_down_w = f32(scatter_sum(bf(mm_tn(inner_b, grad_down_b)), ACROSS))

    grad_resid_two, gain_grad_two = pull_two(grad_normed_two)
    grad_resid = grad_top + grad_resid_two
    grad_mixed, gain_grad_one = pull_one(grad_resid)
    grad_normed, grad_qkv_w, grad_out_w = attention_back(bf(grad_mixed))
    _, pull_zero = jax.vjp(rms_scale, x_rows, gain_vals[0])
    grad_x_zero, gain_grad_zero = pull_zero(grad_normed)
    input_grad = (grad_resid + grad_x_zero)[None]

    grad_gate_up_w = swap(grad_gate_up_w, GROUP).reshape(group, rows, 2, across, ff_piece)
    grad_gate_up_w = f32(jnp.transpose(grad_gate_up_w, (1, 2, 3, 0, 4)).reshape(rows, -1))
    gain_term = jnp.stack([gain_grad_zero, gain_grad_one, gain_grad_two, gain_grad_three], axis=0)
    grad_gains = lax.psum_scatter(gain_term, ALL, scatter_dimension=1, tiled=True)

    return (
        (block_out, input_grad)
        + adam_step(f32(w_qkv), grad_qkv_w, m_qkv, v_qkv, MATRIX_RATE, WEIGHT_DECAY)
        + adam_step(f32(w_out), grad_out_w, m_out, v_out, MATRIX_RATE, WEIGHT_DECAY)
        + adam_step(f32(w_gate_up), grad_gate_up_w, m_gate_up, v_gate_up, MATRIX_RATE, WEIGHT_DECAY)
        + adam_step(f32(w_down), grad_down_w, m_down, v_down, MATRIX_RATE, WEIGHT_DECAY)
        + adam_step(f32(gains), grad_gains, m_gains, v_gains, GAIN_RATE, 0.0)
    )


def solution(mesh):
    sizes = dict(mesh.shape)
    fine = Mesh(
        mesh.devices.reshape(sizes["dp"] // 2, 2, sizes["ctx"], sizes["fsdp"] // 2, 2),
        ("dh", "dl", "ctx", "fy", "core"),
    )
    acts = P(DP, PLANE, None)
    mats = P(ALL, None)
    vecs = P(None, ALL)
    ladder = sizes["dp"] == 4 and sizes["ctx"] == 2 and sizes["fsdp"] == 4
    return jax.shard_map(
        ladder_shards if ladder else wide_shards,
        mesh=fine,
        in_specs=(acts, P(DP, PLANE), acts) + (mats,) * 4 + (vecs,) + (mats,) * 8 + (vecs,) * 2,
        out_specs=(acts, acts) + (mats,) * 12 + (vecs,) * 3,
        check_vma=False,
    )
```

```python
import jax
import jax.numpy as jnp
from jax import lax
from jax.sharding import Mesh, PartitionSpec as P

HEADS = 8
KV_HEADS = 4
HEAD_DIM = 256
STEP = 10

NORM_EPS = 1e-06
SOFT_CAP = 50.0
THETA = 10000.0
BETA_ONE = 0.9
BETA_TWO = 0.95
ADAM_EPS = 1e-08
MATRIX_RATE = 0.03
GAIN_RATE = 0.2
WEIGHT_DECAY = 0.1

DP = ("dh", "dl")
PLANE = ("ctx", "fy", "core")
ALL = DP + PLANE
LADDER = DP + ("ctx",)
GROUP = PLANE
ACROSS = DP


def f32(v):
    return v.astype(jnp.float32)


def bf(v):
    return v.astype(jnp.bfloat16)


def dot(left, right, dims):
    return lax.dot_general(left, right, (dims, ((), ())), preferred_element_type=jnp.float32)


def mm(left, right):
    return dot(left, right, ((1,), (0,)))


def mm_nt(left, right):
    return dot(left, right, ((1,), (1,)))


def mm_tn(left, right):
    return dot(left, right, ((0,), (0,)))


def rms_scale(values, gain):
    inverse = lax.rsqrt(jnp.mean(values * values, axis=-1, keepdims=True) + NORM_EPS)
    return values * inverse * (1.0 + gain)


def rotary_tables(places):
    half = HEAD_DIM // 2
    freqs = THETA ** (-(jnp.arange(half, dtype=jnp.float32) * 2.0 / HEAD_DIM))
    angles = f32(places)[:, None] * freqs[None, :]
    return (jnp.cos(angles), jnp.sin(angles))


def rotary(values, cosine, sine):
    half = HEAD_DIM // 2
    first = values[..., :half]
    second = values[..., half:]
    return jnp.concatenate(
        [first * cosine - second * sine, second * cosine + first * sine], axis=-1
    )


def unrotary(values, cosine, sine):
    return rotary(values, cosine, -sine)


def adam_step(weight, grad, first, second, rate, decay):
    first_new = BETA_ONE * first + (1.0 - BETA_ONE) * grad
    second_new = BETA_TWO * second + (1.0 - BETA_TWO) * grad * grad
    ratio = (
        first_new
        / (1.0 - BETA_ONE**STEP)
        / (jnp.sqrt(second_new / (1.0 - BETA_TWO**STEP)) + ADAM_EPS)
    )
    return (weight - rate * (ratio + decay * weight), first_new, second_new)


def gather(v, axes, axis=0):
    return lax.all_gather(v, axes, axis=axis, tiled=True)


def scatter_sum(v, axes):
    return lax.psum_scatter(v, axes, scatter_dimension=0, tiled=True)


def swap(v, axes):
    return lax.all_to_all(v, axes, split_axis=0, concat_axis=0, tiled=True)


def hold(v):
    return lax.optimization_barrier(v)


def flip(v, axis):
    return lax.ppermute(v, axis, [(0, 1), (1, 0)])


def plane_gather(own):
    me = lax.axis_index(PLANE)
    over_y = flip(own, "fy")
    over_x = flip(own, "ctx")
    blocks = [own, over_y, over_x, flip(over_y, "ctx")]
    whole = jnp.zeros((8,) + own.shape, own.dtype)
    for bits, block in enumerate(blocks):
        whole = lax.dynamic_update_index_in_dim(whole, block, me ^ (2 * bits), 0)
        whole = lax.dynamic_update_index_in_dim(whole, flip(block, "core"), me ^ (2 * bits + 1), 0)
    return whole.reshape((-1,) + own.shape[1:])


def plane_scatter(parts):
    size = parts.shape[0] // 8
    half = size // 2
    col, row, core = (lax.axis_index(axis) for axis in PLANE)
    parts = parts.reshape((4, 2, size) + parts.shape[1:])
    sent = lax.dynamic_index_in_dim(parts, 1 - core, 1, keepdims=False)
    kept = lax.dynamic_index_in_dim(parts, core, 1, keepdims=False)
    both = bf(f32(kept) + f32(flip(sent, "core")))
    own, over_y, over_x, corner = (
        lax.dynamic_index_in_dim(both, (2 * col + row) ^ bits, 0, keepdims=False) for bits in range(4)
    )
    got_y = flip(corner[:half], "ctx")
    got_x = flip(corner[half:], "fy")
    over_y = jnp.concatenate([bf(f32(over_y[:half]) + f32(got_y)), over_y[half:]], axis=0)
    over_x = jnp.concatenate([over_x[:half], bf(f32(over_x[half:]) + f32(got_x))], axis=0)
    return f32(own) + f32(flip(over_x, "ctx")) + f32(flip(over_y, "fy"))


def ring_pairs():
    count = lax.axis_size(DP)
    ring = [2 * z for z in range(count)] + [2 * z + 1 for z in reversed(range(count))]
    onward = [(ring[i], ring[(i + 1) % len(ring)]) for i in range(len(ring))]
    return onward, [(b, a) for a, b in onward]


def ring_gather(own):
    onward, back = ring_pairs()
    half = own.shape[0] // 2
    steps = [[own]]
    behind, ahead = (own, own)
    for _ in range(len(onward) // 2 - 1):
        behind = lax.ppermute(behind, LADDER, onward)
        ahead = lax.ppermute(ahead, LADDER, back)
        steps.append([behind, ahead])
    steps.append(
        [
            lax.ppermute(behind[:half], LADDER, onward),
            lax.ppermute(ahead[half:], LADDER, back),
        ]
    )
    return steps


def two_parts(steps):
    return [
        jnp.concatenate(sum(steps[:3], []), axis=0),
        jnp.concatenate(sum(steps[3:], []), axis=0),
    ]


def steps_of(parts, size):
    early, late = parts
    steps = [early[:size], early[size : 3 * size], early[3 * size :]]
    return steps + [late[: 2 * size], late[2 * size :]]


def ring_scatter(pieces):
    onward, back = ring_pairs()
    size = pieces[0].shape[0]
    half = size // 2
    ahead = lax.ppermute(pieces[-1][:half], LADDER, onward)
    behind = lax.ppermute(pieces[-1][half:], LADDER, back)
    for step in range(len(pieces) - 2, 0, -1):
        to_behind, to_ahead = (pieces[step][:size], pieces[step][size:])
        if step == len(pieces) - 2:
            to_ahead = jnp.concatenate(
                [bf(f32(to_ahead[:half]) + f32(ahead)), to_ahead[half:]], axis=0
            )
            to_behind = jnp.concatenate(
                [to_behind[:half], bf(f32(to_behind[half:]) + f32(behind))], axis=0
            )
        else:
            to_ahead = bf(f32(to_ahead) + f32(ahead))
            to_behind = bf(f32(to_behind) + f32(behind))
        to_ahead, to_behind = hold((to_ahead, to_behind))
        ahead = lax.ppermute(to_ahead, LADDER, onward)
        behind = lax.ppermute(to_behind, LADDER, back)
    return f32(pieces[0]) + f32(ahead) + f32(behind)


def quad_blocks(own, late=None):
    over_y = flip(own, "fy")
    if late is not None:
        over_y, _ = hold((over_y, late))
    return [own, flip(own, "core"), over_y, flip(over_y, "core")]


def quad_place(blocks, parts):
    me = lax.axis_index(("fy", "core"))
    count, rows, cols = blocks[0][0].shape
    whole = jnp.zeros((count, 4, rows, parts * cols), blocks[0][0].dtype)
    for part in range(parts):
        for bits, block in enumerate(blocks[part]):
            whole = lax.dynamic_update_slice(
                whole, block[:, None], (0, me ^ bits, 0, part * cols)
            )
    return whole


def core_sum(parts, late):
    core = lax.axis_index("core")
    parts = parts.reshape(parts.shape[:1] + (2, 2) + parts.shape[2:])
    sent = lax.dynamic_index_in_dim(parts, 1 - core, 2, keepdims=False)
    kept = lax.dynamic_index_in_dim(parts, core, 2, keepdims=False)
    kept, got, _ = hold((kept, flip(sent, "core"), late))
    return bf(f32(kept) + f32(got))


def row_sum(both):
    row = lax.axis_index("fy")
    sent = lax.dynamic_index_in_dim(both, 1 - row, 1, keepdims=False)
    kept = lax.dynamic_index_in_dim(both, row, 1, keepdims=False)
    return bf(f32(kept) + f32(flip(sent, "fy")))


def ladder_shards(
    hidden_in,
    positions,
    cotangent,
    w_qkv,
    w_out,
    w_gate_up,
    w_down,
    gains,
    m_qkv,
    v_qkv,
    m_out,
    v_out,
    m_gate_up,
    v_gate_up,
    m_down,
    v_down,
    m_gains,
    v_gains,
):
    x_own = hidden_in[0]
    tok, width = x_own.shape
    rows = w_qkv.shape[0]
    planes = lax.axis_size(DP)
    group = lax.axis_size(LADDER)
    q_width = HEADS * HEAD_DIM
    core = lax.axis_index("core")

    q_cols = w_qkv[:, :q_width].reshape(rows, HEADS, HEAD_DIM)
    kv_cols = w_qkv[:, q_width:].reshape(rows, 2, KV_HEADS, HEAD_DIM)
    kv_cols = jnp.swapaxes(kv_cols, 1, 2).reshape(rows, HEADS, HEAD_DIM)
    pieces = jnp.swapaxes(jnp.concatenate([q_cols, kv_cols], axis=2), 0, 1)
    first = jnp.stack([positions[0, 0] // 128, positions[0, 0] % 128])
    own_gains = jnp.concatenate([gains.reshape(4 * rows), bf(first)])[None, None]
    own_gains = jnp.pad(own_gains, ((0, 0), (0, 7), (0, 2 * HEAD_DIM - 4 * rows - 2)))
    pieces = jnp.concatenate(
        [pieces, jnp.broadcast_to(own_gains, (HEADS,) + own_gains.shape[1:])], axis=1
    )
    got = swap(pieces, PLANE)
    out_line = lax.all_gather(w_out, DP)
    got, x_sent = hold((got, x_own))
    x_all = plane_gather(x_sent)
    first = got[:, rows, 4 * rows : 4 * rows + 2].astype(jnp.int32)
    pos_all = first[:, :1] * 128 + first[:, 1:] + jnp.arange(tok, dtype=jnp.int32)[None]
    pos_all = pos_all.reshape(-1)
    cosine, sine = rotary_tables(pos_all)
    got = lax.all_gather(got, DP)
    ff_own = w_down.shape[0] * 4
    cols = []
    for part in range(2):
        piece = w_gate_up[:, part * group * ff_own : (part + 1) * group * ff_own]
        cols.append(jnp.swapaxes(piece.reshape(rows, group, ff_own), 0, 1))
    got, out_line, cols[0], w_down_late = hold((got, out_line, cols[0], w_down))
    w_own = got[:, :, :rows].reshape(width, 2 * HEAD_DIM)
    gain_vals = got[:, :, rows, : 4 * rows].reshape(planes * HEADS, 4, rows)
    gain_vals = f32(jnp.swapaxes(gain_vals, 0, 1).reshape(4, width))
    out_full = lax.all_gather(out_line, PLANE, axis=1, tiled=False).reshape(q_width, width)
    cols[0] = swap(cols[0], LADDER)

    normed_all = hold(bf(rms_scale(f32(x_all), gain_vals[0])))
    qkv = mm(normed_all, w_own)
    query = bf(rotary(qkv[:, :HEAD_DIM], cosine, sine) * HEAD_DIM ** (-0.5))
    half = qkv[:, HEAD_DIM:]
    mine = jnp.where(core == 0, bf(rotary(half, cosine, sine)), bf(half))
    other = flip(mine, "core")
    key = jnp.where(core == 0, mine, other)
    value = jnp.where(core == 0, other, mine)
    scores = mm_nt(query, key)
    capped = SOFT_CAP * jnp.tanh(scores / SOFT_CAP)
    weights = jnp.where(pos_all[:, None] >= pos_all[None, :], jnp.exp(capped), 0.0)
    weights_b = bf(weights)
    total = jnp.sum(weights, axis=-1, keepdims=True)
    attn = mm(weights_b, value) / total
    cols[0], attn_sent = hold((cols[0], bf(attn)))
    attn_own = swap(attn_sent.reshape(HEADS, tok, HEAD_DIM), PLANE)
    cols[0], cols[1], _ = hold((cols[0], cols[1], attn_own))
    cols[1] = swap(cols[1], LADDER)
    attn_own = jnp.swapaxes(attn_own, 0, 1).reshape(tok, q_width)
    mixed = mm(attn_own, out_full)

    x_rows = f32(x_own)
    branch_one, pull_one = jax.vjp(rms_scale, mixed, gain_vals[1])
    resid = x_rows + branch_one
    normed_two, pull_two = jax.vjp(rms_scale, resid, gain_vals[2])

    tokens_own = bf(normed_two)
    steps = ring_gather(tokens_own)
    cols[1], _ = hold((cols[1], tokens_own))
    down_own = quad_place([quad_blocks(w_down_late[None], tokens_own)], 1).reshape(ff_own, width)
    gate_up_own = [quad_blocks(cols[0], tokens_own), quad_blocks(cols[1])]
    gate_up_own = quad_place(gate_up_own, 2).reshape(width, 2 * ff_own)
    tokens = jnp.concatenate(sum(steps, []), axis=0)
    gate_up = mm(tokens, gate_up_own)

    def gated(gate, up_part):
        return jax.nn.gelu(gate, approximate=True) * up_part

    inner = bf(gated(gate_up[:, :ff_own], gate_up[:, ff_own:]))
    late = tokens.shape[0] - 3 * tok
    down = bf(mm(inner, down_own))
    attn_cols = attn_own.reshape(tok, planes, HEADS, w_out.shape[0])
    attn_cols = jnp.transpose(attn_cols, (2, 0, 1, 3)).reshape(HEADS, tok, HEAD_DIM)
    attn_cols, down = hold((attn_cols, down))
    attn_cols = swap(attn_cols, PLANE).reshape(HEADS * tok, HEAD_DIM)
    down = ring_scatter(steps_of((down[:late], down[late:]), tok))
    down, attn_cols = hold((down, attn_cols))
    branch_two, pull_three = jax.vjp(rms_scale, down, gain_vals[3])
    block_out = bf(resid + branch_two)[None]
    grad_top = f32(cotangent[0])
    grad_down_in, gain_grad_three = pull_three(grad_top)
    steps = ring_gather(bf(grad_down_in))
    grad_downs = two_parts(steps)
    grad_gus, parts = ([], [])
    for piece, kept in zip(grad_downs, (gate_up[:late], gate_up[late:])):
        _, pull = jax.vjp(gated, kept[:, :ff_own], kept[:, ff_own:])
        grad_gus.append(bf(jnp.concatenate(pull(mm_nt(piece, down_own)), axis=1)))
        grad_gu, _ = hold((grad_gus[-1], steps[3][0]))
        parts.append(bf(mm_nt(grad_gu, gate_up_own)))
    tokens, inner, grad_downs, grad_gus, parts = hold(
        (tokens, inner, grad_downs, grad_gus, parts)
    )
    grad_normed_two = ring_scatter(steps_of(parts, tok))
    grad_gu_b = jnp.concatenate(grad_gus, axis=0)
    grad_halves = [bf(mm_tn(tokens, grad_gu_b[:, :ff_own])), bf(mm_tn(tokens, grad_gu_b[:, ff_own:]))]
    grad_down_w = bf(mm_tn(inner, jnp.concatenate(grad_downs, axis=0)))
    grad_normed_two, _, _ = hold((grad_normed_two, grad_halves, grad_down_w))
    grad_resid_two, _ = pull_two(grad_normed_two)
    grad_resid = grad_top + grad_resid_two
    grad_mixed, gain_grad_one = pull_one(grad_resid)
    grad_mixed_b = bf(grad_mixed)

    grad_attn = bf(mm_nt(grad_mixed_b, out_full)).reshape(tok, HEADS, HEAD_DIM)
    grad_head = swap(jnp.swapaxes(grad_attn, 0, 1), PLANE).reshape(HEADS * tok, HEAD_DIM)
    grad_head = f32(grad_head)
    rho = bf(grad_head / total)
    delta = jnp.sum(grad_head * attn, axis=-1, keepdims=True) / total
    pulled = mm_nt(rho, value)
    grad_scores = bf((pulled - delta) * weights * (1.0 - (capped / SOFT_CAP) ** 2))
    grad_query = mm(grad_scores, key) * HEAD_DIM ** (-0.5)
    grad_key = mm_tn(grad_scores, query)
    grad_value = mm_tn(weights_b, rho)
    sent = jnp.where(core == 0, grad_value, grad_key)
    grad_half = jnp.where(core == 0, grad_key, grad_value) + flip(sent, "core")
    grad_half = jnp.where(core == 0, unrotary(grad_half, cosine, sine), grad_half)
    grad_qkv = bf(jnp.concatenate([unrotary(grad_query, cosine, sine), grad_half], axis=1))
    others = bf(jnp.stack([gain_grad_one, gain_grad_three]))
    others = jnp.concatenate([grad_mixed_b, jnp.pad(others, ((0, 14), (0, 0)))], axis=0)
    others = lax.all_gather(others, PLANE)
    grad_qkv, others = hold((grad_qkv, others))
    grad_mixed_all = others[:, :tok].reshape(HEADS * tok, width)
    others = jnp.sum(f32(others[:, tok : tok + 2]), axis=0).reshape(2, planes, HEADS, rows)
    others = lax.dynamic_index_in_dim(others, lax.axis_index(PLANE), 2, keepdims=False)
    others = jnp.swapaxes(others, 0, 1).reshape(planes, 1, 2 * rows)
    others = bf(jnp.pad(others, ((0, 0), (0, 7), (0, 2 * HEAD_DIM - 2 * rows))))
    grad_w = bf(mm_tn(normed_all, grad_qkv))
    grad_qkv, grad_w = hold((grad_qkv, grad_w))
    sums = [core_sum(v.reshape(group, 4, rows, ff_own), grad_qkv) for v in grad_halves]
    sums.append(core_sum(grad_down_w.reshape(1, 4, ff_own // 4, width), grad_qkv))
    grad_halves = [row_sum(v) for v in sums[:2]]
    grad_down_w, grad_halves[1] = hold((sums[2], grad_halves[1]))
    grad_down_w = f32(row_sum(grad_down_w)[0])
    grad_w = grad_w.reshape(planes, -1, 2 * HEAD_DIM)
    grad_out_w = bf(mm_tn(attn_cols, grad_mixed_all)).reshape(planes, -1, 2 * HEAD_DIM)
    grad_w = jnp.concatenate([grad_w, grad_out_w, others], axis=1)
    grad_w, grad_qkv = hold((grad_w, grad_qkv))
    grad_normed = plane_scatter(bf(mm_nt(grad_qkv, w_own)))
    grad_w = scatter_sum(grad_w, DP)[0]
    others = f32(grad_w[-8, : 2 * rows]).reshape(2, rows)
    grad_out_w = f32(grad_w[HEADS * rows : -8].reshape(w_out.shape))
    grad_w = grad_w[: HEADS * rows].reshape(HEADS, rows, 2 * HEAD_DIM)
    grad_halves = [swap(v, LADDER) for v in grad_halves]
    grad_w, grad_halves[1], grad_normed = hold((grad_w, grad_halves[1], grad_normed))
    grad_halves = [jnp.swapaxes(v, 0, 1).reshape(rows, group * ff_own) for v in grad_halves]
    grad_gate_up_w = f32(jnp.concatenate(grad_halves, axis=1))
    _, pull_zero = jax.vjp(rms_scale, x_rows, gain_vals[0])
    grad_x_zero, _ = pull_zero(grad_normed)
    input_grad = (grad_resid + grad_x_zero)[None]
    grad_w = f32(jnp.swapaxes(swap(grad_w, PLANE), 0, 1))
    grad_q_w = grad_w[:, :, :HEAD_DIM].reshape(rows, q_width)
    grad_kv_w = grad_w[:, :, HEAD_DIM:].reshape(rows, KV_HEADS, 2, HEAD_DIM)
    grad_kv_w = jnp.swapaxes(grad_kv_w, 1, 2).reshape(rows, q_width)
    grad_qkv_w = jnp.concatenate([grad_q_w, grad_kv_w], axis=1)

    gain_zero = jnp.sum(f32(w_qkv) * grad_qkv_w, axis=1) / (1.0 + f32(gains[0]))
    gain_two = jnp.sum(f32(w_gate_up) * grad_gate_up_w, axis=1) / (1.0 + f32(gains[2]))
    grad_gains = jnp.stack([gain_zero, others[0], gain_two, others[1]], axis=0)

    return (
        (block_out, input_grad)
        + adam_step(f32(w_qkv), grad_qkv_w, m_qkv, v_qkv, MATRIX_RATE, WEIGHT_DECAY)
        + adam_step(f32(w_out), grad_out_w, m_out, v_out, MATRIX_RATE, WEIGHT_DECAY)
        + adam_step(f32(w_gate_up), grad_gate_up_w, m_gate_up, v_gate_up, MATRIX_RATE, WEIGHT_DECAY)
        + adam_step(f32(w_down), grad_down_w, m_down, v_down, MATRIX_RATE, WEIGHT_DECAY)
        + adam_step(f32(gains), grad_gains, m_gains, v_gains, GAIN_RATE, 0.0)
    )


def token_attention(x_own, pos_own, w_qkv, w_out, gains):
    tok = x_own.shape[0]
    q_width = HEADS * HEAD_DIM
    k_width = KV_HEADS * HEAD_DIM
    groups = HEADS // KV_HEADS
    qkv_full = gather(w_qkv, ALL)
    out_full = gather(w_out, ALL)
    gain_vals = f32(gather(gains, ALL, 1))
    normed = bf(rms_scale(f32(x_own), gain_vals[0]))
    qkv = mm(normed, qkv_full)
    cosine, sine = rotary_tables(pos_own)
    cosine, sine = (cosine[:, None, :], sine[:, None, :])
    query = rotary(qkv[:, :q_width].reshape(tok, HEADS, HEAD_DIM), cosine, sine)
    query = bf(query * HEAD_DIM ** (-0.5)).reshape(tok, KV_HEADS, groups, HEAD_DIM)
    key_own = qkv[:, q_width : q_width + k_width].reshape(tok, KV_HEADS, HEAD_DIM)
    key = gather(bf(rotary(key_own, cosine, sine)), PLANE)
    value = gather(bf(qkv[:, q_width + k_width :]).reshape(tok, KV_HEADS, HEAD_DIM), PLANE)
    pos_all = gather(pos_own, PLANE)
    count = pos_all.shape[0]
    scores = jnp.einsum("tgjd,sgd->gjts", query, key, preferred_element_type=jnp.float32)
    capped = SOFT_CAP * jnp.tanh(scores / SOFT_CAP)
    weights = jnp.where(pos_own[:, None] >= pos_all[None, :], jnp.exp(capped), 0.0)
    weights_b = bf(weights)
    total = jnp.sum(weights, axis=-1)
    attn = jnp.einsum("gjts,sgd->gjtd", weights_b, value, preferred_element_type=jnp.float32)
    attn = attn / total[..., None]
    attn_b = bf(jnp.transpose(attn, (2, 0, 1, 3)).reshape(tok, q_width))
    mixed = mm(attn_b, out_full)

    def backward(grad_mixed_b):
        grad_attn = mm_nt(grad_mixed_b, out_full).reshape(tok, KV_HEADS, groups, HEAD_DIM)
        grad_heads = jnp.transpose(grad_attn, (1, 2, 0, 3))
        rho = bf(grad_heads / total[..., None])
        delta = jnp.sum(grad_heads * attn, axis=-1) / total
        pulled = jnp.einsum("gjtd,sgd->gjts", rho, value, preferred_element_type=jnp.float32)
        grad_scores = bf(
            (pulled - delta[..., None]) * weights * (1.0 - (capped / SOFT_CAP) ** 2)
        )
        grad_query = jnp.einsum(
            "gjts,sgd->tgjd", grad_scores, key, preferred_element_type=jnp.float32
        ).reshape(tok, HEADS, HEAD_DIM)
        grad_key = jnp.einsum(
            "gjts,tgjd->sgd", grad_scores, query, preferred_element_type=jnp.float32
        ).reshape(count, k_width)
        grad_value = jnp.einsum(
            "gjts,gjtd->sgd", weights_b, rho, preferred_element_type=jnp.float32
        ).reshape(count, k_width)
        grad_kv = scatter_sum(jnp.concatenate([grad_key, grad_value], axis=1), PLANE)
        grad_query = unrotary(grad_query * HEAD_DIM ** (-0.5), cosine, sine)
        grad_key = unrotary(grad_kv[:, :k_width].reshape(tok, KV_HEADS, HEAD_DIM), cosine, sine)
        grad_qkv = bf(
            jnp.concatenate(
                [
                    grad_query.reshape(tok, q_width),
                    grad_key.reshape(tok, k_width),
                    grad_kv[:, k_width:],
                ],
                axis=1,
            )
        )
        grad_normed = mm_nt(grad_qkv, qkv_full)
        grad_qkv_w = f32(scatter_sum(bf(mm_tn(normed, grad_qkv)), ALL))
        grad_out_w = f32(scatter_sum(bf(mm_tn(attn_b, grad_mixed_b)), ALL))
        return grad_normed, grad_qkv_w, grad_out_w

    return mixed, gain_vals, backward


def wide_shards(
    hidden_in,
    positions,
    cotangent,
    w_qkv,
    w_out,
    w_gate_up,
    w_down,
    gains,
    m_qkv,
    v_qkv,
    m_out,
    v_out,
    m_gate_up,
    v_gate_up,
    m_down,
    v_down,
    m_gains,
    v_gains,
):
    x_own = hidden_in[0]
    rows, width = (w_qkv.shape[0], x_own.shape[1])
    group, across = (lax.axis_size(GROUP), lax.axis_size(ACROSS))
    ff_piece = w_down.shape[0]
    ff_own = across * ff_piece
    gu_pieces = w_gate_up.reshape(rows, 2, across, group, ff_piece)
    gu_pieces = jnp.transpose(gu_pieces, (3, 0, 1, 2, 4)).reshape(group * rows, 2 * ff_own)

    mixed, gain_vals, attention_back = token_attention(x_own, positions[0], w_qkv, w_out, gains)
    gu_own = gather(swap(gu_pieces, GROUP), ACROSS)
    down_own = gather(w_down, ACROSS)

    x_rows = f32(x_own)
    branch_one, pull_one = jax.vjp(rms_scale, mixed, gain_vals[1])
    resid = x_rows + branch_one
    normed_two, pull_two = jax.vjp(rms_scale, resid, gain_vals[2])
    tokens_b = gather(bf(normed_two), GROUP)
    gate_up = mm(tokens_b, gu_own)
    inner, pull_gelu = jax.vjp(
        lambda gate, up_part: jax.nn.gelu(gate, approximate=True) * up_part,
        gate_up[:, :ff_own],
        gate_up[:, ff_own:],
    )
    inner_b = bf(inner)
    down = f32(scatter_sum(bf(mm(inner_b, down_own)), GROUP))
    branch_two, pull_three = jax.vjp(rms_scale, down, gain_vals[3])
    block_out = bf(resid + branch_two)[None]
    grad_top = f32(cotangent[0])
    grad_down_in, gain_grad_three = pull_three(grad_top)
    grad_down_b = gather(bf(grad_down_in), GROUP)
    grad_gate, grad_up = pull_gelu(mm_nt(grad_down_b, down_own))
    grad_gu_b = bf(jnp.concatenate([grad_gate, grad_up], axis=1))
    grad_normed_two = f32(scatter_sum(bf(mm_nt(grad_gu_b, gu_own)), GROUP))
    grad_gate_up_w = scatter_sum(bf(mm_tn(tokens_b, grad_gu_b)), ACROSS)
    grad_down_w = f32(scatter_sum(bf(mm_tn(inner_b, grad_down_b)), ACROSS))

    grad_resid_two, gain_grad_two = pull_two(grad_normed_two)
    grad_resid = grad_top + grad_resid_two
    grad_mixed, gain_grad_one = pull_one(grad_resid)
    grad_normed, grad_qkv_w, grad_out_w = attention_back(bf(grad_mixed))
    _, pull_zero = jax.vjp(rms_scale, x_rows, gain_vals[0])
    grad_x_zero, gain_grad_zero = pull_zero(grad_normed)
    input_grad = (grad_resid + grad_x_zero)[None]

    grad_gate_up_w = swap(grad_gate_up_w, GROUP).reshape(group, rows, 2, across, ff_piece)
    grad_gate_up_w = f32(jnp.transpose(grad_gate_up_w, (1, 2, 3, 0, 4)).reshape(rows, -1))
    gain_term = jnp.stack([gain_grad_zero, gain_grad_one, gain_grad_two, gain_grad_three], axis=0)
    grad_gains = lax.psum_scatter(gain_term, ALL, scatter_dimension=1, tiled=True)

    return (
        (block_out, input_grad)
        + adam_step(f32(w_qkv), grad_qkv_w, m_qkv, v_qkv, MATRIX_RATE, WEIGHT_DECAY)
        + adam_step(f32(w_out), grad_out_w, m_out, v_out, MATRIX_RATE, WEIGHT_DECAY)
        + adam_step(f32(w_gate_up), grad_gate_up_w, m_gate_up, v_gate_up, MATRIX_RATE, WEIGHT_DECAY)
        + adam_step(f32(w_down), grad_down_w, m_down, v_down, MATRIX_RATE, WEIGHT_DECAY)
        + adam_step(f32(gains), grad_gains, m_gains, v_gains, GAIN_RATE, 0.0)
    )


def solution(mesh):
    sizes = dict(mesh.shape)
    fine = Mesh(
        mesh.devices.reshape(sizes["dp"] // 2, 2, sizes["ctx"], sizes["fsdp"] // 2, 2),
        ("dh", "dl", "ctx", "fy", "core"),
    )
    acts = P(DP, PLANE, None)
    mats = P(ALL, None)
    vecs = P(None, ALL)
    ladder = sizes["dp"] == 4 and sizes["ctx"] == 2 and sizes["fsdp"] == 4
    return jax.shard_map(
        ladder_shards if ladder else wide_shards,
        mesh=fine,
        in_specs=(acts, P(DP, PLANE), acts) + (mats,) * 4 + (vecs,) + (mats,) * 8 + (vecs,) * 2,
        out_specs=(acts, acts) + (mats,) * 12 + (vecs,) * 3,
        check_vma=False,
    )
```

```python
import jax
import jax.numpy as jnp
from jax import lax
from jax.sharding import Mesh, PartitionSpec as P

HEADS = 8
KV_HEADS = 4
HEAD_DIM = 256
STEP = 10

NORM_EPS = 1e-06
SOFT_CAP = 50.0
THETA = 10000.0
BETA_ONE = 0.9
BETA_TWO = 0.95
ADAM_EPS = 1e-08
MATRIX_RATE = 0.03
GAIN_RATE = 0.2
WEIGHT_DECAY = 0.1

DP = ("dh", "dl")
PLANE = ("ctx", "fy", "core")
ALL = DP + PLANE
LADDER = DP + ("ctx",)
GROUP = PLANE
ACROSS = DP


def f32(v):
    return v.astype(jnp.float32)


def bf(v):
    return v.astype(jnp.bfloat16)


def dot(left, right, dims):
    return lax.dot_general(left, right, (dims, ((), ())), preferred_element_type=jnp.float32)


def mm(left, right):
    return dot(left, right, ((1,), (0,)))


def mm_nt(left, right):
    return dot(left, right, ((1,), (1,)))


def mm_tn(left, right):
    return dot(left, right, ((0,), (0,)))


def rms_scale(values, gain):
    inverse = lax.rsqrt(jnp.mean(values * values, axis=-1, keepdims=True) + NORM_EPS)
    return values * inverse * (1.0 + gain)


def rotary_tables(places):
    half = HEAD_DIM // 2
    freqs = THETA ** (-(jnp.arange(half, dtype=jnp.float32) * 2.0 / HEAD_DIM))
    angles = f32(places)[:, None] * freqs[None, :]
    return (jnp.cos(angles), jnp.sin(angles))


def rotary(values, cosine, sine):
    half = HEAD_DIM // 2
    first = values[..., :half]
    second = values[..., half:]
    return jnp.concatenate(
        [first * cosine - second * sine, second * cosine + first * sine], axis=-1
    )


def unrotary(values, cosine, sine):
    return rotary(values, cosine, -sine)


def adam_step(weight, grad, first, second, rate, decay):
    first_new = BETA_ONE * first + (1.0 - BETA_ONE) * grad
    second_new = BETA_TWO * second + (1.0 - BETA_TWO) * grad * grad
    ratio = (
        first_new
        / (1.0 - BETA_ONE**STEP)
        / (jnp.sqrt(second_new / (1.0 - BETA_TWO**STEP)) + ADAM_EPS)
    )
    return (weight - rate * (ratio + decay * weight), first_new, second_new)


def gather(v, axes, axis=0):
    return lax.all_gather(v, axes, axis=axis, tiled=True)


def scatter_sum(v, axes):
    return lax.psum_scatter(v, axes, scatter_dimension=0, tiled=True)


def swap(v, axes):
    return lax.all_to_all(v, axes, split_axis=0, concat_axis=0, tiled=True)


def hold(v):
    return lax.optimization_barrier(v)


def flip(v, axis):
    return lax.ppermute(v, axis, [(0, 1), (1, 0)])


def plane_gather(own):
    me = lax.axis_index(PLANE)
    over_y = flip(own, "fy")
    over_x = flip(own, "ctx")
    blocks = [own, over_y, over_x, flip(over_y, "ctx")]
    whole = jnp.zeros((8,) + own.shape, own.dtype)
    for bits, block in enumerate(blocks):
        whole = lax.dynamic_update_index_in_dim(whole, block, me ^ (2 * bits), 0)
        whole = lax.dynamic_update_index_in_dim(whole, flip(block, "core"), me ^ (2 * bits + 1), 0)
    return whole.reshape((-1,) + own.shape[1:])


def plane_scatter(parts):
    size = parts.shape[0] // 8
    half = size // 2
    col, row, core = (lax.axis_index(axis) for axis in PLANE)
    parts = parts.reshape((4, 2, size) + parts.shape[1:])
    sent = lax.dynamic_index_in_dim(parts, 1 - core, 1, keepdims=False)
    kept = lax.dynamic_index_in_dim(parts, core, 1, keepdims=False)
    both = bf(f32(kept) + f32(flip(sent, "core")))
    own, over_y, over_x, corner = (
        lax.dynamic_index_in_dim(both, (2 * col + row) ^ bits, 0, keepdims=False) for bits in range(4)
    )
    got_y = flip(corner[:half], "ctx")
    got_x = flip(corner[half:], "fy")
    over_y = jnp.concatenate([bf(f32(over_y[:half]) + f32(got_y)), over_y[half:]], axis=0)
    over_x = jnp.concatenate([over_x[:half], bf(f32(over_x[half:]) + f32(got_x))], axis=0)
    return f32(own) + f32(flip(over_x, "ctx")) + f32(flip(over_y, "fy"))


def ring_pairs():
    count = lax.axis_size(DP)
    ring = [2 * z for z in range(count)] + [2 * z + 1 for z in reversed(range(count))]
    onward = [(ring[i], ring[(i + 1) % len(ring)]) for i in range(len(ring))]
    return onward, [(b, a) for a, b in onward]


def ring_gather(own):
    onward, back = ring_pairs()
    half = own.shape[0] // 2
    steps = [[own]]
    behind, ahead = (own, own)
    for _ in range(len(onward) // 2 - 1):
        behind = lax.ppermute(behind, LADDER, onward)
        ahead = lax.ppermute(ahead, LADDER, back)
        steps.append([behind, ahead])
    steps.append(
        [
            lax.ppermute(behind[:half], LADDER, onward),
            lax.ppermute(ahead[half:], LADDER, back),
        ]
    )
    return steps


def two_parts(steps):
    return [
        jnp.concatenate(sum(steps[:3], []), axis=0),
        jnp.concatenate(sum(steps[3:], []), axis=0),
    ]


def steps_of(parts, size):
    early, late = parts
    steps = [early[:size], early[size : 3 * size], early[3 * size :]]
    return steps + [late[: 2 * size], late[2 * size :]]


def ring_scatter(pieces):
    onward, back = ring_pairs()
    size = pieces[0].shape[0]
    half = size // 2
    ahead = lax.ppermute(pieces[-1][:half], LADDER, onward)
    behind = lax.ppermute(pieces[-1][half:], LADDER, back)
    for step in range(len(pieces) - 2, 0, -1):
        to_behind, to_ahead = (pieces[step][:size], pieces[step][size:])
        if step == len(pieces) - 2:
            to_ahead = jnp.concatenate(
                [bf(f32(to_ahead[:half]) + f32(ahead)), to_ahead[half:]], axis=0
            )
            to_behind = jnp.concatenate(
                [to_behind[:half], bf(f32(to_behind[half:]) + f32(behind))], axis=0
            )
        else:
            to_ahead = bf(f32(to_ahead) + f32(ahead))
            to_behind = bf(f32(to_behind) + f32(behind))
        to_ahead, to_behind = hold((to_ahead, to_behind))
        ahead = lax.ppermute(to_ahead, LADDER, onward)
        behind = lax.ppermute(to_behind, LADDER, back)
    return f32(pieces[0]) + f32(ahead) + f32(behind)


def quad_blocks(own, late=None):
    over_y = flip(own, "fy")
    if late is not None:
        over_y, _ = hold((over_y, late))
    return [own, flip(own, "core"), over_y, flip(over_y, "core")]


def quad_place(blocks, parts):
    me = lax.axis_index(("fy", "core"))
    count, rows, cols = blocks[0][0].shape
    whole = jnp.zeros((count, 4, rows, parts * cols), blocks[0][0].dtype)
    for part in range(parts):
        for bits, block in enumerate(blocks[part]):
            whole = lax.dynamic_update_slice(
                whole, block[:, None], (0, me ^ bits, 0, part * cols)
            )
    return whole


def core_sum(parts, late):
    core = lax.axis_index("core")
    parts = parts.reshape(parts.shape[:1] + (2, 2) + parts.shape[2:])
    sent = lax.dynamic_index_in_dim(parts, 1 - core, 2, keepdims=False)
    kept = lax.dynamic_index_in_dim(parts, core, 2, keepdims=False)
    kept, got, _ = hold((kept, flip(sent, "core"), late))
    return bf(f32(kept) + f32(got))


def row_sum(both, late=()):
    row = lax.axis_index("fy")
    sent = lax.dynamic_index_in_dim(both, 1 - row, 1, keepdims=False)
    kept = lax.dynamic_index_in_dim(both, row, 1, keepdims=False)
    kept, got, _ = hold((kept, flip(sent, "fy"), late))
    return bf(f32(kept) + f32(got))


def ladder_shards(
    hidden_in,
    positions,
    cotangent,
    w_qkv,
    w_out,
    w_gate_up,
    w_down,
    gains,
    m_qkv,
    v_qkv,
    m_out,
    v_out,
    m_gate_up,
    v_gate_up,
    m_down,
    v_down,
    m_gains,
    v_gains,
):
    x_own = hidden_in[0]
    tok, width = x_own.shape
    rows = w_qkv.shape[0]
    planes = lax.axis_size(DP)
    group = lax.axis_size(LADDER)
    q_width = HEADS * HEAD_DIM
    core = lax.axis_index("core")

    q_cols = w_qkv[:, :q_width].reshape(rows, HEADS, HEAD_DIM)
    kv_cols = w_qkv[:, q_width:].reshape(rows, 2, KV_HEADS, HEAD_DIM)
    kv_cols = jnp.swapaxes(kv_cols, 1, 2).reshape(rows, HEADS, HEAD_DIM)
    pieces = jnp.swapaxes(jnp.concatenate([q_cols, kv_cols], axis=2), 0, 1)
    first = jnp.stack([positions[0, 0] // 128, positions[0, 0] % 128])
    own_gains = jnp.concatenate([gains.reshape(4 * rows), bf(first)])[None, None]
    own_gains = jnp.pad(own_gains, ((0, 0), (0, 7), (0, 2 * HEAD_DIM - 4 * rows - 2)))
    pieces = jnp.concatenate(
        [pieces, jnp.broadcast_to(own_gains, (HEADS,) + own_gains.shape[1:])], axis=1
    )
    got = swap(pieces, PLANE)
    out_line = lax.all_gather(w_out, DP)
    x_all = plane_gather(x_own)
    first = got[:, rows, 4 * rows : 4 * rows + 2].astype(jnp.int32)
    pos_all = first[:, :1] * 128 + first[:, 1:] + jnp.arange(tok, dtype=jnp.int32)[None]
    pos_all = pos_all.reshape(-1)
    cosine, sine = rotary_tables(pos_all)
    got = lax.all_gather(got, DP)
    ff_own = w_down.shape[0] * 4
    cols = []
    for part in range(2):
        piece = w_gate_up[:, part * group * ff_own : (part + 1) * group * ff_own]
        cols.append(jnp.swapaxes(piece.reshape(rows, group, ff_own), 0, 1))
    got, out_line, cols[0], w_down_late = hold((got, out_line, cols[0], w_down))
    w_own = got[:, :, :rows].reshape(width, 2 * HEAD_DIM)
    gain_vals = got[:, :, rows, : 4 * rows].reshape(planes * HEADS, 4, rows)
    gain_vals = f32(jnp.swapaxes(gain_vals, 0, 1).reshape(4, width))
    out_full = lax.all_gather(out_line, PLANE, axis=1, tiled=False).reshape(q_width, width)
    cols[0] = swap(cols[0], LADDER)

    normed_all = hold(bf(rms_scale(f32(x_all), gain_vals[0])))
    qkv = mm(normed_all, w_own)
    query = bf(rotary(qkv[:, :HEAD_DIM], cosine, sine) * HEAD_DIM ** (-0.5))
    half = qkv[:, HEAD_DIM:]
    mine = jnp.where(core == 0, bf(rotary(half, cosine, sine)), bf(half))
    other = flip(mine, "core")
    key = jnp.where(core == 0, mine, other)
    value = jnp.where(core == 0, other, mine)
    scores = mm_nt(query, key)
    capped = SOFT_CAP * jnp.tanh(scores / SOFT_CAP)
    weights = jnp.where(pos_all[:, None] >= pos_all[None, :], jnp.exp(capped), 0.0)
    weights_b = bf(weights)
    total = jnp.sum(weights, axis=-1, keepdims=True)
    attn = mm(weights_b, value) / total
    cols[0], attn_sent = hold((cols[0], bf(attn)))
    attn_own = swap(attn_sent.reshape(HEADS, tok, HEAD_DIM), PLANE)
    cols[0], cols[1], _ = hold((cols[0], cols[1], attn_own))
    cols[1] = swap(cols[1], LADDER)
    attn_own = jnp.swapaxes(attn_own, 0, 1).reshape(tok, q_width)
    mixed = mm(attn_own, out_full)

    x_rows = f32(x_own)
    branch_one, pull_one = jax.vjp(rms_scale, mixed, gain_vals[1])
    resid = x_rows + branch_one
    normed_two, pull_two = jax.vjp(rms_scale, resid, gain_vals[2])

    tokens_own = bf(normed_two)
    steps = ring_gather(tokens_own)
    cols[1], _ = hold((cols[1], tokens_own))
    down_own = quad_place([quad_blocks(w_down_late[None], tokens_own)], 1).reshape(ff_own, width)
    gate_up_own = [quad_blocks(cols[0], tokens_own), quad_blocks(cols[1])]
    gate_up_own = quad_place(gate_up_own, 2).reshape(width, 2 * ff_own)
    tokens = jnp.concatenate(sum(steps, []), axis=0)
    gate_up = mm(tokens, gate_up_own)

    def gated(gate, up_part):
        return jax.nn.gelu(gate, approximate=True) * up_part

    inner = bf(gated(gate_up[:, :ff_own], gate_up[:, ff_own:]))
    late = tokens.shape[0] - 3 * tok
    down = bf(mm(inner, down_own))
    attn_cols = attn_own.reshape(tok, planes, HEADS, w_out.shape[0])
    attn_cols = jnp.transpose(attn_cols, (2, 0, 1, 3)).reshape(HEADS, tok, HEAD_DIM)
    attn_cols, down = hold((attn_cols, down))
    attn_cols = swap(attn_cols, PLANE).reshape(HEADS * tok, HEAD_DIM)
    down = ring_scatter(steps_of((down[:late], down[late:]), tok))
    down, attn_cols = hold((down, attn_cols))
    branch_two, pull_three = jax.vjp(rms_scale, down, gain_vals[3])
    block_out = bf(resid + branch_two)[None]
    grad_top = f32(cotangent[0])
    grad_down_in, gain_grad_three = pull_three(grad_top)
    steps = ring_gather(bf(grad_down_in))
    grad_downs = two_parts(steps)
    grad_gus, parts = ([], [])
    for piece, kept in zip(grad_downs, (gate_up[:late], gate_up[late:])):
        _, pull = jax.vjp(gated, kept[:, :ff_own], kept[:, ff_own:])
        grad_gus.append(bf(jnp.concatenate(pull(mm_nt(piece, down_own)), axis=1)))
        grad_gu, _ = hold((grad_gus[-1], steps[3][0]))
        parts.append(bf(mm_nt(grad_gu, gate_up_own)))
    tokens, inner, grad_downs, grad_gus, parts = hold(
        (tokens, inner, grad_downs, grad_gus, parts)
    )
    grad_normed_two = ring_scatter(steps_of(parts, tok))
    grad_gu_b = jnp.concatenate(grad_gus, axis=0)
    grad_halves = [bf(mm_tn(tokens, grad_gu_b[:, :ff_own])), bf(mm_tn(tokens, grad_gu_b[:, ff_own:]))]
    grad_down_w = bf(mm_tn(inner, jnp.concatenate(grad_downs, axis=0)))
    grad_normed_two, _, _ = hold((grad_normed_two, grad_halves, grad_down_w))
    grad_resid_two, _ = pull_two(grad_normed_two)
    grad_resid = grad_top + grad_resid_two
    grad_mixed, gain_grad_one = pull_one(grad_resid)
    grad_mixed_b = bf(grad_mixed)

    grad_attn = bf(mm_nt(grad_mixed_b, out_full)).reshape(tok, HEADS, HEAD_DIM)
    grad_head = swap(jnp.swapaxes(grad_attn, 0, 1), PLANE).reshape(HEADS * tok, HEAD_DIM)
    grad_head = f32(grad_head)
    rho = bf(grad_head / total)
    delta = jnp.sum(grad_head * attn, axis=-1, keepdims=True) / total
    pulled = mm_nt(rho, value)
    grad_scores = bf((pulled - delta) * weights * (1.0 - (capped / SOFT_CAP) ** 2))
    grad_query = mm(grad_scores, key) * HEAD_DIM ** (-0.5)
    grad_key = mm_tn(grad_scores, query)
    grad_value = mm_tn(weights_b, rho)
    sent = jnp.where(core == 0, grad_value, grad_key)
    grad_half = jnp.where(core == 0, grad_key, grad_value) + flip(sent, "core")
    grad_half = jnp.where(core == 0, unrotary(grad_half, cosine, sine), grad_half)
    grad_qkv = bf(jnp.concatenate([unrotary(grad_query, cosine, sine), grad_half], axis=1))
    others = bf(jnp.stack([gain_grad_one, gain_grad_three]))
    others = jnp.concatenate([grad_mixed_b, jnp.pad(others, ((0, 14), (0, 0)))], axis=0)
    others = lax.all_gather(others, PLANE)
    grad_qkv, others = hold((grad_qkv, others))
    grad_mixed_all = others[:, :tok].reshape(HEADS * tok, width)
    others = jnp.sum(f32(others[:, tok : tok + 2]), axis=0).reshape(2, planes, HEADS, rows)
    others = lax.dynamic_index_in_dim(others, lax.axis_index(PLANE), 2, keepdims=False)
    others = jnp.swapaxes(others, 0, 1).reshape(planes, 1, 2 * rows)
    others = bf(jnp.pad(others, ((0, 0), (0, 7), (0, 2 * HEAD_DIM - 2 * rows))))
    grad_w = bf(mm_tn(normed_all, grad_qkv))
    grad_qkv, grad_w = hold((grad_qkv, grad_w))
    grad_w = grad_w.reshape(planes, -1, 2 * HEAD_DIM)
    grad_out_w = bf(mm_tn(attn_cols, grad_mixed_all)).reshape(planes, -1, 2 * HEAD_DIM)
    grad_w = jnp.concatenate([grad_w, grad_out_w, others], axis=1)
    sums = [core_sum(v.reshape(group, 4, rows, ff_own), grad_w) for v in grad_halves]
    sums.append(core_sum(grad_down_w.reshape(1, 4, ff_own // 4, width), grad_w))
    grad_w = scatter_sum(grad_w, DP)[0]
    sums[0], sums[1], grad_qkv = hold((sums[0], sums[1], grad_qkv))
    grad_normed = plane_scatter(bf(mm_nt(grad_qkv, w_own)))
    first, sums[1] = hold((row_sum(sums[0]), sums[1]))
    grad_halves = [swap(first, LADDER)]
    grad_halves.append(row_sum(sums[1], grad_halves[0]))
    grad_down_w, grad_halves[1] = hold((sums[2], grad_halves[1]))
    grad_down_w = f32(row_sum(grad_down_w)[0])
    others = f32(grad_w[-8, : 2 * rows]).reshape(2, rows)
    grad_out_w = f32(grad_w[HEADS * rows : -8].reshape(w_out.shape))
    grad_w = grad_w[: HEADS * rows].reshape(HEADS, rows, 2 * HEAD_DIM)
    grad_halves[1] = swap(grad_halves[1], LADDER)
    grad_w, grad_halves[1], grad_normed = hold((grad_w, grad_halves[1], grad_normed))
    grad_halves = [jnp.swapaxes(v, 0, 1).reshape(rows, group * ff_own) for v in grad_halves]
    grad_gate_up_w = f32(jnp.concatenate(grad_halves, axis=1))
    _, pull_zero = jax.vjp(rms_scale, x_rows, gain_vals[0])
    grad_x_zero, _ = pull_zero(grad_normed)
    input_grad = (grad_resid + grad_x_zero)[None]
    grad_w = f32(jnp.swapaxes(swap(grad_w, PLANE), 0, 1))
    grad_q_w = grad_w[:, :, :HEAD_DIM].reshape(rows, q_width)
    grad_kv_w = grad_w[:, :, HEAD_DIM:].reshape(rows, KV_HEADS, 2, HEAD_DIM)
    grad_kv_w = jnp.swapaxes(grad_kv_w, 1, 2).reshape(rows, q_width)
    grad_qkv_w = jnp.concatenate([grad_q_w, grad_kv_w], axis=1)

    gain_zero = jnp.sum(f32(w_qkv) * grad_qkv_w, axis=1) / (1.0 + f32(gains[0]))
    gain_two = jnp.sum(f32(w_gate_up) * grad_gate_up_w, axis=1) / (1.0 + f32(gains[2]))
    grad_gains = jnp.stack([gain_zero, others[0], gain_two, others[1]], axis=0)

    return (
        (block_out, input_grad)
        + adam_step(f32(w_qkv), grad_qkv_w, m_qkv, v_qkv, MATRIX_RATE, WEIGHT_DECAY)
        + adam_step(f32(w_out), grad_out_w, m_out, v_out, MATRIX_RATE, WEIGHT_DECAY)
        + adam_step(f32(w_gate_up), grad_gate_up_w, m_gate_up, v_gate_up, MATRIX_RATE, WEIGHT_DECAY)
        + adam_step(f32(w_down), grad_down_w, m_down, v_down, MATRIX_RATE, WEIGHT_DECAY)
        + adam_step(f32(gains), grad_gains, m_gains, v_gains, GAIN_RATE, 0.0)
    )


def token_attention(x_own, pos_own, w_qkv, w_out, gains):
    tok = x_own.shape[0]
    q_width = HEADS * HEAD_DIM
    k_width = KV_HEADS * HEAD_DIM
    groups = HEADS // KV_HEADS
    qkv_full = gather(w_qkv, ALL)
    out_full = gather(w_out, ALL)
    gain_vals = f32(gather(gains, ALL, 1))
    normed = bf(rms_scale(f32(x_own), gain_vals[0]))
    qkv = mm(normed, qkv_full)
    cosine, sine = rotary_tables(pos_own)
    cosine, sine = (cosine[:, None, :], sine[:, None, :])
    query = rotary(qkv[:, :q_width].reshape(tok, HEADS, HEAD_DIM), cosine, sine)
    query = bf(query * HEAD_DIM ** (-0.5)).reshape(tok, KV_HEADS, groups, HEAD_DIM)
    key_own = qkv[:, q_width : q_width + k_width].reshape(tok, KV_HEADS, HEAD_DIM)
    key = gather(bf(rotary(key_own, cosine, sine)), PLANE)
    value = gather(bf(qkv[:, q_width + k_width :]).reshape(tok, KV_HEADS, HEAD_DIM), PLANE)
    pos_all = gather(pos_own, PLANE)
    count = pos_all.shape[0]
    scores = jnp.einsum("tgjd,sgd->gjts", query, key, preferred_element_type=jnp.float32)
    capped = SOFT_CAP * jnp.tanh(scores / SOFT_CAP)
    weights = jnp.where(pos_own[:, None] >= pos_all[None, :], jnp.exp(capped), 0.0)
    weights_b = bf(weights)
    total = jnp.sum(weights, axis=-1)
    attn = jnp.einsum("gjts,sgd->gjtd", weights_b, value, preferred_element_type=jnp.float32)
    attn = attn / total[..., None]
    attn_b = bf(jnp.transpose(attn, (2, 0, 1, 3)).reshape(tok, q_width))
    mixed = mm(attn_b, out_full)

    def backward(grad_mixed_b):
        grad_attn = mm_nt(grad_mixed_b, out_full).reshape(tok, KV_HEADS, groups, HEAD_DIM)
        grad_heads = jnp.transpose(grad_attn, (1, 2, 0, 3))
        rho = bf(grad_heads / total[..., None])
        delta = jnp.sum(grad_heads * attn, axis=-1) / total
        pulled = jnp.einsum("gjtd,sgd->gjts", rho, value, preferred_element_type=jnp.float32)
        grad_scores = bf(
            (pulled - delta[..., None]) * weights * (1.0 - (capped / SOFT_CAP) ** 2)
        )
        grad_query = jnp.einsum(
            "gjts,sgd->tgjd", grad_scores, key, preferred_element_type=jnp.float32
        ).reshape(tok, HEADS, HEAD_DIM)
        grad_key = jnp.einsum(
            "gjts,tgjd->sgd", grad_scores, query, preferred_element_type=jnp.float32
        ).reshape(count, k_width)
        grad_value = jnp.einsum(
            "gjts,gjtd->sgd", weights_b, rho, preferred_element_type=jnp.float32
        ).reshape(count, k_width)
        grad_kv = scatter_sum(jnp.concatenate([grad_key, grad_value], axis=1), PLANE)
        grad_query = unrotary(grad_query * HEAD_DIM ** (-0.5), cosine, sine)
        grad_key = unrotary(grad_kv[:, :k_width].reshape(tok, KV_HEADS, HEAD_DIM), cosine, sine)
        grad_qkv = bf(
            jnp.concatenate(
                [
                    grad_query.reshape(tok, q_width),
                    grad_key.reshape(tok, k_width),
                    grad_kv[:, k_width:],
                ],
                axis=1,
            )
        )
        grad_normed = mm_nt(grad_qkv, qkv_full)
        grad_qkv_w = f32(scatter_sum(bf(mm_tn(normed, grad_qkv)), ALL))
        grad_out_w = f32(scatter_sum(bf(mm_tn(attn_b, grad_mixed_b)), ALL))
        return grad_normed, grad_qkv_w, grad_out_w

    return mixed, gain_vals, backward


def wide_shards(
    hidden_in,
    positions,
    cotangent,
    w_qkv,
    w_out,
    w_gate_up,
    w_down,
    gains,
    m_qkv,
    v_qkv,
    m_out,
    v_out,
    m_gate_up,
    v_gate_up,
    m_down,
    v_down,
    m_gains,
    v_gains,
):
    x_own = hidden_in[0]
    rows, width = (w_qkv.shape[0], x_own.shape[1])
    group, across = (lax.axis_size(GROUP), lax.axis_size(ACROSS))
    ff_piece = w_down.shape[0]
    ff_own = across * ff_piece
    gu_pieces = w_gate_up.reshape(rows, 2, across, group, ff_piece)
    gu_pieces = jnp.transpose(gu_pieces, (3, 0, 1, 2, 4)).reshape(group * rows, 2 * ff_own)

    mixed, gain_vals, attention_back = token_attention(x_own, positions[0], w_qkv, w_out, gains)
    gu_own = gather(swap(gu_pieces, GROUP), ACROSS)
    down_own = gather(w_down, ACROSS)

    x_rows = f32(x_own)
    branch_one, pull_one = jax.vjp(rms_scale, mixed, gain_vals[1])
    resid = x_rows + branch_one
    normed_two, pull_two = jax.vjp(rms_scale, resid, gain_vals[2])
    tokens_b = gather(bf(normed_two), GROUP)
    gate_up = mm(tokens_b, gu_own)
    inner, pull_gelu = jax.vjp(
        lambda gate, up_part: jax.nn.gelu(gate, approximate=True) * up_part,
        gate_up[:, :ff_own],
        gate_up[:, ff_own:],
    )
    inner_b = bf(inner)
    down = f32(scatter_sum(bf(mm(inner_b, down_own)), GROUP))
    branch_two, pull_three = jax.vjp(rms_scale, down, gain_vals[3])
    block_out = bf(resid + branch_two)[None]
    grad_top = f32(cotangent[0])
    grad_down_in, gain_grad_three = pull_three(grad_top)
    grad_down_b = gather(bf(grad_down_in), GROUP)
    grad_gate, grad_up = pull_gelu(mm_nt(grad_down_b, down_own))
    grad_gu_b = bf(jnp.concatenate([grad_gate, grad_up], axis=1))
    grad_normed_two = f32(scatter_sum(bf(mm_nt(grad_gu_b, gu_own)), GROUP))
    grad_gate_up_w = scatter_sum(bf(mm_tn(tokens_b, grad_gu_b)), ACROSS)
    grad_down_w = f32(scatter_sum(bf(mm_tn(inner_b, grad_down_b)), ACROSS))

    grad_resid_two, gain_grad_two = pull_two(grad_normed_two)
    grad_resid = grad_top + grad_resid_two
    grad_mixed, gain_grad_one = pull_one(grad_resid)
    grad_normed, grad_qkv_w, grad_out_w = attention_back(bf(grad_mixed))
    _, pull_zero = jax.vjp(rms_scale, x_rows, gain_vals[0])
    grad_x_zero, gain_grad_zero = pull_zero(grad_normed)
    input_grad = (grad_resid + grad_x_zero)[None]

    grad_gate_up_w = swap(grad_gate_up_w, GROUP).reshape(group, rows, 2, across, ff_piece)
    grad_gate_up_w = f32(jnp.transpose(grad_gate_up_w, (1, 2, 3, 0, 4)).reshape(rows, -1))
    gain_term = jnp.stack([gain_grad_zero, gain_grad_one, gain_grad_two, gain_grad_three], axis=0)
    grad_gains = lax.psum_scatter(gain_term, ALL, scatter_dimension=1, tiled=True)

    return (
        (block_out, input_grad)
        + adam_step(f32(w_qkv), grad_qkv_w, m_qkv, v_qkv, MATRIX_RATE, WEIGHT_DECAY)
        + adam_step(f32(w_out), grad_out_w, m_out, v_out, MATRIX_RATE, WEIGHT_DECAY)
        + adam_step(f32(w_gate_up), grad_gate_up_w, m_gate_up, v_gate_up, MATRIX_RATE, WEIGHT_DECAY)
        + adam_step(f32(w_down), grad_down_w, m_down, v_down, MATRIX_RATE, WEIGHT_DECAY)
        + adam_step(f32(gains), grad_gains, m_gains, v_gains, GAIN_RATE, 0.0)
    )


def solution(mesh):
    sizes = dict(mesh.shape)
    fine = Mesh(
        mesh.devices.reshape(sizes["dp"] // 2, 2, sizes["ctx"], sizes["fsdp"] // 2, 2),
        ("dh", "dl", "ctx", "fy", "core"),
    )
    acts = P(DP, PLANE, None)
    mats = P(ALL, None)
    vecs = P(None, ALL)
    ladder = sizes["dp"] == 4 and sizes["ctx"] == 2 and sizes["fsdp"] == 4
    return jax.shard_map(
        ladder_shards if ladder else wide_shards,
        mesh=fine,
        in_specs=(acts, P(DP, PLANE), acts) + (mats,) * 4 + (vecs,) + (mats,) * 8 + (vecs,) * 2,
        out_specs=(acts, acts) + (mats,) * 12 + (vecs,) * 3,
        check_vma=False,
    )
```

```python
import jax
import jax.numpy as jnp
from jax import lax
from jax.sharding import Mesh, PartitionSpec as P

HEADS = 8
KV_HEADS = 4
HEAD_DIM = 256
STEP = 10

NORM_EPS = 1e-06
SOFT_CAP = 50.0
THETA = 10000.0
BETA_ONE = 0.9
BETA_TWO = 0.95
ADAM_EPS = 1e-08
MATRIX_RATE = 0.03
GAIN_RATE = 0.2
WEIGHT_DECAY = 0.1

DP = ("dh", "dl")
PLANE = ("ctx", "fy", "core")
ALL = DP + PLANE
LADDER = DP + ("ctx",)
GROUP = PLANE
ACROSS = DP


def f32(v):
    return v.astype(jnp.float32)


def bf(v):
    return v.astype(jnp.bfloat16)


def dot(left, right, dims):
    return lax.dot_general(left, right, (dims, ((), ())), preferred_element_type=jnp.float32)


def mm(left, right):
    return dot(left, right, ((1,), (0,)))


def mm_nt(left, right):
    return dot(left, right, ((1,), (1,)))


def mm_tn(left, right):
    return dot(left, right, ((0,), (0,)))


def rms_scale(values, gain):
    inverse = lax.rsqrt(jnp.mean(values * values, axis=-1, keepdims=True) + NORM_EPS)
    return values * inverse * (1.0 + gain)


def rotary_tables(places):
    half = HEAD_DIM // 2
    freqs = THETA ** (-(jnp.arange(half, dtype=jnp.float32) * 2.0 / HEAD_DIM))
    angles = f32(places)[:, None] * freqs[None, :]
    return (jnp.cos(angles), jnp.sin(angles))


def rotary(values, cosine, sine):
    half = HEAD_DIM // 2
    first = values[..., :half]
    second = values[..., half:]
    return jnp.concatenate(
        [first * cosine - second * sine, second * cosine + first * sine], axis=-1
    )


def unrotary(values, cosine, sine):
    return rotary(values, cosine, -sine)


def adam_step(weight, grad, first, second, rate, decay):
    first_new = BETA_ONE * first + (1.0 - BETA_ONE) * grad
    second_new = BETA_TWO * second + (1.0 - BETA_TWO) * grad * grad
    ratio = (
        first_new
        / (1.0 - BETA_ONE**STEP)
        / (jnp.sqrt(second_new / (1.0 - BETA_TWO**STEP)) + ADAM_EPS)
    )
    return (weight - rate * (ratio + decay * weight), first_new, second_new)


def gather(v, axes, axis=0):
    return lax.all_gather(v, axes, axis=axis, tiled=True)


def scatter_sum(v, axes):
    return lax.psum_scatter(v, axes, scatter_dimension=0, tiled=True)


def swap(v, axes):
    return lax.all_to_all(v, axes, split_axis=0, concat_axis=0, tiled=True)


def hold(v):
    return lax.optimization_barrier(v)


def flip(v, axis):
    return lax.ppermute(v, axis, [(0, 1), (1, 0)])


def plane_gather(own):
    me = lax.axis_index(PLANE)
    over_y = flip(own, "fy")
    over_x = flip(own, "ctx")
    blocks = [own, over_y, over_x, flip(over_y, "ctx")]
    whole = jnp.zeros((8,) + own.shape, own.dtype)
    for bits, block in enumerate(blocks):
        whole = lax.dynamic_update_index_in_dim(whole, block, me ^ (2 * bits), 0)
        whole = lax.dynamic_update_index_in_dim(whole, flip(block, "core"), me ^ (2 * bits + 1), 0)
    return whole.reshape((-1,) + own.shape[1:])


def plane_scatter(parts):
    size = parts.shape[0] // 8
    half = size // 2
    col, row, core = (lax.axis_index(axis) for axis in PLANE)
    parts = parts.reshape((4, 2, size) + parts.shape[1:])
    sent = lax.dynamic_index_in_dim(parts, 1 - core, 1, keepdims=False)
    kept = lax.dynamic_index_in_dim(parts, core, 1, keepdims=False)
    both = bf(f32(kept) + f32(flip(sent, "core")))
    own, over_y, over_x, corner = (
        lax.dynamic_index_in_dim(both, (2 * col + row) ^ bits, 0, keepdims=False) for bits in range(4)
    )
    got_y = flip(corner[:half], "ctx")
    got_x = flip(corner[half:], "fy")
    over_y = jnp.concatenate([bf(f32(over_y[:half]) + f32(got_y)), over_y[half:]], axis=0)
    over_x = jnp.concatenate([over_x[:half], bf(f32(over_x[half:]) + f32(got_x))], axis=0)
    return f32(own) + f32(flip(over_x, "ctx")) + f32(flip(over_y, "fy"))


def line_gather(own):
    count = lax.axis_size(DP)
    row = [own]
    up, down = (own, own)
    for step in range(1, count):
        up = lax.ppermute(up, DP, [(i, i + 1) for i in range(step - 1, count - 1)])
        down = lax.ppermute(down, DP, [(i + 1, i) for i in range(count - step)])
        row = [up] + row + [down]
    return lax.dynamic_slice_in_dim(jnp.stack(row), count - 1 - lax.axis_index(DP), count, axis=0)


def ring_pairs():
    count = lax.axis_size(DP)
    ring = [2 * z for z in range(count)] + [2 * z + 1 for z in reversed(range(count))]
    onward = [(ring[i], ring[(i + 1) % len(ring)]) for i in range(len(ring))]
    return onward, [(b, a) for a, b in onward]


def ring_gather(own):
    onward, back = ring_pairs()
    half = own.shape[0] // 2
    steps = [[own]]
    behind, ahead = (own, own)
    for _ in range(len(onward) // 2 - 1):
        behind = lax.ppermute(behind, LADDER, onward)
        ahead = lax.ppermute(ahead, LADDER, back)
        steps.append([behind, ahead])
    steps.append(
        [
            lax.ppermute(behind[:half], LADDER, onward),
            lax.ppermute(ahead[half:], LADDER, back),
        ]
    )
    return steps


def two_parts(steps):
    return [
        jnp.concatenate(sum(steps[:3], []), axis=0),
        jnp.concatenate(sum(steps[3:], []), axis=0),
    ]


def steps_of(parts, size):
    early, late = parts
    steps = [early[:size], early[size : 3 * size], early[3 * size :]]
    return steps + [late[: 2 * size], late[2 * size :]]


def ring_scatter(pieces):
    onward, back = ring_pairs()
    size = pieces[0].shape[0]
    half = size // 2
    ahead = lax.ppermute(pieces[-1][:half], LADDER, onward)
    behind = lax.ppermute(pieces[-1][half:], LADDER, back)
    for step in range(len(pieces) - 2, 0, -1):
        to_behind, to_ahead = (pieces[step][:size], pieces[step][size:])
        if step == len(pieces) - 2:
            to_ahead = jnp.concatenate(
                [bf(f32(to_ahead[:half]) + f32(ahead)), to_ahead[half:]], axis=0
            )
            to_behind = jnp.concatenate(
                [to_behind[:half], bf(f32(to_behind[half:]) + f32(behind))], axis=0
            )
        else:
            to_ahead = bf(f32(to_ahead) + f32(ahead))
            to_behind = bf(f32(to_behind) + f32(behind))
        to_ahead, to_behind = hold((to_ahead, to_behind))
        ahead = lax.ppermute(to_ahead, LADDER, onward)
        behind = lax.ppermute(to_behind, LADDER, back)
    return f32(pieces[0]) + f32(ahead) + f32(behind)


def quad_blocks(own, late=None):
    over_y = flip(own, "fy")
    if late is not None:
        over_y, _ = hold((over_y, late))
    return [own, flip(own, "core"), over_y, flip(over_y, "core")]


def quad_place(blocks, parts):
    me = lax.axis_index(("fy", "core"))
    count, rows, cols = blocks[0][0].shape
    whole = jnp.zeros((count, 4, rows, parts * cols), blocks[0][0].dtype)
    for part in range(parts):
        for bits, block in enumerate(blocks[part]):
            whole = lax.dynamic_update_slice(
                whole, block[:, None], (0, me ^ bits, 0, part * cols)
            )
    return whole


def core_sum(parts, late):
    core = lax.axis_index("core")
    parts = parts.reshape(parts.shape[:1] + (2, 2) + parts.shape[2:])
    sent = lax.dynamic_index_in_dim(parts, 1 - core, 2, keepdims=False)
    kept = lax.dynamic_index_in_dim(parts, core, 2, keepdims=False)
    kept, got, _ = hold((kept, flip(sent, "core"), late))
    return bf(f32(kept) + f32(got))


def row_sum(both, late=()):
    row = lax.axis_index("fy")
    sent = lax.dynamic_index_in_dim(both, 1 - row, 1, keepdims=False)
    kept = lax.dynamic_index_in_dim(both, row, 1, keepdims=False)
    kept, got, _ = hold((kept, flip(sent, "fy"), late))
    return bf(f32(kept) + f32(got))


def ladder_shards(
    hidden_in,
    positions,
    cotangent,
    w_qkv,
    w_out,
    w_gate_up,
    w_down,
    gains,
    m_qkv,
    v_qkv,
    m_out,
    v_out,
    m_gate_up,
    v_gate_up,
    m_down,
    v_down,
    m_gains,
    v_gains,
):
    x_own = hidden_in[0]
    tok, width = x_own.shape
    rows = w_qkv.shape[0]
    planes = lax.axis_size(DP)
    group = lax.axis_size(LADDER)
    q_width = HEADS * HEAD_DIM
    core = lax.axis_index("core")

    q_cols = w_qkv[:, :q_width].reshape(rows, HEADS, HEAD_DIM)
    kv_cols = w_qkv[:, q_width:].reshape(rows, 2, KV_HEADS, HEAD_DIM)
    kv_cols = jnp.swapaxes(kv_cols, 1, 2).reshape(rows, HEADS, HEAD_DIM)
    pieces = jnp.swapaxes(jnp.concatenate([q_cols, kv_cols], axis=2), 0, 1)
    first = jnp.stack([positions[0, 0] // 128, positions[0, 0] % 128])
    own_gains = jnp.concatenate([gains.reshape(4 * rows), bf(first)])[None, None]
    own_gains = jnp.pad(own_gains, ((0, 0), (0, 7), (0, 2 * HEAD_DIM - 4 * rows - 2)))
    pieces = jnp.concatenate(
        [pieces, jnp.broadcast_to(own_gains, (HEADS,) + own_gains.shape[1:])], axis=1
    )
    got = swap(pieces, PLANE)
    got, x_sent, out_line = hold((got, x_own, w_out))
    x_all = plane_gather(x_sent)
    out_line = line_gather(out_line)
    first = got[:, rows, 4 * rows : 4 * rows + 2].astype(jnp.int32)
    pos_all = first[:, :1] * 128 + first[:, 1:] + jnp.arange(tok, dtype=jnp.int32)[None]
    pos_all = pos_all.reshape(-1)
    cosine, sine = rotary_tables(pos_all)
    got = lax.all_gather(got, DP)
    ff_own = w_down.shape[0] * 4
    cols = []
    for part in range(2):
        piece = w_gate_up[:, part * group * ff_own : (part + 1) * group * ff_own]
        cols.append(jnp.swapaxes(piece.reshape(rows, group, ff_own), 0, 1))
    got, cols[0], w_down_late = hold((got, cols[0], w_down))
    w_own = got[:, :, :rows].reshape(width, 2 * HEAD_DIM)
    gain_vals = got[:, :, rows, : 4 * rows].reshape(planes * HEADS, 4, rows)
    gain_vals = f32(jnp.swapaxes(gain_vals, 0, 1).reshape(4, width))
    out_full = lax.all_gather(out_line, PLANE, axis=1, tiled=False).reshape(q_width, width)
    cols[0] = swap(cols[0], LADDER)

    normed_all = hold(bf(rms_scale(f32(x_all), gain_vals[0])))
    qkv = mm(normed_all, w_own)
    query = bf(rotary(qkv[:, :HEAD_DIM], cosine, sine) * HEAD_DIM ** (-0.5))
    half = qkv[:, HEAD_DIM:]
    mine = jnp.where(core == 0, bf(rotary(half, cosine, sine)), bf(half))
    other = flip(mine, "core")
    key = jnp.where(core == 0, mine, other)
    value = jnp.where(core == 0, other, mine)
    scores = mm_nt(query, key)
    capped = SOFT_CAP * jnp.tanh(scores / SOFT_CAP)
    weights = jnp.where(pos_all[:, None] >= pos_all[None, :], jnp.exp(capped), 0.0)
    weights_b = bf(weights)
    total = jnp.sum(weights, axis=-1, keepdims=True)
    attn = mm(weights_b, value) / total
    cols[0], attn_sent = hold((cols[0], bf(attn)))
    attn_own = swap(attn_sent.reshape(HEADS, tok, HEAD_DIM), PLANE)
    cols[0], cols[1], _ = hold((cols[0], cols[1], attn_own))
    cols[1] = swap(cols[1], LADDER)
    attn_own = jnp.swapaxes(attn_own, 0, 1).reshape(tok, q_width)
    mixed = mm(attn_own, out_full)

    x_rows = f32(x_own)
    branch_one, pull_one = jax.vjp(rms_scale, mixed, gain_vals[1])
    resid = x_rows + branch_one
    normed_two, pull_two = jax.vjp(rms_scale, resid, gain_vals[2])

    tokens_own = bf(normed_two)
    steps = ring_gather(tokens_own)
    cols[1], _ = hold((cols[1], tokens_own))
    down_own = quad_place([quad_blocks(w_down_late[None], tokens_own)], 1).reshape(ff_own, width)
    gate_up_own = [quad_blocks(cols[0], tokens_own), quad_blocks(cols[1])]
    gate_up_own = quad_place(gate_up_own, 2).reshape(width, 2 * ff_own)
    tokens = jnp.concatenate(sum(steps, []), axis=0)
    gate_up = mm(tokens, gate_up_own)

    def gated(gate, up_part):
        return jax.nn.gelu(gate, approximate=True) * up_part

    inner = bf(gated(gate_up[:, :ff_own], gate_up[:, ff_own:]))
    late = tokens.shape[0] - 3 * tok
    down = bf(mm(inner, down_own))
    attn_cols = attn_own.reshape(tok, planes, HEADS, w_out.shape[0])
    attn_cols = jnp.transpose(attn_cols, (2, 0, 1, 3)).reshape(HEADS, tok, HEAD_DIM)
    attn_cols, down = hold((attn_cols, down))
    attn_cols = swap(attn_cols, PLANE).reshape(HEADS * tok, HEAD_DIM)
    down = ring_scatter(steps_of((down[:late], down[late:]), tok))
    down, attn_cols = hold((down, attn_cols))
    branch_two, pull_three = jax.vjp(rms_scale, down, gain_vals[3])
    block_out = bf(resid + branch_two)[None]
    grad_top = f32(cotangent[0])
    grad_down_in, gain_grad_three = pull_three(grad_top)
    steps = ring_gather(bf(grad_down_in))
    grad_downs = two_parts(steps)
    grad_gus, parts = ([], [])
    for piece, kept in zip(grad_downs, (gate_up[:late], gate_up[late:])):
        _, pull = jax.vjp(gated, kept[:, :ff_own], kept[:, ff_own:])
        grad_gus.append(bf(jnp.concatenate(pull(mm_nt(piece, down_own)), axis=1)))
        grad_gu, _ = hold((grad_gus[-1], steps[3][0]))
        parts.append(bf(mm_nt(grad_gu, gate_up_own)))
    tokens, inner, grad_downs, grad_gus, parts = hold(
        (tokens, inner, grad_downs, grad_gus, parts)
    )
    grad_normed_two = ring_scatter(steps_of(parts, tok))
    grad_gu_b = jnp.concatenate(grad_gus, axis=0)
    grad_halves = [bf(mm_tn(tokens, grad_gu_b[:, :ff_own])), bf(mm_tn(tokens, grad_gu_b[:, ff_own:]))]
    grad_down_w = bf(mm_tn(inner, jnp.concatenate(grad_downs, axis=0)))
    grad_normed_two, _, _ = hold((grad_normed_two, grad_halves, grad_down_w))
    grad_resid_two, _ = pull_two(grad_normed_two)
    grad_resid = grad_top + grad_resid_two
    grad_mixed, gain_grad_one = pull_one(grad_resid)
    grad_mixed_b = bf(grad_mixed)

    grad_attn = bf(mm_nt(grad_mixed_b, out_full)).reshape(tok, HEADS, HEAD_DIM)
    grad_head = swap(jnp.swapaxes(grad_attn, 0, 1), PLANE).reshape(HEADS * tok, HEAD_DIM)
    grad_head = f32(grad_head)
    rho = bf(grad_head / total)
    delta = jnp.sum(grad_head * attn, axis=-1, keepdims=True) / total
    pulled = mm_nt(rho, value)
    grad_scores = bf((pulled - delta) * weights * (1.0 - (capped / SOFT_CAP) ** 2))
    grad_query = mm(grad_scores, key) * HEAD_DIM ** (-0.5)
    grad_key = mm_tn(grad_scores, query)
    grad_value = mm_tn(weights_b, rho)
    sent = jnp.where(core == 0, grad_value, grad_key)
    grad_half = jnp.where(core == 0, grad_key, grad_value) + flip(sent, "core")
    grad_half = jnp.where(core == 0, unrotary(grad_half, cosine, sine), grad_half)
    grad_qkv = bf(jnp.concatenate([unrotary(grad_query, cosine, sine), grad_half], axis=1))
    others = bf(jnp.stack([gain_grad_one, gain_grad_three]))
    others = jnp.concatenate([grad_mixed_b, jnp.pad(others, ((0, 14), (0, 0)))], axis=0)
    others = lax.all_gather(others, PLANE)
    grad_qkv, others = hold((grad_qkv, others))
    grad_mixed_all = others[:, :tok].reshape(HEADS * tok, width)
    others = jnp.sum(f32(others[:, tok : tok + 2]), axis=0).reshape(2, planes, HEADS, rows)
    others = lax.dynamic_index_in_dim(others, lax.axis_index(PLANE), 2, keepdims=False)
    others = jnp.swapaxes(others, 0, 1).reshape(planes, 1, 2 * rows)
    others = bf(jnp.pad(others, ((0, 0), (0, 7), (0, 2 * HEAD_DIM - 2 * rows))))
    grad_w = bf(mm_tn(normed_all, grad_qkv))
    grad_qkv, grad_w = hold((grad_qkv, grad_w))
    sums = [core_sum(v.reshape(group, 4, rows, ff_own), grad_qkv) for v in grad_halves]
    sums.append(core_sum(grad_down_w.reshape(1, 4, ff_own // 4, width), grad_qkv))
    grad_w = grad_w.reshape(planes, -1, 2 * HEAD_DIM)
    grad_out_w = bf(mm_tn(attn_cols, grad_mixed_all)).reshape(planes, -1, 2 * HEAD_DIM)
    grad_w = jnp.concatenate([grad_w, grad_out_w, others], axis=1)
    grad_w, grad_qkv = hold((grad_w, grad_qkv))
    grad_normed = plane_scatter(bf(mm_nt(grad_qkv, w_own)))
    grad_w = scatter_sum(grad_w, DP)[0]
    grad_halves = [swap(row_sum(sums[0]), LADDER)]
    grad_halves.append(row_sum(sums[1], grad_halves[0]))
    grad_down_w, grad_halves[1] = hold((sums[2], grad_halves[1]))
    grad_down_w = f32(row_sum(grad_down_w)[0])
    others = f32(grad_w[-8, : 2 * rows]).reshape(2, rows)
    grad_out_w = f32(grad_w[HEADS * rows : -8].reshape(w_out.shape))
    grad_w = grad_w[: HEADS * rows].reshape(HEADS, rows, 2 * HEAD_DIM)
    grad_halves[1] = swap(grad_halves[1], LADDER)
    grad_w, grad_halves[1], grad_normed = hold((grad_w, grad_halves[1], grad_normed))
    grad_halves = [jnp.swapaxes(v, 0, 1).reshape(rows, group * ff_own) for v in grad_halves]
    grad_gate_up_w = f32(jnp.concatenate(grad_halves, axis=1))
    _, pull_zero = jax.vjp(rms_scale, x_rows, gain_vals[0])
    grad_x_zero, _ = pull_zero(grad_normed)
    input_grad = (grad_resid + grad_x_zero)[None]
    grad_w = f32(jnp.swapaxes(swap(grad_w, PLANE), 0, 1))
    grad_q_w = grad_w[:, :, :HEAD_DIM].reshape(rows, q_width)
    grad_kv_w = grad_w[:, :, HEAD_DIM:].reshape(rows, KV_HEADS, 2, HEAD_DIM)
    grad_kv_w = jnp.swapaxes(grad_kv_w, 1, 2).reshape(rows, q_width)
    grad_qkv_w = jnp.concatenate([grad_q_w, grad_kv_w], axis=1)

    gain_zero = jnp.sum(f32(w_qkv) * grad_qkv_w, axis=1) / (1.0 + f32(gains[0]))
    gain_two = jnp.sum(f32(w_gate_up) * grad_gate_up_w, axis=1) / (1.0 + f32(gains[2]))
    grad_gains = jnp.stack([gain_zero, others[0], gain_two, others[1]], axis=0)

    return (
        (block_out, input_grad)
        + adam_step(f32(w_qkv), grad_qkv_w, m_qkv, v_qkv, MATRIX_RATE, WEIGHT_DECAY)
        + adam_step(f32(w_out), grad_out_w, m_out, v_out, MATRIX_RATE, WEIGHT_DECAY)
        + adam_step(f32(w_gate_up), grad_gate_up_w, m_gate_up, v_gate_up, MATRIX_RATE, WEIGHT_DECAY)
        + adam_step(f32(w_down), grad_down_w, m_down, v_down, MATRIX_RATE, WEIGHT_DECAY)
        + adam_step(f32(gains), grad_gains, m_gains, v_gains, GAIN_RATE, 0.0)
    )


def token_attention(x_own, pos_own, w_qkv, w_out, gains):
    tok = x_own.shape[0]
    q_width = HEADS * HEAD_DIM
    k_width = KV_HEADS * HEAD_DIM
    groups = HEADS // KV_HEADS
    qkv_full = gather(w_qkv, ALL)
    out_full = gather(w_out, ALL)
    gain_vals = f32(gather(gains, ALL, 1))
    normed = bf(rms_scale(f32(x_own), gain_vals[0]))
    qkv = mm(normed, qkv_full)
    cosine, sine = rotary_tables(pos_own)
    cosine, sine = (cosine[:, None, :], sine[:, None, :])
    query = rotary(qkv[:, :q_width].reshape(tok, HEADS, HEAD_DIM), cosine, sine)
    query = bf(query * HEAD_DIM ** (-0.5)).reshape(tok, KV_HEADS, groups, HEAD_DIM)
    key_own = qkv[:, q_width : q_width + k_width].reshape(tok, KV_HEADS, HEAD_DIM)
    key = gather(bf(rotary(key_own, cosine, sine)), PLANE)
    value = gather(bf(qkv[:, q_width + k_width :]).reshape(tok, KV_HEADS, HEAD_DIM), PLANE)
    pos_all = gather(pos_own, PLANE)
    count = pos_all.shape[0]
    scores = jnp.einsum("tgjd,sgd->gjts", query, key, preferred_element_type=jnp.float32)
    capped = SOFT_CAP * jnp.tanh(scores / SOFT_CAP)
    weights = jnp.where(pos_own[:, None] >= pos_all[None, :], jnp.exp(capped), 0.0)
    weights_b = bf(weights)
    total = jnp.sum(weights, axis=-1)
    attn = jnp.einsum("gjts,sgd->gjtd", weights_b, value, preferred_element_type=jnp.float32)
    attn = attn / total[..., None]
    attn_b = bf(jnp.transpose(attn, (2, 0, 1, 3)).reshape(tok, q_width))
    mixed = mm(attn_b, out_full)

    def backward(grad_mixed_b):
        grad_attn = mm_nt(grad_mixed_b, out_full).reshape(tok, KV_HEADS, groups, HEAD_DIM)
        grad_heads = jnp.transpose(grad_attn, (1, 2, 0, 3))
        rho = bf(grad_heads / total[..., None])
        delta = jnp.sum(grad_heads * attn, axis=-1) / total
        pulled = jnp.einsum("gjtd,sgd->gjts", rho, value, preferred_element_type=jnp.float32)
        grad_scores = bf(
            (pulled - delta[..., None]) * weights * (1.0 - (capped / SOFT_CAP) ** 2)
        )
        grad_query = jnp.einsum(
            "gjts,sgd->tgjd", grad_scores, key, preferred_element_type=jnp.float32
        ).reshape(tok, HEADS, HEAD_DIM)
        grad_key = jnp.einsum(
            "gjts,tgjd->sgd", grad_scores, query, preferred_element_type=jnp.float32
        ).reshape(count, k_width)
        grad_value = jnp.einsum(
            "gjts,gjtd->sgd", weights_b, rho, preferred_element_type=jnp.float32
        ).reshape(count, k_width)
        grad_kv = scatter_sum(jnp.concatenate([grad_key, grad_value], axis=1), PLANE)
        grad_query = unrotary(grad_query * HEAD_DIM ** (-0.5), cosine, sine)
        grad_key = unrotary(grad_kv[:, :k_width].reshape(tok, KV_HEADS, HEAD_DIM), cosine, sine)
        grad_qkv = bf(
            jnp.concatenate(
                [
                    grad_query.reshape(tok, q_width),
                    grad_key.reshape(tok, k_width),
                    grad_kv[:, k_width:],
                ],
                axis=1,
            )
        )
        grad_normed = mm_nt(grad_qkv, qkv_full)
        grad_qkv_w = f32(scatter_sum(bf(mm_tn(normed, grad_qkv)), ALL))
        grad_out_w = f32(scatter_sum(bf(mm_tn(attn_b, grad_mixed_b)), ALL))
        return grad_normed, grad_qkv_w, grad_out_w

    return mixed, gain_vals, backward


def wide_shards(
    hidden_in,
    positions,
    cotangent,
    w_qkv,
    w_out,
    w_gate_up,
    w_down,
    gains,
    m_qkv,
    v_qkv,
    m_out,
    v_out,
    m_gate_up,
    v_gate_up,
    m_down,
    v_down,
    m_gains,
    v_gains,
):
    x_own = hidden_in[0]
    rows, width = (w_qkv.shape[0], x_own.shape[1])
    group, across = (lax.axis_size(GROUP), lax.axis_size(ACROSS))
    ff_piece = w_down.shape[0]
    ff_own = across * ff_piece
    gu_pieces = w_gate_up.reshape(rows, 2, across, group, ff_piece)
    gu_pieces = jnp.transpose(gu_pieces, (3, 0, 1, 2, 4)).reshape(group * rows, 2 * ff_own)

    mixed, gain_vals, attention_back = token_attention(x_own, positions[0], w_qkv, w_out, gains)
    gu_own = gather(swap(gu_pieces, GROUP), ACROSS)
    down_own = gather(w_down, ACROSS)

    x_rows = f32(x_own)
    branch_one, pull_one = jax.vjp(rms_scale, mixed, gain_vals[1])
    resid = x_rows + branch_one
    normed_two, pull_two = jax.vjp(rms_scale, resid, gain_vals[2])
    tokens_b = gather(bf(normed_two), GROUP)
    gate_up = mm(tokens_b, gu_own)
    inner, pull_gelu = jax.vjp(
        lambda gate, up_part: jax.nn.gelu(gate, approximate=True) * up_part,
        gate_up[:, :ff_own],
        gate_up[:, ff_own:],
    )
    inner_b = bf(inner)
    down = f32(scatter_sum(bf(mm(inner_b, down_own)), GROUP))
    branch_two, pull_three = jax.vjp(rms_scale, down, gain_vals[3])
    block_out = bf(resid + branch_two)[None]
    grad_top = f32(cotangent[0])
    grad_down_in, gain_grad_three = pull_three(grad_top)
    grad_down_b = gather(bf(grad_down_in), GROUP)
    grad_gate, grad_up = pull_gelu(mm_nt(grad_down_b, down_own))
    grad_gu_b = bf(jnp.concatenate([grad_gate, grad_up], axis=1))
    grad_normed_two = f32(scatter_sum(bf(mm_nt(grad_gu_b, gu_own)), GROUP))
    grad_gate_up_w = scatter_sum(bf(mm_tn(tokens_b, grad_gu_b)), ACROSS)
    grad_down_w = f32(scatter_sum(bf(mm_tn(inner_b, grad_down_b)), ACROSS))

    grad_resid_two, gain_grad_two = pull_two(grad_normed_two)
    grad_resid = grad_top + grad_resid_two
    grad_mixed, gain_grad_one = pull_one(grad_resid)
    grad_normed, grad_qkv_w, grad_out_w = attention_back(bf(grad_mixed))
    _, pull_zero = jax.vjp(rms_scale, x_rows, gain_vals[0])
    grad_x_zero, gain_grad_zero = pull_zero(grad_normed)
    input_grad = (grad_resid + grad_x_zero)[None]

    grad_gate_up_w = swap(grad_gate_up_w, GROUP).reshape(group, rows, 2, across, ff_piece)
    grad_gate_up_w = f32(jnp.transpose(grad_gate_up_w, (1, 2, 3, 0, 4)).reshape(rows, -1))
    gain_term = jnp.stack([gain_grad_zero, gain_grad_one, gain_grad_two, gain_grad_three], axis=0)
    grad_gains = lax.psum_scatter(gain_term, ALL, scatter_dimension=1, tiled=True)

    return (
        (block_out, input_grad)
        + adam_step(f32(w_qkv), grad_qkv_w, m_qkv, v_qkv, MATRIX_RATE, WEIGHT_DECAY)
        + adam_step(f32(w_out), grad_out_w, m_out, v_out, MATRIX_RATE, WEIGHT_DECAY)
        + adam_step(f32(w_gate_up), grad_gate_up_w, m_gate_up, v_gate_up, MATRIX_RATE, WEIGHT_DECAY)
        + adam_step(f32(w_down), grad_down_w, m_down, v_down, MATRIX_RATE, WEIGHT_DECAY)
        + adam_step(f32(gains), grad_gains, m_gains, v_gains, GAIN_RATE, 0.0)
    )


def solution(mesh):
    sizes = dict(mesh.shape)
    fine = Mesh(
        mesh.devices.reshape(sizes["dp"] // 2, 2, sizes["ctx"], sizes["fsdp"] // 2, 2),
        ("dh", "dl", "ctx", "fy", "core"),
    )
    acts = P(DP, PLANE, None)
    mats = P(ALL, None)
    vecs = P(None, ALL)
    ladder = sizes["dp"] == 4 and sizes["ctx"] == 2 and sizes["fsdp"] == 4
    return jax.shard_map(
        ladder_shards if ladder else wide_shards,
        mesh=fine,
        in_specs=(acts, P(DP, PLANE), acts) + (mats,) * 4 + (vecs,) + (mats,) * 8 + (vecs,) * 2,
        out_specs=(acts, acts) + (mats,) * 12 + (vecs,) * 3,
        check_vma=False,
    )
```

```python
import jax
import jax.numpy as jnp
from jax import lax
from jax.sharding import Mesh, PartitionSpec as P

HEADS = 8
KV_HEADS = 4
HEAD_DIM = 256
STEP = 10

NORM_EPS = 1e-06
SOFT_CAP = 50.0
THETA = 10000.0
BETA_ONE = 0.9
BETA_TWO = 0.95
ADAM_EPS = 1e-08
MATRIX_RATE = 0.03
GAIN_RATE = 0.2
WEIGHT_DECAY = 0.1

DP = ("dh", "dl")
PLANE = ("ctx", "fy", "core")
ALL = DP + PLANE
LADDER = DP + ("ctx",)
GROUP = PLANE
ACROSS = DP


def f32(v):
    return v.astype(jnp.float32)


def bf(v):
    return v.astype(jnp.bfloat16)


def dot(left, right, dims):
    return lax.dot_general(left, right, (dims, ((), ())), preferred_element_type=jnp.float32)


def mm(left, right):
    return dot(left, right, ((1,), (0,)))


def mm_nt(left, right):
    return dot(left, right, ((1,), (1,)))


def mm_tn(left, right):
    return dot(left, right, ((0,), (0,)))


def rms_scale(values, gain):
    inverse = lax.rsqrt(jnp.mean(values * values, axis=-1, keepdims=True) + NORM_EPS)
    return values * inverse * (1.0 + gain)


def rotary_tables(places):
    half = HEAD_DIM // 2
    freqs = THETA ** (-(jnp.arange(half, dtype=jnp.float32) * 2.0 / HEAD_DIM))
    angles = f32(places)[:, None] * freqs[None, :]
    return (jnp.cos(angles), jnp.sin(angles))


def rotary(values, cosine, sine):
    half = HEAD_DIM // 2
    first = values[..., :half]
    second = values[..., half:]
    return jnp.concatenate(
        [first * cosine - second * sine, second * cosine + first * sine], axis=-1
    )


def unrotary(values, cosine, sine):
    return rotary(values, cosine, -sine)


def adam_step(weight, grad, first, second, rate, decay):
    first_new = BETA_ONE * first + (1.0 - BETA_ONE) * grad
    second_new = BETA_TWO * second + (1.0 - BETA_TWO) * grad * grad
    ratio = (
        first_new
        / (1.0 - BETA_ONE**STEP)
        / (jnp.sqrt(second_new / (1.0 - BETA_TWO**STEP)) + ADAM_EPS)
    )
    return (weight - rate * (ratio + decay * weight), first_new, second_new)


def gather(v, axes, axis=0):
    return lax.all_gather(v, axes, axis=axis, tiled=True)


def scatter_sum(v, axes):
    return lax.psum_scatter(v, axes, scatter_dimension=0, tiled=True)


def swap(v, axes):
    return lax.all_to_all(v, axes, split_axis=0, concat_axis=0, tiled=True)


def hold(v):
    return lax.optimization_barrier(v)


def flip(v, axis):
    return lax.ppermute(v, axis, [(0, 1), (1, 0)])


def plane_gather(own):
    me = lax.axis_index(PLANE)
    over_y = flip(own, "fy")
    over_x = flip(own, "ctx")
    blocks = [own, over_y, over_x, flip(over_y, "ctx")]
    whole = jnp.zeros((8,) + own.shape, own.dtype)
    for bits, block in enumerate(blocks):
        whole = lax.dynamic_update_index_in_dim(whole, block, me ^ (2 * bits), 0)
        whole = lax.dynamic_update_index_in_dim(whole, flip(block, "core"), me ^ (2 * bits + 1), 0)
    return whole.reshape((-1,) + own.shape[1:])


def plane_scatter(parts):
    size = parts.shape[0] // 8
    half = size // 2
    col, row, core = (lax.axis_index(axis) for axis in PLANE)
    parts = parts.reshape((4, 2, size) + parts.shape[1:])
    sent = lax.dynamic_index_in_dim(parts, 1 - core, 1, keepdims=False)
    kept = lax.dynamic_index_in_dim(parts, core, 1, keepdims=False)
    both = bf(f32(kept) + f32(flip(sent, "core")))
    own, over_y, over_x, corner = (
        lax.dynamic_index_in_dim(both, (2 * col + row) ^ bits, 0, keepdims=False) for bits in range(4)
    )
    got_y = flip(corner[:half], "ctx")
    got_x = flip(corner[half:], "fy")
    over_y = jnp.concatenate([bf(f32(over_y[:half]) + f32(got_y)), over_y[half:]], axis=0)
    over_x = jnp.concatenate([over_x[:half], bf(f32(over_x[half:]) + f32(got_x))], axis=0)
    return f32(own) + f32(flip(over_x, "ctx")) + f32(flip(over_y, "fy"))


def line_gather(own):
    count = lax.axis_size(DP)
    row = [own]
    up, down = (own, own)
    for step in range(1, count):
        up = lax.ppermute(up, DP, [(i, i + 1) for i in range(step - 1, count - 1)])
        down = lax.ppermute(down, DP, [(i + 1, i) for i in range(count - step)])
        row = [up] + row + [down]
    return lax.dynamic_slice_in_dim(jnp.stack(row), count - 1 - lax.axis_index(DP), count, axis=0)


def ring_pairs():
    count = lax.axis_size(DP)
    ring = [2 * z for z in range(count)] + [2 * z + 1 for z in reversed(range(count))]
    onward = [(ring[i], ring[(i + 1) % len(ring)]) for i in range(len(ring))]
    return onward, [(b, a) for a, b in onward]


def ring_gather(own):
    onward, back = ring_pairs()
    half = own.shape[0] // 2
    steps = [[own]]
    behind, ahead = (own, own)
    for _ in range(len(onward) // 2 - 1):
        behind = lax.ppermute(behind, LADDER, onward)
        ahead = lax.ppermute(ahead, LADDER, back)
        steps.append([behind, ahead])
    steps.append(
        [
            lax.ppermute(behind[:half], LADDER, onward),
            lax.ppermute(ahead[half:], LADDER, back),
        ]
    )
    return steps


def two_parts(steps):
    return [
        jnp.concatenate(sum(steps[:3], []), axis=0),
        jnp.concatenate(sum(steps[3:], []), axis=0),
    ]


def steps_of(parts, size):
    early, late = parts
    steps = [early[:size], early[size : 3 * size], early[3 * size :]]
    return steps + [late[: 2 * size], late[2 * size :]]


def ring_scatter(pieces):
    onward, back = ring_pairs()
    size = pieces[0].shape[0]
    half = size // 2
    ahead = lax.ppermute(pieces[-1][:half], LADDER, onward)
    behind = lax.ppermute(pieces[-1][half:], LADDER, back)
    for step in range(len(pieces) - 2, 0, -1):
        to_behind, to_ahead = (pieces[step][:size], pieces[step][size:])
        if step == len(pieces) - 2:
            to_ahead = jnp.concatenate(
                [bf(f32(to_ahead[:half]) + f32(ahead)), to_ahead[half:]], axis=0
            )
            to_behind = jnp.concatenate(
                [to_behind[:half], bf(f32(to_behind[half:]) + f32(behind))], axis=0
            )
        else:
            to_ahead = bf(f32(to_ahead) + f32(ahead))
            to_behind = bf(f32(to_behind) + f32(behind))
        to_ahead, to_behind = hold((to_ahead, to_behind))
        ahead = lax.ppermute(to_ahead, LADDER, onward)
        behind = lax.ppermute(to_behind, LADDER, back)
    return f32(pieces[0]) + f32(ahead) + f32(behind)


def quad_blocks(own, late=None):
    over_y = flip(own, "fy")
    if late is not None:
        over_y, _ = hold((over_y, late))
    return [own, flip(own, "core"), over_y, flip(over_y, "core")]


def quad_place(blocks, parts):
    me = lax.axis_index(("fy", "core"))
    count, rows, cols = blocks[0][0].shape
    whole = jnp.zeros((count, 4, rows, parts * cols), blocks[0][0].dtype)
    for part in range(parts):
        for bits, block in enumerate(blocks[part]):
            whole = lax.dynamic_update_slice(
                whole, block[:, None], (0, me ^ bits, 0, part * cols)
            )
    return whole


def core_sum(parts, late):
    core = lax.axis_index("core")
    parts = parts.reshape(parts.shape[:1] + (2, 2) + parts.shape[2:])
    sent = lax.dynamic_index_in_dim(parts, 1 - core, 2, keepdims=False)
    kept = lax.dynamic_index_in_dim(parts, core, 2, keepdims=False)
    kept, got, _ = hold((kept, flip(sent, "core"), late))
    return bf(f32(kept) + f32(got))


def row_sum(both, late=()):
    row = lax.axis_index("fy")
    sent = lax.dynamic_index_in_dim(both, 1 - row, 1, keepdims=False)
    kept = lax.dynamic_index_in_dim(both, row, 1, keepdims=False)
    kept, got, _ = hold((kept, flip(sent, "fy"), late))
    return bf(f32(kept) + f32(got))


def ladder_shards(
    hidden_in,
    positions,
    cotangent,
    w_qkv,
    w_out,
    w_gate_up,
    w_down,
    gains,
    m_qkv,
    v_qkv,
    m_out,
    v_out,
    m_gate_up,
    v_gate_up,
    m_down,
    v_down,
    m_gains,
    v_gains,
):
    x_own = hidden_in[0]
    tok, width = x_own.shape
    rows = w_qkv.shape[0]
    planes = lax.axis_size(DP)
    group = lax.axis_size(LADDER)
    q_width = HEADS * HEAD_DIM
    core = lax.axis_index("core")

    q_cols = w_qkv[:, :q_width].reshape(rows, HEADS, HEAD_DIM)
    kv_cols = w_qkv[:, q_width:].reshape(rows, 2, KV_HEADS, HEAD_DIM)
    kv_cols = jnp.swapaxes(kv_cols, 1, 2).reshape(rows, HEADS, HEAD_DIM)
    pieces = jnp.swapaxes(jnp.concatenate([q_cols, kv_cols], axis=2), 0, 1)
    first = jnp.stack([positions[0, 0] // 128, positions[0, 0] % 128])
    own_gains = jnp.concatenate([gains.reshape(4 * rows), bf(first)])[None, None]
    own_gains = jnp.pad(own_gains, ((0, 0), (0, 7), (0, 2 * HEAD_DIM - 4 * rows - 2)))
    pieces = jnp.concatenate(
        [pieces, jnp.broadcast_to(own_gains, (HEADS,) + own_gains.shape[1:])], axis=1
    )
    got = swap(pieces, PLANE)
    got, x_sent, out_line = hold((got, x_own, w_out))
    x_all = plane_gather(x_sent)
    out_line = line_gather(out_line)
    first = got[:, rows, 4 * rows : 4 * rows + 2].astype(jnp.int32)
    pos_all = first[:, :1] * 128 + first[:, 1:] + jnp.arange(tok, dtype=jnp.int32)[None]
    pos_all = pos_all.reshape(-1)
    cosine, sine = rotary_tables(pos_all)
    got = lax.all_gather(got, DP)
    ff_own = w_down.shape[0] * 4
    cols = []
    for part in range(2):
        piece = w_gate_up[:, part * group * ff_own : (part + 1) * group * ff_own]
        cols.append(jnp.swapaxes(piece.reshape(rows, group, ff_own), 0, 1))
    got, cols[0] = hold((got, cols[0]))
    w_own = got[:, :, :rows].reshape(width, 2 * HEAD_DIM)
    gain_vals = got[:, :, rows, : 4 * rows].reshape(planes * HEADS, 4, rows)
    gain_vals = f32(jnp.swapaxes(gain_vals, 0, 1).reshape(4, width))
    out_full = lax.all_gather(out_line, PLANE, axis=1, tiled=False).reshape(q_width, width)
    cols[0] = swap(cols[0], LADDER)

    normed_all = hold(bf(rms_scale(f32(x_all), gain_vals[0])))
    qkv = mm(normed_all, w_own)
    query = bf(rotary(qkv[:, :HEAD_DIM], cosine, sine) * HEAD_DIM ** (-0.5))
    half = qkv[:, HEAD_DIM:]
    mine = jnp.where(core == 0, bf(rotary(half, cosine, sine)), bf(half))
    other = flip(mine, "core")
    key = jnp.where(core == 0, mine, other)
    value = jnp.where(core == 0, other, mine)
    scores = mm_nt(query, key)
    capped = SOFT_CAP * jnp.tanh(scores / SOFT_CAP)
    weights = jnp.where(pos_all[:, None] >= pos_all[None, :], jnp.exp(capped), 0.0)
    weights_b = bf(weights)
    total = jnp.sum(weights, axis=-1, keepdims=True)
    attn = mm(weights_b, value) / total
    cols[0], attn_sent = hold((cols[0], bf(attn)))
    attn_own = swap(attn_sent.reshape(HEADS, tok, HEAD_DIM), PLANE)
    cols[0], cols[1], _ = hold((cols[0], cols[1], attn_own))
    cols[1] = swap(cols[1], LADDER)
    attn_own = jnp.swapaxes(attn_own, 0, 1).reshape(tok, q_width)
    mixed = mm(attn_own, out_full)

    x_rows = f32(x_own)
    branch_one, pull_one = jax.vjp(rms_scale, mixed, gain_vals[1])
    resid = x_rows + branch_one
    normed_two, pull_two = jax.vjp(rms_scale, resid, gain_vals[2])

    tokens_own = bf(normed_two)
    steps = ring_gather(tokens_own)
    cols[1], _ = hold((cols[1], tokens_own))
    w_down_late, _ = hold((w_down, steps[2][0]))
    down_own = quad_place([quad_blocks(w_down_late[None])], 1).reshape(ff_own, width)
    gate_up_own = [quad_blocks(cols[0], tokens_own), quad_blocks(cols[1])]
    gate_up_own = quad_place(gate_up_own, 2).reshape(width, 2 * ff_own)
    tokens = jnp.concatenate(sum(steps, []), axis=0)
    gate_up = mm(tokens, gate_up_own)

    def gated(gate, up_part):
        return jax.nn.gelu(gate, approximate=True) * up_part

    inner = bf(gated(gate_up[:, :ff_own], gate_up[:, ff_own:]))
    late = tokens.shape[0] - 3 * tok
    down = bf(mm(inner, down_own))
    attn_cols = attn_own.reshape(tok, planes, HEADS, w_out.shape[0])
    attn_cols = jnp.transpose(attn_cols, (2, 0, 1, 3)).reshape(HEADS, tok, HEAD_DIM)
    attn_cols, down = hold((attn_cols, down))
    attn_cols = swap(attn_cols, PLANE)
    attn_cols = jnp.pad(attn_cols, ((0, 0), (0, 16), (0, 0))).reshape(-1, HEAD_DIM)
    down = ring_scatter(steps_of((down[:late], down[late:]), tok))
    down, attn_cols = hold((down, attn_cols))
    branch_two, pull_three = jax.vjp(rms_scale, down, gain_vals[3])
    block_out = bf(resid + branch_two)[None]
    grad_top = f32(cotangent[0])
    grad_down_in, gain_grad_three = pull_three(grad_top)
    steps = ring_gather(bf(grad_down_in))
    grad_downs = two_parts(steps)
    grad_gus, parts = ([], [])
    for piece, kept in zip(grad_downs, (gate_up[:late], gate_up[late:])):
        _, pull = jax.vjp(gated, kept[:, :ff_own], kept[:, ff_own:])
        grad_gus.append(bf(jnp.concatenate(pull(mm_nt(piece, down_own)), axis=1)))
        grad_gu, _ = hold((grad_gus[-1], steps[3][0]))
        parts.append(bf(mm_nt(grad_gu, gate_up_own)))
    tokens, inner, grad_downs, grad_gus, parts = hold(
        (tokens, inner, grad_downs, grad_gus, parts)
    )
    grad_normed_two = ring_scatter(steps_of(parts, tok))
    grad_gu_b = jnp.concatenate(grad_gus, axis=0)
    grad_halves = [bf(mm_tn(tokens, grad_gu_b[:, :ff_own])), bf(mm_tn(tokens, grad_gu_b[:, ff_own:]))]
    grad_down_w = bf(mm_tn(inner, jnp.concatenate(grad_downs, axis=0)))
    grad_normed_two, _, _ = hold((grad_normed_two, grad_halves, grad_down_w))
    grad_resid_two, _ = pull_two(grad_normed_two)
    grad_resid = grad_top + grad_resid_two
    grad_mixed, gain_grad_one = pull_one(grad_resid)
    grad_mixed_b = bf(grad_mixed)

    grad_attn = bf(mm_nt(grad_mixed_b, out_full)).reshape(tok, HEADS, HEAD_DIM)
    grad_head = swap(jnp.swapaxes(grad_attn, 0, 1), PLANE).reshape(HEADS * tok, HEAD_DIM)
    grad_head = f32(grad_head)
    rho = bf(grad_head / total)
    delta = jnp.sum(grad_head * attn, axis=-1, keepdims=True) / total
    pulled = mm_nt(rho, value)
    grad_scores = bf((pulled - delta) * weights * (1.0 - (capped / SOFT_CAP) ** 2))
    grad_query = mm(grad_scores, key) * HEAD_DIM ** (-0.5)
    grad_key = mm_tn(grad_scores, query)
    grad_value = mm_tn(weights_b, rho)
    sent = jnp.where(core == 0, grad_value, grad_key)
    grad_half = jnp.where(core == 0, grad_key, grad_value) + flip(sent, "core")
    grad_half = jnp.where(core == 0, unrotary(grad_half, cosine, sine), grad_half)
    grad_qkv = bf(jnp.concatenate([unrotary(grad_query, cosine, sine), grad_half], axis=1))
    others = bf(jnp.stack([gain_grad_one, gain_grad_three]))
    others = jnp.concatenate([grad_mixed_b, jnp.pad(others, ((0, 14), (0, 0)))], axis=0)
    others = lax.all_gather(others, PLANE)
    grad_qkv, others = hold((grad_qkv, others))
    grad_mixed_all = others.reshape(-1, width)
    others = jnp.sum(f32(others[:, tok : tok + 2]), axis=0).reshape(2, planes, HEADS, rows)
    others = lax.dynamic_index_in_dim(others, lax.axis_index(PLANE), 2, keepdims=False)
    others = jnp.swapaxes(others, 0, 1).reshape(planes, 1, 2 * rows)
    others = bf(jnp.pad(others, ((0, 0), (0, 7), (0, 2 * HEAD_DIM - 2 * rows))))
    grad_w = bf(mm_tn(normed_all, grad_qkv))
    grad_qkv, grad_w = hold((grad_qkv, grad_w))
    sums = [
        core_sum(v.reshape(group, 4, rows, ff_own), late)
        for v, late in zip(grad_halves, (grad_head, grad_qkv))
    ]
    sums.append(core_sum(grad_down_w.reshape(1, 4, ff_own // 4, width), grad_qkv))
    grad_w = grad_w.reshape(planes, -1, 2 * HEAD_DIM)
    grad_out_w = bf(mm_tn(attn_cols, grad_mixed_all)).reshape(planes, -1, 2 * HEAD_DIM)
    grad_w = jnp.concatenate([grad_w, grad_out_w, others], axis=1)
    grad_w, grad_qkv = hold((grad_w, grad_qkv))
    grad_normed = plane_scatter(bf(mm_nt(grad_qkv, w_own)))
    grad_w = scatter_sum(grad_w, DP)[0]
    grad_halves = [swap(row_sum(sums[0]), LADDER)]
    grad_halves.append(row_sum(sums[1], grad_halves[0]))
    grad_down_w, grad_halves[1] = hold((sums[2], grad_halves[1]))
    grad_down_w = f32(row_sum(grad_down_w)[0])
    others = f32(grad_w[-8, : 2 * rows]).reshape(2, rows)
    grad_out_w = f32(grad_w[HEADS * rows : -8].reshape(w_out.shape))
    grad_w = grad_w[: HEADS * rows].reshape(HEADS, rows, 2 * HEAD_DIM)
    grad_halves[1] = swap(grad_halves[1], LADDER)
    grad_w, grad_halves[1], grad_normed = hold((grad_w, grad_halves[1], grad_normed))
    grad_halves = [jnp.swapaxes(v, 0, 1).reshape(rows, group * ff_own) for v in grad_halves]
    grad_gate_up_w = f32(jnp.concatenate(grad_halves, axis=1))
    _, pull_zero = jax.vjp(rms_scale, x_rows, gain_vals[0])
    grad_x_zero, _ = pull_zero(grad_normed)
    input_grad = (grad_resid + grad_x_zero)[None]
    grad_w = f32(jnp.swapaxes(swap(grad_w, PLANE), 0, 1))
    grad_q_w = grad_w[:, :, :HEAD_DIM].reshape(rows, q_width)
    grad_kv_w = grad_w[:, :, HEAD_DIM:].reshape(rows, KV_HEADS, 2, HEAD_DIM)
    grad_kv_w = jnp.swapaxes(grad_kv_w, 1, 2).reshape(rows, q_width)
    grad_qkv_w = jnp.concatenate([grad_q_w, grad_kv_w], axis=1)

    gain_zero = jnp.sum(f32(w_qkv) * grad_qkv_w, axis=1) / (1.0 + f32(gains[0]))
    gain_two = jnp.sum(f32(w_gate_up) * grad_gate_up_w, axis=1) / (1.0 + f32(gains[2]))
    grad_gains = jnp.stack([gain_zero, others[0], gain_two, others[1]], axis=0)

    return (
        (block_out, input_grad)
        + adam_step(f32(w_qkv), grad_qkv_w, m_qkv, v_qkv, MATRIX_RATE, WEIGHT_DECAY)
        + adam_step(f32(w_out), grad_out_w, m_out, v_out, MATRIX_RATE, WEIGHT_DECAY)
        + adam_step(f32(w_gate_up), grad_gate_up_w, m_gate_up, v_gate_up, MATRIX_RATE, WEIGHT_DECAY)
        + adam_step(f32(w_down), grad_down_w, m_down, v_down, MATRIX_RATE, WEIGHT_DECAY)
        + adam_step(f32(gains), grad_gains, m_gains, v_gains, GAIN_RATE, 0.0)
    )


def token_attention(x_own, pos_own, w_qkv, w_out, gains):
    tok = x_own.shape[0]
    q_width = HEADS * HEAD_DIM
    k_width = KV_HEADS * HEAD_DIM
    groups = HEADS // KV_HEADS
    qkv_full = gather(w_qkv, ALL)
    out_full = gather(w_out, ALL)
    gain_vals = f32(gather(gains, ALL, 1))
    normed = bf(rms_scale(f32(x_own), gain_vals[0]))
    qkv = mm(normed, qkv_full)
    cosine, sine = rotary_tables(pos_own)
    cosine, sine = (cosine[:, None, :], sine[:, None, :])
    query = rotary(qkv[:, :q_width].reshape(tok, HEADS, HEAD_DIM), cosine, sine)
    query = bf(query * HEAD_DIM ** (-0.5)).reshape(tok, KV_HEADS, groups, HEAD_DIM)
    key_own = qkv[:, q_width : q_width + k_width].reshape(tok, KV_HEADS, HEAD_DIM)
    key = gather(bf(rotary(key_own, cosine, sine)), PLANE)
    value = gather(bf(qkv[:, q_width + k_width :]).reshape(tok, KV_HEADS, HEAD_DIM), PLANE)
    pos_all = gather(pos_own, PLANE)
    count = pos_all.shape[0]
    scores = jnp.einsum("tgjd,sgd->gjts", query, key, preferred_element_type=jnp.float32)
    capped = SOFT_CAP * jnp.tanh(scores / SOFT_CAP)
    weights = jnp.where(pos_own[:, None] >= pos_all[None, :], jnp.exp(capped), 0.0)
    weights_b = bf(weights)
    total = jnp.sum(weights, axis=-1)
    attn = jnp.einsum("gjts,sgd->gjtd", weights_b, value, preferred_element_type=jnp.float32)
    attn = attn / total[..., None]
    attn_b = bf(jnp.transpose(attn, (2, 0, 1, 3)).reshape(tok, q_width))
    mixed = mm(attn_b, out_full)

    def backward(grad_mixed_b):
        grad_attn = mm_nt(grad_mixed_b, out_full).reshape(tok, KV_HEADS, groups, HEAD_DIM)
        grad_heads = jnp.transpose(grad_attn, (1, 2, 0, 3))
        rho = bf(grad_heads / total[..., None])
        delta = jnp.sum(grad_heads * attn, axis=-1) / total
        pulled = jnp.einsum("gjtd,sgd->gjts", rho, value, preferred_element_type=jnp.float32)
        grad_scores = bf(
            (pulled - delta[..., None]) * weights * (1.0 - (capped / SOFT_CAP) ** 2)
        )
        grad_query = jnp.einsum(
            "gjts,sgd->tgjd", grad_scores, key, preferred_element_type=jnp.float32
        ).reshape(tok, HEADS, HEAD_DIM)
        grad_key = jnp.einsum(
            "gjts,tgjd->sgd", grad_scores, query, preferred_element_type=jnp.float32
        ).reshape(count, k_width)
        grad_value = jnp.einsum(
            "gjts,gjtd->sgd", weights_b, rho, preferred_element_type=jnp.float32
        ).reshape(count, k_width)
        grad_kv = scatter_sum(jnp.concatenate([grad_key, grad_value], axis=1), PLANE)
        grad_query = unrotary(grad_query * HEAD_DIM ** (-0.5), cosine, sine)
        grad_key = unrotary(grad_kv[:, :k_width].reshape(tok, KV_HEADS, HEAD_DIM), cosine, sine)
        grad_qkv = bf(
            jnp.concatenate(
                [
                    grad_query.reshape(tok, q_width),
                    grad_key.reshape(tok, k_width),
                    grad_kv[:, k_width:],
                ],
                axis=1,
            )
        )
        grad_normed = mm_nt(grad_qkv, qkv_full)
        grad_qkv_w = f32(scatter_sum(bf(mm_tn(normed, grad_qkv)), ALL))
        grad_out_w = f32(scatter_sum(bf(mm_tn(attn_b, grad_mixed_b)), ALL))
        return grad_normed, grad_qkv_w, grad_out_w

    return mixed, gain_vals, backward


def wide_shards(
    hidden_in,
    positions,
    cotangent,
    w_qkv,
    w_out,
    w_gate_up,
    w_down,
    gains,
    m_qkv,
    v_qkv,
    m_out,
    v_out,
    m_gate_up,
    v_gate_up,
    m_down,
    v_down,
    m_gains,
    v_gains,
):
    x_own = hidden_in[0]
    rows, width = (w_qkv.shape[0], x_own.shape[1])
    group, across = (lax.axis_size(GROUP), lax.axis_size(ACROSS))
    ff_piece = w_down.shape[0]
    ff_own = across * ff_piece
    gu_pieces = w_gate_up.reshape(rows, 2, across, group, ff_piece)
    gu_pieces = jnp.transpose(gu_pieces, (3, 0, 1, 2, 4)).reshape(group * rows, 2 * ff_own)

    mixed, gain_vals, attention_back = token_attention(x_own, positions[0], w_qkv, w_out, gains)
    gu_own = gather(swap(gu_pieces, GROUP), ACROSS)
    down_own = gather(w_down, ACROSS)

    x_rows = f32(x_own)
    branch_one, pull_one = jax.vjp(rms_scale, mixed, gain_vals[1])
    resid = x_rows + branch_one
    normed_two, pull_two = jax.vjp(rms_scale, resid, gain_vals[2])
    tokens_b = gather(bf(normed_two), GROUP)
    gate_up = mm(tokens_b, gu_own)
    inner, pull_gelu = jax.vjp(
        lambda gate, up_part: jax.nn.gelu(gate, approximate=True) * up_part,
        gate_up[:, :ff_own],
        gate_up[:, ff_own:],
    )
    inner_b = bf(inner)
    down = f32(scatter_sum(bf(mm(inner_b, down_own)), GROUP))
    branch_two, pull_three = jax.vjp(rms_scale, down, gain_vals[3])
    block_out = bf(resid + branch_two)[None]
    grad_top = f32(cotangent[0])
    grad_down_in, gain_grad_three = pull_three(grad_top)
    grad_down_b = gather(bf(grad_down_in), GROUP)
    grad_gate, grad_up = pull_gelu(mm_nt(grad_down_b, down_own))
    grad_gu_b = bf(jnp.concatenate([grad_gate, grad_up], axis=1))
    grad_normed_two = f32(scatter_sum(bf(mm_nt(grad_gu_b, gu_own)), GROUP))
    grad_gate_up_w = scatter_sum(bf(mm_tn(tokens_b, grad_gu_b)), ACROSS)
    grad_down_w = f32(scatter_sum(bf(mm_tn(inner_b, grad_down_b)), ACROSS))

    grad_resid_two, gain_grad_two = pull_two(grad_normed_two)
    grad_resid = grad_top + grad_resid_two
    grad_mixed, gain_grad_one = pull_one(grad_resid)
    grad_normed, grad_qkv_w, grad_out_w = attention_back(bf(grad_mixed))
    _, pull_zero = jax.vjp(rms_scale, x_rows, gain_vals[0])
    grad_x_zero, gain_grad_zero = pull_zero(grad_normed)
    input_grad = (grad_resid + grad_x_zero)[None]

    grad_gate_up_w = swap(grad_gate_up_w, GROUP).reshape(group, rows, 2, across, ff_piece)
    grad_gate_up_w = f32(jnp.transpose(grad_gate_up_w, (1, 2, 3, 0, 4)).reshape(rows, -1))
    gain_term = jnp.stack([gain_grad_zero, gain_grad_one, gain_grad_two, gain_grad_three], axis=0)
    grad_gains = lax.psum_scatter(gain_term, ALL, scatter_dimension=1, tiled=True)

    return (
        (block_out, input_grad)
        + adam_step(f32(w_qkv), grad_qkv_w, m_qkv, v_qkv, MATRIX_RATE, WEIGHT_DECAY)
        + adam_step(f32(w_out), grad_out_w, m_out, v_out, MATRIX_RATE, WEIGHT_DECAY)
        + adam_step(f32(w_gate_up), grad_gate_up_w, m_gate_up, v_gate_up, MATRIX_RATE, WEIGHT_DECAY)
        + adam_step(f32(w_down), grad_down_w, m_down, v_down, MATRIX_RATE, WEIGHT_DECAY)
        + adam_step(f32(gains), grad_gains, m_gains, v_gains, GAIN_RATE, 0.0)
    )


def solution(mesh):
    sizes = dict(mesh.shape)
    fine = Mesh(
        mesh.devices.reshape(sizes["dp"] // 2, 2, sizes["ctx"], sizes["fsdp"] // 2, 2),
        ("dh", "dl", "ctx", "fy", "core"),
    )
    acts = P(DP, PLANE, None)
    mats = P(ALL, None)
    vecs = P(None, ALL)
    ladder = sizes["dp"] == 4 and sizes["ctx"] == 2 and sizes["fsdp"] == 4
    return jax.shard_map(
        ladder_shards if ladder else wide_shards,
        mesh=fine,
        in_specs=(acts, P(DP, PLANE), acts) + (mats,) * 4 + (vecs,) + (mats,) * 8 + (vecs,) * 2,
        out_specs=(acts, acts) + (mats,) * 12 + (vecs,) * 3,
        check_vma=False,
    )
```

```python
import jax
import jax.numpy as jnp
from jax import lax
from jax.sharding import Mesh, PartitionSpec as P

HEADS = 8
KV_HEADS = 4
HEAD_DIM = 256
STEP = 10

NORM_EPS = 1e-06
SOFT_CAP = 50.0
THETA = 10000.0
BETA_ONE = 0.9
BETA_TWO = 0.95
ADAM_EPS = 1e-08
MATRIX_RATE = 0.03
GAIN_RATE = 0.2
WEIGHT_DECAY = 0.1

DP = ("dh", "dl")
PLANE = ("ctx", "fy", "core")
ALL = DP + PLANE
LADDER = DP + ("ctx",)
GROUP = PLANE
ACROSS = DP


def f32(v):
    return v.astype(jnp.float32)


def bf(v):
    return v.astype(jnp.bfloat16)


def dot(left, right, dims):
    return lax.dot_general(left, right, (dims, ((), ())), preferred_element_type=jnp.float32)


def mm(left, right):
    return dot(left, right, ((1,), (0,)))


def mm_nt(left, right):
    return dot(left, right, ((1,), (1,)))


def mm_tn(left, right):
    return dot(left, right, ((0,), (0,)))


def rms_scale(values, gain):
    inverse = lax.rsqrt(jnp.mean(values * values, axis=-1, keepdims=True) + NORM_EPS)
    return values * inverse * (1.0 + gain)


def rotary_tables(places):
    half = HEAD_DIM // 2
    freqs = THETA ** (-(jnp.arange(half, dtype=jnp.float32) * 2.0 / HEAD_DIM))
    angles = f32(places)[:, None] * freqs[None, :]
    return (jnp.cos(angles), jnp.sin(angles))


def rotary(values, cosine, sine):
    half = HEAD_DIM // 2
    first = values[..., :half]
    second = values[..., half:]
    return jnp.concatenate(
        [first * cosine - second * sine, second * cosine + first * sine], axis=-1
    )


def unrotary(values, cosine, sine):
    return rotary(values, cosine, -sine)


def adam_step(weight, grad, first, second, rate, decay):
    first_new = BETA_ONE * first + (1.0 - BETA_ONE) * grad
    second_new = BETA_TWO * second + (1.0 - BETA_TWO) * grad * grad
    ratio = (
        first_new
        / (1.0 - BETA_ONE**STEP)
        / (jnp.sqrt(second_new / (1.0 - BETA_TWO**STEP)) + ADAM_EPS)
    )
    return (weight - rate * (ratio + decay * weight), first_new, second_new)


def gather(v, axes, axis=0):
    return lax.all_gather(v, axes, axis=axis, tiled=True)


def scatter_sum(v, axes):
    return lax.psum_scatter(v, axes, scatter_dimension=0, tiled=True)


def swap(v, axes):
    return lax.all_to_all(v, axes, split_axis=0, concat_axis=0, tiled=True)


def hold(v):
    return lax.optimization_barrier(v)


def flip(v, axis):
    return lax.ppermute(v, axis, [(0, 1), (1, 0)])


def plane_gather(own):
    me = lax.axis_index(PLANE)
    over_y = flip(own, "fy")
    over_x = flip(own, "ctx")
    blocks = [own, over_y, over_x, flip(over_y, "ctx")]
    whole = jnp.zeros((8,) + own.shape, own.dtype)
    for bits, block in enumerate(blocks):
        whole = lax.dynamic_update_index_in_dim(whole, block, me ^ (2 * bits), 0)
        whole = lax.dynamic_update_index_in_dim(whole, flip(block, "core"), me ^ (2 * bits + 1), 0)
    return whole.reshape((-1,) + own.shape[1:])


def plane_scatter(parts):
    size = parts.shape[0] // 8
    half = size // 2
    col, row, core = (lax.axis_index(axis) for axis in PLANE)
    parts = parts.reshape((4, 2, size) + parts.shape[1:])
    sent = lax.dynamic_index_in_dim(parts, 1 - core, 1, keepdims=False)
    kept = lax.dynamic_index_in_dim(parts, core, 1, keepdims=False)
    both = bf(f32(kept) + f32(flip(sent, "core")))
    own, over_y, over_x, corner = (
        lax.dynamic_index_in_dim(both, (2 * col + row) ^ bits, 0, keepdims=False) for bits in range(4)
    )
    got_y = flip(corner[:half], "ctx")
    got_x = flip(corner[half:], "fy")
    over_y = jnp.concatenate([bf(f32(over_y[:half]) + f32(got_y)), over_y[half:]], axis=0)
    over_x = jnp.concatenate([over_x[:half], bf(f32(over_x[half:]) + f32(got_x))], axis=0)
    return f32(own) + f32(flip(over_x, "ctx")) + f32(flip(over_y, "fy"))


def line_gather(own):
    count = lax.axis_size(DP)
    row = [own]
    up, down = (own, own)
    for step in range(1, count):
        up = lax.ppermute(up, DP, [(i, i + 1) for i in range(step - 1, count - 1)])
        down = lax.ppermute(down, DP, [(i + 1, i) for i in range(count - step)])
        row = [up] + row + [down]
    return lax.dynamic_slice_in_dim(jnp.stack(row), count - 1 - lax.axis_index(DP), count, axis=0)


def ring_pairs():
    count = lax.axis_size(DP)
    ring = [2 * z for z in range(count)] + [2 * z + 1 for z in reversed(range(count))]
    onward = [(ring[i], ring[(i + 1) % len(ring)]) for i in range(len(ring))]
    return onward, [(b, a) for a, b in onward]


def ring_gather(own):
    onward, back = ring_pairs()
    half = own.shape[0] // 2
    steps = [[own]]
    behind, ahead = (own, own)
    for _ in range(len(onward) // 2 - 1):
        behind = lax.ppermute(behind, LADDER, onward)
        ahead = lax.ppermute(ahead, LADDER, back)
        steps.append([behind, ahead])
    steps.append(
        [
            lax.ppermute(behind[:half], LADDER, onward),
            lax.ppermute(ahead[half:], LADDER, back),
        ]
    )
    return steps


def two_parts(steps):
    return [
        jnp.concatenate(sum(steps[:3], []), axis=0),
        jnp.concatenate(sum(steps[3:], []), axis=0),
    ]


def steps_of(parts, size):
    early, late = parts
    steps = [early[:size], early[size : 3 * size], early[3 * size :]]
    return steps + [late[: 2 * size], late[2 * size :]]


def ring_scatter(pieces):
    onward, back = ring_pairs()
    size = pieces[0].shape[0]
    half = size // 2
    ahead = lax.ppermute(pieces[-1][:half], LADDER, onward)
    behind = lax.ppermute(pieces[-1][half:], LADDER, back)
    for step in range(len(pieces) - 2, 0, -1):
        to_behind, to_ahead = (pieces[step][:size], pieces[step][size:])
        if step == len(pieces) - 2:
            to_ahead = jnp.concatenate(
                [bf(f32(to_ahead[:half]) + f32(ahead)), to_ahead[half:]], axis=0
            )
            to_behind = jnp.concatenate(
                [to_behind[:half], bf(f32(to_behind[half:]) + f32(behind))], axis=0
            )
        else:
            to_ahead = bf(f32(to_ahead) + f32(ahead))
            to_behind = bf(f32(to_behind) + f32(behind))
        to_ahead, to_behind = hold((to_ahead, to_behind))
        ahead = lax.ppermute(to_ahead, LADDER, onward)
        behind = lax.ppermute(to_behind, LADDER, back)
    return f32(pieces[0]) + f32(ahead) + f32(behind)


def quad_blocks(own, late=None):
    over_y = flip(own, "fy")
    if late is not None:
        over_y, _ = hold((over_y, late))
    return [own, flip(own, "core"), over_y, flip(over_y, "core")]


def quad_place(blocks, parts):
    me = lax.axis_index(("fy", "core"))
    count, rows, cols = blocks[0][0].shape
    whole = jnp.zeros((count, 4, rows, parts * cols), blocks[0][0].dtype)
    for part in range(parts):
        for bits, block in enumerate(blocks[part]):
            whole = lax.dynamic_update_slice(
                whole, block[:, None], (0, me ^ bits, 0, part * cols)
            )
    return whole


def core_sum(parts, late):
    core = lax.axis_index("core")
    parts = parts.reshape(parts.shape[:1] + (2, 2) + parts.shape[2:])
    sent = lax.dynamic_index_in_dim(parts, 1 - core, 2, keepdims=False)
    kept = lax.dynamic_index_in_dim(parts, core, 2, keepdims=False)
    kept, got, _ = hold((kept, flip(sent, "core"), late))
    return bf(f32(kept) + f32(got))


def row_sum(both, late=()):
    row = lax.axis_index("fy")
    sent = lax.dynamic_index_in_dim(both, 1 - row, 1, keepdims=False)
    kept = lax.dynamic_index_in_dim(both, row, 1, keepdims=False)
    kept, got, _ = hold((kept, flip(sent, "fy"), late))
    return bf(f32(kept) + f32(got))


def ladder_shards(
    hidden_in,
    positions,
    cotangent,
    w_qkv,
    w_out,
    w_gate_up,
    w_down,
    gains,
    m_qkv,
    v_qkv,
    m_out,
    v_out,
    m_gate_up,
    v_gate_up,
    m_down,
    v_down,
    m_gains,
    v_gains,
):
    x_own = hidden_in[0]
    tok, width = x_own.shape
    rows = w_qkv.shape[0]
    planes = lax.axis_size(DP)
    group = lax.axis_size(LADDER)
    q_width = HEADS * HEAD_DIM
    core = lax.axis_index("core")

    q_cols = w_qkv[:, :q_width].reshape(rows, HEADS, HEAD_DIM)
    kv_cols = w_qkv[:, q_width:].reshape(rows, 2, KV_HEADS, HEAD_DIM)
    kv_cols = jnp.swapaxes(kv_cols, 1, 2).reshape(rows, HEADS, HEAD_DIM)
    pieces = jnp.swapaxes(jnp.concatenate([q_cols, kv_cols], axis=2), 0, 1)
    first = jnp.stack([positions[0, 0] // 128, positions[0, 0] % 128])
    own_gains = jnp.concatenate([gains.reshape(4 * rows), bf(first)])[None, None]
    own_gains = jnp.pad(own_gains, ((0, 0), (0, 7), (0, 2 * HEAD_DIM - 4 * rows - 2)))
    pieces = jnp.concatenate(
        [pieces, jnp.broadcast_to(own_gains, (HEADS,) + own_gains.shape[1:])], axis=1
    )
    got = swap(pieces, PLANE)
    got, x_sent, out_line = hold((got, x_own, w_out))
    x_all = plane_gather(x_sent)
    out_line = line_gather(out_line)
    first = got[:, rows, 4 * rows : 4 * rows + 2].astype(jnp.int32)
    pos_all = first[:, :1] * 128 + first[:, 1:] + jnp.arange(tok, dtype=jnp.int32)[None]
    pos_all = pos_all.reshape(-1)
    cosine, sine = rotary_tables(pos_all)
    got = lax.all_gather(got, DP)
    ff_own = w_down.shape[0] * 4
    cols = []
    for part in range(2):
        piece = w_gate_up[:, part * group * ff_own : (part + 1) * group * ff_own]
        cols.append(jnp.swapaxes(piece.reshape(rows, group, ff_own), 0, 1))
    got, cols[0] = hold((got, cols[0]))
    w_own = got[:, :, :rows].reshape(width, 2 * HEAD_DIM)
    gain_vals = got[:, :, rows, : 4 * rows].reshape(planes * HEADS, 4, rows)
    gain_vals = f32(jnp.swapaxes(gain_vals, 0, 1).reshape(4, width))
    out_full = lax.all_gather(out_line, PLANE, axis=1, tiled=False).reshape(q_width, width)
    cols[0] = swap(cols[0], LADDER)

    normed_all = hold(bf(rms_scale(f32(x_all), gain_vals[0])))
    qkv = mm(normed_all, w_own)
    query = bf(rotary(qkv[:, :HEAD_DIM], cosine, sine) * HEAD_DIM ** (-0.5))
    half = qkv[:, HEAD_DIM:]
    mine = jnp.where(core == 0, bf(rotary(half, cosine, sine)), bf(half))
    other = flip(mine, "core")
    key = jnp.where(core == 0, mine, other)
    value = jnp.where(core == 0, other, mine)
    scores = mm_nt(query, key)
    capped = SOFT_CAP * jnp.tanh(scores / SOFT_CAP)
    weights = jnp.where(pos_all[:, None] >= pos_all[None, :], jnp.exp(capped), 0.0)
    weights_b = bf(weights)
    total = jnp.sum(weights, axis=-1, keepdims=True)
    attn = mm(weights_b, value) / total
    cols[0], attn_sent = hold((cols[0], bf(attn)))
    attn_own = swap(attn_sent.reshape(HEADS, tok, HEAD_DIM), PLANE)
    cols[0], cols[1], _ = hold((cols[0], cols[1], attn_own))
    cols[1] = swap(cols[1], LADDER)
    attn_own = jnp.swapaxes(attn_own, 0, 1).reshape(tok, q_width)
    mixed = mm(attn_own, out_full)

    x_rows = f32(x_own)
    branch_one, pull_one = jax.vjp(rms_scale, mixed, gain_vals[1])
    resid = x_rows + branch_one
    normed_two, pull_two = jax.vjp(rms_scale, resid, gain_vals[2])

    tokens_own = bf(normed_two)
    steps = ring_gather(tokens_own)
    cols[1], _ = hold((cols[1], tokens_own))
    w_down_late, _ = hold((w_down, steps[2][0]))
    down_own = quad_place([quad_blocks(w_down_late[None])], 1).reshape(ff_own, width)
    gate_up_own = [quad_blocks(cols[0], tokens_own), quad_blocks(cols[1])]
    gate_up_own = quad_place(gate_up_own, 2).reshape(width, 2 * ff_own)
    tokens = jnp.concatenate(sum(steps, []), axis=0)
    gate_up = mm(tokens, gate_up_own)

    def gated(gate, up_part):
        return jax.nn.gelu(gate, approximate=True) * up_part

    inner = bf(gated(gate_up[:, :ff_own], gate_up[:, ff_own:]))
    late = tokens.shape[0] - 3 * tok
    down = bf(mm(inner, down_own))
    attn_cols = attn_own.reshape(tok, planes, HEADS, w_out.shape[0])
    attn_cols = jnp.transpose(attn_cols, (2, 0, 1, 3)).reshape(HEADS, tok, HEAD_DIM)
    attn_cols, down = hold((attn_cols, down))
    attn_cols = swap(attn_cols, PLANE)
    attn_cols = jnp.pad(attn_cols, ((0, 0), (0, 16), (0, 0))).reshape(-1, HEAD_DIM)
    down = ring_scatter(steps_of((down[:late], down[late:]), tok))
    down, attn_cols = hold((down, attn_cols))
    branch_two, pull_three = jax.vjp(rms_scale, down, gain_vals[3])
    block_out = bf(resid + branch_two)[None]
    grad_top = f32(cotangent[0])
    grad_down_in, gain_grad_three = pull_three(grad_top)
    steps = ring_gather(bf(grad_down_in))
    grad_downs = two_parts(steps)
    grad_gus, parts = ([], [])
    for piece, kept in zip(grad_downs, (gate_up[:late], gate_up[late:])):
        _, pull = jax.vjp(gated, kept[:, :ff_own], kept[:, ff_own:])
        grad_gus.append(bf(jnp.concatenate(pull(mm_nt(piece, down_own)), axis=1)))
        grad_gu, _ = hold((grad_gus[-1], steps[3][0]))
        parts.append(bf(mm_nt(grad_gu, gate_up_own)))
    tokens, inner, grad_downs, grad_gus, parts = hold(
        (tokens, inner, grad_downs, grad_gus, parts)
    )
    grad_normed_two = ring_scatter(steps_of(parts, tok))
    grad_gu_b = jnp.concatenate(grad_gus, axis=0)
    grad_halves = [bf(mm_tn(tokens, grad_gu_b[:, :ff_own])), bf(mm_tn(tokens, grad_gu_b[:, ff_own:]))]
    grad_down_w = bf(mm_tn(inner, jnp.concatenate(grad_downs, axis=0)))
    grad_normed_two, _, _ = hold((grad_normed_two, grad_halves, grad_down_w))
    grad_resid_two, _ = pull_two(grad_normed_two)
    grad_resid = grad_top + grad_resid_two
    grad_mixed, gain_grad_one = pull_one(grad_resid)
    grad_mixed_b = bf(grad_mixed)

    grad_attn = bf(mm_nt(grad_mixed_b, out_full)).reshape(tok, HEADS, HEAD_DIM)
    grad_head = swap(jnp.swapaxes(grad_attn, 0, 1), PLANE).reshape(HEADS * tok, HEAD_DIM)
    grad_head = f32(grad_head)
    rho = bf(grad_head / total)
    delta = jnp.sum(grad_head * attn, axis=-1, keepdims=True) / total
    pulled = mm_nt(rho, value)
    grad_scores = bf((pulled - delta) * weights * (1.0 - (capped / SOFT_CAP) ** 2))
    grad_query = mm(grad_scores, key) * HEAD_DIM ** (-0.5)
    grad_key = mm_tn(grad_scores, query)
    grad_value = mm_tn(weights_b, rho)
    sent = jnp.where(core == 0, grad_value, grad_key)
    grad_half = jnp.where(core == 0, grad_key, grad_value) + flip(sent, "core")
    grad_half = jnp.where(core == 0, unrotary(grad_half, cosine, sine), grad_half)
    grad_qkv = bf(jnp.concatenate([unrotary(grad_query, cosine, sine), grad_half], axis=1))
    others = bf(jnp.stack([gain_grad_one, gain_grad_three]))
    others = jnp.concatenate([grad_mixed_b, jnp.pad(others, ((0, 14), (0, 0)))], axis=0)
    others = lax.all_gather(others, PLANE)
    grad_qkv, others = hold((grad_qkv, others))
    grad_mixed_all = others.reshape(-1, width)
    others = jnp.sum(f32(others[:, tok : tok + 2]), axis=0).reshape(2, planes, HEADS, rows)
    others = lax.dynamic_index_in_dim(others, lax.axis_index(PLANE), 2, keepdims=False)
    others = jnp.swapaxes(others, 0, 1).reshape(planes, 1, 2 * rows)
    others = bf(jnp.pad(others, ((0, 0), (0, 7), (0, 2 * HEAD_DIM - 2 * rows))))
    grad_w = bf(mm_tn(normed_all, grad_qkv))
    grad_qkv, grad_w = hold((grad_qkv, grad_w))
    grad_halves, _ = hold((grad_halves, grad_attn))
    sums = [
        core_sum(v.reshape(group, 4, rows, ff_own), late)
        for v, late in zip(grad_halves, (grad_head, grad_qkv))
    ]
    sums.append(core_sum(grad_down_w.reshape(1, 4, ff_own // 4, width), grad_qkv))
    grad_w = grad_w.reshape(planes, -1, 2 * HEAD_DIM)
    grad_out_w = bf(mm_tn(attn_cols, grad_mixed_all)).reshape(planes, -1, 2 * HEAD_DIM)
    grad_w = jnp.concatenate([grad_w, grad_out_w, others], axis=1)
    grad_w, grad_qkv = hold((grad_w, grad_qkv))
    grad_normed = plane_scatter(bf(mm_nt(grad_qkv, w_own)))
    grad_w = scatter_sum(grad_w, DP)[0]
    grad_halves = [swap(row_sum(sums[0], grad_qkv), LADDER)]
    grad_halves.append(row_sum(sums[1], grad_halves[0]))
    grad_down_w, grad_halves[1] = hold((sums[2], grad_halves[1]))
    grad_down_w = f32(row_sum(grad_down_w)[0])
    others = f32(grad_w[-8, : 2 * rows]).reshape(2, rows)
    grad_out_w = f32(grad_w[HEADS * rows : -8].reshape(w_out.shape))
    grad_w = grad_w[: HEADS * rows].reshape(HEADS, rows, 2 * HEAD_DIM)
    grad_halves[1] = swap(grad_halves[1], LADDER)
    grad_w, grad_halves[1], grad_normed = hold((grad_w, grad_halves[1], grad_normed))
    grad_halves = [jnp.swapaxes(v, 0, 1).reshape(rows, group * ff_own) for v in grad_halves]
    grad_gate_up_w = f32(jnp.concatenate(grad_halves, axis=1))
    _, pull_zero = jax.vjp(rms_scale, x_rows, gain_vals[0])
    grad_x_zero, _ = pull_zero(grad_normed)
    input_grad = (grad_resid + grad_x_zero)[None]
    grad_w = f32(jnp.swapaxes(swap(grad_w, PLANE), 0, 1))
    grad_q_w = grad_w[:, :, :HEAD_DIM].reshape(rows, q_width)
    grad_kv_w = grad_w[:, :, HEAD_DIM:].reshape(rows, KV_HEADS, 2, HEAD_DIM)
    grad_kv_w = jnp.swapaxes(grad_kv_w, 1, 2).reshape(rows, q_width)
    grad_qkv_w = jnp.concatenate([grad_q_w, grad_kv_w], axis=1)

    gain_zero = jnp.sum(f32(w_qkv) * grad_qkv_w, axis=1) / (1.0 + f32(gains[0]))
    gain_two = jnp.sum(f32(w_gate_up) * grad_gate_up_w, axis=1) / (1.0 + f32(gains[2]))
    grad_gains = jnp.stack([gain_zero, others[0], gain_two, others[1]], axis=0)

    return (
        (block_out, input_grad)
        + adam_step(f32(w_qkv), grad_qkv_w, m_qkv, v_qkv, MATRIX_RATE, WEIGHT_DECAY)
        + adam_step(f32(w_out), grad_out_w, m_out, v_out, MATRIX_RATE, WEIGHT_DECAY)
        + adam_step(f32(w_gate_up), grad_gate_up_w, m_gate_up, v_gate_up, MATRIX_RATE, WEIGHT_DECAY)
        + adam_step(f32(w_down), grad_down_w, m_down, v_down, MATRIX_RATE, WEIGHT_DECAY)
        + adam_step(f32(gains), grad_gains, m_gains, v_gains, GAIN_RATE, 0.0)
    )


def token_attention(x_own, pos_own, w_qkv, w_out, gains):
    tok = x_own.shape[0]
    q_width = HEADS * HEAD_DIM
    k_width = KV_HEADS * HEAD_DIM
    groups = HEADS // KV_HEADS
    qkv_full = gather(w_qkv, ALL)
    out_full = gather(w_out, ALL)
    gain_vals = f32(gather(gains, ALL, 1))
    normed = bf(rms_scale(f32(x_own), gain_vals[0]))
    qkv = mm(normed, qkv_full)
    cosine, sine = rotary_tables(pos_own)
    cosine, sine = (cosine[:, None, :], sine[:, None, :])
    query = rotary(qkv[:, :q_width].reshape(tok, HEADS, HEAD_DIM), cosine, sine)
    query = bf(query * HEAD_DIM ** (-0.5)).reshape(tok, KV_HEADS, groups, HEAD_DIM)
    key_own = qkv[:, q_width : q_width + k_width].reshape(tok, KV_HEADS, HEAD_DIM)
    key = gather(bf(rotary(key_own, cosine, sine)), PLANE)
    value = gather(bf(qkv[:, q_width + k_width :]).reshape(tok, KV_HEADS, HEAD_DIM), PLANE)
    pos_all = gather(pos_own, PLANE)
    count = pos_all.shape[0]
    scores = jnp.einsum("tgjd,sgd->gjts", query, key, preferred_element_type=jnp.float32)
    capped = SOFT_CAP * jnp.tanh(scores / SOFT_CAP)
    weights = jnp.where(pos_own[:, None] >= pos_all[None, :], jnp.exp(capped), 0.0)
    weights_b = bf(weights)
    total = jnp.sum(weights, axis=-1)
    attn = jnp.einsum("gjts,sgd->gjtd", weights_b, value, preferred_element_type=jnp.float32)
    attn = attn / total[..., None]
    attn_b = bf(jnp.transpose(attn, (2, 0, 1, 3)).reshape(tok, q_width))
    mixed = mm(attn_b, out_full)

    def backward(grad_mixed_b):
        grad_attn = mm_nt(grad_mixed_b, out_full).reshape(tok, KV_HEADS, groups, HEAD_DIM)
        grad_heads = jnp.transpose(grad_attn, (1, 2, 0, 3))
        rho = bf(grad_heads / total[..., None])
        delta = jnp.sum(grad_heads * attn, axis=-1) / total
        pulled = jnp.einsum("gjtd,sgd->gjts", rho, value, preferred_element_type=jnp.float32)
        grad_scores = bf(
            (pulled - delta[..., None]) * weights * (1.0 - (capped / SOFT_CAP) ** 2)
        )
        grad_query = jnp.einsum(
            "gjts,sgd->tgjd", grad_scores, key, preferred_element_type=jnp.float32
        ).reshape(tok, HEADS, HEAD_DIM)
        grad_key = jnp.einsum(
            "gjts,tgjd->sgd", grad_scores, query, preferred_element_type=jnp.float32
        ).reshape(count, k_width)
        grad_value = jnp.einsum(
            "gjts,gjtd->sgd", weights_b, rho, preferred_element_type=jnp.float32
        ).reshape(count, k_width)
        grad_kv = scatter_sum(jnp.concatenate([grad_key, grad_value], axis=1), PLANE)
        grad_query = unrotary(grad_query * HEAD_DIM ** (-0.5), cosine, sine)
        grad_key = unrotary(grad_kv[:, :k_width].reshape(tok, KV_HEADS, HEAD_DIM), cosine, sine)
        grad_qkv = bf(
            jnp.concatenate(
                [
                    grad_query.reshape(tok, q_width),
                    grad_key.reshape(tok, k_width),
                    grad_kv[:, k_width:],
                ],
                axis=1,
            )
        )
        grad_normed = mm_nt(grad_qkv, qkv_full)
        grad_qkv_w = f32(scatter_sum(bf(mm_tn(normed, grad_qkv)), ALL))
        grad_out_w = f32(scatter_sum(bf(mm_tn(attn_b, grad_mixed_b)), ALL))
        return grad_normed, grad_qkv_w, grad_out_w

    return mixed, gain_vals, backward


def wide_shards(
    hidden_in,
    positions,
    cotangent,
    w_qkv,
    w_out,
    w_gate_up,
    w_down,
    gains,
    m_qkv,
    v_qkv,
    m_out,
    v_out,
    m_gate_up,
    v_gate_up,
    m_down,
    v_down,
    m_gains,
    v_gains,
):
    x_own = hidden_in[0]
    rows, width = (w_qkv.shape[0], x_own.shape[1])
    group, across = (lax.axis_size(GROUP), lax.axis_size(ACROSS))
    ff_piece = w_down.shape[0]
    ff_own = across * ff_piece
    gu_pieces = w_gate_up.reshape(rows, 2, across, group, ff_piece)
    gu_pieces = jnp.transpose(gu_pieces, (3, 0, 1, 2, 4)).reshape(group * rows, 2 * ff_own)

    mixed, gain_vals, attention_back = token_attention(x_own, positions[0], w_qkv, w_out, gains)
    gu_own = gather(swap(gu_pieces, GROUP), ACROSS)
    down_own = gather(w_down, ACROSS)

    x_rows = f32(x_own)
    branch_one, pull_one = jax.vjp(rms_scale, mixed, gain_vals[1])
    resid = x_rows + branch_one
    normed_two, pull_two = jax.vjp(rms_scale, resid, gain_vals[2])
    tokens_b = gather(bf(normed_two), GROUP)
    gate_up = mm(tokens_b, gu_own)
    inner, pull_gelu = jax.vjp(
        lambda gate, up_part: jax.nn.gelu(gate, approximate=True) * up_part,
        gate_up[:, :ff_own],
        gate_up[:, ff_own:],
    )
    inner_b = bf(inner)
    down = f32(scatter_sum(bf(mm(inner_b, down_own)), GROUP))
    branch_two, pull_three = jax.vjp(rms_scale, down, gain_vals[3])
    block_out = bf(resid + branch_two)[None]
    grad_top = f32(cotangent[0])
    grad_down_in, gain_grad_three = pull_three(grad_top)
    grad_down_b = gather(bf(grad_down_in), GROUP)
    grad_gate, grad_up = pull_gelu(mm_nt(grad_down_b, down_own))
    grad_gu_b = bf(jnp.concatenate([grad_gate, grad_up], axis=1))
    grad_normed_two = f32(scatter_sum(bf(mm_nt(grad_gu_b, gu_own)), GROUP))
    grad_gate_up_w = scatter_sum(bf(mm_tn(tokens_b, grad_gu_b)), ACROSS)
    grad_down_w = f32(scatter_sum(bf(mm_tn(inner_b, grad_down_b)), ACROSS))

    grad_resid_two, gain_grad_two = pull_two(grad_normed_two)
    grad_resid = grad_top + grad_resid_two
    grad_mixed, gain_grad_one = pull_one(grad_resid)
    grad_normed, grad_qkv_w, grad_out_w = attention_back(bf(grad_mixed))
    _, pull_zero = jax.vjp(rms_scale, x_rows, gain_vals[0])
    grad_x_zero, gain_grad_zero = pull_zero(grad_normed)
    input_grad = (grad_resid + grad_x_zero)[None]

    grad_gate_up_w = swap(grad_gate_up_w, GROUP).reshape(group, rows, 2, across, ff_piece)
    grad_gate_up_w = f32(jnp.transpose(grad_gate_up_w, (1, 2, 3, 0, 4)).reshape(rows, -1))
    gain_term = jnp.stack([gain_grad_zero, gain_grad_one, gain_grad_two, gain_grad_three], axis=0)
    grad_gains = lax.psum_scatter(gain_term, ALL, scatter_dimension=1, tiled=True)

    return (
        (block_out, input_grad)
        + adam_step(f32(w_qkv), grad_qkv_w, m_qkv, v_qkv, MATRIX_RATE, WEIGHT_DECAY)
        + adam_step(f32(w_out), grad_out_w, m_out, v_out, MATRIX_RATE, WEIGHT_DECAY)
        + adam_step(f32(w_gate_up), grad_gate_up_w, m_gate_up, v_gate_up, MATRIX_RATE, WEIGHT_DECAY)
        + adam_step(f32(w_down), grad_down_w, m_down, v_down, MATRIX_RATE, WEIGHT_DECAY)
        + adam_step(f32(gains), grad_gains, m_gains, v_gains, GAIN_RATE, 0.0)
    )


def solution(mesh):
    sizes = dict(mesh.shape)
    fine = Mesh(
        mesh.devices.reshape(sizes["dp"] // 2, 2, sizes["ctx"], sizes["fsdp"] // 2, 2),
        ("dh", "dl", "ctx", "fy", "core"),
    )
    acts = P(DP, PLANE, None)
    mats = P(ALL, None)
    vecs = P(None, ALL)
    ladder = sizes["dp"] == 4 and sizes["ctx"] == 2 and sizes["fsdp"] == 4
    return jax.shard_map(
        ladder_shards if ladder else wide_shards,
        mesh=fine,
        in_specs=(acts, P(DP, PLANE), acts) + (mats,) * 4 + (vecs,) + (mats,) * 8 + (vecs,) * 2,
        out_specs=(acts, acts) + (mats,) * 12 + (vecs,) * 3,
        check_vma=False,
    )
```
